32 devices in a mesh: dp: 4 (over z), blk: 8 (over y, x, core).
Axes of the slice: x: 2, y: 2, z: 4, core: 2. Of those that a mesh axis runs over, the one named last changes fastest.
Arguments:
- tokens: bfloat16 [8, 2048, 1024], P('dp', 'blk'), may hold values from -6 to 6
- doc_lengths: int32 [8, 8], P('dp'), may hold values from 1 to 1793, 2048 in all within a row
- g_attn: float32 [1024], replicated, may hold values from 0.5 to 1.5
- w_query: bfloat16 [1024, 1024], replicated, may hold values from -0.1875 to 0.1875
- w_key: bfloat16 [1024, 512], replicated, may hold values from -0.1875 to 0.1875
- w_value: bfloat16 [1024, 512], replicated, may hold values from -0.1875 to 0.1875
- q_gain: float32 [64], replicated, may hold values from 0.1 to 1.9
- k_gain: float32 [64], replicated, may hold values from 0.1 to 1.9
- w_out: bfloat16 [1024, 1024], replicated, may hold values from -1 to 1
- g_ffn: float32 [1024], replicated, may hold values from 0.5 to 1.5
- w_gate: bfloat16 [1024, 4608], replicated, may hold values from -0.1875 to 0.1875
- w_up: bfloat16 [1024, 4608], replicated, may hold values from -0.1875 to 0.1875
- w_down: bfloat16 [4608, 1024], replicated, may hold values from -0.09375 to 0.09375
- cotangent: bfloat16 [8, 2048, 1024], P('dp', 'blk'), may hold values from -6 to 6
Outputs:
- output: bfloat16 [8, 2048, 1024], P('dp', 'blk')
- input_grad: bfloat16 [8, 2048, 1024], P('dp', 'blk')
- grad_g_attn: float32 [1024], replicated
- grad_w_query: float32 [1024, 1024], P(('dp', 'blk'))
- grad_w_key: float32 [1024, 512], P(('dp', 'blk'))
- grad_w_value: float32 [1024, 512], P(('dp', 'blk'))
- grad_q_gain: float32 [64], replicated
- grad_k_gain: float32 [64], replicated
- grad_w_out: float32 [1024, 1024], P(('dp', 'blk'))
- grad_g_ffn: float32 [1024], replicated
- grad_w_gate: float32 [1024, 4608], P(('dp', 'blk'))
- grad_w_up: float32 [1024, 4608], P(('dp', 'blk'))
- grad_w_down: float32 [4608, 1024], P(('dp', 'blk'))
The draws below stay inside these ranges and needn't reach their ends.
Inputs may be any that keep to these rules, and one draw needn't show every extreme that they name: `doc_lengths`: in each sequence the lengths sum to 2048, and one document has exactly 1793 tokens.
All inputs are finite; a program needn't handle non-finite values.
Results may differ from the reference program's by a relative error of at most 0.02.
Values may be sent and summed in bfloat16 or wider, within the bound.
A program may use at most 384 MiB of HBM per device.

```python
import math
import jax
import jax.numpy as jnp
import numpy as np
from jax import lax

D = 1024
HEADS = 16
KV_HEADS = 8
HEAD_DIM = 64
FF = 4608
DOCS = 8
TOK_ROW = 256
SEQ_LEN = 2048
ROWS = 8


def levels(key, dims, shards, least, largest):
    def one(position, shards_of):
        draws = jax.random.uniform(jax.random.fold_in(jax.random.fold_in(key, 6), position), (shards_of,), jnp.float32, least / len(shards), largest / len(shards))
        return jnp.repeat(jnp.exp(draws), dims[position] // shards_of).reshape((-1,) + (1,) * (len(dims) - position - 1))

    gain = one(*shards[0])
    for cut in shards[1:]:
        gain = gain * one(*cut)
    return gain


def split_up(count, total, bound, slope):
    loads = [(1 << 20) // math.isqrt(standing ** slope) + 1 for standing in range(2, count + 1)]
    spare, given = total - bound - (count - 1), [1] * (count - 1)
    while spare > 0:
        movable = [i for i in range(count - 1) if given[i] < bound]
        whole, left = sum([loads[i] for i in movable]), spare
        for i in movable:
            addition = min(bound - given[i], max(1, left * loads[i] // whole), spare)
            given[i] = given[i] + addition
            spare = spare - addition
    return np.array([bound] + given)


def ragged_sizes(key, amount, total, limit, slope):
    if amount == 2:
        one = jax.random.randint(key, (), max(1, total - limit), min(limit, total - 1) + 1)
        return jnp.stack([one, total - one])
    sizes = jnp.asarray(split_up(amount, total, limit, slope), jnp.int32)
    couples = (amount - 1) // 2
    donor, sink = sizes[1:1 + 2 * couples:2], sizes[2:2 + 2 * couples:2]
    room = jnp.minimum(donor - 1, limit - sink)
    shifted = jax.random.randint(jax.random.fold_in(key, 1), (couples,), 0, 1 << 20) % (room + 1)
    sizes = sizes.at[1:1 + 2 * couples:2].set(donor - shifted).at[2:2 + 2 * couples:2].set(sink + shifted)
    return sizes[jax.random.permutation(jax.random.fold_in(key, 2), amount)]


def noise(own_key, extent, spread, bound, pieces=(), kind=jnp.bfloat16):
    drawn = jax.random.normal(own_key, extent, jnp.float32) * spread
    if len(pieces) > 0:
        drawn = levels(own_key, extent, pieces, -0.22, 0.18) * drawn
    return jnp.clip(drawn, min=-bound, max=bound).astype(kind)


def setup_inputs(seed: int = 0) -> dict:
    seeds = jax.random.split(jax.random.key(seed), 15)
    tokens = noise(seeds[0], (ROWS, SEQ_LEN, D), 1.0, 6.0, ((0, 4), (1, 8)))
    doc_lengths = jax.vmap(lambda own: ragged_sizes(own, DOCS, SEQ_LEN, SEQ_LEN - TOK_ROW + 1, 2))(jax.random.split(seeds[1], ROWS)).reshape((ROWS, DOCS)).astype(jnp.int32)
    g_attn = jnp.clip(1.0 + 0.1 * jax.random.normal(seeds[2], (D,), jnp.float32), 0.5, 1.5)
    w_query = noise(seeds[3], (D, HEADS * HEAD_DIM), D ** -0.5, 0.1875)
    w_key = noise(seeds[4], (D, KV_HEADS * HEAD_DIM), D ** -0.5, 0.1875)
    w_value = noise(seeds[5], (D, KV_HEADS * HEAD_DIM), D ** -0.5, 0.1875)
    q_gain = jnp.clip(1.0 + 0.18 * jax.random.normal(seeds[6], (HEAD_DIM,), jnp.float32), 0.1, 1.9)
    k_gain = jnp.clip(1.0 + 0.18 * jax.random.normal(seeds[7], (HEAD_DIM,), jnp.float32), 0.1, 1.9)
    w_out = noise(seeds[8], (HEADS * HEAD_DIM, D), (D // 32) ** -0.5, 1.0)
    g_ffn = jnp.clip(1.0 + 0.1 * jax.random.normal(seeds[9], (D,), jnp.float32), 0.5, 1.5)
    w_gate = noise(seeds[10], (D, FF), D ** -0.5, 0.1875)
    w_up = noise(seeds[11], (D, FF), D ** -0.5, 0.1875)
    w_down = noise(seeds[12], (FF, D), FF ** -0.5, 0.09375)
    cotangent = noise(seeds[13], (ROWS, SEQ_LEN, D), 1.0, 6.0, ((0, 4), (1, 8)))
    return {"tokens": tokens, "doc_lengths": doc_lengths, "g_attn": g_attn, "w_query": w_query, "w_key": w_key, "w_value": w_value, "q_gain": q_gain, "k_gain": k_gain, "w_out": w_out, "g_ffn": g_ffn, "w_gate": w_gate, "w_up": w_up, "w_down": w_down, "cotangent": cotangent}


EPSILON = 1e-05
ROPE_BASE = 1000000.0

@jax.custom_vjp
def low(v):
    return lax.optimization_barrier(v.astype(jnp.bfloat16)).astype(jnp.float32)

@jax.custom_vjp
def low_back(v):
    return v

def low_keep(v):
    return (low(v), None)

def low_pass(kept, grad):
    return (grad,)

def back_keep(v):
    return (v, None)

def back_low(kept, grad):
    return (low(grad),)
low.defvjp(low_keep, low_pass)
low_back.defvjp(back_keep, back_low)

def hi_dot(left, right):
    return jnp.dot(left, right, precision=lax.Precision.HIGHEST)

def rms(values, norm_gain):
    return values * lax.rsqrt(lax.optimization_barrier(jnp.mean(values * values, axis=-1, keepdims=True)) + EPSILON) * norm_gain

def doc_layout(lengths, places):
    ends = jnp.cumsum(lengths).astype(jnp.int32)
    past = places[:, None] >= ends[None, :]
    docs = lax.optimization_barrier(jnp.sum(past.astype(jnp.int32), axis=1)).astype(jnp.int32)
    before = lax.optimization_barrier(jnp.sum(jnp.where(past, lengths[None, :], 0), axis=1)).astype(jnp.int32)
    return (docs, places - before)

def rotate(values, cosine, sine):
    half = values.shape[-1] // 2
    first_half = values[..., :half]
    second_half = values[..., half:]
    cos_col = cosine[:, None, :]
    sin_col = sine[:, None, :]
    return jnp.concatenate([first_half * cos_col - second_half * sin_col, second_half * cos_col + first_half * sin_col], axis=-1)

def attention(queries, keys, values, places, docs):
    total = queries.shape[0]
    block = min(512, total)
    grouping = HEADS // KV_HEADS
    key_heads = jnp.repeat(keys, grouping, axis=1)
    value_heads = jnp.repeat(values, grouping, axis=1)
    softmax_scale = HEAD_DIM ** (-0.5)

    def one_block(blocked):
        query_block, query_places, query_docs = blocked
        raw_scores = jnp.einsum('qhd,khd->hqk', query_block, key_heads, precision=lax.Precision.HIGHEST) * softmax_scale
        raw_scores = low_back(raw_scores)
        allowed = (places[None, :] <= query_places[:, None]) & (docs[None, :] == query_docs[:, None])
        scores = jnp.where(allowed[None], raw_scores, -1e+30)
        highest = lax.optimization_barrier(jnp.max(scores, axis=-1, keepdims=True))
        weights = jnp.exp(scores - highest)
        probs = weights / lax.optimization_barrier(jnp.sum(weights, axis=-1, keepdims=True))
        return jnp.einsum('hqk,khd->qhd', low(probs), value_heads, precision=lax.Precision.HIGHEST)
    blocked_in = (queries.reshape(total // block, block, HEADS, HEAD_DIM), places.reshape(total // block, block), docs.reshape(total // block, block))
    result = lax.map(jax.checkpoint(one_block), blocked_in)
    return result.reshape(total, HEADS, HEAD_DIM)

def layer(inputs, weights, lengths):
    g_attn, w_query, w_key, w_value, q_gain, k_gain, w_out, g_ffn, w_gate, w_up, w_down = weights
    total = inputs.shape[0]
    places = jnp.arange(total, dtype=jnp.int32)
    docs, positions = doc_layout(lengths, places)
    half = HEAD_DIM // 2
    freqs = ROPE_BASE ** (-jnp.arange(half, dtype=jnp.float32) / half)
    angles = positions.astype(jnp.float32)[:, None] * freqs[None, :]
    cosine = jnp.cos(angles)
    sine = jnp.sin(angles)
    hidden_in = low(rms(inputs, g_attn))
    query_proj = low_back(hi_dot(hidden_in, w_query)).reshape(total, HEADS, HEAD_DIM)
    key_proj = low_back(hi_dot(hidden_in, w_key)).reshape(total, KV_HEADS, HEAD_DIM)
    value_b = low(low_back(hi_dot(hidden_in, w_value))).reshape(total, KV_HEADS, HEAD_DIM)
    query_b = low(rotate(rms(query_proj, q_gain), cosine, sine))
    key_b = low(rotate(rms(key_proj, k_gain), cosine, sine))
    attended = attention(query_b, key_b, value_b, places, docs)
    attended = low(low_back(attended)).reshape(total, HEADS * HEAD_DIM)
    middle = inputs + low_back(hi_dot(attended, w_out))
    hidden_ffn = low(rms(middle, g_ffn))
    gate = low_back(hi_dot(hidden_ffn, w_gate))
    up_proj = low_back(hi_dot(hidden_ffn, w_up))
    hidden = low(jax.nn.silu(gate) * up_proj)
    return middle + low_back(hi_dot(hidden, w_down))

def reference(tokens, doc_lengths, g_attn, w_query, w_key, w_value, q_gain, k_gain, w_out, g_ffn, w_gate, w_up, w_down, cotangent):
    weights = tuple((item.astype(jnp.float32) for item in (g_attn, w_query, w_key, w_value, q_gain, k_gain, w_out, g_ffn, w_gate, w_up, w_down)))

    def one_row(sums, row_data):
        token_row, length_row, cot_row = row_data
        inputs = token_row.astype(jnp.float32)
        result, pullback = jax.vjp(lambda inside, params: layer(inside, params, length_row), inputs, weights)
        grad_in, grad_params = pullback(cot_row.astype(jnp.float32))
        sums = jax.tree.map(lambda left, right: left + right, sums, grad_params)
        return (sums, (result.astype(jnp.bfloat16), grad_in.astype(jnp.bfloat16)))
    zeros = tuple((jnp.zeros(item.shape, jnp.float32) for item in weights))
    sums, (results, grads_in) = lax.scan(one_row, zeros, (tokens, doc_lengths, cotangent))
    return (results, grads_in, sums[0], sums[1], sums[2], sums[3], sums[4], sums[5], sums[6], sums[7], sums[8], sums[9], sums[10])
```

```python
import functools
import math

import jax
import jax.numpy as jnp
from jax import lax
from jax.experimental import pallas as pl
from jax.experimental.pallas import tpu as pltpu
from jax.sharding import PartitionSpec as P

HEADS = 16
KV_HEADS = 8
HEAD_DIM = 64


EPSILON = 1e-05
ROPE_BASE = 1000000.0
NEGATIVE = -1e30


def norm_rows(values, norm_gain):
    row_scale = lax.rsqrt(jnp.mean(values * values, axis=-1, keepdims=True) + EPSILON)
    normal = values * row_scale
    return (normal * norm_gain, normal, row_scale)


def norm_back(normal, row_scale, norm_gain, grad_out):
    pushed = grad_out * norm_gain
    inner = jnp.mean(pushed * normal, axis=-1, keepdims=True)
    grad_in = row_scale * (pushed - normal * inner)
    leading = tuple(range(grad_out.ndim - 1))
    return (grad_in, jnp.sum(grad_out * normal, axis=leading))


def doc_layout(lengths, places):
    ends = jnp.cumsum(lengths, axis=1)
    past = places[None, :, None] >= ends[:, None, :]
    docs = jnp.sum(past.astype(jnp.int32), axis=2)
    before = jnp.sum(jnp.where(past, lengths[:, None, :], 0), axis=2)
    return (docs, places[None, :] - before)


def rope_angles(positions):
    half = HEAD_DIM // 2
    freqs = ROPE_BASE ** (-jnp.arange(half, dtype=jnp.float32) / half)
    angles = positions.astype(jnp.float32)[..., None] * freqs
    return (jnp.cos(angles), jnp.sin(angles))


def rotate(values, cosine, sine):
    half = values.shape[-1] // 2
    first_half = values[..., :half]
    second_half = values[..., half:]
    cos_col = cosine[:, :, None, :]
    sin_col = sine[:, :, None, :]
    return jnp.concatenate(
        [
            first_half * cos_col - second_half * sin_col,
            second_half * cos_col + first_half * sin_col,
        ],
        axis=-1,
    )


def local(
    tokens,
    doc_lengths,
    g_attn,
    w_query,
    w_key,
    w_value,
    q_gain,
    k_gain,
    w_out,
    g_ffn,
    w_gate,
    w_up,
    w_down,
    cotangent,
):
    row_count, tok_count, width = tokens.shape
    grouping = HEADS // KV_HEADS
    flat_rows = row_count * tok_count
    kv_width = KV_HEADS * HEAD_DIM
    softmax_scale = HEAD_DIM ** (-0.5)
    places = lax.axis_index("blk") * tok_count + jnp.arange(tok_count, dtype=jnp.int32)
    query_docs, query_pos = doc_layout(doc_lengths, places)
    cosine, sine = rope_angles(query_pos)
    inputs = tokens.reshape(flat_rows, width).astype(jnp.float32)
    normed, normal_in, scale_in = norm_rows(inputs, g_attn)
    hidden_in = normed.astype(jnp.bfloat16)
    query_proj = jnp.dot(hidden_in, w_query, preferred_element_type=jnp.float32).reshape(
        row_count, tok_count, HEADS, HEAD_DIM
    )
    key_proj = jnp.dot(hidden_in, w_key, preferred_element_type=jnp.float32).reshape(
        row_count, tok_count, KV_HEADS, HEAD_DIM
    )
    value_b = (
        jnp.dot(hidden_in, w_value, preferred_element_type=jnp.float32)
        .astype(jnp.bfloat16)
        .reshape(row_count, tok_count, kv_width)
    )
    query_norm, query_normal, query_scale = norm_rows(query_proj, q_gain)
    key_norm, key_normal, key_scale = norm_rows(key_proj, k_gain)
    query_b = (
        rotate(query_norm, cosine, sine)
        .astype(jnp.bfloat16)
        .reshape(row_count, tok_count, KV_HEADS, grouping, HEAD_DIM)
    )
    key_b = (
        rotate(key_norm, cosine, sine).astype(jnp.bfloat16).reshape(row_count, tok_count, kv_width)
    )

    def piece_mask(size):
        key_places = jnp.arange(size, dtype=jnp.int32)
        key_docs, unused = doc_layout(doc_lengths, key_places)
        return (key_places[None, None, :] <= places[None, :, None]) & (
            key_docs[:, None, :] == query_docs[:, :, None]
        )

    def piece_scores(key_piece, allowed):
        key_heads = key_piece.reshape(row_count, key_piece.shape[1], KV_HEADS, HEAD_DIM)
        raw_scores = (
            jnp.einsum("rqkgd,rpkd->rkgqp", query_b, key_heads, preferred_element_type=jnp.float32)
            * softmax_scale
        )
        return (jnp.where(allowed[:, None, None], raw_scores, -jnp.inf), key_heads)

    stat_shape = (row_count, KV_HEADS, grouping, tok_count)
    key_piece = lax.all_gather(key_b, "blk", axis=1, tiled=True)
    value_piece = lax.all_gather(value_b, "blk", axis=1, tiled=True)
    allowed = piece_mask(key_piece.shape[1])
    running_max = jnp.full(stat_shape, NEGATIVE, jnp.float32)
    scores, key_heads = piece_scores(key_piece, allowed)
    new_max = jnp.maximum(running_max, jnp.max(scores, axis=-1))
    weights = jnp.exp(scores - new_max[..., None])
    value_heads = value_piece.reshape(row_count, value_piece.shape[1], KV_HEADS, HEAD_DIM)
    added = jnp.einsum(
        "rkgqp,rpkd->rkgqd",
        weights.astype(jnp.bfloat16),
        value_heads,
        preferred_element_type=jnp.float32,
    )
    running_sum = jnp.sum(weights, axis=-1)
    attended = added / running_sum[..., None]
    log_total = new_max + jnp.log(running_sum)
    attended_b = (
        jnp.transpose(attended, (0, 3, 1, 2, 4))
        .reshape(flat_rows, HEADS * HEAD_DIM)
        .astype(jnp.bfloat16)
    )
    middle = inputs + jnp.dot(attended_b, w_out, preferred_element_type=jnp.float32)
    normed_ffn, normal_ffn, scale_ffn = norm_rows(middle, g_ffn)
    hidden_ffn = normed_ffn.astype(jnp.bfloat16)
    gate = jnp.dot(hidden_ffn, w_gate, preferred_element_type=jnp.float32)
    up_proj = jnp.dot(hidden_ffn, w_up, preferred_element_type=jnp.float32)
    sigmoid_gate = jax.nn.sigmoid(gate)
    silu_gate = gate * sigmoid_gate
    hidden = (silu_gate * up_proj).astype(jnp.bfloat16)
    result = middle + jnp.dot(hidden, w_down, preferred_element_type=jnp.float32)
    output = result.astype(jnp.bfloat16).reshape(row_count, tok_count, width)
    grad_out = cotangent.reshape(flat_rows, width)
    grad_w_down = jnp.einsum("tf,td->fd", hidden, grad_out, preferred_element_type=jnp.float32)
    grad_hidden = jnp.einsum("td,fd->tf", grad_out, w_down, preferred_element_type=jnp.float32)
    grad_gate = (grad_hidden * up_proj * sigmoid_gate * (1.0 + gate * (1.0 - sigmoid_gate))).astype(
        jnp.bfloat16
    )
    grad_up = (grad_hidden * silu_gate).astype(jnp.bfloat16)
    grad_w_gate = jnp.einsum("td,tf->df", hidden_ffn, grad_gate, preferred_element_type=jnp.float32)
    grad_w_up = jnp.einsum("td,tf->df", hidden_ffn, grad_up, preferred_element_type=jnp.float32)
    grad_h2 = jnp.einsum(
        "tf,df->td", grad_gate, w_gate, preferred_element_type=jnp.float32
    ) + jnp.einsum("tf,df->td", grad_up, w_up, preferred_element_type=jnp.float32)
    grad_mid, grad_ffn_gain = norm_back(normal_ffn, scale_ffn, g_ffn, grad_h2)
    grad_mid = grad_out.astype(jnp.float32) + grad_mid
    grad_attn = grad_mid.astype(jnp.bfloat16)
    grad_w_out = jnp.einsum("tc,td->cd", attended_b, grad_attn, preferred_element_type=jnp.float32)
    grad_attended = jnp.einsum(
        "td,cd->tc", grad_attn, w_out, preferred_element_type=jnp.float32
    ).astype(jnp.bfloat16)
    grad_heads = grad_attended.reshape(row_count, tok_count, KV_HEADS, grouping, HEAD_DIM)
    deltas = jnp.einsum("rqkgd,rkgqd->rkgq", grad_heads.astype(jnp.float32), attended)
    key_piece = lax.all_gather(key_b, "blk", axis=1, tiled=True)
    value_piece = lax.all_gather(value_b, "blk", axis=1, tiled=True)
    size = key_piece.shape[1]
    allowed = piece_mask(size)
    scores, key_heads = piece_scores(key_piece, allowed)
    probs = jnp.exp(scores - log_total[..., None])
    value_heads = value_piece.reshape(row_count, size, KV_HEADS, HEAD_DIM)
    value_piece_grad = jnp.einsum(
        "rkgqp,rqkgd->rpkd",
        probs.astype(jnp.bfloat16),
        grad_heads,
        preferred_element_type=jnp.float32,
    )
    grad_probs = jnp.einsum(
        "rqkgd,rpkd->rkgqp", grad_heads, value_heads, preferred_element_type=jnp.float32
    )
    grad_scores = (probs * (grad_probs - deltas[..., None])).astype(jnp.bfloat16)
    grad_query = jnp.einsum(
        "rkgqp,rpkd->rkgqd", grad_scores, key_heads, preferred_element_type=jnp.float32
    )
    key_piece_grad = jnp.einsum(
        "rkgqp,rqkgd->rpkd", grad_scores, query_b, preferred_element_type=jnp.float32
    )
    grad_keys = key_piece_grad.reshape(row_count, size, kv_width)
    grad_values = value_piece_grad.reshape(row_count, size, kv_width)
    grad_query, grad_keys, grad_values = (grad_query, grad_keys, grad_values)
    key_grad_mine, value_grad_mine = (
        lax.psum_scatter(
            grad_keys.astype(jnp.bfloat16), "blk", scatter_dimension=1, tiled=True
        ).astype(jnp.float32),
        lax.psum_scatter(
            grad_values.astype(jnp.bfloat16), "blk", scatter_dimension=1, tiled=True
        ).astype(jnp.float32),
    )
    grad_q_rot = (jnp.transpose(grad_query, (0, 3, 1, 2, 4)) * softmax_scale).reshape(
        row_count, tok_count, HEADS, HEAD_DIM
    )
    grad_k_rot = (key_grad_mine * softmax_scale).reshape(row_count, tok_count, KV_HEADS, HEAD_DIM)
    grad_q_proj, grad_query_gain = norm_back(
        query_normal, query_scale, q_gain, rotate(grad_q_rot, cosine, -sine)
    )
    grad_k_proj, grad_key_gain = norm_back(
        key_normal, key_scale, k_gain, rotate(grad_k_rot, cosine, -sine)
    )
    grad_q_b = grad_q_proj.astype(jnp.bfloat16).reshape(flat_rows, HEADS * HEAD_DIM)
    grad_k_b = grad_k_proj.astype(jnp.bfloat16).reshape(flat_rows, kv_width)
    grad_v_b = value_grad_mine.astype(jnp.bfloat16).reshape(flat_rows, kv_width)
    grad_w_query = jnp.einsum("td,tc->dc", hidden_in, grad_q_b, preferred_element_type=jnp.float32)
    grad_w_key = jnp.einsum("td,tc->dc", hidden_in, grad_k_b, preferred_element_type=jnp.float32)
    grad_w_value = jnp.einsum("td,tc->dc", hidden_in, grad_v_b, preferred_element_type=jnp.float32)
    grad_h1 = jnp.einsum("tc,dc->td", grad_q_b, w_query, preferred_element_type=jnp.float32)
    grad_h1 = grad_h1 + jnp.einsum("tc,dc->td", grad_k_b, w_key, preferred_element_type=jnp.float32)
    grad_h1 = grad_h1 + jnp.einsum(
        "tc,dc->td", grad_v_b, w_value, preferred_element_type=jnp.float32
    )
    grad_base, grad_attn_gain = norm_back(normal_in, scale_in, g_attn, grad_h1)
    input_grad = (grad_mid + grad_base).astype(jnp.bfloat16).reshape(row_count, tok_count, width)
    gain_attn, gain_query, gain_key, gain_ffn = lax.psum(
        (grad_attn_gain, grad_query_gain, grad_key_gain, grad_ffn_gain), ("dp", "blk")
    )
    locals_all = (
        grad_w_query,
        grad_w_key,
        grad_w_value,
        grad_w_out,
        grad_w_gate,
        grad_w_up,
        grad_w_down,
    )
    shared = (
        lax.psum_scatter(locals_all[0], ("dp", "blk"), scatter_dimension=0, tiled=True),
        lax.psum_scatter(locals_all[1], ("dp", "blk"), scatter_dimension=0, tiled=True),
        lax.psum_scatter(locals_all[2], ("dp", "blk"), scatter_dimension=0, tiled=True),
        lax.psum_scatter(locals_all[3], ("dp", "blk"), scatter_dimension=0, tiled=True),
        lax.psum_scatter(locals_all[4], ("dp", "blk"), scatter_dimension=0, tiled=True),
        lax.psum_scatter(locals_all[5], ("dp", "blk"), scatter_dimension=0, tiled=True),
        lax.psum_scatter(locals_all[6], ("dp", "blk"), scatter_dimension=0, tiled=True),
    )
    return (
        output,
        input_grad,
        gain_attn,
        shared[0],
        shared[1],
        shared[2],
        gain_query,
        gain_key,
        shared[3],
        gain_ffn,
        shared[4],
        shared[5],
        shared[6],
    )


BF16 = jnp.bfloat16
F32 = jnp.float32
LANES = 128
FF_TILE = 256
FFN_CALLS = 3
VMEM_BYTES = 56 * 1024 * 1024
LOG2_E = math.log2(math.e)
QUERY_SCALE = HEAD_DIM ** (-0.5) * LOG2_E
MASKED = -1e30


def nn_dot(left, right):
    return lax.dot_general(left, right, (((1,), (0,)), ((), ())), preferred_element_type=F32)


def nt_dot(left, right):
    return lax.dot_general(left, right, (((1,), (1,)), ((), ())), preferred_element_type=F32)


def tn_dot(left, right):
    return lax.dot_general(left, right, (((0,), (0,)), ((), ())), preferred_element_type=F32)


def kernel_params(**more):
    return pltpu.CompilerParams(vmem_limit_bytes=VMEM_BYTES, **more)


def whole_block(shape):
    return pl.BlockSpec(shape, lambda *ids: (0,) * len(shape))


def swap_blocks_kernel(send_ref, out_ref, send_sem, recv_sem, own_sem):
    count = send_ref.shape[0]
    mine = lax.axis_index("blk")
    group = lax.axis_index("dp")
    barrier = pltpu.get_barrier_semaphore()
    for step in range(1, count):
        pl.semaphore_signal(
            barrier,
            inc=1,
            device_id=(group, lax.rem(mine + step, count)),
            device_id_type=pl.DeviceIdType.MESH,
        )
    pl.semaphore_wait(barrier, count - 1)
    copies = []
    for step in range(1, count):
        target = lax.rem(mine + step, count)
        copy = pltpu.make_async_remote_copy(
            src_ref=send_ref.at[target],
            dst_ref=out_ref.at[mine],
            send_sem=send_sem.at[step],
            recv_sem=recv_sem.at[step],
            device_id=(group, target),
            device_id_type=pl.DeviceIdType.MESH,
        )
        copy.start()
        copies.append(copy)
    own = pltpu.make_async_copy(send_ref.at[mine], out_ref.at[mine], own_sem)
    own.start()
    own.wait()
    for copy in copies:
        copy.wait()


def swap_blocks(blocks, collective_id):
    count = blocks.shape[0]
    return pl.pallas_call(
        swap_blocks_kernel,
        name=f"swap_blocks_{collective_id}",
        out_shape=jax.ShapeDtypeStruct(blocks.shape, blocks.dtype),
        in_specs=[pl.BlockSpec(memory_space=pl.ANY)],
        out_specs=pl.BlockSpec(memory_space=pl.ANY),
        scratch_shapes=[
            pltpu.SemaphoreType.DMA((count,)),
            pltpu.SemaphoreType.DMA((count,)),
            pltpu.SemaphoreType.DMA,
        ],
        compiler_params=kernel_params(collective_id=collective_id, has_side_effects=True),
    )(blocks)


def head_means(values):
    rows = lax.broadcasted_iota(jnp.int32, (LANES, LANES), 0) // HEAD_DIM
    cols = lax.broadcasted_iota(jnp.int32, (LANES, LANES), 1) // HEAD_DIM
    spread = jnp.where(rows == cols, 1.0 / HEAD_DIM, 0.0).astype(BF16)
    high = values.astype(BF16)
    low = (values - high.astype(F32)).astype(BF16)
    return nn_dot(high, spread) + nn_dot(low, spread)


def half_partner(values):
    lane = lax.broadcasted_iota(jnp.int32, values.shape, 1)
    half = HEAD_DIM // 2
    ahead = pltpu.roll(values, LANES - half, 1)
    behind = pltpu.roll(values, half, 1)
    return jnp.where(lane % HEAD_DIM < half, ahead, behind)


def project_kernel(
    tokens_ref,
    gain_ref,
    wq_ref,
    wk_ref,
    wv_ref,
    q_gain_ref,
    k_gain_ref,
    cos_ref,
    sin_ref,
    hidden_ref,
    proj_ref,
    send_ref,
):
    rows = tokens_ref.shape[0]

    @pl.when(pl.program_id(0) == 0)
    def _():
        inputs = tokens_ref[...].astype(F32)
        scale = lax.rsqrt(jnp.mean(inputs * inputs, axis=-1, keepdims=True) + EPSILON)
        hidden_ref[...] = (inputs * scale * gain_ref[...]).astype(BF16)

    hidden = hidden_ref[...]
    half = rows // 2

    def put(block, lane):
        send_ref[0, :, lane : lane + LANES] = block[:half]
        send_ref[1, :, lane : lane + LANES] = block[half:]

    queries = nn_dot(hidden, wq_ref[...])
    keys = nn_dot(hidden, wk_ref[...])
    values = nn_dot(hidden, wv_ref[...])
    q_width = queries.shape[1]
    blocks = [(queries[:, at : at + LANES], at, q_gain_ref, QUERY_SCALE) for at in range(0, q_width, LANES)]
    blocks.append((keys, q_width, k_gain_ref, 1.0))
    for block, lane, head_gain, factor in blocks:
        proj_ref[0, :, lane : lane + LANES] = block
        scale = lax.rsqrt(head_means(block * block) + EPSILON)
        normed = block * scale * head_gain[...]
        turned = normed * cos_ref[...] + half_partner(normed) * sin_ref[...]
        put((turned * factor).astype(BF16), lane)
    put(values.astype(BF16), q_width + LANES)


def project(tokens, gain, wq, wk, wv, q_gain, k_gain, cosine, sine):
    rows, width = tokens.shape
    chips = wk.shape[1] // LANES
    q_width = wq.shape[1] // chips
    block_width = q_width + 2 * LANES
    return pl.pallas_call(
        project_kernel,
        name="project",
        grid=(chips,),
        in_specs=[
            whole_block((rows, width)),
            whole_block((1, width)),
            pl.BlockSpec((width, q_width), lambda p: (0, p)),
            pl.BlockSpec((width, LANES), lambda p: (0, p)),
            pl.BlockSpec((width, LANES), lambda p: (0, p)),
            whole_block((1, LANES)),
            whole_block((1, LANES)),
            whole_block((rows, LANES)),
            whole_block((rows, LANES)),
        ],
        out_specs=[
            whole_block((rows, width)),
            pl.BlockSpec((1, rows, q_width + LANES), lambda p: (p, 0, 0)),
            pl.BlockSpec((2, rows // 2, block_width), lambda p: (p, 0, 0)),
        ],
        out_shape=[
            jax.ShapeDtypeStruct((rows, width), BF16),
            jax.ShapeDtypeStruct((chips, rows, q_width + LANES), F32),
            jax.ShapeDtypeStruct((2 * chips, rows // 2, block_width), BF16),
        ],
        compiler_params=kernel_params(),
    )(tokens, gain, wq, wk, wv, q_gain, k_gain, cosine, sine)


def low_lanes(shape):
    return lax.broadcasted_iota(jnp.int32, shape, 1) < HEAD_DIM


def doubled(pair, group):
    turned = pltpu.roll(pair.astype(F32), HEAD_DIM, 1).astype(BF16)
    low = low_lanes(pair.shape)
    return jnp.where(low, pair, turned) if group == 0 else jnp.where(low, turned, pair)


def stacked_heads(pair):
    low = low_lanes(pair.shape)
    none = jnp.zeros_like(pair)
    return jnp.concatenate([jnp.where(low, pair, none), jnp.where(low, none, pair)], axis=0)


def in_three(column):
    lane = lax.broadcasted_iota(jnp.int32, (column.shape[0], LANES), 1)
    wide = jnp.broadcast_to(column, (column.shape[0], LANES))
    first = wide.astype(BF16).astype(F32)
    second = (wide - first).astype(BF16).astype(F32)
    third = wide - first - second
    return jnp.where(
        lane == 0, first, jnp.where(lane == 1, second, jnp.where(lane == 2, third, 0.0))
    ).astype(BF16)


def minus_three(rows):
    lane = lax.broadcasted_iota(jnp.int32, (rows, LANES), 1)
    return jnp.where(lane < 3, -1.0, 0.0).astype(BF16)


def attend_kernel(groups, block, qkv_ref, starts_ref, out_ref, logs_ref, keys, values, total):
    size = qkv_ref.shape[0]
    q_width = groups * LANES
    here = pl.program_id(0)

    @pl.when(here == 0)
    def _():
        for g in range(groups):
            keys[g] = doubled(qkv_ref[:, q_width : q_width + LANES], g)
            values[g, :, :LANES] = doubled(qkv_ref[:, q_width + LANES : q_width + 2 * LANES], g)
            values[g, :, LANES:] = jnp.ones((size, LANES), BF16)

    at = pl.multiple_of(here * block, block)
    starts = jnp.concatenate([starts_ref[pl.ds(at, block), :]] * 2, axis=0)
    queries = [
        stacked_heads(qkv_ref[pl.ds(at, block), g * LANES : (g + 1) * LANES]) for g in range(groups)
    ]
    column = lax.broadcasted_iota(jnp.int32, (2 * block, block), 1)
    row = lax.broadcasted_iota(jnp.int32, (2 * block, block), 0) % block

    def step(j, diagonal):
        key_at = pl.multiple_of(j * block, block)
        allowed = column >= starts - key_at
        if diagonal:
            allowed = allowed & (column <= row)
        for g in range(groups):
            scores = nt_dot(queries[g], keys[g, pl.ds(key_at, block), :])
            weights = jnp.exp2(jnp.where(allowed, scores, MASKED)).astype(BF16)
            part = nn_dot(weights, values[g, pl.ds(key_at, block), :])
            if diagonal:
                total[g] = part
            else:
                total[g] += part

    step(here, True)

    def body(j, carry):
        step(j, False)
        return carry

    lax.fori_loop(0, here, body, 0)
    for g in range(groups):
        sums = total[g, :, LANES:]
        mean = total[g, :, :LANES] / sums
        low = low_lanes((block, LANES))
        out_ref[0, :, g * LANES : (g + 1) * LANES] = jnp.where(low, mean[:block], mean[block:]).astype(BF16)
        logs_ref[g] = in_three(jnp.log2(sums[:, :1]))


def attend(qkv, starts, block):
    size, width = qkv.shape
    groups = (width - 2 * LANES) // LANES
    blocks = size // block
    return pl.pallas_call(
        functools.partial(attend_kernel, groups, block),
        name="attend",
        grid=(blocks,),
        in_specs=[whole_block((size, width)), whole_block((size, 1))],
        out_specs=[
            pl.BlockSpec((1, block, groups * LANES), lambda i: (i, 0, 0)),
            pl.BlockSpec((groups, 2 * block, LANES), lambda i: (0, i, 0)),
        ],
        out_shape=[
            jax.ShapeDtypeStruct((blocks, block, groups * LANES), BF16),
            jax.ShapeDtypeStruct((groups, 2 * size, LANES), BF16),
        ],
        scratch_shapes=[
            pltpu.VMEM((groups, size, LANES), BF16),
            pltpu.VMEM((groups, size, 2 * LANES), BF16),
            pltpu.VMEM((groups, 2 * block, 2 * LANES), F32),
        ],
        compiler_params=kernel_params(),
    )(qkv, starts)


def attend_back_kernel(
    groups,
    block,
    qkv_ref,
    logs_ref,
    out_ref,
    grad_ref,
    starts_ref,
    result_ref,
    queries,
    keys,
    values,
    grads,
    query_grad,
    pair_grad,
):
    size = qkv_ref.shape[0]
    blocks = size // block
    q_width = groups * LANES
    here = pl.program_id(0)

    @pl.when(here == 0)
    def _():
        query_grad[...] = jnp.zeros_like(query_grad)
        for g in range(groups):
            lanes = slice(g * LANES, (g + 1) * LANES)
            keys[g, :, :LANES] = doubled(qkv_ref[:, q_width : q_width + LANES], g)
            keys[g, :, LANES:] = minus_three(size)
            values[g, :, :LANES] = doubled(qkv_ref[:, q_width + LANES : q_width + 2 * LANES], g)
            values[g, :, LANES:] = minus_three(size)

            def fill(i, carry):
                at = pl.multiple_of(i * block, block)
                to = pl.multiple_of(i * 2 * block, 2 * block)
                queries[g, pl.ds(to, 2 * block), :LANES] = stacked_heads(qkv_ref[pl.ds(at, block), lanes])
                queries[g, pl.ds(to, 2 * block), LANES:] = logs_ref[g, pl.ds(to, 2 * block), :]
                grad = stacked_heads(grad_ref[pl.ds(at, block), lanes])
                mean = stacked_heads(out_ref[pl.ds(at, block), lanes])
                delta = jnp.sum(grad.astype(F32) * mean.astype(F32), axis=1, keepdims=True)
                grads[g, pl.ds(to, 2 * block), :LANES] = grad
                grads[g, pl.ds(to, 2 * block), LANES:] = in_three(delta)
                return carry

            lax.fori_loop(0, blocks, fill, 0)

    key_at = pl.multiple_of(here * block, block)
    key_rows = pl.ds(key_at, block)
    row = lax.broadcasted_iota(jnp.int32, (block, 2 * block), 0)
    column = lax.broadcasted_iota(jnp.int32, (block, 2 * block), 1) % block

    def step(i, diagonal):
        at = pl.multiple_of(i * 2 * block, 2 * block)
        stack = pl.ds(at, 2 * block)
        allowed = row >= starts_ref[:, stack] - key_at
        if diagonal:
            allowed = allowed & (row <= column)
        for g in range(groups):
            query = queries[g, stack, :]
            grad = grads[g, stack, :]
            key = keys[g, key_rows, :]
            scores = nt_dot(key, query)
            probs = jnp.exp2(jnp.where(allowed, scores, MASKED))
            pushed = (probs * nt_dot(values[g, key_rows, :], grad)).astype(BF16)
            value_part = nn_dot(probs.astype(BF16), grad[:, :LANES])
            key_part = nn_dot(pushed, query[:, :LANES])
            if diagonal:
                pair_grad[g, :, LANES:] = value_part
                pair_grad[g, :, :LANES] = key_part
            else:
                pair_grad[g, :, LANES:] += value_part
                pair_grad[g, :, :LANES] += key_part
            query_grad[g, stack, :] += tn_dot(pushed, key[:, :LANES])

    step(here, True)

    def body(i, carry):
        step(i, False)
        return carry

    lax.fori_loop(here + 1, blocks, body, 0)
    low = low_lanes((block, LANES))
    for part in range(2):
        sums = []
        for g in range(groups):
            both = pair_grad[g, :, part * LANES : (part + 1) * LANES]
            sums.append(both + pltpu.roll(both, HEAD_DIM, 1))
        joined = jnp.where(low, sums[0], sums[1])
        if part == 0:
            joined = joined * (1.0 / LOG2_E)
        lane = q_width + part * LANES
        result_ref[key_rows, lane : lane + LANES] = joined.astype(BF16)

    @pl.when(here == blocks - 1)
    def _():
        for g in range(groups):

            def finish(i, carry):
                at = pl.multiple_of(i * block, block)
                to = pl.multiple_of(i * 2 * block, 2 * block)
                first = query_grad[g, pl.ds(to, block), :]
                second = query_grad[g, pl.ds(to + block, block), :]
                joined = jnp.where(low, first, second) * HEAD_DIM ** (-0.5)
                result_ref[pl.ds(at, block), g * LANES : (g + 1) * LANES] = joined.astype(BF16)
                return carry

            lax.fori_loop(0, blocks, finish, 0)


def attend_back(qkv, logs, out, grad, starts, block):
    size, width = qkv.shape
    groups = (width - 2 * LANES) // LANES
    return pl.pallas_call(
        functools.partial(attend_back_kernel, groups, block),
        name="attend_back",
        grid=(size // block,),
        in_specs=[
            whole_block(qkv.shape),
            whole_block(logs.shape),
            whole_block(out.shape),
            whole_block(grad.shape),
            whole_block(starts.shape),
        ],
        out_specs=whole_block(qkv.shape),
        out_shape=jax.ShapeDtypeStruct(qkv.shape, BF16),
        scratch_shapes=[
            pltpu.VMEM((groups, 2 * size, 2 * LANES), BF16),
            pltpu.VMEM((groups, size, 2 * LANES), BF16),
            pltpu.VMEM((groups, size, 2 * LANES), BF16),
            pltpu.VMEM((groups, 2 * size, 2 * LANES), BF16),
            pltpu.VMEM((groups, 2 * size, LANES), F32),
            pltpu.VMEM((groups, block, 2 * LANES), F32),
        ],
        compiler_params=kernel_params(),
    )(qkv, logs, out, grad, starts)


def middle_kernel(tokens_ref, heads_ref, w_out_ref, gain_ref, middle_ref, hidden_ref):
    half = heads_ref.shape[1]
    width = heads_ref.shape[2]
    total = tokens_ref[...].astype(F32)
    for p in range(heads_ref.shape[0] // 2):
        block = jnp.concatenate([heads_ref[2 * p], heads_ref[2 * p + 1]], axis=0)
        total = total + nn_dot(block, w_out_ref[p * width : (p + 1) * width, :])
    middle_ref[...] = total
    scale = lax.rsqrt(jnp.mean(total * total, axis=-1, keepdims=True) + EPSILON)
    hidden_ref[...] = (total * scale * gain_ref[...]).astype(BF16)


def middle_layer(tokens, heads, w_out, gain):
    return pl.pallas_call(
        middle_kernel,
        name="middle",
        out_shape=[
            jax.ShapeDtypeStruct(tokens.shape, F32),
            jax.ShapeDtypeStruct(tokens.shape, BF16),
        ],
        compiler_params=kernel_params(),
    )(tokens, heads, w_out, gain)


def ffn_kernel(
    first,
    last,
    core_ref,
    hidden_ref,
    flipped_ref,
    grad_ref,
    w_gate_ref,
    w_up_ref,
    w_down_ref,
    *refs,
):
    if first:
        sums_in, refs = None, refs
    else:
        sums_in, refs = refs[:2], refs[2:]
    g_gate_ref, g_up_ref, g_down_ref = refs[:3]
    if last:
        finals, refs = refs[3:7], refs[7:]
    else:
        finals, refs = refs[3:5], refs[5:]
    out_sum, back_sum, acts, gate_grads, up_grads = refs
    step = pl.program_id(0)
    count = pl.num_programs(0)
    rows = hidden_ref.shape[0]
    chunk = min(256, rows)

    @pl.when(step == 0)
    def _():
        if first:
            out_sum[...] = jnp.zeros_like(out_sum)
            back_sum[...] = jnp.zeros_like(back_sum)
        else:
            out_sum[...] = sums_in[0][...]
            back_sum[...] = sums_in[1][...]

    def forward(m, carry):
        part = pl.ds(pl.multiple_of(m * chunk, chunk), chunk)
        hidden = hidden_ref[part, :]
        gate = nn_dot(hidden, w_gate_ref[...])
        up = nn_dot(hidden, w_up_ref[...])
        pushed = nt_dot(grad_ref[part, :], w_down_ref[...])
        opened = jax.nn.sigmoid(gate)
        silu = gate * opened
        act = (silu * up).astype(BF16)
        gate_grad = (pushed * up * opened * (1.0 + gate * (1.0 - opened))).astype(BF16)
        up_grad = (pushed * silu).astype(BF16)
        acts[part, :] = act
        gate_grads[part, :] = gate_grad
        up_grads[part, :] = up_grad
        out_sum[part, :] += nn_dot(act, w_down_ref[...])
        back_sum[part, :] += nt_dot(gate_grad, w_gate_ref[...]) + nt_dot(up_grad, w_up_ref[...])
        return carry

    lax.fori_loop(0, rows // chunk, forward, 0)
    width = flipped_ref.shape[0]

    def weights(m, carry):
        part = pl.ds(pl.multiple_of(m * chunk, chunk), chunk)
        flipped = flipped_ref[part, :]
        g_gate_ref[part, :] = nn_dot(flipped, gate_grads[...]).astype(BF16)
        g_up_ref[part, :] = nn_dot(flipped, up_grads[...]).astype(BF16)
        return carry

    lax.fori_loop(0, width // chunk, weights, 0)
    g_down_ref[...] = tn_dot(acts[...], grad_ref[...]).astype(BF16)

    @pl.when(step == count - 1)
    def _():
        if last:
            half = rows // 2
            finals[0][...] = out_sum[:half, :]
            finals[1][...] = out_sum[half:, :].astype(BF16)
            finals[2][...] = back_sum[:half, :]
            finals[3][...] = back_sum[half:, :].astype(BF16)
        else:
            finals[0][...] = out_sum[...]
            finals[1][...] = back_sum[...]


def ffn_part(core, hidden, flipped, grad, w_gate, w_up, w_down, sums, begin, tiles, last):
    rows, width = hidden.shape
    per_core = w_gate.shape[1] // 2 // FF_TILE
    first = sums is None

    def keep(shape):
        return pl.BlockSpec(shape, lambda f, c: (0,) * len(shape), pipeline_mode=pl.Buffered(1))

    in_specs = [
        keep((rows, width)),
        keep((width, rows)),
        keep((rows, width)),
        pl.BlockSpec((width, FF_TILE), lambda f, c: (0, c[0] * per_core + begin + f)),
        pl.BlockSpec((width, FF_TILE), lambda f, c: (0, c[0] * per_core + begin + f)),
        pl.BlockSpec((FF_TILE, width), lambda f, c: (c[0] * per_core + begin + f, 0)),
    ]
    args = [hidden, flipped, grad, w_gate, w_up, w_down]
    if not first:
        in_specs += [keep((rows, width))] * 2
        args += list(sums)
    out_specs = [
        pl.BlockSpec((width, FF_TILE), lambda f, c: (0, f)),
        pl.BlockSpec((width, FF_TILE), lambda f, c: (0, f)),
        pl.BlockSpec((FF_TILE, width), lambda f, c: (f, 0)),
    ]
    out_shape = [
        jax.ShapeDtypeStruct((width, tiles * FF_TILE), BF16),
        jax.ShapeDtypeStruct((width, tiles * FF_TILE), BF16),
        jax.ShapeDtypeStruct((tiles * FF_TILE, width), BF16),
    ]
    if last:
        half = (rows // 2, width)
        out_specs += [keep(half)] * 4
        out_shape += [jax.ShapeDtypeStruct(half, kind) for kind in (F32, BF16, F32, BF16)]
    else:
        out_specs += [keep((rows, width))] * 2
        out_shape += [jax.ShapeDtypeStruct((rows, width), F32)] * 2
    flops = 18 * rows * width * FF_TILE * tiles
    return pl.pallas_call(
        functools.partial(ffn_kernel, first, last),
        name=f"ffn_{begin}",
        grid_spec=pltpu.PrefetchScalarGridSpec(
            num_scalar_prefetch=1,
            grid=(tiles,),
            in_specs=in_specs,
            out_specs=out_specs,
            scratch_shapes=[
                pltpu.VMEM((rows, width), F32),
                pltpu.VMEM((rows, width), F32),
                pltpu.VMEM((rows, FF_TILE), BF16),
                pltpu.VMEM((rows, FF_TILE), BF16),
                pltpu.VMEM((rows, FF_TILE), BF16),
            ],
        ),
        out_shape=out_shape,
        compiler_params=kernel_params(),
        cost_estimate=pl.CostEstimate(
            flops=flops, bytes_accessed=12 * width * FF_TILE * tiles, transcendentals=0
        ),
    )(core, *args)


def turn_kernel(
    middle_ref,
    out_own_ref,
    out_got_ref,
    back_own_ref,
    back_got_ref,
    grad_ref,
    gain_ref,
    heads_ref,
    w_out_ref,
    output_ref,
    mid_ref,
    gain_grad_ref,
    w_grad_ref,
    send_ref,
    low_grad,
):
    @pl.when(pl.program_id(0) == 0)
    def _():
        middle = middle_ref[...]
        result = middle + (out_own_ref[...] + out_got_ref[...].astype(F32))
        output_ref[...] = result.astype(BF16)
        scale = lax.rsqrt(jnp.mean(middle * middle, axis=-1, keepdims=True) + EPSILON)
        normal = middle * scale
        back = back_own_ref[...] + back_got_ref[...].astype(F32)
        gain_grad_ref[...] = jnp.sum(back * normal, axis=0, keepdims=True)
        pushed = back * gain_ref[...]
        inner = jnp.mean(pushed * normal, axis=-1, keepdims=True)
        mid = grad_ref[...].astype(F32) + scale * (pushed - normal * inner)
        mid_ref[...] = mid
        low_grad[...] = mid.astype(BF16)

    half = heads_ref.shape[1]
    heads = jnp.concatenate([heads_ref[0], heads_ref[1]], axis=0)
    grad = low_grad[...]
    w_grad_ref[...] = tn_dot(heads, grad).astype(BF16)
    send = nt_dot(grad, w_out_ref[...]).astype(BF16)
    send_ref[0] = send[:half]
    send_ref[1] = send[half:]


def turn(middle, out_own, out_got, back_own, back_got, grad, gain, heads, w_out):
    rows, width = middle.shape
    count, half, lanes = heads.shape
    chips = count // 2
    return pl.pallas_call(
        turn_kernel,
        name="turn",
        grid=(chips,),
        in_specs=[whole_block((rows, width))] * 6
        + [
            whole_block((1, width)),
            pl.BlockSpec((2, half, lanes), lambda p: (p, 0, 0)),
            pl.BlockSpec((lanes, width), lambda p: (p, 0)),
        ],
        out_specs=[
            whole_block((rows, width)),
            whole_block((rows, width)),
            whole_block((1, width)),
            pl.BlockSpec((lanes, width), lambda p: (p, 0)),
            pl.BlockSpec((2, half, lanes), lambda p: (p, 0, 0)),
        ],
        out_shape=[
            jax.ShapeDtypeStruct((rows, width), BF16),
            jax.ShapeDtypeStruct((rows, width), F32),
            jax.ShapeDtypeStruct((1, width), F32),
            jax.ShapeDtypeStruct((chips * lanes, width), BF16),
            jax.ShapeDtypeStruct(heads.shape, BF16),
        ],
        scratch_shapes=[pltpu.VMEM((rows, width), BF16)],
        compiler_params=kernel_params(),
    )(middle, out_own, out_got, back_own, back_got, grad, gain, heads, w_out)


def project_back_kernel(
    got_ref,
    proj_ref,
    hidden_ref,
    tokens_ref,
    mid_ref,
    gain_ref,
    wq_ref,
    wk_ref,
    wv_ref,
    q_gain_ref,
    k_gain_ref,
    cos_ref,
    sin_ref,
    input_ref,
    gain_grad_ref,
    q_gain_grad_ref,
    k_gain_grad_ref,
    gq_ref,
    gk_ref,
    gv_ref,
    total,
):
    step = pl.program_id(0)

    @pl.when(step == 0)
    def _():
        total[...] = jnp.zeros_like(total)
        q_gain_grad_ref[...] = jnp.zeros_like(q_gain_grad_ref)
        k_gain_grad_ref[...] = jnp.zeros_like(k_gain_grad_ref)

    q_width = wq_ref.shape[1]
    hidden = hidden_ref[...]

    def back(lane, head_gain, gain_out):
        got = jnp.concatenate(
            [got_ref[0, :, lane : lane + LANES], got_ref[1, :, lane : lane + LANES]], axis=0
        ).astype(F32)
        turned = got * cos_ref[...] - half_partner(got) * sin_ref[...]
        block = proj_ref[0, :, lane : lane + LANES]
        scale = lax.rsqrt(head_means(block * block) + EPSILON)
        normal = block * scale
        gain_out[...] += jnp.sum(turned * normal, axis=0, keepdims=True)
        pushed = turned * head_gain[...]
        inner = head_means(pushed * normal)
        return (scale * (pushed - normal * inner)).astype(BF16)

    query = jnp.concatenate(
        [back(at, q_gain_ref, q_gain_grad_ref) for at in range(0, q_width, LANES)], axis=1
    )
    key = back(q_width, k_gain_ref, k_gain_grad_ref)
    lane = q_width + LANES
    value = jnp.concatenate(
        [got_ref[0, :, lane : lane + LANES], got_ref[1, :, lane : lane + LANES]], axis=0
    )
    gq_ref[...] = tn_dot(hidden, query).astype(BF16)
    gk_ref[...] = tn_dot(hidden, key).astype(BF16)
    gv_ref[...] = tn_dot(hidden, value).astype(BF16)
    total[...] += (
        nt_dot(query, wq_ref[...]) + nt_dot(key, wk_ref[...]) + nt_dot(value, wv_ref[...])
    )

    @pl.when(step == pl.num_programs(0) - 1)
    def _():
        inputs = tokens_ref[...].astype(F32)
        scale = lax.rsqrt(jnp.mean(inputs * inputs, axis=-1, keepdims=True) + EPSILON)
        normal = inputs * scale
        grad = total[...]
        gain_grad_ref[...] = jnp.sum(grad * normal, axis=0, keepdims=True)
        pushed = grad * gain_ref[...]
        inner = jnp.mean(pushed * normal, axis=-1, keepdims=True)
        input_ref[...] = (mid_ref[...] + scale * (pushed - normal * inner)).astype(BF16)


def project_back(got, proj, hidden, tokens, mid, gain, wq, wk, wv, q_gain, k_gain, cosine, sine):
    rows, width = tokens.shape
    count, half, lanes = got.shape
    chips = count // 2
    q_width = wq.shape[1] // chips
    return pl.pallas_call(
        project_back_kernel,
        name="project_back",
        grid=(chips,),
        in_specs=[
            pl.BlockSpec((2, half, lanes), lambda p: (p, 0, 0)),
            pl.BlockSpec((1, rows, q_width + LANES), lambda p: (p, 0, 0)),
            whole_block((rows, width)),
            whole_block((rows, width)),
            whole_block((rows, width)),
            whole_block((1, width)),
            pl.BlockSpec((width, q_width), lambda p: (0, p)),
            pl.BlockSpec((width, LANES), lambda p: (0, p)),
            pl.BlockSpec((width, LANES), lambda p: (0, p)),
            whole_block((1, LANES)),
            whole_block((1, LANES)),
            whole_block((rows, LANES)),
            whole_block((rows, LANES)),
        ],
        out_specs=[
            whole_block((rows, width)),
            whole_block((1, width)),
            whole_block((1, LANES)),
            whole_block((1, LANES)),
            pl.BlockSpec((width, q_width), lambda p: (0, p)),
            pl.BlockSpec((width, LANES), lambda p: (0, p)),
            pl.BlockSpec((width, LANES), lambda p: (0, p)),
        ],
        out_shape=[
            jax.ShapeDtypeStruct((rows, width), BF16),
            jax.ShapeDtypeStruct((1, width), F32),
            jax.ShapeDtypeStruct((1, LANES), F32),
            jax.ShapeDtypeStruct((1, LANES), F32),
            jax.ShapeDtypeStruct(wq.shape, BF16),
            jax.ShapeDtypeStruct(wk.shape, BF16),
            jax.ShapeDtypeStruct(wv.shape, BF16),
        ],
        scratch_shapes=[pltpu.VMEM((rows, width), F32)],
        compiler_params=kernel_params(),
    )(got, proj, hidden, tokens, mid, gain, wq, wk, wv, q_gain, k_gain, cosine, sine)


def flip_pairs(count, bit):
    return [(i, i ^ bit) for i in range(count)]


def sum_pair(parts, axis, count, bit, dim):
    mine = (lax.axis_index(axis) // bit) % 2
    send = lax.dynamic_index_in_dim(parts, 1 - mine, dim, keepdims=False)
    own = lax.dynamic_index_in_dim(parts, mine, dim, keepdims=False)
    return own + lax.ppermute(send, axis, flip_pairs(count, bit))


def sum_line(parts, axis, count):
    mine = lax.axis_index(axis)
    total = lax.dynamic_index_in_dim(parts, mine, 0, keepdims=False)
    for way in (1, -1):
        got = None
        for step in range(1, count):
            target = jnp.clip(mine + way * (count - step), 0, count - 1)
            send = lax.dynamic_index_in_dim(parts, target, 0, keepdims=False)
            if got is not None:
                send = send + got
            if way == 1:
                pairs = [(i, i + 1) for i in range(step)]
            else:
                pairs = [(count - 1 - i, count - 2 - i) for i in range(step)]
            got = lax.ppermute(send, axis, pairs)
        total = total + got
    return total


def sum_chips(parts, order, dp_count, blk_count):
    bits = []
    bit = blk_count // 2
    while bit > 1:
        bits.append(bit)
        bit //= 2
    left = ["z"] + bits
    for stage in order:
        dim = left.index(stage)
        left.pop(dim)
        if stage == "z":
            parts = sum_line(jnp.moveaxis(parts, dim, 0) if dim else parts, "dp", dp_count)
        else:
            parts = sum_pair(parts, "blk", blk_count, stage, dim)
    return parts


def swap_core(block, blk_count):
    return lax.ppermute(block, "blk", flip_pairs(blk_count, 1))


def fast_local(
    dp_count,
    blk_count,
    tokens,
    doc_lengths,
    g_attn,
    w_query,
    w_key,
    w_value,
    q_gain,
    k_gain,
    w_out,
    g_ffn,
    w_gate,
    w_up,
    w_down,
    cotangent,
):
    row_count, tok_count, width = tokens.shape
    rows = row_count * tok_count
    chips = blk_count // 2
    size = tok_count * blk_count
    index = lax.axis_index("blk")
    core = index % 2
    bits = []
    bit = blk_count // 2
    while bit > 1:
        bits.append(bit)
        bit //= 2
    chip_dims = (dp_count,) + (2,) * len(bits)
    all_chips = dp_count * chips
    places = index * tok_count + jnp.arange(tok_count, dtype=jnp.int32)
    unused, positions = doc_layout(doc_lengths, places)
    cosine, sine = rope_angles(positions)
    cosine = jnp.tile(cosine.reshape(rows, -1), (1, 4))
    sine = sine.reshape(rows, -1)
    sine = jnp.concatenate([-sine, sine, -sine, sine], axis=1)
    q_gain2 = jnp.tile(q_gain, 2)[None]
    k_gain2 = jnp.tile(k_gain, 2)[None]
    all_places = jnp.arange(size, dtype=jnp.int32)
    row_lengths = lax.dynamic_slice_in_dim(doc_lengths, core, 1, axis=0)
    unused, all_positions = doc_layout(row_lengths, all_places)
    starts = all_places - all_positions[0]
    starts_two = jnp.broadcast_to(
        starts.reshape(blk_count, 1, tok_count), (blk_count, 2, tok_count)
    ).reshape(1, 2 * size)
    flat = tokens.reshape(rows, width)
    grad_own = cotangent.reshape(rows, width)
    grad_both = jnp.concatenate([grad_own, swap_core(grad_own, blk_count)], axis=0)

    hidden_in, proj, send = project(
        flat, g_attn[None], w_query, w_key, w_value, q_gain2, k_gain2, cosine, sine
    )
    qkv = swap_blocks(send, 0).reshape(size, -1)
    attended, logs = attend(qkv, starts[:, None], tok_count)
    heads = swap_blocks(attended, 1)
    middle, hidden_own = middle_layer(flat, heads, w_out, g_ffn[None])
    hidden = jnp.concatenate([hidden_own, swap_core(hidden_own, blk_count)], axis=0)
    flipped = hidden.T
    core_arg = core.reshape(1)
    tiles = w_gate.shape[1] // 2 // FF_TILE
    sums = None
    gate_sums, up_sums, down_parts = [], [], []
    each = tiles // FFN_CALLS
    forward_order = bits + ["z"]
    other_order = bits[::-1] + ["z"]
    for call in range(FFN_CALLS):
        last = call == FFN_CALLS - 1
        made = ffn_part(
            core_arg, hidden, flipped, grad_both, w_gate, w_up, w_down, sums, call * each, each, last
        )
        gate_parts, up_parts, down_part = made[:3]
        sums = made[3:]
        down_parts.append(down_part)
        gate_sums.append(
            sum_chips(gate_parts.reshape(chip_dims + (-1, each * FF_TILE)), forward_order, dp_count, blk_count)
        )
        up_sums.append(
            sum_chips(up_parts.reshape(chip_dims + (-1, each * FF_TILE)), other_order, dp_count, blk_count)
        )
    out_own, out_send, back_own, back_send = sums
    back_got = swap_core(back_send, blk_count)
    out_got = swap_core(out_send, blk_count)
    output, mid, ffn_gain_grad, w_out_parts, send = turn(
        middle, out_own, out_got, back_own, back_got, grad_own, g_ffn[None], heads, w_out
    )
    half_width = width // 2
    down_half = jnp.concatenate(down_parts, axis=0)
    down_own = lax.dynamic_slice_in_dim(down_half, core * half_width, half_width, axis=1)
    down_got = swap_core(
        lax.dynamic_slice_in_dim(down_half, (1 - core) * half_width, half_width, axis=1), blk_count
    )
    down_low = jnp.where(core == 0, down_own, down_got)
    down_high = jnp.where(core == 0, down_got, down_own)
    down_all = jnp.concatenate([down_low, down_high], axis=0).reshape(
        chip_dims + (-1, half_width)
    )
    quarter = half_width // 2
    down_sums = [
        sum_chips(down_all[..., :quarter], ["z"] + bits, dp_count, blk_count),
        sum_chips(down_all[..., quarter:], ["z"] + bits[::-1], dp_count, blk_count),
    ]
    grad_heads = swap_blocks(send, 2).reshape(size, -1)
    back = attend_back(qkv, logs, attended.reshape(size, -1), grad_heads, starts_two, tok_count)
    got = swap_blocks(back.reshape(blk_count, tok_count, -1), 3)
    input_grad, attn_gain_grad, query_gain_grad, key_gain_grad, gq, gk, gv = project_back(
        got,
        proj,
        hidden_in,
        flat,
        mid,
        g_attn[None],
        w_query,
        w_key,
        w_value,
        q_gain2,
        k_gain2,
        cosine,
        sine,
    )

    def sum_all(parts, order):
        parts = parts.reshape(chip_dims + (2, -1, parts.shape[-1]))
        parts = sum_pair(parts, "blk", blk_count, 1, len(chip_dims))
        return sum_chips(parts, order, dp_count, blk_count).astype(F32)

    grad_w_out = sum_all(w_out_parts, forward_order)
    grad_w_query = sum_all(gq, forward_order)
    both = sum_all(jnp.concatenate([gk, gv], axis=1), other_order)
    grad_w_key, grad_w_value = jnp.split(both, 2, axis=1)

    def join(block, dim):
        count = block.shape[0] // 2
        own = lax.dynamic_slice_in_dim(block, core * count, count, axis=0)
        got = swap_core(
            lax.dynamic_slice_in_dim(block, (1 - core) * count, count, axis=0), blk_count
        )
        low = jnp.where(core == 0, own, got)
        high = jnp.where(core == 0, got, own)
        return jnp.concatenate([low, high], axis=1).astype(F32)

    grad_w_gate = join(jnp.concatenate(gate_sums, axis=1), 1)
    grad_w_up = join(jnp.concatenate(up_sums, axis=1), 1)
    grad_w_down = join(jnp.concatenate(down_sums, axis=1), 1)
    fold = lambda both: both[0, :HEAD_DIM] + both[0, HEAD_DIM:]
    gain_attn, gain_query, gain_key, gain_ffn = lax.psum(
        (attn_gain_grad[0], fold(query_gain_grad), fold(key_gain_grad), ffn_gain_grad[0]),
        ("dp", "blk"),
    )
    return (
        output.reshape(tokens.shape),
        input_grad.reshape(tokens.shape),
        gain_attn,
        grad_w_query,
        grad_w_key,
        grad_w_value,
        gain_query,
        gain_key,
        grad_w_out,
        gain_ffn,
        grad_w_gate,
        grad_w_up,
        grad_w_down,
    )


def fits(mesh):
    blk_count = mesh.shape["blk"]
    chips = blk_count // 2
    power = blk_count & (blk_count - 1) == 0
    return power and blk_count > 2 and (KV_HEADS * HEAD_DIM) == chips * LANES


def solution(mesh):
    if fits(mesh):
        body = functools.partial(fast_local, mesh.shape["dp"], mesh.shape["blk"])
    else:
        body = local
    return jax.shard_map(
        body,
        mesh=mesh,
        in_specs=(
            P("dp", "blk", None),
            P("dp", None),
            P(),
            P(),
            P(),
            P(),
            P(),
            P(),
            P(),
            P(),
            P(),
            P(),
            P(),
            P("dp", "blk", None),
        ),
        out_specs=(
            P("dp", "blk", None),
            P("dp", "blk", None),
            P(),
            P(("dp", "blk"), None),
            P(("dp", "blk"), None),
            P(("dp", "blk"), None),
            P(),
            P(),
            P(("dp", "blk"), None),
            P(),
            P(("dp", "blk"), None),
            P(("dp", "blk"), None),
            P(("dp", "blk"), None),
        ),
        check_vma=False,
    )
```

```python
import functools
import math

import jax
import jax.numpy as jnp
from jax import lax
from jax.experimental import pallas as pl
from jax.experimental.pallas import tpu as pltpu
from jax.sharding import PartitionSpec as P

HEADS = 16
KV_HEADS = 8
HEAD_DIM = 64


EPSILON = 1e-05
ROPE_BASE = 1000000.0
NEGATIVE = -1e30


def norm_rows(values, norm_gain):
    row_scale = lax.rsqrt(jnp.mean(values * values, axis=-1, keepdims=True) + EPSILON)
    normal = values * row_scale
    return (normal * norm_gain, normal, row_scale)


def norm_back(normal, row_scale, norm_gain, grad_out):
    pushed = grad_out * norm_gain
    inner = jnp.mean(pushed * normal, axis=-1, keepdims=True)
    grad_in = row_scale * (pushed - normal * inner)
    leading = tuple(range(grad_out.ndim - 1))
    return (grad_in, jnp.sum(grad_out * normal, axis=leading))


def doc_layout(lengths, places):
    ends = jnp.cumsum(lengths, axis=1)
    past = places[None, :, None] >= ends[:, None, :]
    docs = jnp.sum(past.astype(jnp.int32), axis=2)
    before = jnp.sum(jnp.where(past, lengths[:, None, :], 0), axis=2)
    return (docs, places[None, :] - before)


def rope_angles(positions):
    half = HEAD_DIM // 2
    freqs = ROPE_BASE ** (-jnp.arange(half, dtype=jnp.float32) / half)
    angles = positions.astype(jnp.float32)[..., None] * freqs
    return (jnp.cos(angles), jnp.sin(angles))


def rotate(values, cosine, sine):
    half = values.shape[-1] // 2
    first_half = values[..., :half]
    second_half = values[..., half:]
    cos_col = cosine[:, :, None, :]
    sin_col = sine[:, :, None, :]
    return jnp.concatenate(
        [
            first_half * cos_col - second_half * sin_col,
            second_half * cos_col + first_half * sin_col,
        ],
        axis=-1,
    )


def local(
    tokens,
    doc_lengths,
    g_attn,
    w_query,
    w_key,
    w_value,
    q_gain,
    k_gain,
    w_out,
    g_ffn,
    w_gate,
    w_up,
    w_down,
    cotangent,
):
    row_count, tok_count, width = tokens.shape
    grouping = HEADS // KV_HEADS
    flat_rows = row_count * tok_count
    kv_width = KV_HEADS * HEAD_DIM
    softmax_scale = HEAD_DIM ** (-0.5)
    places = lax.axis_index("blk") * tok_count + jnp.arange(tok_count, dtype=jnp.int32)
    query_docs, query_pos = doc_layout(doc_lengths, places)
    cosine, sine = rope_angles(query_pos)
    inputs = tokens.reshape(flat_rows, width).astype(jnp.float32)
    normed, normal_in, scale_in = norm_rows(inputs, g_attn)
    hidden_in = normed.astype(jnp.bfloat16)
    query_proj = jnp.dot(hidden_in, w_query, preferred_element_type=jnp.float32).reshape(
        row_count, tok_count, HEADS, HEAD_DIM
    )
    key_proj = jnp.dot(hidden_in, w_key, preferred_element_type=jnp.float32).reshape(
        row_count, tok_count, KV_HEADS, HEAD_DIM
    )
    value_b = (
        jnp.dot(hidden_in, w_value, preferred_element_type=jnp.float32)
        .astype(jnp.bfloat16)
        .reshape(row_count, tok_count, kv_width)
    )
    query_norm, query_normal, query_scale = norm_rows(query_proj, q_gain)
    key_norm, key_normal, key_scale = norm_rows(key_proj, k_gain)
    query_b = (
        rotate(query_norm, cosine, sine)
        .astype(jnp.bfloat16)
        .reshape(row_count, tok_count, KV_HEADS, grouping, HEAD_DIM)
    )
    key_b = (
        rotate(key_norm, cosine, sine).astype(jnp.bfloat16).reshape(row_count, tok_count, kv_width)
    )

    def piece_mask(size):
        key_places = jnp.arange(size, dtype=jnp.int32)
        key_docs, unused = doc_layout(doc_lengths, key_places)
        return (key_places[None, None, :] <= places[None, :, None]) & (
            key_docs[:, None, :] == query_docs[:, :, None]
        )

    def piece_scores(key_piece, allowed):
        key_heads = key_piece.reshape(row_count, key_piece.shape[1], KV_HEADS, HEAD_DIM)
        raw_scores = (
            jnp.einsum("rqkgd,rpkd->rkgqp", query_b, key_heads, preferred_element_type=jnp.float32)
            * softmax_scale
        )
        return (jnp.where(allowed[:, None, None], raw_scores, -jnp.inf), key_heads)

    stat_shape = (row_count, KV_HEADS, grouping, tok_count)
    key_piece = lax.all_gather(key_b, "blk", axis=1, tiled=True)
    value_piece = lax.all_gather(value_b, "blk", axis=1, tiled=True)
    allowed = piece_mask(key_piece.shape[1])
    running_max = jnp.full(stat_shape, NEGATIVE, jnp.float32)
    scores, key_heads = piece_scores(key_piece, allowed)
    new_max = jnp.maximum(running_max, jnp.max(scores, axis=-1))
    weights = jnp.exp(scores - new_max[..., None])
    value_heads = value_piece.reshape(row_count, value_piece.shape[1], KV_HEADS, HEAD_DIM)
    added = jnp.einsum(
        "rkgqp,rpkd->rkgqd",
        weights.astype(jnp.bfloat16),
        value_heads,
        preferred_element_type=jnp.float32,
    )
    running_sum = jnp.sum(weights, axis=-1)
    attended = added / running_sum[..., None]
    log_total = new_max + jnp.log(running_sum)
    attended_b = (
        jnp.transpose(attended, (0, 3, 1, 2, 4))
        .reshape(flat_rows, HEADS * HEAD_DIM)
        .astype(jnp.bfloat16)
    )
    middle = inputs + jnp.dot(attended_b, w_out, preferred_element_type=jnp.float32)
    normed_ffn, normal_ffn, scale_ffn = norm_rows(middle, g_ffn)
    hidden_ffn = normed_ffn.astype(jnp.bfloat16)
    gate = jnp.dot(hidden_ffn, w_gate, preferred_element_type=jnp.float32)
    up_proj = jnp.dot(hidden_ffn, w_up, preferred_element_type=jnp.float32)
    sigmoid_gate = jax.nn.sigmoid(gate)
    silu_gate = gate * sigmoid_gate
    hidden = (silu_gate * up_proj).astype(jnp.bfloat16)
    result = middle + jnp.dot(hidden, w_down, preferred_element_type=jnp.float32)
    output = result.astype(jnp.bfloat16).reshape(row_count, tok_count, width)
    grad_out = cotangent.reshape(flat_rows, width)
    grad_w_down = jnp.einsum("tf,td->fd", hidden, grad_out, preferred_element_type=jnp.float32)
    grad_hidden = jnp.einsum("td,fd->tf", grad_out, w_down, preferred_element_type=jnp.float32)
    grad_gate = (grad_hidden * up_proj * sigmoid_gate * (1.0 + gate * (1.0 - sigmoid_gate))).astype(
        jnp.bfloat16
    )
    grad_up = (grad_hidden * silu_gate).astype(jnp.bfloat16)
    grad_w_gate = jnp.einsum("td,tf->df", hidden_ffn, grad_gate, preferred_element_type=jnp.float32)
    grad_w_up = jnp.einsum("td,tf->df", hidden_ffn, grad_up, preferred_element_type=jnp.float32)
    grad_h2 = jnp.einsum(
        "tf,df->td", grad_gate, w_gate, preferred_element_type=jnp.float32
    ) + jnp.einsum("tf,df->td", grad_up, w_up, preferred_element_type=jnp.float32)
    grad_mid, grad_ffn_gain = norm_back(normal_ffn, scale_ffn, g_ffn, grad_h2)
    grad_mid = grad_out.astype(jnp.float32) + grad_mid
    grad_attn = grad_mid.astype(jnp.bfloat16)
    grad_w_out = jnp.einsum("tc,td->cd", attended_b, grad_attn, preferred_element_type=jnp.float32)
    grad_attended = jnp.einsum(
        "td,cd->tc", grad_attn, w_out, preferred_element_type=jnp.float32
    ).astype(jnp.bfloat16)
    grad_heads = grad_attended.reshape(row_count, tok_count, KV_HEADS, grouping, HEAD_DIM)
    deltas = jnp.einsum("rqkgd,rkgqd->rkgq", grad_heads.astype(jnp.float32), attended)
    key_piece = lax.all_gather(key_b, "blk", axis=1, tiled=True)
    value_piece = lax.all_gather(value_b, "blk", axis=1, tiled=True)
    size = key_piece.shape[1]
    allowed = piece_mask(size)
    scores, key_heads = piece_scores(key_piece, allowed)
    probs = jnp.exp(scores - log_total[..., None])
    value_heads = value_piece.reshape(row_count, size, KV_HEADS, HEAD_DIM)
    value_piece_grad = jnp.einsum(
        "rkgqp,rqkgd->rpkd",
        probs.astype(jnp.bfloat16),
        grad_heads,
        preferred_element_type=jnp.float32,
    )
    grad_probs = jnp.einsum(
        "rqkgd,rpkd->rkgqp", grad_heads, value_heads, preferred_element_type=jnp.float32
    )
    grad_scores = (probs * (grad_probs - deltas[..., None])).astype(jnp.bfloat16)
    grad_query = jnp.einsum(
        "rkgqp,rpkd->rkgqd", grad_scores, key_heads, preferred_element_type=jnp.float32
    )
    key_piece_grad = jnp.einsum(
        "rkgqp,rqkgd->rpkd", grad_scores, query_b, preferred_element_type=jnp.float32
    )
    grad_keys = key_piece_grad.reshape(row_count, size, kv_width)
    grad_values = value_piece_grad.reshape(row_count, size, kv_width)
    grad_query, grad_keys, grad_values = (grad_query, grad_keys, grad_values)
    key_grad_mine, value_grad_mine = (
        lax.psum_scatter(
            grad_keys.astype(jnp.bfloat16), "blk", scatter_dimension=1, tiled=True
        ).astype(jnp.float32),
        lax.psum_scatter(
            grad_values.astype(jnp.bfloat16), "blk", scatter_dimension=1, tiled=True
        ).astype(jnp.float32),
    )
    grad_q_rot = (jnp.transpose(grad_query, (0, 3, 1, 2, 4)) * softmax_scale).reshape(
        row_count, tok_count, HEADS, HEAD_DIM
    )
    grad_k_rot = (key_grad_mine * softmax_scale).reshape(row_count, tok_count, KV_HEADS, HEAD_DIM)
    grad_q_proj, grad_query_gain = norm_back(
        query_normal, query_scale, q_gain, rotate(grad_q_rot, cosine, -sine)
    )
    grad_k_proj, grad_key_gain = norm_back(
        key_normal, key_scale, k_gain, rotate(grad_k_rot, cosine, -sine)
    )
    grad_q_b = grad_q_proj.astype(jnp.bfloat16).reshape(flat_rows, HEADS * HEAD_DIM)
    grad_k_b = grad_k_proj.astype(jnp.bfloat16).reshape(flat_rows, kv_width)
    grad_v_b = value_grad_mine.astype(jnp.bfloat16).reshape(flat_rows, kv_width)
    grad_w_query = jnp.einsum("td,tc->dc", hidden_in, grad_q_b, preferred_element_type=jnp.float32)
    grad_w_key = jnp.einsum("td,tc->dc", hidden_in, grad_k_b, preferred_element_type=jnp.float32)
    grad_w_value = jnp.einsum("td,tc->dc", hidden_in, grad_v_b, preferred_element_type=jnp.float32)
    grad_h1 = jnp.einsum("tc,dc->td", grad_q_b, w_query, preferred_element_type=jnp.float32)
    grad_h1 = grad_h1 + jnp.einsum("tc,dc->td", grad_k_b, w_key, preferred_element_type=jnp.float32)
    grad_h1 = grad_h1 + jnp.einsum(
        "tc,dc->td", grad_v_b, w_value, preferred_element_type=jnp.float32
    )
    grad_base, grad_attn_gain = norm_back(normal_in, scale_in, g_attn, grad_h1)
    input_grad = (grad_mid + grad_base).astype(jnp.bfloat16).reshape(row_count, tok_count, width)
    gain_attn, gain_query, gain_key, gain_ffn = lax.psum(
        (grad_attn_gain, grad_query_gain, grad_key_gain, grad_ffn_gain), ("dp", "blk")
    )
    locals_all = (
        grad_w_query,
        grad_w_key,
        grad_w_value,
        grad_w_out,
        grad_w_gate,
        grad_w_up,
        grad_w_down,
    )
    shared = (
        lax.psum_scatter(locals_all[0], ("dp", "blk"), scatter_dimension=0, tiled=True),
        lax.psum_scatter(locals_all[1], ("dp", "blk"), scatter_dimension=0, tiled=True),
        lax.psum_scatter(locals_all[2], ("dp", "blk"), scatter_dimension=0, tiled=True),
        lax.psum_scatter(locals_all[3], ("dp", "blk"), scatter_dimension=0, tiled=True),
        lax.psum_scatter(locals_all[4], ("dp", "blk"), scatter_dimension=0, tiled=True),
        lax.psum_scatter(locals_all[5], ("dp", "blk"), scatter_dimension=0, tiled=True),
        lax.psum_scatter(locals_all[6], ("dp", "blk"), scatter_dimension=0, tiled=True),
    )
    return (
        output,
        input_grad,
        gain_attn,
        shared[0],
        shared[1],
        shared[2],
        gain_query,
        gain_key,
        shared[3],
        gain_ffn,
        shared[4],
        shared[5],
        shared[6],
    )


BF16 = jnp.bfloat16
F32 = jnp.float32
LANES = 128
FF_TILE = 256
VMEM_BYTES = 56 * 1024 * 1024
LOG2_E = math.log2(math.e)
QUERY_SCALE = HEAD_DIM ** (-0.5) * LOG2_E
MASKED = -1e30


def nn_dot(left, right):
    return lax.dot_general(left, right, (((1,), (0,)), ((), ())), preferred_element_type=F32)


def nt_dot(left, right):
    return lax.dot_general(left, right, (((1,), (1,)), ((), ())), preferred_element_type=F32)


def tn_dot(left, right):
    return lax.dot_general(left, right, (((0,), (0,)), ((), ())), preferred_element_type=F32)


def kernel_params(**more):
    return pltpu.CompilerParams(vmem_limit_bytes=VMEM_BYTES, **more)


def whole_block(shape):
    return pl.BlockSpec(shape, lambda *ids: (0,) * len(shape))


def swap_blocks_kernel(send_ref, out_ref, send_sem, recv_sem, own_sem):
    count = send_ref.shape[0]
    mine = lax.axis_index("blk")
    group = lax.axis_index("dp")
    barrier = pltpu.get_barrier_semaphore()
    for step in range(1, count):
        pl.semaphore_signal(
            barrier,
            inc=1,
            device_id=(group, lax.rem(mine + step, count)),
            device_id_type=pl.DeviceIdType.MESH,
        )
    pl.semaphore_wait(barrier, count - 1)
    copies = []
    for step in range(1, count):
        target = lax.rem(mine + step, count)
        copy = pltpu.make_async_remote_copy(
            src_ref=send_ref.at[target],
            dst_ref=out_ref.at[mine],
            send_sem=send_sem.at[step],
            recv_sem=recv_sem.at[step],
            device_id=(group, target),
            device_id_type=pl.DeviceIdType.MESH,
        )
        copy.start()
        copies.append(copy)
    own = pltpu.make_async_copy(send_ref.at[mine], out_ref.at[mine], own_sem)
    own.start()
    own.wait()
    for copy in copies:
        copy.wait()


def swap_blocks(blocks, collective_id):
    count = blocks.shape[0]
    return pl.pallas_call(
        swap_blocks_kernel,
        name=f"swap_blocks_{collective_id}",
        out_shape=jax.ShapeDtypeStruct(blocks.shape, blocks.dtype),
        in_specs=[pl.BlockSpec(memory_space=pl.ANY)],
        out_specs=pl.BlockSpec(memory_space=pl.ANY),
        scratch_shapes=[
            pltpu.SemaphoreType.DMA((count,)),
            pltpu.SemaphoreType.DMA((count,)),
            pltpu.SemaphoreType.DMA,
        ],
        compiler_params=kernel_params(collective_id=collective_id, has_side_effects=True),
    )(blocks)


def head_means(values):
    rows = lax.broadcasted_iota(jnp.int32, (LANES, LANES), 0) // HEAD_DIM
    cols = lax.broadcasted_iota(jnp.int32, (LANES, LANES), 1) // HEAD_DIM
    spread = jnp.where(rows == cols, 1.0 / HEAD_DIM, 0.0).astype(BF16)
    high = values.astype(BF16)
    low = (values - high.astype(F32)).astype(BF16)
    return nn_dot(high, spread) + nn_dot(low, spread)


def half_partner(values):
    lane = lax.broadcasted_iota(jnp.int32, values.shape, 1)
    half = HEAD_DIM // 2
    ahead = pltpu.roll(values, LANES - half, 1)
    behind = pltpu.roll(values, half, 1)
    return jnp.where(lane % HEAD_DIM < half, ahead, behind)


def project_kernel(
    tokens_ref,
    gain_ref,
    wq_ref,
    wk_ref,
    wv_ref,
    q_gain_ref,
    k_gain_ref,
    cos_ref,
    sin_ref,
    hidden_ref,
    proj_ref,
    send_ref,
):
    rows = tokens_ref.shape[0]

    @pl.when(pl.program_id(0) == 0)
    def _():
        inputs = tokens_ref[...].astype(F32)
        scale = lax.rsqrt(jnp.mean(inputs * inputs, axis=-1, keepdims=True) + EPSILON)
        hidden_ref[...] = (inputs * scale * gain_ref[...]).astype(BF16)

    hidden = hidden_ref[...]
    half = rows // 2

    def put(block, lane):
        send_ref[0, :, lane : lane + LANES] = block[:half]
        send_ref[1, :, lane : lane + LANES] = block[half:]

    queries = nn_dot(hidden, wq_ref[...])
    keys = nn_dot(hidden, wk_ref[...])
    values = nn_dot(hidden, wv_ref[...])
    q_width = queries.shape[1]
    blocks = [(queries[:, at : at + LANES], at, q_gain_ref, QUERY_SCALE) for at in range(0, q_width, LANES)]
    blocks.append((keys, q_width, k_gain_ref, 1.0))
    for block, lane, head_gain, factor in blocks:
        proj_ref[0, :, lane : lane + LANES] = block
        scale = lax.rsqrt(head_means(block * block) + EPSILON)
        normed = block * scale * head_gain[...]
        turned = normed * cos_ref[...] + half_partner(normed) * sin_ref[...]
        put((turned * factor).astype(BF16), lane)
    put(values.astype(BF16), q_width + LANES)


def project(tokens, gain, wq, wk, wv, q_gain, k_gain, cosine, sine):
    rows, width = tokens.shape
    chips = wk.shape[1] // LANES
    q_width = wq.shape[1] // chips
    block_width = q_width + 2 * LANES
    return pl.pallas_call(
        project_kernel,
        name="project",
        grid=(chips,),
        in_specs=[
            whole_block((rows, width)),
            whole_block((1, width)),
            pl.BlockSpec((width, q_width), lambda p: (0, p)),
            pl.BlockSpec((width, LANES), lambda p: (0, p)),
            pl.BlockSpec((width, LANES), lambda p: (0, p)),
            whole_block((1, LANES)),
            whole_block((1, LANES)),
            whole_block((rows, LANES)),
            whole_block((rows, LANES)),
        ],
        out_specs=[
            whole_block((rows, width)),
            pl.BlockSpec((1, rows, q_width + LANES), lambda p: (p, 0, 0)),
            pl.BlockSpec((2, rows // 2, block_width), lambda p: (p, 0, 0)),
        ],
        out_shape=[
            jax.ShapeDtypeStruct((rows, width), BF16),
            jax.ShapeDtypeStruct((chips, rows, q_width + LANES), F32),
            jax.ShapeDtypeStruct((2 * chips, rows // 2, block_width), BF16),
        ],
        compiler_params=kernel_params(),
    )(tokens, gain, wq, wk, wv, q_gain, k_gain, cosine, sine)


def low_lanes(shape):
    return lax.broadcasted_iota(jnp.int32, shape, 1) < HEAD_DIM


def doubled(pair, group):
    turned = pltpu.roll(pair.astype(F32), HEAD_DIM, 1).astype(BF16)
    low = low_lanes(pair.shape)
    return jnp.where(low, pair, turned) if group == 0 else jnp.where(low, turned, pair)


def stacked_heads(pair):
    low = low_lanes(pair.shape)
    none = jnp.zeros_like(pair)
    return jnp.concatenate([jnp.where(low, pair, none), jnp.where(low, none, pair)], axis=0)


def in_three(column):
    lane = lax.broadcasted_iota(jnp.int32, (column.shape[0], LANES), 1)
    wide = jnp.broadcast_to(column, (column.shape[0], LANES))
    first = wide.astype(BF16).astype(F32)
    second = (wide - first).astype(BF16).astype(F32)
    third = wide - first - second
    return jnp.where(
        lane == 0, first, jnp.where(lane == 1, second, jnp.where(lane == 2, third, 0.0))
    ).astype(BF16)


def minus_three(rows):
    lane = lax.broadcasted_iota(jnp.int32, (rows, LANES), 1)
    return jnp.where(lane < 3, -1.0, 0.0).astype(BF16)


def attend_kernel(groups, block, qkv_ref, starts_ref, out_ref, logs_ref, keys, values, total):
    size = qkv_ref.shape[0]
    q_width = groups * LANES
    here = pl.program_id(0)

    @pl.when(here == 0)
    def _():
        for g in range(groups):
            keys[g] = doubled(qkv_ref[:, q_width : q_width + LANES], g)
            values[g, :, :LANES] = doubled(qkv_ref[:, q_width + LANES : q_width + 2 * LANES], g)
            values[g, :, LANES:] = jnp.ones((size, LANES), BF16)

    at = pl.multiple_of(here * block, block)
    starts = jnp.concatenate([starts_ref[pl.ds(at, block), :]] * 2, axis=0)
    queries = [
        stacked_heads(qkv_ref[pl.ds(at, block), g * LANES : (g + 1) * LANES]) for g in range(groups)
    ]
    column = lax.broadcasted_iota(jnp.int32, (2 * block, block), 1)
    row = lax.broadcasted_iota(jnp.int32, (2 * block, block), 0) % block

    def step(j, diagonal):
        key_at = pl.multiple_of(j * block, block)
        allowed = column >= starts - key_at
        if diagonal:
            allowed = allowed & (column <= row)
        for g in range(groups):
            scores = nt_dot(queries[g], keys[g, pl.ds(key_at, block), :])
            weights = jnp.exp2(jnp.where(allowed, scores, MASKED)).astype(BF16)
            part = nn_dot(weights, values[g, pl.ds(key_at, block), :])
            if diagonal:
                total[g] = part
            else:
                total[g] += part

    step(here, True)

    def body(j, carry):
        step(j, False)
        return carry

    lax.fori_loop(0, here, body, 0)
    for g in range(groups):
        sums = total[g, :, LANES:]
        mean = total[g, :, :LANES] / sums
        low = low_lanes((block, LANES))
        out_ref[0, :, g * LANES : (g + 1) * LANES] = jnp.where(low, mean[:block], mean[block:]).astype(BF16)
        logs_ref[g] = in_three(jnp.log2(sums[:, :1]))


def attend(qkv, starts, block):
    size, width = qkv.shape
    groups = (width - 2 * LANES) // LANES
    blocks = size // block
    return pl.pallas_call(
        functools.partial(attend_kernel, groups, block),
        name="attend",
        grid=(blocks,),
        in_specs=[whole_block((size, width)), whole_block((size, 1))],
        out_specs=[
            pl.BlockSpec((1, block, groups * LANES), lambda i: (i, 0, 0)),
            pl.BlockSpec((groups, 2 * block, LANES), lambda i: (0, i, 0)),
        ],
        out_shape=[
            jax.ShapeDtypeStruct((blocks, block, groups * LANES), BF16),
            jax.ShapeDtypeStruct((groups, 2 * size, LANES), BF16),
        ],
        scratch_shapes=[
            pltpu.VMEM((groups, size, LANES), BF16),
            pltpu.VMEM((groups, size, 2 * LANES), BF16),
            pltpu.VMEM((groups, 2 * block, 2 * LANES), F32),
        ],
        compiler_params=kernel_params(),
    )(qkv, starts)


def middle_kernel(tokens_ref, heads_ref, w_out_ref, gain_ref, middle_ref, hidden_ref):
    half = heads_ref.shape[1]
    width = heads_ref.shape[2]
    total = tokens_ref[...].astype(F32)
    for p in range(heads_ref.shape[0] // 2):
        block = jnp.concatenate([heads_ref[2 * p], heads_ref[2 * p + 1]], axis=0)
        total = total + nn_dot(block, w_out_ref[p * width : (p + 1) * width, :])
    middle_ref[...] = total
    scale = lax.rsqrt(jnp.mean(total * total, axis=-1, keepdims=True) + EPSILON)
    hidden_ref[...] = (total * scale * gain_ref[...]).astype(BF16)


def middle_layer(tokens, heads, w_out, gain):
    return pl.pallas_call(
        middle_kernel,
        name="middle",
        out_shape=[
            jax.ShapeDtypeStruct(tokens.shape, F32),
            jax.ShapeDtypeStruct(tokens.shape, BF16),
        ],
        compiler_params=kernel_params(),
    )(tokens, heads, w_out, gain)


def ffn_kernel(
    core_ref,
    hidden_ref,
    grad_ref,
    w_gate_ref,
    w_up_ref,
    w_down_ref,
    gate_grad_ref,
    up_grad_ref,
    acts_ref,
    out_own_ref,
    out_send_ref,
    back_own_ref,
    back_send_ref,
    out_sum,
    back_sum,
):
    step = pl.program_id(0)
    rows = hidden_ref.shape[0]
    chunk = min(256, rows)

    @pl.when(step == 0)
    def _():
        out_sum[...] = jnp.zeros_like(out_sum)
        back_sum[...] = jnp.zeros_like(back_sum)

    for m in range(rows // chunk):
        part = slice(m * chunk, (m + 1) * chunk)
        hidden = hidden_ref[part, :]
        gate = nn_dot(hidden, w_gate_ref[...])
        up = nn_dot(hidden, w_up_ref[...])
        pushed = nt_dot(grad_ref[part, :], w_down_ref[...])
        opened = jax.nn.sigmoid(gate)
        silu = gate * opened
        act = (silu * up).astype(BF16)
        gate_grad = (pushed * up * opened * (1.0 + gate * (1.0 - opened))).astype(BF16)
        up_grad = (pushed * silu).astype(BF16)
        acts_ref[:, part] = act.T
        gate_grad_ref[part, :] = gate_grad
        up_grad_ref[part, :] = up_grad
        out_sum[part, :] += nn_dot(act, w_down_ref[...])
        back_sum[part, :] += nt_dot(gate_grad, w_gate_ref[...]) + nt_dot(up_grad, w_up_ref[...])

    @pl.when(step == pl.num_programs(0) - 1)
    def _():
        half = rows // 2
        out_own_ref[...] = out_sum[:half, :]
        out_send_ref[...] = out_sum[half:, :].astype(BF16)
        back_own_ref[...] = back_sum[:half, :]
        back_send_ref[...] = back_sum[half:, :].astype(BF16)


def feed_forward(core, hidden, grad, w_gate, w_up, w_down):
    rows, width = hidden.shape
    tiles = w_gate.shape[1] // 2 // FF_TILE
    half = (rows // 2, width)

    def keep(shape):
        return pl.BlockSpec(shape, lambda f, c: (0,) * len(shape), pipeline_mode=pl.Buffered(1))

    return pl.pallas_call(
        ffn_kernel,
        name="feed_forward",
        grid_spec=pltpu.PrefetchScalarGridSpec(
            num_scalar_prefetch=1,
            grid=(tiles,),
            in_specs=[
                keep((rows, width)),
                keep((rows, width)),
                pl.BlockSpec((width, FF_TILE), lambda f, c: (0, c[0] * tiles + f)),
                pl.BlockSpec((width, FF_TILE), lambda f, c: (0, c[0] * tiles + f)),
                pl.BlockSpec((FF_TILE, width), lambda f, c: (c[0] * tiles + f, 0)),
            ],
            out_specs=[
                pl.BlockSpec((rows, FF_TILE), lambda f, c: (0, f)),
                pl.BlockSpec((rows, FF_TILE), lambda f, c: (0, f)),
                pl.BlockSpec((FF_TILE, rows), lambda f, c: (f, 0)),
            ]
            + [keep(half)] * 4,
            scratch_shapes=[pltpu.VMEM((rows, width), F32), pltpu.VMEM((rows, width), F32)],
        ),
        out_shape=[
            jax.ShapeDtypeStruct((rows, tiles * FF_TILE), BF16),
            jax.ShapeDtypeStruct((rows, tiles * FF_TILE), BF16),
            jax.ShapeDtypeStruct((tiles * FF_TILE, rows), BF16),
        ]
        + [jax.ShapeDtypeStruct(half, kind) for kind in (F32, BF16, F32, BF16)],
        compiler_params=kernel_params(),
    )(core, hidden, grad, w_gate, w_up, w_down)


def turn_kernel(
    middle_ref,
    out_own_ref,
    out_got_ref,
    back_own_ref,
    back_got_ref,
    grad_ref,
    gain_ref,
    heads_ref,
    w_out_ref,
    output_ref,
    mid_ref,
    gain_grad_ref,
    w_grad_ref,
    send_ref,
    low_grad,
):
    @pl.when(pl.program_id(0) == 0)
    def _():
        middle = middle_ref[...]
        result = middle + (out_own_ref[...] + out_got_ref[...].astype(F32))
        output_ref[...] = result.astype(BF16)
        scale = lax.rsqrt(jnp.mean(middle * middle, axis=-1, keepdims=True) + EPSILON)
        normal = middle * scale
        back = back_own_ref[...] + back_got_ref[...].astype(F32)
        gain_grad_ref[...] = jnp.sum(back * normal, axis=0, keepdims=True)
        pushed = back * gain_ref[...]
        inner = jnp.mean(pushed * normal, axis=-1, keepdims=True)
        mid = grad_ref[...].astype(F32) + scale * (pushed - normal * inner)
        mid_ref[...] = mid
        low_grad[...] = mid.astype(BF16)

    half = heads_ref.shape[1]
    heads = jnp.concatenate([heads_ref[0], heads_ref[1]], axis=0)
    grad = low_grad[...]
    w_grad_ref[...] = tn_dot(heads, grad).astype(BF16)
    send = nt_dot(grad, w_out_ref[...]).astype(BF16)
    send_ref[0] = send[:half]
    send_ref[1] = send[half:]


def turn(middle, out_own, out_got, back_own, back_got, grad, gain, heads, w_out):
    rows, width = middle.shape
    count, half, lanes = heads.shape
    chips = count // 2
    return pl.pallas_call(
        turn_kernel,
        name="turn",
        grid=(chips,),
        in_specs=[whole_block((rows, width))] * 6
        + [
            whole_block((1, width)),
            pl.BlockSpec((2, half, lanes), lambda p: (p, 0, 0)),
            pl.BlockSpec((lanes, width), lambda p: (p, 0)),
        ],
        out_specs=[
            whole_block((rows, width)),
            whole_block((rows, width)),
            whole_block((1, width)),
            pl.BlockSpec((lanes, width), lambda p: (p, 0)),
            pl.BlockSpec((2, half, lanes), lambda p: (p, 0, 0)),
        ],
        out_shape=[
            jax.ShapeDtypeStruct((rows, width), BF16),
            jax.ShapeDtypeStruct((rows, width), F32),
            jax.ShapeDtypeStruct((1, width), F32),
            jax.ShapeDtypeStruct((chips * lanes, width), BF16),
            jax.ShapeDtypeStruct(heads.shape, BF16),
        ],
        scratch_shapes=[pltpu.VMEM((rows, width), BF16)],
        compiler_params=kernel_params(),
    )(middle, out_own, out_got, back_own, back_got, grad, gain, heads, w_out)


def project_back_kernel(
    got_ref,
    proj_ref,
    hidden_ref,
    tokens_ref,
    mid_ref,
    gain_ref,
    wq_ref,
    wk_ref,
    wv_ref,
    q_gain_ref,
    k_gain_ref,
    cos_ref,
    sin_ref,
    input_ref,
    gain_grad_ref,
    q_gain_grad_ref,
    k_gain_grad_ref,
    gq_ref,
    gk_ref,
    gv_ref,
    total,
):
    step = pl.program_id(0)

    @pl.when(step == 0)
    def _():
        total[...] = jnp.zeros_like(total)
        q_gain_grad_ref[...] = jnp.zeros_like(q_gain_grad_ref)
        k_gain_grad_ref[...] = jnp.zeros_like(k_gain_grad_ref)

    q_width = wq_ref.shape[1]
    hidden = hidden_ref[...]

    def back(lane, head_gain, gain_out):
        got = jnp.concatenate(
            [got_ref[0, :, lane : lane + LANES], got_ref[1, :, lane : lane + LANES]], axis=0
        ).astype(F32)
        turned = got * cos_ref[...] - half_partner(got) * sin_ref[...]
        block = proj_ref[0, :, lane : lane + LANES]
        scale = lax.rsqrt(head_means(block * block) + EPSILON)
        normal = block * scale
        gain_out[...] += jnp.sum(turned * normal, axis=0, keepdims=True)
        pushed = turned * head_gain[...]
        inner = head_means(pushed * normal)
        return (scale * (pushed - normal * inner)).astype(BF16)

    query = jnp.concatenate(
        [back(at, q_gain_ref, q_gain_grad_ref) for at in range(0, q_width, LANES)], axis=1
    )
    key = back(q_width, k_gain_ref, k_gain_grad_ref)
    lane = q_width + LANES
    value = jnp.concatenate(
        [got_ref[0, :, lane : lane + LANES], got_ref[1, :, lane : lane + LANES]], axis=0
    )
    gq_ref[...] = tn_dot(hidden, query).astype(BF16)
    gk_ref[...] = tn_dot(hidden, key).astype(BF16)
    gv_ref[...] = tn_dot(hidden, value).astype(BF16)
    total[...] += (
        nt_dot(query, wq_ref[...]) + nt_dot(key, wk_ref[...]) + nt_dot(value, wv_ref[...])
    )

    @pl.when(step == pl.num_programs(0) - 1)
    def _():
        inputs = tokens_ref[...].astype(F32)
        scale = lax.rsqrt(jnp.mean(inputs * inputs, axis=-1, keepdims=True) + EPSILON)
        normal = inputs * scale
        grad = total[...]
        gain_grad_ref[...] = jnp.sum(grad * normal, axis=0, keepdims=True)
        pushed = grad * gain_ref[...]
        inner = jnp.mean(pushed * normal, axis=-1, keepdims=True)
        input_ref[...] = (mid_ref[...] + scale * (pushed - normal * inner)).astype(BF16)


def project_back(got, proj, hidden, tokens, mid, gain, wq, wk, wv, q_gain, k_gain, cosine, sine):
    rows, width = tokens.shape
    count, half, lanes = got.shape
    chips = count // 2
    q_width = wq.shape[1] // chips
    return pl.pallas_call(
        project_back_kernel,
        name="project_back",
        grid=(chips,),
        in_specs=[
            pl.BlockSpec((2, half, lanes), lambda p: (p, 0, 0)),
            pl.BlockSpec((1, rows, q_width + LANES), lambda p: (p, 0, 0)),
            whole_block((rows, width)),
            whole_block((rows, width)),
            whole_block((rows, width)),
            whole_block((1, width)),
            pl.BlockSpec((width, q_width), lambda p: (0, p)),
            pl.BlockSpec((width, LANES), lambda p: (0, p)),
            pl.BlockSpec((width, LANES), lambda p: (0, p)),
            whole_block((1, LANES)),
            whole_block((1, LANES)),
            whole_block((rows, LANES)),
            whole_block((rows, LANES)),
        ],
        out_specs=[
            whole_block((rows, width)),
            whole_block((1, width)),
            whole_block((1, LANES)),
            whole_block((1, LANES)),
            pl.BlockSpec((width, q_width), lambda p: (0, p)),
            pl.BlockSpec((width, LANES), lambda p: (0, p)),
            pl.BlockSpec((width, LANES), lambda p: (0, p)),
        ],
        out_shape=[
            jax.ShapeDtypeStruct((rows, width), BF16),
            jax.ShapeDtypeStruct((1, width), F32),
            jax.ShapeDtypeStruct((1, LANES), F32),
            jax.ShapeDtypeStruct((1, LANES), F32),
            jax.ShapeDtypeStruct(wq.shape, BF16),
            jax.ShapeDtypeStruct(wk.shape, BF16),
            jax.ShapeDtypeStruct(wv.shape, BF16),
        ],
        scratch_shapes=[pltpu.VMEM((rows, width), F32)],
        compiler_params=kernel_params(),
    )(got, proj, hidden, tokens, mid, gain, wq, wk, wv, q_gain, k_gain, cosine, sine)


def pair_of(bit):
    index = lax.axis_index("blk")
    mine = lax.rem(index // bit, 2)
    return mine, (lax.axis_index("dp"), index + bit * (1 - 2 * mine))


class Stream:
    def __init__(self, path, dims, block, line, kind=BF16):
        self.path, self.block, self.line, self.kind = path, block, line, kind
        self.dims = [tuple(dims)]
        left = list(dims)
        names = [name for name, unused in dims]
        for stage in path:
            if isinstance(stage, tuple):
                if stage[1] == line - 1:
                    at = [n for n, unused in left].index("z")
                    left = left[:at] + left[at + 1 :]
            else:
                at = [n for n, unused in left].index(stage)
                left = left[:at] + left[at + 1 :]
            self.dims.append(tuple(left))
        assert not left and "z" in names

    def is_hop(self, k):
        return isinstance(self.path[k], tuple)

    def starts_work(self, k):
        return k == 0 or not self.is_hop(k) or self.path[k][1] == 1

    def shape(self, dims):
        return tuple(count for unused, count in dims) + self.block

    def slots(self, k):
        return self.line if self.is_hop(k) else 2

    def scratch(self):
        shapes = []
        for k in range(len(self.path)):
            if self.starts_work(k):
                shapes.append(pltpu.VMEM((self.slots(k),) + self.shape(self.dims[k]), self.kind))
            if self.is_hop(k):
                rest = tuple(d for d in self.dims[k] if d[0] != "z")
                shapes.append(pltpu.VMEM((2, 2) + self.shape(rest), self.kind))
                shapes += [pltpu.SemaphoreType.DMA((2, 2))] * 2
            else:
                shapes.append(pltpu.VMEM((2,) + self.shape(self.dims[k + 1]), self.kind))
                shapes += [pltpu.SemaphoreType.DMA((2,))] * 2
        return shapes

    def bind(self, refs, units, finish, first_z=None):
        refs = list(refs)
        self.units, self.finish = units, finish
        self.first_z = 0 if first_z is None else first_z
        self.work, self.got, self.sent_sem, self.got_sem = [], [], [], []
        for k in range(len(self.path)):
            self.work.append(refs.pop(0) if self.starts_work(k) else self.work[-1])
            self.got.append(refs.pop(0))
            self.sent_sem.append(refs.pop(0))
            self.got_sem.append(refs.pop(0))
        self.source = self.work[0]

    def z_count(self, k):
        return dict(self.dims[k])["z"]

    def keeps(self, z, k):
        return (z >= self.first_z) & (z < self.first_z + self.z_count(k))

    def keeper(self, k):
        if "z" in [name for name, unused in self.dims[k]] or dict(self.dims[0])["z"] == self.line:
            return None
        z = lax.axis_index("dp")
        return (z >= self.first_z) & (z < self.first_z + dict(self.dims[0])["z"])

    def pair_copy(self, k, u):
        bit = self.path[k]
        mine, partner = pair_of(bit)
        at = [name for name, unused in self.dims[k]].index(bit)
        whole = (slice(None),) * at
        slot = lax.rem(u, 2)
        copy = pltpu.make_async_remote_copy(
            src_ref=self.work[k].at[(lax.rem(u, self.slots(k)),) + whole + (1 - mine,)],
            dst_ref=self.got[k].at[slot],
            send_sem=self.sent_sem[k].at[slot],
            recv_sem=self.got_sem[k].at[slot],
            device_id=partner,
            device_id_type=pl.DeviceIdType.MESH,
        )
        return copy, whole + (mine,)

    def hop_copy(self, k, u, way, block):
        z, index = lax.axis_index("dp"), lax.axis_index("blk")
        slot = lax.rem(u, 2)
        side = (1 - way) // 2
        return pltpu.make_async_remote_copy(
            src_ref=self.work[k].at[lax.rem(u, self.slots(k)), block],
            dst_ref=self.got[k].at[slot, side],
            send_sem=self.sent_sem[k].at[slot, side],
            recv_sem=self.got_sem[k].at[slot, side],
            device_id=(z + way, index),
            device_id_type=pl.DeviceIdType.MESH,
        )

    def hop_ends(self, k, way):
        z = lax.axis_index("dp")
        reach = way * (self.line - self.path[k][1])
        goes, comes = z + reach, z - way + reach
        sends = self.keeps(goes, k)
        takes = self.keeps(comes, k) & (z - way >= 0) & (z - way < self.line)
        return goes - self.first_z, sends, comes - self.first_z, takes

    def send(self, k, step):
        u = step - k - 1
        due = (u >= 0) & (u < self.units)
        if not self.is_hop(k):
            keeper = self.keeper(k)

            @pl.when(due if keeper is None else due & keeper)
            def _():
                self.pair_copy(k, u)[0].start()

            return
        for way in (1, -1):
            block, sends, unused, unused = self.hop_ends(k, way)

            @pl.when(due & sends)
            def _():
                self.hop_copy(k, u, way, block).start()

    def take(self, k, step):
        u = step - k - 2
        due = (u >= 0) & (u < self.units)
        keeper = self.keeper(k + 1)
        last = k == len(self.path) - 1

        def pass_on(value):
            if last:
                self.finish(u, value)
            else:
                self.work[k + 1][lax.rem(u, self.slots(k + 1))] = value

        if not self.is_hop(k):
            keeper = self.keeper(k)

            @pl.when(due if keeper is None else due & keeper)
            def _():
                copy, mine = self.pair_copy(k, u)
                copy.wait()
                own = self.work[k][(lax.rem(u, self.slots(k)),) + mine]
                pass_on(own + self.got[k][lax.rem(u, 2)])

            return
        slot = lax.rem(u, self.slots(k))
        for way in (1, -1):
            out_block, sends, in_block, takes = self.hop_ends(k, way)

            @pl.when(due & sends)
            def _():
                self.hop_copy(k, u, way, out_block).wait_send()

            @pl.when(due & takes)
            def _():
                self.hop_copy(k, u, way, in_block).wait_recv()
                self.work[k][slot, in_block] += self.got[k][lax.rem(u, 2), (1 - way) // 2]

        if self.path[k][1] == self.line - 1:
            own = lax.axis_index("dp") - self.first_z

            @pl.when(due if keeper is None else due & keeper)
            def _():
                pass_on(self.work[k][slot, own])


def hops(line):
    return [("z", t) for t in range(1, line)]


def greet(bits, line):
    barrier = pltpu.get_barrier_semaphore()
    z, index = lax.axis_index("dp"), lax.axis_index("blk")
    for bit in bits:
        pl.semaphore_signal(barrier, inc=1, device_id=pair_of(bit)[1], device_id_type=pl.DeviceIdType.MESH)
    for way in (1, -1):

        @pl.when((z + way >= 0) & (z + way < line))
        def _():
            pl.semaphore_signal(
                barrier, inc=1, device_id=(z + way, index), device_id_type=pl.DeviceIdType.MESH
            )

    beside = jnp.minimum(z, 1) + jnp.minimum(line - 1 - z, 1)
    pl.semaphore_wait(barrier, len(bits) + beside)


def step_streams(streams, step, steps, line, ready):
    longest = max(len(stream.path) for stream in streams)
    z, index = lax.axis_index("dp"), lax.axis_index("blk")
    for k in range(longest):
        for stream in streams:
            if k < len(stream.path):
                stream.take(k, step)
    for way in (1, -1):
        there = (z + way >= 0) & (z + way < line)

        @pl.when(there & (step < steps - 1))
        def _():
            pl.semaphore_signal(
                ready.at[(1 - way) // 2],
                inc=1,
                device_id=(z + way, index),
                device_id_type=pl.DeviceIdType.MESH,
            )

        @pl.when(there & (step > 0))
        def _():
            pl.semaphore_wait(ready.at[(1 + way) // 2], 1)

    for k in range(longest):
        for stream in streams:
            if k < len(stream.path):
                stream.send(k, step)


def back_kernel(
    groups,
    block,
    line,
    bits,
    streams,
    units,
    qkv_ref,
    logs_ref,
    out_ref,
    grad_ref,
    starts_ref,
    flipped_ref,
    dy_ref,
    gate_grad_ref,
    up_grad_ref,
    acts_ref,
    result_ref,
    gate_out_ref,
    up_out_ref,
    down_out_ref,
    queries,
    keys,
    values,
    grads,
    query_grad,
    pair_grad,
    ready,
    *refs,
):
    size = qkv_ref.shape[0]
    blocks = size // block
    q_width = groups * LANES
    n = pl.program_id(0)
    core = lax.rem(lax.axis_index("blk"), 2)
    gate_stream, up_stream, down_stream = streams

    def finish_gate(u, value):
        gate_out_ref[:, pl.ds(pl.multiple_of(u * FF_TILE, FF_TILE), FF_TILE)] = value

    def finish_up(u, value):
        up_out_ref[:, pl.ds(pl.multiple_of(u * FF_TILE, FF_TILE), FF_TILE)] = value

    def finish_down(u, value):
        rows = value.shape[0]
        down_out_ref[pl.ds(pl.multiple_of(u * rows, rows), rows), :] = value

    at = 0
    for stream, finish, first_z in (
        (gate_stream, finish_gate, None),
        (up_stream, finish_up, None),
        (down_stream, finish_down, core * (line // 2)),
    ):
        count = len(stream.scratch())
        stream.bind(refs[at : at + count], units, finish, first_z)
        at += count

    @pl.when(n == 0)
    def _():
        greet(bits, line)
        down_out_ref[...] = jnp.zeros_like(down_out_ref)
        query_grad[...] = jnp.zeros_like(query_grad)
        pair_grad[...] = jnp.zeros_like(pair_grad)
        for g in range(groups):
            lanes = slice(g * LANES, (g + 1) * LANES)
            keys[g, :, :LANES] = doubled(qkv_ref[:, q_width : q_width + LANES], g)
            keys[g, :, LANES:] = minus_three(size)
            values[g, :, :LANES] = doubled(qkv_ref[:, q_width + LANES : q_width + 2 * LANES], g)
            values[g, :, LANES:] = minus_three(size)

            def fill(i, carry):
                at = pl.multiple_of(i * block, block)
                to = pl.multiple_of(i * 2 * block, 2 * block)
                queries[g, pl.ds(to, 2 * block), :LANES] = stacked_heads(qkv_ref[pl.ds(at, block), lanes])
                queries[g, pl.ds(to, 2 * block), LANES:] = logs_ref[g, pl.ds(to, 2 * block), :]
                grad = stacked_heads(grad_ref[pl.ds(at, block), lanes])
                mean = stacked_heads(out_ref[pl.ds(at, block), lanes])
                delta = jnp.sum(grad.astype(F32) * mean.astype(F32), axis=1, keepdims=True)
                grads[g, pl.ds(to, 2 * block), :LANES] = grad
                grads[g, pl.ds(to, 2 * block), LANES:] = in_three(delta)
                return carry

            lax.fori_loop(0, blocks, fill, 0)

    step_streams(streams, n, pl.num_programs(0), line, ready)

    @pl.when(n < units)
    def _():
        chunk = 256
        width = flipped_ref.shape[0]
        gate_shape = gate_stream.shape(gate_stream.dims[0])
        down_shape = down_stream.shape(down_stream.dims[0])
        slot = lax.rem(n, 2)
        each = chunk * gate_shape[0] // width

        def weights(m, carry):
            flipped = flipped_ref[pl.ds(pl.multiple_of(m * chunk, chunk), chunk), :]
            part = pl.ds(m * each, each)
            piece = (each,) + gate_shape[1:]
            gate_stream.source[slot, part] = nn_dot(flipped, gate_grad_ref[...]).astype(BF16).reshape(piece)
            up_stream.source[slot, part] = nn_dot(flipped, up_grad_ref[...]).astype(BF16).reshape(piece)
            return carry

        lax.fori_loop(0, width // chunk, weights, 0)
        acts = acts_ref[...].reshape(-1, acts_ref.shape[-1])
        made = nn_dot(acts, dy_ref[...]).astype(BF16)
        down_stream.source[lax.rem(n, down_stream.slots(0))] = made.reshape(down_shape)

    row = lax.broadcasted_iota(jnp.int32, (block, 2 * block), 0)
    column = lax.broadcasted_iota(jnp.int32, (block, 2 * block), 1) % block

    @pl.when(n < blocks + 1)
    def _():
        def pair(m, carry):
            late = (n + m) // blocks
            j = m + late * (blocks - 1 - 2 * m)
            i = (1 - late) * (m + n) + late * (n - 1)
            key_at = pl.multiple_of(j * block, block)
            at = pl.multiple_of(i * 2 * block, 2 * block)
            key_rows = pl.ds(key_at, block)
            stack = pl.ds(at, 2 * block)
            allowed = (row >= starts_ref[:, stack] - key_at) & (row - column <= (i - j) * block)
            for g in range(groups):
                query = queries[g, stack, :]
                grad = grads[g, stack, :]
                key = keys[g, key_rows, :]
                scores = nt_dot(key, query)
                probs = jnp.exp2(jnp.where(allowed, scores, MASKED))
                pushed = (probs * nt_dot(values[g, key_rows, :], grad)).astype(BF16)
                pair_grad[g, key_rows, LANES:] += nn_dot(probs.astype(BF16), grad[:, :LANES])
                pair_grad[g, key_rows, :LANES] += nn_dot(pushed, query[:, :LANES])
                query_grad[g, stack, :] += tn_dot(pushed, key[:, :LANES])
            return carry

        lax.fori_loop(0, blocks // 2, pair, 0)

    @pl.when(n == blocks + 1)
    def _():
        low = low_lanes((block, LANES))

        def finish(i, carry):
            at = pl.multiple_of(i * block, block)
            to = pl.multiple_of(i * 2 * block, 2 * block)
            here = pl.ds(at, block)
            for g in range(groups):
                first = query_grad[g, pl.ds(to, block), :]
                second = query_grad[g, pl.ds(to + block, block), :]
                joined = jnp.where(low, first, second) * HEAD_DIM ** (-0.5)
                result_ref[here, g * LANES : (g + 1) * LANES] = joined.astype(BF16)
            for part in range(2):
                sums = []
                for g in range(groups):
                    both = pair_grad[g, here, part * LANES : (part + 1) * LANES]
                    sums.append(both + pltpu.roll(both, HEAD_DIM, 1))
                joined = jnp.where(low, sums[0], sums[1])
                if part == 0:
                    joined = joined * (1.0 / LOG2_E)
                lane = q_width + part * LANES
                result_ref[here, lane : lane + LANES] = joined.astype(BF16)
            return carry

        lax.fori_loop(0, blocks, finish, 0)


def back(line, bits, qkv, logs, out, grad, starts, block, flipped, dy, gate_grad, up_grad, acts):
    size, width = qkv.shape
    groups = (width - 2 * LANES) // LANES
    units = gate_grad.shape[1] // FF_TILE
    model, rows = flipped.shape
    chips = line * 2 ** len(bits)
    sides = [(bit, 2) for bit in bits]
    gate_block = (model // chips, FF_TILE)
    down_rows = acts.shape[0] // (chips // 2)
    down_block = (down_rows // units, model)
    whole = [("z", line)] + sides
    half = [("z", line // 2)] + sides
    streams = [
        Stream(bits[::-1] + hops(line), whole, gate_block, line),
        Stream(bits + hops(line), whole, gate_block, line),
        Stream(hops(line) + bits, half, down_block, line),
    ]
    longest = max(len(stream.path) for stream in streams)
    steps = units + longest + 1

    def keep(shape):
        return pl.BlockSpec(shape, lambda n: (0,) * len(shape), pipeline_mode=pl.Buffered(1))

    tile = lambda n: (0, jnp.minimum(n, units - 1))
    acts = acts.reshape(chips // 2, down_rows, rows)
    scratch = [
        pltpu.VMEM((groups, 2 * size, 2 * LANES), BF16),
        pltpu.VMEM((groups, size, 2 * LANES), BF16),
        pltpu.VMEM((groups, size, 2 * LANES), BF16),
        pltpu.VMEM((groups, 2 * size, 2 * LANES), BF16),
        pltpu.VMEM((groups, 2 * size, LANES), F32),
        pltpu.VMEM((groups, size, 2 * LANES), F32),
        pltpu.SemaphoreType.REGULAR((2,)),
    ]
    for stream in streams:
        scratch += stream.scratch()
    return pl.pallas_call(
        functools.partial(back_kernel, groups, block, line, bits, streams, units),
        name="back",
        grid=(steps,),
        in_specs=[
            keep(qkv.shape),
            keep(logs.shape),
            keep(out.shape),
            keep(grad.shape),
            keep(starts.shape),
            keep(flipped.shape),
            keep(dy.shape),
            pl.BlockSpec((rows, FF_TILE), tile),
            pl.BlockSpec((rows, FF_TILE), tile),
            pl.BlockSpec(
                (chips // 2, down_block[0], rows), lambda n: (0, jnp.minimum(n, units - 1), 0)
            ),
        ],
        out_specs=[
            keep(qkv.shape),
            keep((gate_block[0], units * FF_TILE)),
            keep((gate_block[0], units * FF_TILE)),
            keep((down_rows, model)),
        ],
        out_shape=[
            jax.ShapeDtypeStruct(qkv.shape, BF16),
            jax.ShapeDtypeStruct((gate_block[0], units * FF_TILE), BF16),
            jax.ShapeDtypeStruct((gate_block[0], units * FF_TILE), BF16),
            jax.ShapeDtypeStruct((down_rows, model), BF16),
        ],
        scratch_shapes=scratch,
        compiler_params=kernel_params(collective_id=4, has_side_effects=True),
    )(qkv, logs, out, grad, starts, flipped, dy, gate_grad, up_grad, acts)


def flip_pairs(count, bit):
    return [(i, i ^ bit) for i in range(count)]


def sum_pair(parts, axis, count, bit, dim):
    mine = (lax.axis_index(axis) // bit) % 2
    send = lax.dynamic_index_in_dim(parts, 1 - mine, dim, keepdims=False)
    own = lax.dynamic_index_in_dim(parts, mine, dim, keepdims=False)
    return own + lax.ppermute(send, axis, flip_pairs(count, bit))


def sum_line(parts, axis, count):
    mine = lax.axis_index(axis)
    total = lax.dynamic_index_in_dim(parts, mine, 0, keepdims=False)
    for way in (1, -1):
        got = None
        for step in range(1, count):
            target = jnp.clip(mine + way * (count - step), 0, count - 1)
            send = lax.dynamic_index_in_dim(parts, target, 0, keepdims=False)
            if got is not None:
                send = send + got
            if way == 1:
                pairs = [(i, i + 1) for i in range(step)]
            else:
                pairs = [(count - 1 - i, count - 2 - i) for i in range(step)]
            got = lax.ppermute(send, axis, pairs)
        total = total + got
    return total


def sum_chips(parts, order, dp_count, blk_count):
    bits = []
    bit = blk_count // 2
    while bit > 1:
        bits.append(bit)
        bit //= 2
    left = ["z"] + bits
    for stage in order:
        dim = left.index(stage)
        left.pop(dim)
        if stage == "z":
            parts = sum_line(jnp.moveaxis(parts, dim, 0) if dim else parts, "dp", dp_count)
        else:
            parts = sum_pair(parts, "blk", blk_count, stage, dim)
    return parts


def swap_core(block, blk_count):
    return lax.ppermute(block, "blk", flip_pairs(blk_count, 1))


def fast_local(
    dp_count,
    blk_count,
    tokens,
    doc_lengths,
    g_attn,
    w_query,
    w_key,
    w_value,
    q_gain,
    k_gain,
    w_out,
    g_ffn,
    w_gate,
    w_up,
    w_down,
    cotangent,
):
    row_count, tok_count, width = tokens.shape
    rows = row_count * tok_count
    chips = blk_count // 2
    size = tok_count * blk_count
    index = lax.axis_index("blk")
    core = index % 2
    bits = []
    bit = blk_count // 2
    while bit > 1:
        bits.append(bit)
        bit //= 2
    chip_dims = (dp_count,) + (2,) * len(bits)
    all_chips = dp_count * chips
    places = index * tok_count + jnp.arange(tok_count, dtype=jnp.int32)
    unused, positions = doc_layout(doc_lengths, places)
    cosine, sine = rope_angles(positions)
    cosine = jnp.tile(cosine.reshape(rows, -1), (1, 4))
    sine = sine.reshape(rows, -1)
    sine = jnp.concatenate([-sine, sine, -sine, sine], axis=1)
    q_gain2 = jnp.tile(q_gain, 2)[None]
    k_gain2 = jnp.tile(k_gain, 2)[None]
    all_places = jnp.arange(size, dtype=jnp.int32)
    row_lengths = lax.dynamic_slice_in_dim(doc_lengths, core, 1, axis=0)
    unused, all_positions = doc_layout(row_lengths, all_places)
    starts = all_places - all_positions[0]
    starts_two = jnp.broadcast_to(
        starts.reshape(blk_count, 1, tok_count), (blk_count, 2, tok_count)
    ).reshape(1, 2 * size)
    flat = tokens.reshape(rows, width)
    grad_own = cotangent.reshape(rows, width)
    grad_both = jnp.concatenate([grad_own, swap_core(grad_own, blk_count)], axis=0)

    hidden_in, proj, send = project(
        flat, g_attn[None], w_query, w_key, w_value, q_gain2, k_gain2, cosine, sine
    )
    qkv = swap_blocks(send, 0).reshape(size, -1)
    attended, logs = attend(qkv, starts[:, None], tok_count)
    heads = swap_blocks(attended, 1)
    middle, hidden_own = middle_layer(flat, heads, w_out, g_ffn[None])
    hidden = jnp.concatenate([hidden_own, swap_core(hidden_own, blk_count)], axis=0)
    flipped = hidden.T
    core_arg = core.reshape(1)
    gate_grad, up_grad, acts, out_own, out_send, back_own, back_send = feed_forward(
        core_arg, hidden, grad_both, w_gate, w_up, w_down
    )
    back_got = swap_core(back_send, blk_count)
    out_got = swap_core(out_send, blk_count)
    output, mid, ffn_gain_grad, w_out_parts, send = turn(
        middle, out_own, out_got, back_own, back_got, grad_own, g_ffn[None], heads, w_out
    )
    grad_heads = swap_blocks(send, 2).reshape(size, -1)
    qkv_grad, gate_sum, up_sum, down_sum = back(
        dp_count,
        bits,
        qkv,
        logs,
        attended.reshape(size, -1),
        grad_heads,
        starts_two,
        tok_count,
        flipped,
        grad_both,
        gate_grad,
        up_grad,
        acts,
    )
    forward_order = bits + ["z"]
    other_order = bits[::-1] + ["z"]
    got = swap_blocks(qkv_grad.reshape(blk_count, tok_count, -1), 3)
    input_grad, attn_gain_grad, query_gain_grad, key_gain_grad, gq, gk, gv = project_back(
        got,
        proj,
        hidden_in,
        flat,
        mid,
        g_attn[None],
        w_query,
        w_key,
        w_value,
        q_gain2,
        k_gain2,
        cosine,
        sine,
    )

    def sum_all(parts, order):
        parts = parts.reshape(chip_dims + (2, -1, parts.shape[-1]))
        parts = sum_pair(parts, "blk", blk_count, 1, len(chip_dims))
        return sum_chips(parts, order, dp_count, blk_count).astype(F32)

    grad_w_out = sum_all(w_out_parts, forward_order)
    grad_w_query = sum_all(gq, forward_order)
    both = sum_all(jnp.concatenate([gk, gv], axis=1), other_order)
    grad_w_key, grad_w_value = jnp.split(both, 2, axis=1)

    def join(block, dim):
        count = block.shape[0] // 2
        own = lax.dynamic_slice_in_dim(block, core * count, count, axis=0)
        got = swap_core(
            lax.dynamic_slice_in_dim(block, (1 - core) * count, count, axis=0), blk_count
        )
        low = jnp.where(core == 0, own, got)
        high = jnp.where(core == 0, got, own)
        return jnp.concatenate([low, high], axis=1).astype(F32)

    grad_w_gate = join(gate_sum, 1)
    grad_w_up = join(up_sum, 1)
    down_rows = down_sum.shape[0] // 2
    down_own = lax.dynamic_slice_in_dim(down_sum, core * down_rows, down_rows, axis=0)
    down_got = swap_core(
        lax.dynamic_slice_in_dim(down_sum, (1 - core) * down_rows, down_rows, axis=0), blk_count
    )
    holder = lax.axis_index("dp") // (dp_count // 2)
    grad_w_down = jnp.where(holder == core, down_own, down_got).astype(F32)
    fold = lambda both: both[0, :HEAD_DIM] + both[0, HEAD_DIM:]
    gain_attn, gain_query, gain_key, gain_ffn = lax.psum(
        (attn_gain_grad[0], fold(query_gain_grad), fold(key_gain_grad), ffn_gain_grad[0]),
        ("dp", "blk"),
    )
    return (
        output.reshape(tokens.shape),
        input_grad.reshape(tokens.shape),
        gain_attn,
        grad_w_query,
        grad_w_key,
        grad_w_value,
        gain_query,
        gain_key,
        grad_w_out,
        gain_ffn,
        grad_w_gate,
        grad_w_up,
        grad_w_down,
    )


def fits(mesh):
    blk_count = mesh.shape["blk"]
    chips = blk_count // 2
    power = blk_count & (blk_count - 1) == 0
    return power and blk_count > 2 and (KV_HEADS * HEAD_DIM) == chips * LANES


def solution(mesh):
    if fits(mesh):
        body = functools.partial(fast_local, mesh.shape["dp"], mesh.shape["blk"])
    else:
        body = local
    return jax.shard_map(
        body,
        mesh=mesh,
        in_specs=(
            P("dp", "blk", None),
            P("dp", None),
            P(),
            P(),
            P(),
            P(),
            P(),
            P(),
            P(),
            P(),
            P(),
            P(),
            P(),
            P("dp", "blk", None),
        ),
        out_specs=(
            P("dp", "blk", None),
            P("dp", "blk", None),
            P(),
            P(("dp", "blk"), None),
            P(("dp", "blk"), None),
            P(("dp", "blk"), None),
            P(),
            P(),
            P(("dp", "blk"), None),
            P(),
            P(("dp", "blk"), None),
            P(("dp", "blk"), None),
            P(("dp", "blk"), None),
        ),
        check_vma=False,
    )
```

```python
import functools
import math

import jax
import jax.numpy as jnp
from jax import lax
from jax.experimental import pallas as pl
from jax.experimental.pallas import tpu as pltpu
from jax.sharding import PartitionSpec as P

HEADS = 16
KV_HEADS = 8
HEAD_DIM = 64


EPSILON = 1e-05
ROPE_BASE = 1000000.0
NEGATIVE = -1e30


def norm_rows(values, norm_gain):
    row_scale = lax.rsqrt(jnp.mean(values * values, axis=-1, keepdims=True) + EPSILON)
    normal = values * row_scale
    return (normal * norm_gain, normal, row_scale)


def norm_back(normal, row_scale, norm_gain, grad_out):
    pushed = grad_out * norm_gain
    inner = jnp.mean(pushed * normal, axis=-1, keepdims=True)
    grad_in = row_scale * (pushed - normal * inner)
    leading = tuple(range(grad_out.ndim - 1))
    return (grad_in, jnp.sum(grad_out * normal, axis=leading))


def doc_layout(lengths, places):
    ends = jnp.cumsum(lengths, axis=1)
    past = places[None, :, None] >= ends[:, None, :]
    docs = jnp.sum(past.astype(jnp.int32), axis=2)
    before = jnp.sum(jnp.where(past, lengths[:, None, :], 0), axis=2)
    return (docs, places[None, :] - before)


def rope_angles(positions):
    half = HEAD_DIM // 2
    freqs = ROPE_BASE ** (-jnp.arange(half, dtype=jnp.float32) / half)
    angles = positions.astype(jnp.float32)[..., None] * freqs
    return (jnp.cos(angles), jnp.sin(angles))


def rotate(values, cosine, sine):
    half = values.shape[-1] // 2
    first_half = values[..., :half]
    second_half = values[..., half:]
    cos_col = cosine[:, :, None, :]
    sin_col = sine[:, :, None, :]
    return jnp.concatenate(
        [
            first_half * cos_col - second_half * sin_col,
            second_half * cos_col + first_half * sin_col,
        ],
        axis=-1,
    )


def local(
    tokens,
    doc_lengths,
    g_attn,
    w_query,
    w_key,
    w_value,
    q_gain,
    k_gain,
    w_out,
    g_ffn,
    w_gate,
    w_up,
    w_down,
    cotangent,
):
    row_count, tok_count, width = tokens.shape
    grouping = HEADS // KV_HEADS
    flat_rows = row_count * tok_count
    kv_width = KV_HEADS * HEAD_DIM
    softmax_scale = HEAD_DIM ** (-0.5)
    places = lax.axis_index("blk") * tok_count + jnp.arange(tok_count, dtype=jnp.int32)
    query_docs, query_pos = doc_layout(doc_lengths, places)
    cosine, sine = rope_angles(query_pos)
    inputs = tokens.reshape(flat_rows, width).astype(jnp.float32)
    normed, normal_in, scale_in = norm_rows(inputs, g_attn)
    hidden_in = normed.astype(jnp.bfloat16)
    query_proj = jnp.dot(hidden_in, w_query, preferred_element_type=jnp.float32).reshape(
        row_count, tok_count, HEADS, HEAD_DIM
    )
    key_proj = jnp.dot(hidden_in, w_key, preferred_element_type=jnp.float32).reshape(
        row_count, tok_count, KV_HEADS, HEAD_DIM
    )
    value_b = (
        jnp.dot(hidden_in, w_value, preferred_element_type=jnp.float32)
        .astype(jnp.bfloat16)
        .reshape(row_count, tok_count, kv_width)
    )
    query_norm, query_normal, query_scale = norm_rows(query_proj, q_gain)
    key_norm, key_normal, key_scale = norm_rows(key_proj, k_gain)
    query_b = (
        rotate(query_norm, cosine, sine)
        .astype(jnp.bfloat16)
        .reshape(row_count, tok_count, KV_HEADS, grouping, HEAD_DIM)
    )
    key_b = (
        rotate(key_norm, cosine, sine).astype(jnp.bfloat16).reshape(row_count, tok_count, kv_width)
    )

    def piece_mask(size):
        key_places = jnp.arange(size, dtype=jnp.int32)
        key_docs, unused = doc_layout(doc_lengths, key_places)
        return (key_places[None, None, :] <= places[None, :, None]) & (
            key_docs[:, None, :] == query_docs[:, :, None]
        )

    def piece_scores(key_piece, allowed):
        key_heads = key_piece.reshape(row_count, key_piece.shape[1], KV_HEADS, HEAD_DIM)
        raw_scores = (
            jnp.einsum("rqkgd,rpkd->rkgqp", query_b, key_heads, preferred_element_type=jnp.float32)
            * softmax_scale
        )
        return (jnp.where(allowed[:, None, None], raw_scores, -jnp.inf), key_heads)

    stat_shape = (row_count, KV_HEADS, grouping, tok_count)
    key_piece = lax.all_gather(key_b, "blk", axis=1, tiled=True)
    value_piece = lax.all_gather(value_b, "blk", axis=1, tiled=True)
    allowed = piece_mask(key_piece.shape[1])
    running_max = jnp.full(stat_shape, NEGATIVE, jnp.float32)
    scores, key_heads = piece_scores(key_piece, allowed)
    new_max = jnp.maximum(running_max, jnp.max(scores, axis=-1))
    weights = jnp.exp(scores - new_max[..., None])
    value_heads = value_piece.reshape(row_count, value_piece.shape[1], KV_HEADS, HEAD_DIM)
    added = jnp.einsum(
        "rkgqp,rpkd->rkgqd",
        weights.astype(jnp.bfloat16),
        value_heads,
        preferred_element_type=jnp.float32,
    )
    running_sum = jnp.sum(weights, axis=-1)
    attended = added / running_sum[..., None]
    log_total = new_max + jnp.log(running_sum)
    attended_b = (
        jnp.transpose(attended, (0, 3, 1, 2, 4))
        .reshape(flat_rows, HEADS * HEAD_DIM)
        .astype(jnp.bfloat16)
    )
    middle = inputs + jnp.dot(attended_b, w_out, preferred_element_type=jnp.float32)
    normed_ffn, normal_ffn, scale_ffn = norm_rows(middle, g_ffn)
    hidden_ffn = normed_ffn.astype(jnp.bfloat16)
    gate = jnp.dot(hidden_ffn, w_gate, preferred_element_type=jnp.float32)
    up_proj = jnp.dot(hidden_ffn, w_up, preferred_element_type=jnp.float32)
    sigmoid_gate = jax.nn.sigmoid(gate)
    silu_gate = gate * sigmoid_gate
    hidden = (silu_gate * up_proj).astype(jnp.bfloat16)
    result = middle + jnp.dot(hidden, w_down, preferred_element_type=jnp.float32)
    output = result.astype(jnp.bfloat16).reshape(row_count, tok_count, width)
    grad_out = cotangent.reshape(flat_rows, width)
    grad_w_down = jnp.einsum("tf,td->fd", hidden, grad_out, preferred_element_type=jnp.float32)
    grad_hidden = jnp.einsum("td,fd->tf", grad_out, w_down, preferred_element_type=jnp.float32)
    grad_gate = (grad_hidden * up_proj * sigmoid_gate * (1.0 + gate * (1.0 - sigmoid_gate))).astype(
        jnp.bfloat16
    )
    grad_up = (grad_hidden * silu_gate).astype(jnp.bfloat16)
    grad_w_gate = jnp.einsum("td,tf->df", hidden_ffn, grad_gate, preferred_element_type=jnp.float32)
    grad_w_up = jnp.einsum("td,tf->df", hidden_ffn, grad_up, preferred_element_type=jnp.float32)
    grad_h2 = jnp.einsum(
        "tf,df->td", grad_gate, w_gate, preferred_element_type=jnp.float32
    ) + jnp.einsum("tf,df->td", grad_up, w_up, preferred_element_type=jnp.float32)
    grad_mid, grad_ffn_gain = norm_back(normal_ffn, scale_ffn, g_ffn, grad_h2)
    grad_mid = grad_out.astype(jnp.float32) + grad_mid
    grad_attn = grad_mid.astype(jnp.bfloat16)
    grad_w_out = jnp.einsum("tc,td->cd", attended_b, grad_attn, preferred_element_type=jnp.float32)
    grad_attended = jnp.einsum(
        "td,cd->tc", grad_attn, w_out, preferred_element_type=jnp.float32
    ).astype(jnp.bfloat16)
    grad_heads = grad_attended.reshape(row_count, tok_count, KV_HEADS, grouping, HEAD_DIM)
    deltas = jnp.einsum("rqkgd,rkgqd->rkgq", grad_heads.astype(jnp.float32), attended)
    key_piece = lax.all_gather(key_b, "blk", axis=1, tiled=True)
    value_piece = lax.all_gather(value_b, "blk", axis=1, tiled=True)
    size = key_piece.shape[1]
    allowed = piece_mask(size)
    scores, key_heads = piece_scores(key_piece, allowed)
    probs = jnp.exp(scores - log_total[..., None])
    value_heads = value_piece.reshape(row_count, size, KV_HEADS, HEAD_DIM)
    value_piece_grad = jnp.einsum(
        "rkgqp,rqkgd->rpkd",
        probs.astype(jnp.bfloat16),
        grad_heads,
        preferred_element_type=jnp.float32,
    )
    grad_probs = jnp.einsum(
        "rqkgd,rpkd->rkgqp", grad_heads, value_heads, preferred_element_type=jnp.float32
    )
    grad_scores = (probs * (grad_probs - deltas[..., None])).astype(jnp.bfloat16)
    grad_query = jnp.einsum(
        "rkgqp,rpkd->rkgqd", grad_scores, key_heads, preferred_element_type=jnp.float32
    )
    key_piece_grad = jnp.einsum(
        "rkgqp,rqkgd->rpkd", grad_scores, query_b, preferred_element_type=jnp.float32
    )
    grad_keys = key_piece_grad.reshape(row_count, size, kv_width)
    grad_values = value_piece_grad.reshape(row_count, size, kv_width)
    grad_query, grad_keys, grad_values = (grad_query, grad_keys, grad_values)
    key_grad_mine, value_grad_mine = (
        lax.psum_scatter(
            grad_keys.astype(jnp.bfloat16), "blk", scatter_dimension=1, tiled=True
        ).astype(jnp.float32),
        lax.psum_scatter(
            grad_values.astype(jnp.bfloat16), "blk", scatter_dimension=1, tiled=True
        ).astype(jnp.float32),
    )
    grad_q_rot = (jnp.transpose(grad_query, (0, 3, 1, 2, 4)) * softmax_scale).reshape(
        row_count, tok_count, HEADS, HEAD_DIM
    )
    grad_k_rot = (key_grad_mine * softmax_scale).reshape(row_count, tok_count, KV_HEADS, HEAD_DIM)
    grad_q_proj, grad_query_gain = norm_back(
        query_normal, query_scale, q_gain, rotate(grad_q_rot, cosine, -sine)
    )
    grad_k_proj, grad_key_gain = norm_back(
        key_normal, key_scale, k_gain, rotate(grad_k_rot, cosine, -sine)
    )
    grad_q_b = grad_q_proj.astype(jnp.bfloat16).reshape(flat_rows, HEADS * HEAD_DIM)
    grad_k_b = grad_k_proj.astype(jnp.bfloat16).reshape(flat_rows, kv_width)
    grad_v_b = value_grad_mine.astype(jnp.bfloat16).reshape(flat_rows, kv_width)
    grad_w_query = jnp.einsum("td,tc->dc", hidden_in, grad_q_b, preferred_element_type=jnp.float32)
    grad_w_key = jnp.einsum("td,tc->dc", hidden_in, grad_k_b, preferred_element_type=jnp.float32)
    grad_w_value = jnp.einsum("td,tc->dc", hidden_in, grad_v_b, preferred_element_type=jnp.float32)
    grad_h1 = jnp.einsum("tc,dc->td", grad_q_b, w_query, preferred_element_type=jnp.float32)
    grad_h1 = grad_h1 + jnp.einsum("tc,dc->td", grad_k_b, w_key, preferred_element_type=jnp.float32)
    grad_h1 = grad_h1 + jnp.einsum(
        "tc,dc->td", grad_v_b, w_value, preferred_element_type=jnp.float32
    )
    grad_base, grad_attn_gain = norm_back(normal_in, scale_in, g_attn, grad_h1)
    input_grad = (grad_mid + grad_base).astype(jnp.bfloat16).reshape(row_count, tok_count, width)
    gain_attn, gain_query, gain_key, gain_ffn = lax.psum(
        (grad_attn_gain, grad_query_gain, grad_key_gain, grad_ffn_gain), ("dp", "blk")
    )
    locals_all = (
        grad_w_query,
        grad_w_key,
        grad_w_value,
        grad_w_out,
        grad_w_gate,
        grad_w_up,
        grad_w_down,
    )
    shared = (
        lax.psum_scatter(locals_all[0], ("dp", "blk"), scatter_dimension=0, tiled=True),
        lax.psum_scatter(locals_all[1], ("dp", "blk"), scatter_dimension=0, tiled=True),
        lax.psum_scatter(locals_all[2], ("dp", "blk"), scatter_dimension=0, tiled=True),
        lax.psum_scatter(locals_all[3], ("dp", "blk"), scatter_dimension=0, tiled=True),
        lax.psum_scatter(locals_all[4], ("dp", "blk"), scatter_dimension=0, tiled=True),
        lax.psum_scatter(locals_all[5], ("dp", "blk"), scatter_dimension=0, tiled=True),
        lax.psum_scatter(locals_all[6], ("dp", "blk"), scatter_dimension=0, tiled=True),
    )
    return (
        output,
        input_grad,
        gain_attn,
        shared[0],
        shared[1],
        shared[2],
        gain_query,
        gain_key,
        shared[3],
        gain_ffn,
        shared[4],
        shared[5],
        shared[6],
    )


BF16 = jnp.bfloat16
F32 = jnp.float32
LANES = 128
FF_TILE = 256
VMEM_BYTES = 56 * 1024 * 1024
LOG2_E = math.log2(math.e)
QUERY_SCALE = HEAD_DIM ** (-0.5) * LOG2_E
MASKED = -1e30


def nn_dot(left, right):
    return lax.dot_general(left, right, (((1,), (0,)), ((), ())), preferred_element_type=F32)


def nt_dot(left, right):
    return lax.dot_general(left, right, (((1,), (1,)), ((), ())), preferred_element_type=F32)


def tn_dot(left, right):
    return lax.dot_general(left, right, (((0,), (0,)), ((), ())), preferred_element_type=F32)


def kernel_params(**more):
    return pltpu.CompilerParams(vmem_limit_bytes=VMEM_BYTES, **more)


def whole_block(shape):
    return pl.BlockSpec(shape, lambda *ids: (0,) * len(shape))


def swap_blocks_kernel(send_ref, out_ref, send_sem, recv_sem, own_sem):
    count = send_ref.shape[0]
    mine = lax.axis_index("blk")
    group = lax.axis_index("dp")
    barrier = pltpu.get_barrier_semaphore()
    for step in range(1, count):
        pl.semaphore_signal(
            barrier,
            inc=1,
            device_id=(group, lax.rem(mine + step, count)),
            device_id_type=pl.DeviceIdType.MESH,
        )
    pl.semaphore_wait(barrier, count - 1)
    copies = []
    for step in range(1, count):
        target = lax.rem(mine + step, count)
        copy = pltpu.make_async_remote_copy(
            src_ref=send_ref.at[target],
            dst_ref=out_ref.at[mine],
            send_sem=send_sem.at[step],
            recv_sem=recv_sem.at[step],
            device_id=(group, target),
            device_id_type=pl.DeviceIdType.MESH,
        )
        copy.start()
        copies.append(copy)
    own = pltpu.make_async_copy(send_ref.at[mine], out_ref.at[mine], own_sem)
    own.start()
    own.wait()
    for copy in copies:
        copy.wait()


def swap_blocks(blocks, collective_id):
    count = blocks.shape[0]
    return pl.pallas_call(
        swap_blocks_kernel,
        name=f"swap_blocks_{collective_id}",
        out_shape=jax.ShapeDtypeStruct(blocks.shape, blocks.dtype),
        in_specs=[pl.BlockSpec(memory_space=pl.ANY)],
        out_specs=pl.BlockSpec(memory_space=pl.ANY),
        scratch_shapes=[
            pltpu.SemaphoreType.DMA((count,)),
            pltpu.SemaphoreType.DMA((count,)),
            pltpu.SemaphoreType.DMA,
        ],
        compiler_params=kernel_params(collective_id=collective_id, has_side_effects=True),
    )(blocks)


def head_means(values):
    rows = lax.broadcasted_iota(jnp.int32, (LANES, LANES), 0) // HEAD_DIM
    cols = lax.broadcasted_iota(jnp.int32, (LANES, LANES), 1) // HEAD_DIM
    spread = jnp.where(rows == cols, 1.0 / HEAD_DIM, 0.0).astype(BF16)
    high = values.astype(BF16)
    low = (values - high.astype(F32)).astype(BF16)
    return nn_dot(high, spread) + nn_dot(low, spread)


def half_partner(values):
    lane = lax.broadcasted_iota(jnp.int32, values.shape, 1)
    half = HEAD_DIM // 2
    ahead = pltpu.roll(values, LANES - half, 1)
    behind = pltpu.roll(values, half, 1)
    return jnp.where(lane % HEAD_DIM < half, ahead, behind)


def project_kernel(
    tokens_ref,
    gain_ref,
    wq_ref,
    wk_ref,
    wv_ref,
    q_gain_ref,
    k_gain_ref,
    cos_ref,
    sin_ref,
    hidden_ref,
    proj_ref,
    send_ref,
):
    rows = tokens_ref.shape[0]

    @pl.when(pl.program_id(0) == 0)
    def _():
        inputs = tokens_ref[...].astype(F32)
        scale = lax.rsqrt(jnp.mean(inputs * inputs, axis=-1, keepdims=True) + EPSILON)
        hidden_ref[...] = (inputs * scale * gain_ref[...]).astype(BF16)

    hidden = hidden_ref[...]
    half = rows // 2

    def put(block, lane):
        send_ref[0, :, lane : lane + LANES] = block[:half]
        send_ref[1, :, lane : lane + LANES] = block[half:]

    queries = nn_dot(hidden, wq_ref[...])
    keys = nn_dot(hidden, wk_ref[...])
    values = nn_dot(hidden, wv_ref[...])
    q_width = queries.shape[1]
    blocks = [(queries[:, at : at + LANES], at, q_gain_ref, QUERY_SCALE) for at in range(0, q_width, LANES)]
    blocks.append((keys, q_width, k_gain_ref, 1.0))
    for block, lane, head_gain, factor in blocks:
        proj_ref[0, :, lane : lane + LANES] = block
        scale = lax.rsqrt(head_means(block * block) + EPSILON)
        normed = block * scale * head_gain[...]
        turned = normed * cos_ref[...] + half_partner(normed) * sin_ref[...]
        put((turned * factor).astype(BF16), lane)
    put(values.astype(BF16), q_width + LANES)


def project(tokens, gain, wq, wk, wv, q_gain, k_gain, cosine, sine):
    rows, width = tokens.shape
    chips = wk.shape[1] // LANES
    q_width = wq.shape[1] // chips
    block_width = q_width + 2 * LANES
    return pl.pallas_call(
        project_kernel,
        name="project",
        grid=(chips,),
        in_specs=[
            whole_block((rows, width)),
            whole_block((1, width)),
            pl.BlockSpec((width, q_width), lambda p: (0, p)),
            pl.BlockSpec((width, LANES), lambda p: (0, p)),
            pl.BlockSpec((width, LANES), lambda p: (0, p)),
            whole_block((1, LANES)),
            whole_block((1, LANES)),
            whole_block((rows, LANES)),
            whole_block((rows, LANES)),
        ],
        out_specs=[
            whole_block((rows, width)),
            pl.BlockSpec((1, rows, q_width + LANES), lambda p: (p, 0, 0)),
            pl.BlockSpec((2, rows // 2, block_width), lambda p: (p, 0, 0)),
        ],
        out_shape=[
            jax.ShapeDtypeStruct((rows, width), BF16),
            jax.ShapeDtypeStruct((chips, rows, q_width + LANES), F32),
            jax.ShapeDtypeStruct((2 * chips, rows // 2, block_width), BF16),
        ],
        compiler_params=kernel_params(),
    )(tokens, gain, wq, wk, wv, q_gain, k_gain, cosine, sine)


def low_lanes(shape):
    return lax.broadcasted_iota(jnp.int32, shape, 1) < HEAD_DIM


def doubled(pair, group):
    turned = pltpu.roll(pair.astype(F32), HEAD_DIM, 1).astype(BF16)
    low = low_lanes(pair.shape)
    return jnp.where(low, pair, turned) if group == 0 else jnp.where(low, turned, pair)


def stacked_heads(pair):
    low = low_lanes(pair.shape)
    none = jnp.zeros_like(pair)
    return jnp.concatenate([jnp.where(low, pair, none), jnp.where(low, none, pair)], axis=0)


def in_three(column):
    lane = lax.broadcasted_iota(jnp.int32, (column.shape[0], LANES), 1)
    wide = jnp.broadcast_to(column, (column.shape[0], LANES))
    first = wide.astype(BF16).astype(F32)
    second = (wide - first).astype(BF16).astype(F32)
    third = wide - first - second
    return jnp.where(
        lane == 0, first, jnp.where(lane == 1, second, jnp.where(lane == 2, third, 0.0))
    ).astype(BF16)


def minus_three(rows):
    lane = lax.broadcasted_iota(jnp.int32, (rows, LANES), 1)
    return jnp.where(lane < 3, -1.0, 0.0).astype(BF16)


def attend_kernel(groups, block, qkv_ref, starts_ref, out_ref, logs_ref, keys, values, total):
    size = qkv_ref.shape[0]
    q_width = groups * LANES
    here = pl.program_id(0)

    @pl.when(here == 0)
    def _():
        for g in range(groups):
            keys[g] = doubled(qkv_ref[:, q_width : q_width + LANES], g)
            values[g, :, :LANES] = doubled(qkv_ref[:, q_width + LANES : q_width + 2 * LANES], g)
            values[g, :, LANES:] = jnp.ones((size, LANES), BF16)

    at = pl.multiple_of(here * block, block)
    starts = jnp.concatenate([starts_ref[pl.ds(at, block), :]] * 2, axis=0)
    queries = [
        stacked_heads(qkv_ref[pl.ds(at, block), g * LANES : (g + 1) * LANES]) for g in range(groups)
    ]
    column = lax.broadcasted_iota(jnp.int32, (2 * block, block), 1)
    row = lax.broadcasted_iota(jnp.int32, (2 * block, block), 0) % block

    def step(j, diagonal):
        key_at = pl.multiple_of(j * block, block)
        allowed = column >= starts - key_at
        if diagonal:
            allowed = allowed & (column <= row)
        for g in range(groups):
            scores = nt_dot(queries[g], keys[g, pl.ds(key_at, block), :])
            weights = jnp.exp2(jnp.where(allowed, scores, MASKED)).astype(BF16)
            part = nn_dot(weights, values[g, pl.ds(key_at, block), :])
            if diagonal:
                total[g] = part
            else:
                total[g] += part

    step(here, True)

    def body(j, carry):
        step(j, False)
        return carry

    lax.fori_loop(0, here, body, 0)
    for g in range(groups):
        sums = total[g, :, LANES:]
        mean = total[g, :, :LANES] / sums
        low = low_lanes((block, LANES))
        out_ref[0, :, g * LANES : (g + 1) * LANES] = jnp.where(low, mean[:block], mean[block:]).astype(BF16)
        logs_ref[g] = in_three(jnp.log2(sums[:, :1]))


def attend(qkv, starts, block):
    size, width = qkv.shape
    groups = (width - 2 * LANES) // LANES
    blocks = size // block
    return pl.pallas_call(
        functools.partial(attend_kernel, groups, block),
        name="attend",
        grid=(blocks,),
        in_specs=[whole_block((size, width)), whole_block((size, 1))],
        out_specs=[
            pl.BlockSpec((1, block, groups * LANES), lambda i: (i, 0, 0)),
            pl.BlockSpec((groups, 2 * block, LANES), lambda i: (0, i, 0)),
        ],
        out_shape=[
            jax.ShapeDtypeStruct((blocks, block, groups * LANES), BF16),
            jax.ShapeDtypeStruct((groups, 2 * size, LANES), BF16),
        ],
        scratch_shapes=[
            pltpu.VMEM((groups, size, LANES), BF16),
            pltpu.VMEM((groups, size, 2 * LANES), BF16),
            pltpu.VMEM((groups, 2 * block, 2 * LANES), F32),
        ],
        compiler_params=kernel_params(),
    )(qkv, starts)


def middle_kernel(tokens_ref, heads_ref, w_out_ref, gain_ref, middle_ref, hidden_ref):
    half = heads_ref.shape[1]
    width = heads_ref.shape[2]
    total = tokens_ref[...].astype(F32)
    for p in range(heads_ref.shape[0] // 2):
        block = jnp.concatenate([heads_ref[2 * p], heads_ref[2 * p + 1]], axis=0)
        total = total + nn_dot(block, w_out_ref[p * width : (p + 1) * width, :])
    middle_ref[...] = total
    scale = lax.rsqrt(jnp.mean(total * total, axis=-1, keepdims=True) + EPSILON)
    hidden_ref[...] = (total * scale * gain_ref[...]).astype(BF16)


def middle_layer(tokens, heads, w_out, gain):
    return pl.pallas_call(
        middle_kernel,
        name="middle",
        out_shape=[
            jax.ShapeDtypeStruct(tokens.shape, F32),
            jax.ShapeDtypeStruct(tokens.shape, BF16),
        ],
        compiler_params=kernel_params(),
    )(tokens, heads, w_out, gain)


def ffn_kernel(
    core_ref,
    hidden_ref,
    grad_ref,
    w_gate_ref,
    w_up_ref,
    w_down_ref,
    gate_grad_ref,
    up_grad_ref,
    acts_ref,
    out_own_ref,
    out_send_ref,
    back_own_ref,
    back_send_ref,
    out_sum,
    back_sum,
):
    step = pl.program_id(0)
    rows = hidden_ref.shape[0]
    chunk = min(256, rows)

    @pl.when(step == 0)
    def _():
        out_sum[...] = jnp.zeros_like(out_sum)
        back_sum[...] = jnp.zeros_like(back_sum)

    for m in range(rows // chunk):
        part = slice(m * chunk, (m + 1) * chunk)
        hidden = hidden_ref[part, :]
        gate = nn_dot(hidden, w_gate_ref[...])
        up = nn_dot(hidden, w_up_ref[...])
        pushed = nt_dot(grad_ref[part, :], w_down_ref[...])
        opened = jax.nn.sigmoid(gate)
        silu = gate * opened
        act = (silu * up).astype(BF16)
        gate_grad = (pushed * up * opened * (1.0 + gate * (1.0 - opened))).astype(BF16)
        up_grad = (pushed * silu).astype(BF16)
        acts_ref[:, part] = act.T
        gate_grad_ref[part, :] = gate_grad
        up_grad_ref[part, :] = up_grad
        out_sum[part, :] += nn_dot(act, w_down_ref[...])
        back_sum[part, :] += nt_dot(gate_grad, w_gate_ref[...]) + nt_dot(up_grad, w_up_ref[...])

    @pl.when(step == pl.num_programs(0) - 1)
    def _():
        half = rows // 2
        out_own_ref[...] = out_sum[:half, :]
        out_send_ref[...] = out_sum[half:, :].astype(BF16)
        back_own_ref[...] = back_sum[:half, :]
        back_send_ref[...] = back_sum[half:, :].astype(BF16)


def feed_forward(core, hidden, grad, w_gate, w_up, w_down):
    rows, width = hidden.shape
    tiles = w_gate.shape[1] // 2 // FF_TILE
    half = (rows // 2, width)

    def keep(shape):
        return pl.BlockSpec(shape, lambda f, c: (0,) * len(shape), pipeline_mode=pl.Buffered(1))

    return pl.pallas_call(
        ffn_kernel,
        name="feed_forward",
        grid_spec=pltpu.PrefetchScalarGridSpec(
            num_scalar_prefetch=1,
            grid=(tiles,),
            in_specs=[
                keep((rows, width)),
                keep((rows, width)),
                pl.BlockSpec((width, FF_TILE), lambda f, c: (0, c[0] * tiles + f)),
                pl.BlockSpec((width, FF_TILE), lambda f, c: (0, c[0] * tiles + f)),
                pl.BlockSpec((FF_TILE, width), lambda f, c: (c[0] * tiles + f, 0)),
            ],
            out_specs=[
                pl.BlockSpec((rows, FF_TILE), lambda f, c: (0, f)),
                pl.BlockSpec((rows, FF_TILE), lambda f, c: (0, f)),
                pl.BlockSpec((FF_TILE, rows), lambda f, c: (f, 0)),
            ]
            + [keep(half)] * 4,
            scratch_shapes=[pltpu.VMEM((rows, width), F32), pltpu.VMEM((rows, width), F32)],
        ),
        out_shape=[
            jax.ShapeDtypeStruct((rows, tiles * FF_TILE), BF16),
            jax.ShapeDtypeStruct((rows, tiles * FF_TILE), BF16),
            jax.ShapeDtypeStruct((tiles * FF_TILE, rows), BF16),
        ]
        + [jax.ShapeDtypeStruct(half, kind) for kind in (F32, BF16, F32, BF16)],
        compiler_params=kernel_params(),
    )(core, hidden, grad, w_gate, w_up, w_down)


def turn_kernel(
    middle_ref,
    out_own_ref,
    out_got_ref,
    back_own_ref,
    back_got_ref,
    grad_ref,
    gain_ref,
    heads_ref,
    w_out_ref,
    output_ref,
    mid_ref,
    gain_grad_ref,
    w_grad_ref,
    send_ref,
    low_grad,
):
    @pl.when(pl.program_id(0) == 0)
    def _():
        middle = middle_ref[...]
        result = middle + (out_own_ref[...] + out_got_ref[...].astype(F32))
        output_ref[...] = result.astype(BF16)
        scale = lax.rsqrt(jnp.mean(middle * middle, axis=-1, keepdims=True) + EPSILON)
        normal = middle * scale
        back = back_own_ref[...] + back_got_ref[...].astype(F32)
        gain_grad_ref[...] = jnp.sum(back * normal, axis=0, keepdims=True)
        pushed = back * gain_ref[...]
        inner = jnp.mean(pushed * normal, axis=-1, keepdims=True)
        mid = grad_ref[...].astype(F32) + scale * (pushed - normal * inner)
        mid_ref[...] = mid
        low_grad[...] = mid.astype(BF16)

    half = heads_ref.shape[1]
    heads = jnp.concatenate([heads_ref[0], heads_ref[1]], axis=0)
    grad = low_grad[...]
    w_grad_ref[...] = tn_dot(heads, grad).astype(BF16)
    send = nt_dot(grad, w_out_ref[...]).astype(BF16)
    send_ref[0] = send[:half]
    send_ref[1] = send[half:]


def turn(middle, out_own, out_got, back_own, back_got, grad, gain, heads, w_out):
    rows, width = middle.shape
    count, half, lanes = heads.shape
    chips = count // 2
    return pl.pallas_call(
        turn_kernel,
        name="turn",
        grid=(chips,),
        in_specs=[whole_block((rows, width))] * 6
        + [
            whole_block((1, width)),
            pl.BlockSpec((2, half, lanes), lambda p: (p, 0, 0)),
            pl.BlockSpec((lanes, width), lambda p: (p, 0)),
        ],
        out_specs=[
            whole_block((rows, width)),
            whole_block((rows, width)),
            whole_block((1, width)),
            pl.BlockSpec((lanes, width), lambda p: (p, 0)),
            pl.BlockSpec((2, half, lanes), lambda p: (p, 0, 0)),
        ],
        out_shape=[
            jax.ShapeDtypeStruct((rows, width), BF16),
            jax.ShapeDtypeStruct((rows, width), F32),
            jax.ShapeDtypeStruct((1, width), F32),
            jax.ShapeDtypeStruct((chips * lanes, width), BF16),
            jax.ShapeDtypeStruct(heads.shape, BF16),
        ],
        scratch_shapes=[pltpu.VMEM((rows, width), BF16)],
        compiler_params=kernel_params(),
    )(middle, out_own, out_got, back_own, back_got, grad, gain, heads, w_out)


def pair_of(bit):
    index = lax.axis_index("blk")
    mine = lax.rem(index // bit, 2)
    return mine, (lax.axis_index("dp"), index + bit * (1 - 2 * mine))


class Stream:
    def __init__(self, path, dims, block, line, kind=BF16):
        self.path, self.block, self.line, self.kind = path, block, line, kind
        self.dims = [tuple(dims)]
        left = list(dims)
        names = [name for name, unused in dims]
        for stage in path:
            if isinstance(stage, tuple):
                if stage[1] == line - 1:
                    at = [n for n, unused in left].index("z")
                    left = left[:at] + left[at + 1 :]
            else:
                at = [n for n, unused in left].index(stage)
                left = left[:at] + left[at + 1 :]
            self.dims.append(tuple(left))
        assert not left and "z" in names

    def is_hop(self, k):
        return isinstance(self.path[k], tuple)

    def starts_work(self, k):
        return k == 0 or not self.is_hop(k) or self.path[k][1] == 1

    def shape(self, dims):
        return tuple(count for unused, count in dims) + self.block

    def slots(self, k):
        return self.line if self.is_hop(k) else 2

    def scratch(self):
        shapes = []
        for k in range(len(self.path)):
            if self.starts_work(k):
                shapes.append(pltpu.VMEM((self.slots(k),) + self.shape(self.dims[k]), self.kind))
            if self.is_hop(k):
                rest = tuple(d for d in self.dims[k] if d[0] != "z")
                shapes.append(pltpu.VMEM((2, 2) + self.shape(rest), self.kind))
                shapes += [pltpu.SemaphoreType.DMA((2, 2))] * 2
            else:
                shapes.append(pltpu.VMEM((2,) + self.shape(self.dims[k + 1]), self.kind))
                shapes += [pltpu.SemaphoreType.DMA((2,))] * 2
        return shapes

    def bind(self, refs, units, finish, first_z=None):
        refs = list(refs)
        self.units, self.finish = units, finish
        self.first_z = 0 if first_z is None else first_z
        self.work, self.got, self.sent_sem, self.got_sem = [], [], [], []
        for k in range(len(self.path)):
            self.work.append(refs.pop(0) if self.starts_work(k) else self.work[-1])
            self.got.append(refs.pop(0))
            self.sent_sem.append(refs.pop(0))
            self.got_sem.append(refs.pop(0))
        self.source = self.work[0]

    def z_count(self, k):
        return dict(self.dims[k])["z"]

    def keeps(self, z, k):
        return (z >= self.first_z) & (z < self.first_z + self.z_count(k))

    def keeper(self, k):
        if "z" in [name for name, unused in self.dims[k]] or dict(self.dims[0])["z"] == self.line:
            return None
        z = lax.axis_index("dp")
        return (z >= self.first_z) & (z < self.first_z + dict(self.dims[0])["z"])

    def pair_copy(self, k, u):
        bit = self.path[k]
        mine, partner = pair_of(bit)
        at = [name for name, unused in self.dims[k]].index(bit)
        whole = (slice(None),) * at
        slot = lax.rem(u, 2)
        copy = pltpu.make_async_remote_copy(
            src_ref=self.work[k].at[(lax.rem(u, self.slots(k)),) + whole + (1 - mine,)],
            dst_ref=self.got[k].at[slot],
            send_sem=self.sent_sem[k].at[slot],
            recv_sem=self.got_sem[k].at[slot],
            device_id=partner,
            device_id_type=pl.DeviceIdType.MESH,
        )
        return copy, whole + (mine,)

    def hop_copy(self, k, u, way, block):
        z, index = lax.axis_index("dp"), lax.axis_index("blk")
        slot = lax.rem(u, 2)
        side = (1 - way) // 2
        return pltpu.make_async_remote_copy(
            src_ref=self.work[k].at[lax.rem(u, self.slots(k)), block],
            dst_ref=self.got[k].at[slot, side],
            send_sem=self.sent_sem[k].at[slot, side],
            recv_sem=self.got_sem[k].at[slot, side],
            device_id=(z + way, index),
            device_id_type=pl.DeviceIdType.MESH,
        )

    def hop_ends(self, k, way):
        z = lax.axis_index("dp")
        reach = way * (self.line - self.path[k][1])
        goes, comes = z + reach, z - way + reach
        sends = self.keeps(goes, k)
        takes = self.keeps(comes, k) & (z - way >= 0) & (z - way < self.line)
        return goes - self.first_z, sends, comes - self.first_z, takes

    def send(self, k, step):
        u = step - k - 1
        due = (u >= 0) & (u < self.units)
        if not self.is_hop(k):
            keeper = self.keeper(k)

            @pl.when(due if keeper is None else due & keeper)
            def _():
                self.pair_copy(k, u)[0].start()

            return
        for way in (1, -1):
            block, sends, unused, unused = self.hop_ends(k, way)

            @pl.when(due & sends)
            def _():
                self.hop_copy(k, u, way, block).start()

    def take(self, k, step):
        u = step - k - 2
        due = (u >= 0) & (u < self.units)
        keeper = self.keeper(k + 1)
        last = k == len(self.path) - 1

        def pass_on(value):
            if last:
                self.finish(u, value)
            else:
                self.work[k + 1][lax.rem(u, self.slots(k + 1))] = value

        if not self.is_hop(k):
            keeper = self.keeper(k)

            @pl.when(due if keeper is None else due & keeper)
            def _():
                copy, mine = self.pair_copy(k, u)
                copy.wait()
                own = self.work[k][(lax.rem(u, self.slots(k)),) + mine]
                pass_on(own + self.got[k][lax.rem(u, 2)])

            return
        slot = lax.rem(u, self.slots(k))
        for way in (1, -1):
            out_block, sends, in_block, takes = self.hop_ends(k, way)

            @pl.when(due & sends)
            def _():
                self.hop_copy(k, u, way, out_block).wait_send()

            @pl.when(due & takes)
            def _():
                self.hop_copy(k, u, way, in_block).wait_recv()
                self.work[k][slot, in_block] += self.got[k][lax.rem(u, 2), (1 - way) // 2]

        if self.path[k][1] == self.line - 1:
            own = lax.axis_index("dp") - self.first_z

            @pl.when(due if keeper is None else due & keeper)
            def _():
                pass_on(self.work[k][slot, own])


def hops(line):
    return [("z", t) for t in range(1, line)]


def greet(bits, line):
    barrier = pltpu.get_barrier_semaphore()
    z, index = lax.axis_index("dp"), lax.axis_index("blk")
    for bit in bits:
        pl.semaphore_signal(barrier, inc=1, device_id=pair_of(bit)[1], device_id_type=pl.DeviceIdType.MESH)
    for way in (1, -1):

        @pl.when((z + way >= 0) & (z + way < line))
        def _():
            pl.semaphore_signal(
                barrier, inc=1, device_id=(z + way, index), device_id_type=pl.DeviceIdType.MESH
            )

    beside = jnp.minimum(z, 1) + jnp.minimum(line - 1 - z, 1)
    pl.semaphore_wait(barrier, len(bits) + beside)


def step_streams(streams, step, steps, line, ready):
    longest = max(len(stream.path) for stream in streams)
    z, index = lax.axis_index("dp"), lax.axis_index("blk")
    for k in range(longest):
        for stream in streams:
            if k < len(stream.path):
                stream.take(k, step)
    for way in (1, -1):
        there = (z + way >= 0) & (z + way < line)

        @pl.when(there & (step < steps - 1))
        def _():
            pl.semaphore_signal(
                ready.at[(1 - way) // 2],
                inc=1,
                device_id=(z + way, index),
                device_id_type=pl.DeviceIdType.MESH,
            )

        @pl.when(there & (step > 0))
        def _():
            pl.semaphore_wait(ready.at[(1 + way) // 2], 1)

    for k in range(longest):
        for stream in streams:
            if k < len(stream.path):
                stream.send(k, step)


def back_kernel(
    groups,
    block,
    line,
    bits,
    streams,
    units,
    qkv_ref,
    logs_ref,
    out_ref,
    grad_ref,
    starts_ref,
    flipped_ref,
    dy_ref,
    gate_grad_ref,
    up_grad_ref,
    acts_ref,
    result_ref,
    gate_out_ref,
    up_out_ref,
    down_out_ref,
    queries,
    keys,
    values,
    grads,
    query_grad,
    pair_grad,
    ready,
    *refs,
):
    size = qkv_ref.shape[0]
    blocks = size // block
    q_width = groups * LANES
    n = pl.program_id(0)
    core = lax.rem(lax.axis_index("blk"), 2)
    gate_stream, up_stream, down_stream = streams

    def finish_gate(u, value):
        gate_out_ref[:, pl.ds(pl.multiple_of(u * FF_TILE, FF_TILE), FF_TILE)] = value

    def finish_up(u, value):
        up_out_ref[:, pl.ds(pl.multiple_of(u * FF_TILE, FF_TILE), FF_TILE)] = value

    def finish_down(u, value):
        rows = value.shape[0]
        down_out_ref[pl.ds(pl.multiple_of(u * rows, rows), rows), :] = value

    at = 0
    for stream, finish, first_z in (
        (gate_stream, finish_gate, None),
        (up_stream, finish_up, None),
        (down_stream, finish_down, core * (line // 2)),
    ):
        count = len(stream.scratch())
        stream.bind(refs[at : at + count], units, finish, first_z)
        at += count

    @pl.when(n == 0)
    def _():
        greet(bits, line)
        down_out_ref[...] = jnp.zeros_like(down_out_ref)
        query_grad[...] = jnp.zeros_like(query_grad)
        pair_grad[...] = jnp.zeros_like(pair_grad)
        for g in range(groups):
            lanes = slice(g * LANES, (g + 1) * LANES)
            keys[g, :, :LANES] = doubled(qkv_ref[:, q_width : q_width + LANES], g)
            keys[g, :, LANES:] = minus_three(size)
            values[g, :, :LANES] = doubled(qkv_ref[:, q_width + LANES : q_width + 2 * LANES], g)
            values[g, :, LANES:] = minus_three(size)

            def fill(i, carry):
                at = pl.multiple_of(i * block, block)
                to = pl.multiple_of(i * 2 * block, 2 * block)
                queries[g, pl.ds(to, 2 * block), :LANES] = stacked_heads(qkv_ref[pl.ds(at, block), lanes])
                queries[g, pl.ds(to, 2 * block), LANES:] = logs_ref[g, pl.ds(to, 2 * block), :]
                grad = stacked_heads(grad_ref[pl.ds(at, block), lanes])
                mean = stacked_heads(out_ref[pl.ds(at, block), lanes])
                delta = jnp.sum(grad.astype(F32) * mean.astype(F32), axis=1, keepdims=True)
                grads[g, pl.ds(to, 2 * block), :LANES] = grad
                grads[g, pl.ds(to, 2 * block), LANES:] = in_three(delta)
                return carry

            lax.fori_loop(0, blocks, fill, 0)

    step_streams(streams, n, pl.num_programs(0), line, ready)

    @pl.when(n < units)
    def _():
        chunk = 256
        width = flipped_ref.shape[0]
        gate_shape = gate_stream.shape(gate_stream.dims[0])
        down_shape = down_stream.shape(down_stream.dims[0])
        slot = lax.rem(n, 2)
        each = chunk * gate_shape[0] // width

        def weights(m, carry):
            flipped = flipped_ref[pl.ds(pl.multiple_of(m * chunk, chunk), chunk), :]
            part = pl.ds(m * each, each)
            piece = (each,) + gate_shape[1:]
            gate_stream.source[slot, part] = nn_dot(flipped, gate_grad_ref[...]).astype(BF16).reshape(piece)
            up_stream.source[slot, part] = nn_dot(flipped, up_grad_ref[...]).astype(BF16).reshape(piece)
            return carry

        lax.fori_loop(0, width // chunk, weights, 0)
        acts = acts_ref[...].reshape(-1, acts_ref.shape[-1])
        made = nn_dot(acts, dy_ref[...]).astype(BF16)
        down_stream.source[lax.rem(n, down_stream.slots(0))] = made.reshape(down_shape)

    row = lax.broadcasted_iota(jnp.int32, (block, 2 * block), 0)
    column = lax.broadcasted_iota(jnp.int32, (block, 2 * block), 1) % block

    @pl.when(n < blocks + 1)
    def _():
        def pair(m, carry):
            late = (n + m) // blocks
            j = m + late * (blocks - 1 - 2 * m)
            i = (1 - late) * (m + n) + late * (n - 1)
            key_at = pl.multiple_of(j * block, block)
            at = pl.multiple_of(i * 2 * block, 2 * block)
            key_rows = pl.ds(key_at, block)
            stack = pl.ds(at, 2 * block)
            allowed = (row >= starts_ref[:, stack] - key_at) & (row - column <= (i - j) * block)
            for g in range(groups):
                query = queries[g, stack, :]
                grad = grads[g, stack, :]
                key = keys[g, key_rows, :]
                scores = nt_dot(key, query)
                probs = jnp.exp2(jnp.where(allowed, scores, MASKED))
                pushed = (probs * nt_dot(values[g, key_rows, :], grad)).astype(BF16)
                pair_grad[g, key_rows, LANES:] += nn_dot(probs.astype(BF16), grad[:, :LANES])
                pair_grad[g, key_rows, :LANES] += nn_dot(pushed, query[:, :LANES])
                query_grad[g, stack, :] += tn_dot(pushed, key[:, :LANES])
            return carry

        lax.fori_loop(0, blocks // 2, pair, 0)

    @pl.when(n == blocks + 1)
    def _():
        low = low_lanes((block, LANES))

        def finish(i, carry):
            at = pl.multiple_of(i * block, block)
            to = pl.multiple_of(i * 2 * block, 2 * block)
            here = pl.ds(at, block)
            for g in range(groups):
                first = query_grad[g, pl.ds(to, block), :]
                second = query_grad[g, pl.ds(to + block, block), :]
                joined = jnp.where(low, first, second) * HEAD_DIM ** (-0.5)
                result_ref[here, g * LANES : (g + 1) * LANES] = joined.astype(BF16)
            for part in range(2):
                sums = []
                for g in range(groups):
                    both = pair_grad[g, here, part * LANES : (part + 1) * LANES]
                    sums.append(both + pltpu.roll(both, HEAD_DIM, 1))
                joined = jnp.where(low, sums[0], sums[1])
                if part == 0:
                    joined = joined * (1.0 / LOG2_E)
                lane = q_width + part * LANES
                result_ref[here, lane : lane + LANES] = joined.astype(BF16)
            return carry

        lax.fori_loop(0, blocks, finish, 0)


def back(line, bits, qkv, logs, out, grad, starts, block, flipped, dy, gate_grad, up_grad, acts):
    size, width = qkv.shape
    groups = (width - 2 * LANES) // LANES
    units = gate_grad.shape[1] // FF_TILE
    model, rows = flipped.shape
    chips = line * 2 ** len(bits)
    sides = [(bit, 2) for bit in bits]
    gate_block = (model // chips, FF_TILE)
    down_rows = acts.shape[0] // (chips // 2)
    down_block = (down_rows // units, model)
    whole = [("z", line)] + sides
    half = [("z", line // 2)] + sides
    streams = [
        Stream(bits[::-1] + hops(line), whole, gate_block, line),
        Stream(bits + hops(line), whole, gate_block, line),
        Stream(hops(line) + bits, half, down_block, line),
    ]
    longest = max(len(stream.path) for stream in streams)
    steps = units + longest + 1

    def keep(shape):
        return pl.BlockSpec(shape, lambda n: (0,) * len(shape), pipeline_mode=pl.Buffered(1))

    tile = lambda n: (0, jnp.minimum(n, units - 1))
    acts = acts.reshape(chips // 2, down_rows, rows)
    scratch = [
        pltpu.VMEM((groups, 2 * size, 2 * LANES), BF16),
        pltpu.VMEM((groups, size, 2 * LANES), BF16),
        pltpu.VMEM((groups, size, 2 * LANES), BF16),
        pltpu.VMEM((groups, 2 * size, 2 * LANES), BF16),
        pltpu.VMEM((groups, 2 * size, LANES), F32),
        pltpu.VMEM((groups, size, 2 * LANES), F32),
        pltpu.SemaphoreType.REGULAR((2,)),
    ]
    for stream in streams:
        scratch += stream.scratch()
    return pl.pallas_call(
        functools.partial(back_kernel, groups, block, line, bits, streams, units),
        name="back",
        grid=(steps,),
        in_specs=[
            keep(qkv.shape),
            keep(logs.shape),
            keep(out.shape),
            keep(grad.shape),
            keep(starts.shape),
            keep(flipped.shape),
            keep(dy.shape),
            pl.BlockSpec((rows, FF_TILE), tile),
            pl.BlockSpec((rows, FF_TILE), tile),
            pl.BlockSpec(
                (chips // 2, down_block[0], rows), lambda n: (0, jnp.minimum(n, units - 1), 0)
            ),
        ],
        out_specs=[
            keep(qkv.shape),
            keep((gate_block[0], units * FF_TILE)),
            keep((gate_block[0], units * FF_TILE)),
            keep((down_rows, model)),
        ],
        out_shape=[
            jax.ShapeDtypeStruct(qkv.shape, BF16),
            jax.ShapeDtypeStruct((gate_block[0], units * FF_TILE), BF16),
            jax.ShapeDtypeStruct((gate_block[0], units * FF_TILE), BF16),
            jax.ShapeDtypeStruct((down_rows, model), BF16),
        ],
        scratch_shapes=scratch,
        compiler_params=kernel_params(collective_id=4, has_side_effects=True),
    )(qkv, logs, out, grad, starts, flipped, dy, gate_grad, up_grad, acts)


def sum_gains(rounds, n, first, gains, gains_got, sent_sem, got_sem):
    for r, partner in enumerate(rounds):

        def copy():
            return pltpu.make_async_remote_copy(
                src_ref=gains.at[r],
                dst_ref=gains_got.at[r],
                send_sem=sent_sem.at[r],
                recv_sem=got_sem.at[r],
                device_id=partner,
                device_id_type=pl.DeviceIdType.MESH,
            )

        @pl.when(n == first + r + 1)
        def _():
            copy().wait()
            gains[r + 1] = gains[r] + gains_got[r]

    for r, partner in enumerate(rounds):

        @pl.when(n == first + r)
        def _():
            pltpu.make_async_remote_copy(
                src_ref=gains.at[r],
                dst_ref=gains_got.at[r],
                send_sem=sent_sem.at[r],
                recv_sem=got_sem.at[r],
                device_id=partner,
                device_id_type=pl.DeviceIdType.MESH,
            ).start()


def finish_kernel(
    line,
    bits,
    streams,
    units,
    got_ref,
    proj_ref,
    hidden_ref,
    tokens_ref,
    mid_ref,
    gain_ref,
    wq_ref,
    wk_ref,
    wv_ref,
    q_gain_ref,
    k_gain_ref,
    cos_ref,
    sin_ref,
    w_out_parts_ref,
    ffn_gain_ref,
    gate_ref,
    up_ref,
    down_ref,
    input_ref,
    gains_ref,
    gq_ref,
    gk_ref,
    gv_ref,
    go_ref,
    gate_out_ref,
    up_out_ref,
    down_out_ref,
    total,
    gains,
    gains_got,
    gains_sent_sem,
    gains_got_sem,
    half_got,
    down_got,
    half_sent_sem,
    half_got_sem,
    ready,
    *refs,
):
    n = pl.program_id(0)
    z, index = lax.axis_index("dp"), lax.axis_index("blk")
    core, sibling = pair_of(1)
    steps = pl.num_programs(0)
    qkv_stream, out_stream = streams
    q_width = wq_ref.shape[1]

    def finish_qkv(u, value):
        gq_ref[:, pl.ds(pl.multiple_of(u * q_width, q_width), q_width)] = value[:, :q_width]
        here = pl.ds(pl.multiple_of(u * LANES, LANES), LANES)
        gk_ref[:, here] = value[:, q_width : q_width + LANES]
        gv_ref[:, here] = value[:, q_width + LANES :]

    def finish_out(u, value):
        go_ref[:, pl.ds(pl.multiple_of(u * q_width, q_width), q_width)] = value

    at = 0
    for stream, finish in ((qkv_stream, finish_qkv), (out_stream, finish_out)):
        count = len(stream.scratch())
        stream.bind(refs[at : at + count], units, finish)
        at += count

    rounds = [pair_of(bit)[1] for bit in (1,) + tuple(bits)]
    reach = 1
    while reach < line:
        rounds.append((z + reach * (1 - 2 * lax.rem(z // reach, 2)), index))
        reach *= 2

    rows = gate_ref.shape[0] // 2
    columns = gate_ref.shape[1]
    down_rows = down_ref.shape[0] // 2
    give = pl.ds(pl.multiple_of((1 - core) * rows, rows), rows)
    keep = pl.ds(pl.multiple_of(core * rows, rows), rows)
    down_give = pl.ds(pl.multiple_of((1 - core) * down_rows, down_rows), down_rows)
    down_keep = pl.ds(pl.multiple_of(core * down_rows, down_rows), down_rows)

    def half_copies():
        sources = (gate_ref.at[give, :], up_ref.at[give, :], down_ref.at[down_give, :])
        targets = (half_got.at[0], half_got.at[1], down_got)
        return [
            pltpu.make_async_remote_copy(
                src_ref=source,
                dst_ref=target,
                send_sem=half_sent_sem.at[i],
                recv_sem=half_got_sem.at[i],
                device_id=sibling,
                device_id_type=pl.DeviceIdType.MESH,
            )
            for i, (source, target) in enumerate(zip(sources, targets))
        ]

    @pl.when(n == 0)
    def _():
        barrier = pltpu.get_barrier_semaphore()
        for peer in rounds:
            pl.semaphore_signal(barrier, inc=1, device_id=peer, device_id_type=pl.DeviceIdType.MESH)
        for way in (1, -1):

            @pl.when((z + way >= 0) & (z + way < line))
            def _():
                pl.semaphore_signal(
                    barrier, inc=1, device_id=(z + way, index), device_id_type=pl.DeviceIdType.MESH
                )

        beside = jnp.minimum(z, 1) + jnp.minimum(line - 1 - z, 1)
        pl.semaphore_wait(barrier, len(rounds) + beside)
        for copy in half_copies():
            copy.start()
        total[...] = jnp.zeros_like(total)
        gains[0] = jnp.zeros_like(gains[0])

    @pl.when(n == units)
    def _():
        for copy in half_copies():
            copy.wait()
        own = pl.ds(pl.multiple_of(core * columns, LANES), columns)
        other = pl.ds(pl.multiple_of((1 - core) * columns, LANES), columns)
        gate_out_ref[:, own] = gate_ref[keep, :]
        gate_out_ref[:, other] = half_got[0]
        up_out_ref[:, own] = up_ref[keep, :]
        up_out_ref[:, other] = half_got[1]
        holder = z // (line // 2)

        @pl.when(holder == core)
        def _():
            down_out_ref[...] = down_ref[down_keep, :]

        @pl.when(holder != core)
        def _():
            down_out_ref[...] = down_got[...]

    step_streams(streams, n, steps, line, ready)
    sum_gains(rounds, n, units, gains, gains_got, gains_sent_sem, gains_got_sem)

    @pl.when(n == steps - 1)
    def _():
        gains_ref[...] = gains[len(rounds)]

    @pl.when(n < units)
    def _():
        hidden = hidden_ref[...]

        def back(lane, head_gain, place):
            got = jnp.concatenate(
                [got_ref[0, :, lane : lane + LANES], got_ref[1, :, lane : lane + LANES]], axis=0
            ).astype(F32)
            turned = got * cos_ref[...] - half_partner(got) * sin_ref[...]
            block = proj_ref[0, :, lane : lane + LANES]
            scale = lax.rsqrt(head_means(block * block) + EPSILON)
            normal = block * scale
            gains[0, place : place + 1, :] += jnp.sum(turned * normal, axis=0, keepdims=True)
            pushed = turned * head_gain[...]
            inner = head_means(pushed * normal)
            return (scale * (pushed - normal * inner)).astype(BF16)

        width = tokens_ref.shape[1]
        lines = width // LANES
        query = jnp.concatenate(
            [back(at, q_gain_ref, 2 * lines) for at in range(0, q_width, LANES)], axis=1
        )
        key = back(q_width, k_gain_ref, 2 * lines + 1)
        lane = q_width + LANES
        value = jnp.concatenate(
            [got_ref[0, :, lane : lane + LANES], got_ref[1, :, lane : lane + LANES]], axis=0
        )
        slot = lax.rem(n, 2)
        shape = qkv_stream.shape(qkv_stream.dims[0])
        whole = (slot,) + (slice(None),) * (len(shape) - 1)
        both = jnp.concatenate([query, key, value], axis=1)
        made = tn_dot(hidden, both).astype(BF16)
        qkv_stream.source[whole] = made.reshape(shape)
        out_stream.source[slot] = w_out_parts_ref[...].reshape(out_stream.shape(out_stream.dims[0]))
        total[...] += (
            nt_dot(query, wq_ref[...]) + nt_dot(key, wk_ref[...]) + nt_dot(value, wv_ref[...])
        )

        @pl.when(n == units - 1)
        def _():
            inputs = tokens_ref[...].astype(F32)
            scale = lax.rsqrt(jnp.mean(inputs * inputs, axis=-1, keepdims=True) + EPSILON)
            normal = inputs * scale
            grad = total[...]
            gain_grad = jnp.sum(grad * normal, axis=0, keepdims=True)
            for i in range(lines):
                here = slice(i * LANES, (i + 1) * LANES)
                gains[0, i : i + 1, :] = gain_grad[:, here]
                gains[0, lines + i : lines + i + 1, :] = ffn_gain_ref[:, here]
            pushed = grad * gain_ref[...]
            inner = jnp.mean(pushed * normal, axis=-1, keepdims=True)
            input_ref[...] = (mid_ref[...] + scale * (pushed - normal * inner)).astype(BF16)


def finish(
    line,
    bits,
    got,
    proj,
    hidden,
    tokens,
    mid,
    gain,
    wq,
    wk,
    wv,
    q_gain,
    k_gain,
    cosine,
    sine,
    w_out_parts,
    ffn_gain,
    gate_sum,
    up_sum,
    down_sum,
):
    rows, width = tokens.shape
    count, half, lanes = got.shape
    units = count // 2
    q_width = wq.shape[1] // units
    chips = line * 2 ** len(bits)
    sides = [(bit, 2) for bit in bits]
    dims = [("z", line)] + sides + [(1, 2)]
    mine = width // chips // 2
    streams = [
        Stream([1] + bits[::-1] + hops(line), dims, (mine, lanes), line),
        Stream([1] + bits + hops(line), dims, (mine, q_width), line),
    ]
    rounds = 1 + len(bits) + (line - 1).bit_length()
    steps = units + max(len(stream.path) for stream in streams) + 1
    gain_rows = -(-(2 * width // LANES + 2) // 8) * 8
    half_rows = gate_sum.shape[0] // 2
    down_rows = down_sum.shape[0] // 2
    columns = gate_sum.shape[1]

    def keep(shape):
        return pl.BlockSpec(shape, lambda n: (0,) * len(shape), pipeline_mode=pl.Buffered(1))

    def at(n):
        return jnp.minimum(n, units - 1)

    scratch = [
        pltpu.VMEM((rows, width), F32),
        pltpu.VMEM((rounds + 1, gain_rows, LANES), F32),
        pltpu.VMEM((rounds, gain_rows, LANES), F32),
        pltpu.SemaphoreType.DMA((rounds,)),
        pltpu.SemaphoreType.DMA((rounds,)),
        pltpu.VMEM((2, half_rows, columns), BF16),
        pltpu.VMEM((down_rows, down_sum.shape[1]), BF16),
        pltpu.SemaphoreType.DMA((3,)),
        pltpu.SemaphoreType.DMA((3,)),
        pltpu.SemaphoreType.REGULAR((2,)),
    ]
    for stream in streams:
        scratch += stream.scratch()
    outs = [
        ((rows, width), BF16),
        ((gain_rows, LANES), F32),
        ((mine, wq.shape[1]), BF16),
        ((mine, wk.shape[1]), BF16),
        ((mine, wv.shape[1]), BF16),
        ((mine, width), BF16),
        ((half_rows, 2 * columns), BF16),
        ((half_rows, 2 * columns), BF16),
        ((down_rows, down_sum.shape[1]), BF16),
    ]
    return pl.pallas_call(
        functools.partial(finish_kernel, line, bits, streams, units),
        name="finish",
        grid=(steps,),
        in_specs=[
            pl.BlockSpec((2, half, lanes), lambda n: (at(n), 0, 0)),
            pl.BlockSpec((1, rows, q_width + LANES), lambda n: (at(n), 0, 0)),
            keep((rows, width)),
            keep((rows, width)),
            keep((rows, width)),
            keep((1, width)),
            pl.BlockSpec((width, q_width), lambda n: (0, at(n))),
            pl.BlockSpec((width, LANES), lambda n: (0, at(n))),
            pl.BlockSpec((width, LANES), lambda n: (0, at(n))),
            keep((1, LANES)),
            keep((1, LANES)),
            keep((rows, LANES)),
            keep((rows, LANES)),
            pl.BlockSpec((width, q_width), lambda n: (0, at(n))),
            keep((1, width)),
            keep(gate_sum.shape),
            keep(up_sum.shape),
            keep(down_sum.shape),
        ],
        out_specs=[keep(shape) for shape, unused in outs],
        out_shape=[jax.ShapeDtypeStruct(shape, kind) for shape, kind in outs],
        scratch_shapes=scratch,
        compiler_params=kernel_params(collective_id=5, has_side_effects=True),
    )(
        got,
        proj,
        hidden,
        tokens,
        mid,
        gain,
        wq,
        wk,
        wv,
        q_gain,
        k_gain,
        cosine,
        sine,
        w_out_parts,
        ffn_gain,
        gate_sum,
        up_sum,
        down_sum,
    )


def flip_pairs(count, bit):
    return [(i, i ^ bit) for i in range(count)]


def swap_core(block, blk_count):
    return lax.ppermute(block, "blk", flip_pairs(blk_count, 1))


def fast_local(
    dp_count,
    blk_count,
    tokens,
    doc_lengths,
    g_attn,
    w_query,
    w_key,
    w_value,
    q_gain,
    k_gain,
    w_out,
    g_ffn,
    w_gate,
    w_up,
    w_down,
    cotangent,
):
    row_count, tok_count, width = tokens.shape
    rows = row_count * tok_count
    chips = blk_count // 2
    size = tok_count * blk_count
    index = lax.axis_index("blk")
    core = index % 2
    bits = []
    bit = blk_count // 2
    while bit > 1:
        bits.append(bit)
        bit //= 2
    chip_dims = (dp_count,) + (2,) * len(bits)
    all_chips = dp_count * chips
    places = index * tok_count + jnp.arange(tok_count, dtype=jnp.int32)
    unused, positions = doc_layout(doc_lengths, places)
    cosine, sine = rope_angles(positions)
    cosine = jnp.tile(cosine.reshape(rows, -1), (1, 4))
    sine = sine.reshape(rows, -1)
    sine = jnp.concatenate([-sine, sine, -sine, sine], axis=1)
    q_gain2 = jnp.tile(q_gain, 2)[None]
    k_gain2 = jnp.tile(k_gain, 2)[None]
    all_places = jnp.arange(size, dtype=jnp.int32)
    row_lengths = lax.dynamic_slice_in_dim(doc_lengths, core, 1, axis=0)
    unused, all_positions = doc_layout(row_lengths, all_places)
    starts = all_places - all_positions[0]
    starts_two = jnp.broadcast_to(
        starts.reshape(blk_count, 1, tok_count), (blk_count, 2, tok_count)
    ).reshape(1, 2 * size)
    flat = tokens.reshape(rows, width)
    grad_own = cotangent.reshape(rows, width)
    grad_both = jnp.concatenate([grad_own, swap_core(grad_own, blk_count)], axis=0)

    hidden_in, proj, send = project(
        flat, g_attn[None], w_query, w_key, w_value, q_gain2, k_gain2, cosine, sine
    )
    qkv = swap_blocks(send, 0).reshape(size, -1)
    attended, logs = attend(qkv, starts[:, None], tok_count)
    heads = swap_blocks(attended, 1)
    middle, hidden_own = middle_layer(flat, heads, w_out, g_ffn[None])
    hidden = jnp.concatenate([hidden_own, swap_core(hidden_own, blk_count)], axis=0)
    flipped = hidden.T
    core_arg = core.reshape(1)
    gate_grad, up_grad, acts, out_own, out_send, back_own, back_send = feed_forward(
        core_arg, hidden, grad_both, w_gate, w_up, w_down
    )
    back_got = swap_core(back_send, blk_count)
    out_got = swap_core(out_send, blk_count)
    output, mid, ffn_gain_grad, w_out_parts, send = turn(
        middle, out_own, out_got, back_own, back_got, grad_own, g_ffn[None], heads, w_out
    )
    grad_heads = swap_blocks(send, 2).reshape(size, -1)
    qkv_grad, gate_sum, up_sum, down_sum = back(
        dp_count,
        bits,
        qkv,
        logs,
        attended.reshape(size, -1),
        grad_heads,
        starts_two,
        tok_count,
        flipped,
        grad_both,
        gate_grad,
        up_grad,
        acts,
    )
    got = swap_blocks(qkv_grad.reshape(blk_count, tok_count, -1), 3)
    input_grad, gains, *sums = finish(
        dp_count,
        bits,
        got,
        proj,
        hidden_in,
        flat,
        mid,
        g_attn[None],
        w_query,
        w_key,
        w_value,
        q_gain2,
        k_gain2,
        cosine,
        sine,
        w_out_parts,
        ffn_gain_grad,
        gate_sum,
        up_sum,
        down_sum,
    )
    grad_w_query, grad_w_key, grad_w_value, grad_w_out, grad_w_gate, grad_w_up, grad_w_down = [
        part.astype(F32) for part in sums
    ]
    lines = width // LANES
    gain_attn = gains[:lines].reshape(width)
    gain_ffn = gains[lines : 2 * lines].reshape(width)
    gain_query = gains[2 * lines, :HEAD_DIM] + gains[2 * lines, HEAD_DIM:]
    gain_key = gains[2 * lines + 1, :HEAD_DIM] + gains[2 * lines + 1, HEAD_DIM:]
    return (
        output.reshape(tokens.shape),
        input_grad.reshape(tokens.shape),
        gain_attn,
        grad_w_query,
        grad_w_key,
        grad_w_value,
        gain_query,
        gain_key,
        grad_w_out,
        gain_ffn,
        grad_w_gate,
        grad_w_up,
        grad_w_down,
    )


def fits(mesh):
    blk_count = mesh.shape["blk"]
    chips = blk_count // 2
    power = blk_count & (blk_count - 1) == 0
    return power and blk_count > 2 and (KV_HEADS * HEAD_DIM) == chips * LANES


def solution(mesh):
    if fits(mesh):
        body = functools.partial(fast_local, mesh.shape["dp"], mesh.shape["blk"])
    else:
        body = local
    return jax.shard_map(
        body,
        mesh=mesh,
        in_specs=(
            P("dp", "blk", None),
            P("dp", None),
            P(),
            P(),
            P(),
            P(),
            P(),
            P(),
            P(),
            P(),
            P(),
            P(),
            P(),
            P("dp", "blk", None),
        ),
        out_specs=(
            P("dp", "blk", None),
            P("dp", "blk", None),
            P(),
            P(("dp", "blk"), None),
            P(("dp", "blk"), None),
            P(("dp", "blk"), None),
            P(),
            P(),
            P(("dp", "blk"), None),
            P(),
            P(("dp", "blk"), None),
            P(("dp", "blk"), None),
            P(("dp", "blk"), None),
        ),
        check_vma=False,
    )
```

```python
import functools
import math

import jax
import jax.numpy as jnp
from jax import lax
from jax.experimental import pallas as pl
from jax.experimental.pallas import tpu as pltpu
from jax.sharding import PartitionSpec as P

HEADS = 16
KV_HEADS = 8
HEAD_DIM = 64


EPSILON = 1e-05
ROPE_BASE = 1000000.0
NEGATIVE = -1e30


def norm_rows(values, norm_gain):
    row_scale = lax.rsqrt(jnp.mean(values * values, axis=-1, keepdims=True) + EPSILON)
    normal = values * row_scale
    return (normal * norm_gain, normal, row_scale)


def norm_back(normal, row_scale, norm_gain, grad_out):
    pushed = grad_out * norm_gain
    inner = jnp.mean(pushed * normal, axis=-1, keepdims=True)
    grad_in = row_scale * (pushed - normal * inner)
    leading = tuple(range(grad_out.ndim - 1))
    return (grad_in, jnp.sum(grad_out * normal, axis=leading))


def doc_layout(lengths, places):
    ends = jnp.cumsum(lengths, axis=1)
    past = places[None, :, None] >= ends[:, None, :]
    docs = jnp.sum(past.astype(jnp.int32), axis=2)
    before = jnp.sum(jnp.where(past, lengths[:, None, :], 0), axis=2)
    return (docs, places[None, :] - before)


def rope_angles(positions):
    half = HEAD_DIM // 2
    freqs = ROPE_BASE ** (-jnp.arange(half, dtype=jnp.float32) / half)
    angles = positions.astype(jnp.float32)[..., None] * freqs
    return (jnp.cos(angles), jnp.sin(angles))


def rotate(values, cosine, sine):
    half = values.shape[-1] // 2
    first_half = values[..., :half]
    second_half = values[..., half:]
    cos_col = cosine[:, :, None, :]
    sin_col = sine[:, :, None, :]
    return jnp.concatenate(
        [
            first_half * cos_col - second_half * sin_col,
            second_half * cos_col + first_half * sin_col,
        ],
        axis=-1,
    )


def local(
    tokens,
    doc_lengths,
    g_attn,
    w_query,
    w_key,
    w_value,
    q_gain,
    k_gain,
    w_out,
    g_ffn,
    w_gate,
    w_up,
    w_down,
    cotangent,
):
    row_count, tok_count, width = tokens.shape
    grouping = HEADS // KV_HEADS
    flat_rows = row_count * tok_count
    kv_width = KV_HEADS * HEAD_DIM
    softmax_scale = HEAD_DIM ** (-0.5)
    places = lax.axis_index("blk") * tok_count + jnp.arange(tok_count, dtype=jnp.int32)
    query_docs, query_pos = doc_layout(doc_lengths, places)
    cosine, sine = rope_angles(query_pos)
    inputs = tokens.reshape(flat_rows, width).astype(jnp.float32)
    normed, normal_in, scale_in = norm_rows(inputs, g_attn)
    hidden_in = normed.astype(jnp.bfloat16)
    query_proj = jnp.dot(hidden_in, w_query, preferred_element_type=jnp.float32).reshape(
        row_count, tok_count, HEADS, HEAD_DIM
    )
    key_proj = jnp.dot(hidden_in, w_key, preferred_element_type=jnp.float32).reshape(
        row_count, tok_count, KV_HEADS, HEAD_DIM
    )
    value_b = (
        jnp.dot(hidden_in, w_value, preferred_element_type=jnp.float32)
        .astype(jnp.bfloat16)
        .reshape(row_count, tok_count, kv_width)
    )
    query_norm, query_normal, query_scale = norm_rows(query_proj, q_gain)
    key_norm, key_normal, key_scale = norm_rows(key_proj, k_gain)
    query_b = (
        rotate(query_norm, cosine, sine)
        .astype(jnp.bfloat16)
        .reshape(row_count, tok_count, KV_HEADS, grouping, HEAD_DIM)
    )
    key_b = (
        rotate(key_norm, cosine, sine).astype(jnp.bfloat16).reshape(row_count, tok_count, kv_width)
    )

    def piece_mask(size):
        key_places = jnp.arange(size, dtype=jnp.int32)
        key_docs, unused = doc_layout(doc_lengths, key_places)
        return (key_places[None, None, :] <= places[None, :, None]) & (
            key_docs[:, None, :] == query_docs[:, :, None]
        )

    def piece_scores(key_piece, allowed):
        key_heads = key_piece.reshape(row_count, key_piece.shape[1], KV_HEADS, HEAD_DIM)
        raw_scores = (
            jnp.einsum("rqkgd,rpkd->rkgqp", query_b, key_heads, preferred_element_type=jnp.float32)
            * softmax_scale
        )
        return (jnp.where(allowed[:, None, None], raw_scores, -jnp.inf), key_heads)

    stat_shape = (row_count, KV_HEADS, grouping, tok_count)
    key_piece = lax.all_gather(key_b, "blk", axis=1, tiled=True)
    value_piece = lax.all_gather(value_b, "blk", axis=1, tiled=True)
    allowed = piece_mask(key_piece.shape[1])
    running_max = jnp.full(stat_shape, NEGATIVE, jnp.float32)
    scores, key_heads = piece_scores(key_piece, allowed)
    new_max = jnp.maximum(running_max, jnp.max(scores, axis=-1))
    weights = jnp.exp(scores - new_max[..., None])
    value_heads = value_piece.reshape(row_count, value_piece.shape[1], KV_HEADS, HEAD_DIM)
    added = jnp.einsum(
        "rkgqp,rpkd->rkgqd",
        weights.astype(jnp.bfloat16),
        value_heads,
        preferred_element_type=jnp.float32,
    )
    running_sum = jnp.sum(weights, axis=-1)
    attended = added / running_sum[..., None]
    log_total = new_max + jnp.log(running_sum)
    attended_b = (
        jnp.transpose(attended, (0, 3, 1, 2, 4))
        .reshape(flat_rows, HEADS * HEAD_DIM)
        .astype(jnp.bfloat16)
    )
    middle = inputs + jnp.dot(attended_b, w_out, preferred_element_type=jnp.float32)
    normed_ffn, normal_ffn, scale_ffn = norm_rows(middle, g_ffn)
    hidden_ffn = normed_ffn.astype(jnp.bfloat16)
    gate = jnp.dot(hidden_ffn, w_gate, preferred_element_type=jnp.float32)
    up_proj = jnp.dot(hidden_ffn, w_up, preferred_element_type=jnp.float32)
    sigmoid_gate = jax.nn.sigmoid(gate)
    silu_gate = gate * sigmoid_gate
    hidden = (silu_gate * up_proj).astype(jnp.bfloat16)
    result = middle + jnp.dot(hidden, w_down, preferred_element_type=jnp.float32)
    output = result.astype(jnp.bfloat16).reshape(row_count, tok_count, width)
    grad_out = cotangent.reshape(flat_rows, width)
    grad_w_down = jnp.einsum("tf,td->fd", hidden, grad_out, preferred_element_type=jnp.float32)
    grad_hidden = jnp.einsum("td,fd->tf", grad_out, w_down, preferred_element_type=jnp.float32)
    grad_gate = (grad_hidden * up_proj * sigmoid_gate * (1.0 + gate * (1.0 - sigmoid_gate))).astype(
        jnp.bfloat16
    )
    grad_up = (grad_hidden * silu_gate).astype(jnp.bfloat16)
    grad_w_gate = jnp.einsum("td,tf->df", hidden_ffn, grad_gate, preferred_element_type=jnp.float32)
    grad_w_up = jnp.einsum("td,tf->df", hidden_ffn, grad_up, preferred_element_type=jnp.float32)
    grad_h2 = jnp.einsum(
        "tf,df->td", grad_gate, w_gate, preferred_element_type=jnp.float32
    ) + jnp.einsum("tf,df->td", grad_up, w_up, preferred_element_type=jnp.float32)
    grad_mid, grad_ffn_gain = norm_back(normal_ffn, scale_ffn, g_ffn, grad_h2)
    grad_mid = grad_out.astype(jnp.float32) + grad_mid
    grad_attn = grad_mid.astype(jnp.bfloat16)
    grad_w_out = jnp.einsum("tc,td->cd", attended_b, grad_attn, preferred_element_type=jnp.float32)
    grad_attended = jnp.einsum(
        "td,cd->tc", grad_attn, w_out, preferred_element_type=jnp.float32
    ).astype(jnp.bfloat16)
    grad_heads = grad_attended.reshape(row_count, tok_count, KV_HEADS, grouping, HEAD_DIM)
    deltas = jnp.einsum("rqkgd,rkgqd->rkgq", grad_heads.astype(jnp.float32), attended)
    key_piece = lax.all_gather(key_b, "blk", axis=1, tiled=True)
    value_piece = lax.all_gather(value_b, "blk", axis=1, tiled=True)
    size = key_piece.shape[1]
    allowed = piece_mask(size)
    scores, key_heads = piece_scores(key_piece, allowed)
    probs = jnp.exp(scores - log_total[..., None])
    value_heads = value_piece.reshape(row_count, size, KV_HEADS, HEAD_DIM)
    value_piece_grad = jnp.einsum(
        "rkgqp,rqkgd->rpkd",
        probs.astype(jnp.bfloat16),
        grad_heads,
        preferred_element_type=jnp.float32,
    )
    grad_probs = jnp.einsum(
        "rqkgd,rpkd->rkgqp", grad_heads, value_heads, preferred_element_type=jnp.float32
    )
    grad_scores = (probs * (grad_probs - deltas[..., None])).astype(jnp.bfloat16)
    grad_query = jnp.einsum(
        "rkgqp,rpkd->rkgqd", grad_scores, key_heads, preferred_element_type=jnp.float32
    )
    key_piece_grad = jnp.einsum(
        "rkgqp,rqkgd->rpkd", grad_scores, query_b, preferred_element_type=jnp.float32
    )
    grad_keys = key_piece_grad.reshape(row_count, size, kv_width)
    grad_values = value_piece_grad.reshape(row_count, size, kv_width)
    grad_query, grad_keys, grad_values = (grad_query, grad_keys, grad_values)
    key_grad_mine, value_grad_mine = (
        lax.psum_scatter(
            grad_keys.astype(jnp.bfloat16), "blk", scatter_dimension=1, tiled=True
        ).astype(jnp.float32),
        lax.psum_scatter(
            grad_values.astype(jnp.bfloat16), "blk", scatter_dimension=1, tiled=True
        ).astype(jnp.float32),
    )
    grad_q_rot = (jnp.transpose(grad_query, (0, 3, 1, 2, 4)) * softmax_scale).reshape(
        row_count, tok_count, HEADS, HEAD_DIM
    )
    grad_k_rot = (key_grad_mine * softmax_scale).reshape(row_count, tok_count, KV_HEADS, HEAD_DIM)
    grad_q_proj, grad_query_gain = norm_back(
        query_normal, query_scale, q_gain, rotate(grad_q_rot, cosine, -sine)
    )
    grad_k_proj, grad_key_gain = norm_back(
        key_normal, key_scale, k_gain, rotate(grad_k_rot, cosine, -sine)
    )
    grad_q_b = grad_q_proj.astype(jnp.bfloat16).reshape(flat_rows, HEADS * HEAD_DIM)
    grad_k_b = grad_k_proj.astype(jnp.bfloat16).reshape(flat_rows, kv_width)
    grad_v_b = value_grad_mine.astype(jnp.bfloat16).reshape(flat_rows, kv_width)
    grad_w_query = jnp.einsum("td,tc->dc", hidden_in, grad_q_b, preferred_element_type=jnp.float32)
    grad_w_key = jnp.einsum("td,tc->dc", hidden_in, grad_k_b, preferred_element_type=jnp.float32)
    grad_w_value = jnp.einsum("td,tc->dc", hidden_in, grad_v_b, preferred_element_type=jnp.float32)
    grad_h1 = jnp.einsum("tc,dc->td", grad_q_b, w_query, preferred_element_type=jnp.float32)
    grad_h1 = grad_h1 + jnp.einsum("tc,dc->td", grad_k_b, w_key, preferred_element_type=jnp.float32)
    grad_h1 = grad_h1 + jnp.einsum(
        "tc,dc->td", grad_v_b, w_value, preferred_element_type=jnp.float32
    )
    grad_base, grad_attn_gain = norm_back(normal_in, scale_in, g_attn, grad_h1)
    input_grad = (grad_mid + grad_base).astype(jnp.bfloat16).reshape(row_count, tok_count, width)
    gain_attn, gain_query, gain_key, gain_ffn = lax.psum(
        (grad_attn_gain, grad_query_gain, grad_key_gain, grad_ffn_gain), ("dp", "blk")
    )
    locals_all = (
        grad_w_query,
        grad_w_key,
        grad_w_value,
        grad_w_out,
        grad_w_gate,
        grad_w_up,
        grad_w_down,
    )
    shared = (
        lax.psum_scatter(locals_all[0], ("dp", "blk"), scatter_dimension=0, tiled=True),
        lax.psum_scatter(locals_all[1], ("dp", "blk"), scatter_dimension=0, tiled=True),
        lax.psum_scatter(locals_all[2], ("dp", "blk"), scatter_dimension=0, tiled=True),
        lax.psum_scatter(locals_all[3], ("dp", "blk"), scatter_dimension=0, tiled=True),
        lax.psum_scatter(locals_all[4], ("dp", "blk"), scatter_dimension=0, tiled=True),
        lax.psum_scatter(locals_all[5], ("dp", "blk"), scatter_dimension=0, tiled=True),
        lax.psum_scatter(locals_all[6], ("dp", "blk"), scatter_dimension=0, tiled=True),
    )
    return (
        output,
        input_grad,
        gain_attn,
        shared[0],
        shared[1],
        shared[2],
        gain_query,
        gain_key,
        shared[3],
        gain_ffn,
        shared[4],
        shared[5],
        shared[6],
    )


BF16 = jnp.bfloat16
F32 = jnp.float32
LANES = 128
FF_TILE = 256
VMEM_BYTES = 56 * 1024 * 1024
LOG2_E = math.log2(math.e)
QUERY_SCALE = HEAD_DIM ** (-0.5) * LOG2_E
MASKED = -1e30


def nn_dot(left, right):
    return lax.dot_general(left, right, (((1,), (0,)), ((), ())), preferred_element_type=F32)


def nt_dot(left, right):
    return lax.dot_general(left, right, (((1,), (1,)), ((), ())), preferred_element_type=F32)


def tn_dot(left, right):
    return lax.dot_general(left, right, (((0,), (0,)), ((), ())), preferred_element_type=F32)


def kernel_params(**more):
    return pltpu.CompilerParams(vmem_limit_bytes=VMEM_BYTES, **more)


def whole_block(shape):
    return pl.BlockSpec(shape, lambda *ids: (0,) * len(shape))


def swap_blocks_kernel(send_ref, out_ref, send_sem, recv_sem, own_sem):
    count = send_ref.shape[0]
    mine = lax.axis_index("blk")
    group = lax.axis_index("dp")
    barrier = pltpu.get_barrier_semaphore()
    for step in range(1, count):
        pl.semaphore_signal(
            barrier,
            inc=1,
            device_id=(group, lax.rem(mine + step, count)),
            device_id_type=pl.DeviceIdType.MESH,
        )
    pl.semaphore_wait(barrier, count - 1)
    copies = []
    for step in range(1, count):
        target = lax.rem(mine + step, count)
        copy = pltpu.make_async_remote_copy(
            src_ref=send_ref.at[target],
            dst_ref=out_ref.at[mine],
            send_sem=send_sem.at[step],
            recv_sem=recv_sem.at[step],
            device_id=(group, target),
            device_id_type=pl.DeviceIdType.MESH,
        )
        copy.start()
        copies.append(copy)
    own = pltpu.make_async_copy(send_ref.at[mine], out_ref.at[mine], own_sem)
    own.start()
    own.wait()
    for copy in copies:
        copy.wait()


def swap_blocks(blocks, collective_id):
    count = blocks.shape[0]
    return pl.pallas_call(
        swap_blocks_kernel,
        name=f"swap_blocks_{collective_id}",
        out_shape=jax.ShapeDtypeStruct(blocks.shape, blocks.dtype),
        in_specs=[pl.BlockSpec(memory_space=pl.ANY)],
        out_specs=pl.BlockSpec(memory_space=pl.ANY),
        scratch_shapes=[
            pltpu.SemaphoreType.DMA((count,)),
            pltpu.SemaphoreType.DMA((count,)),
            pltpu.SemaphoreType.DMA,
        ],
        compiler_params=kernel_params(collective_id=collective_id, has_side_effects=True),
    )(blocks)


def head_means(values):
    rows = lax.broadcasted_iota(jnp.int32, (LANES, LANES), 0) // HEAD_DIM
    cols = lax.broadcasted_iota(jnp.int32, (LANES, LANES), 1) // HEAD_DIM
    spread = jnp.where(rows == cols, 1.0 / HEAD_DIM, 0.0).astype(BF16)
    high = values.astype(BF16)
    low = (values - high.astype(F32)).astype(BF16)
    return nn_dot(high, spread) + nn_dot(low, spread)


def half_partner(values):
    lane = lax.broadcasted_iota(jnp.int32, values.shape, 1)
    half = HEAD_DIM // 2
    ahead = pltpu.roll(values, LANES - half, 1)
    behind = pltpu.roll(values, half, 1)
    return jnp.where(lane % HEAD_DIM < half, ahead, behind)


def project_kernel(
    tokens_ref,
    gain_ref,
    wq_ref,
    wk_ref,
    wv_ref,
    q_gain_ref,
    k_gain_ref,
    cos_ref,
    sin_ref,
    hidden_ref,
    proj_ref,
    send_ref,
):
    rows = tokens_ref.shape[0]

    @pl.when(pl.program_id(0) == 0)
    def _():
        inputs = tokens_ref[...].astype(F32)
        scale = lax.rsqrt(jnp.mean(inputs * inputs, axis=-1, keepdims=True) + EPSILON)
        hidden_ref[...] = (inputs * scale * gain_ref[...]).astype(BF16)

    hidden = hidden_ref[...]
    half = rows // 2

    def put(block, lane):
        send_ref[0, :, lane : lane + LANES] = block[:half]
        send_ref[1, :, lane : lane + LANES] = block[half:]

    queries = nn_dot(hidden, wq_ref[...])
    keys = nn_dot(hidden, wk_ref[...])
    values = nn_dot(hidden, wv_ref[...])
    q_width = queries.shape[1]
    blocks = [(queries[:, at : at + LANES], at, q_gain_ref, QUERY_SCALE) for at in range(0, q_width, LANES)]
    blocks.append((keys, q_width, k_gain_ref, 1.0))
    for block, lane, head_gain, factor in blocks:
        proj_ref[0, :, lane : lane + LANES] = block
        scale = lax.rsqrt(head_means(block * block) + EPSILON)
        normed = block * scale * head_gain[...]
        turned = normed * cos_ref[...] + half_partner(normed) * sin_ref[...]
        put((turned * factor).astype(BF16), lane)
    put(values.astype(BF16), q_width + LANES)


def project(tokens, gain, wq, wk, wv, q_gain, k_gain, cosine, sine):
    rows, width = tokens.shape
    chips = wk.shape[1] // LANES
    q_width = wq.shape[1] // chips
    block_width = q_width + 2 * LANES
    return pl.pallas_call(
        project_kernel,
        name="project",
        grid=(chips,),
        in_specs=[
            whole_block((rows, width)),
            whole_block((1, width)),
            pl.BlockSpec((width, q_width), lambda p: (0, p)),
            pl.BlockSpec((width, LANES), lambda p: (0, p)),
            pl.BlockSpec((width, LANES), lambda p: (0, p)),
            whole_block((1, LANES)),
            whole_block((1, LANES)),
            whole_block((rows, LANES)),
            whole_block((rows, LANES)),
        ],
        out_specs=[
            whole_block((rows, width)),
            pl.BlockSpec((1, rows, q_width + LANES), lambda p: (p, 0, 0)),
            pl.BlockSpec((2, rows // 2, block_width), lambda p: (p, 0, 0)),
        ],
        out_shape=[
            jax.ShapeDtypeStruct((rows, width), BF16),
            jax.ShapeDtypeStruct((chips, rows, q_width + LANES), F32),
            jax.ShapeDtypeStruct((2 * chips, rows // 2, block_width), BF16),
        ],
        compiler_params=kernel_params(),
    )(tokens, gain, wq, wk, wv, q_gain, k_gain, cosine, sine)


def low_lanes(shape):
    return lax.broadcasted_iota(jnp.int32, shape, 1) < HEAD_DIM


def doubled(pair, group):
    turned = pltpu.roll(pair.astype(F32), HEAD_DIM, 1).astype(BF16)
    low = low_lanes(pair.shape)
    return jnp.where(low, pair, turned) if group == 0 else jnp.where(low, turned, pair)


def stacked_heads(pair):
    low = low_lanes(pair.shape)
    none = jnp.zeros_like(pair)
    return jnp.concatenate([jnp.where(low, pair, none), jnp.where(low, none, pair)], axis=0)


def in_three(column):
    lane = lax.broadcasted_iota(jnp.int32, (column.shape[0], LANES), 1)
    wide = jnp.broadcast_to(column, (column.shape[0], LANES))
    first = wide.astype(BF16).astype(F32)
    second = (wide - first).astype(BF16).astype(F32)
    third = wide - first - second
    return jnp.where(
        lane == 0, first, jnp.where(lane == 1, second, jnp.where(lane == 2, third, 0.0))
    ).astype(BF16)


def minus_three(rows):
    lane = lax.broadcasted_iota(jnp.int32, (rows, LANES), 1)
    return jnp.where(lane < 3, -1.0, 0.0).astype(BF16)


def attend_kernel(groups, block, qkv_ref, starts_ref, out_ref, logs_ref, keys, values, total):
    size = qkv_ref.shape[0]
    q_width = groups * LANES
    here = pl.program_id(0)

    @pl.when(here == 0)
    def _():
        for g in range(groups):
            keys[g] = doubled(qkv_ref[:, q_width : q_width + LANES], g)
            values[g, :, :LANES] = doubled(qkv_ref[:, q_width + LANES : q_width + 2 * LANES], g)
            values[g, :, LANES:] = jnp.ones((size, LANES), BF16)

    at = pl.multiple_of(here * block, block)
    starts = jnp.concatenate([starts_ref[pl.ds(at, block), :]] * 2, axis=0)
    queries = [
        stacked_heads(qkv_ref[pl.ds(at, block), g * LANES : (g + 1) * LANES]) for g in range(groups)
    ]
    column = lax.broadcasted_iota(jnp.int32, (2 * block, block), 1)
    row = lax.broadcasted_iota(jnp.int32, (2 * block, block), 0) % block

    def step(j, diagonal):
        key_at = pl.multiple_of(j * block, block)
        allowed = column >= starts - key_at
        if diagonal:
            allowed = allowed & (column <= row)
        for g in range(groups):
            scores = nt_dot(queries[g], keys[g, pl.ds(key_at, block), :])
            weights = jnp.exp2(jnp.where(allowed, scores, MASKED)).astype(BF16)
            part = nn_dot(weights, values[g, pl.ds(key_at, block), :])
            if diagonal:
                total[g] = part
            else:
                total[g] += part

    step(here, True)

    def body(j, carry):
        step(j, False)
        return carry

    lax.fori_loop(0, here, body, 0)
    for g in range(groups):
        sums = total[g, :, LANES:]
        mean = total[g, :, :LANES] / sums
        low = low_lanes((block, LANES))
        out_ref[0, :, g * LANES : (g + 1) * LANES] = jnp.where(low, mean[:block], mean[block:]).astype(BF16)
        logs_ref[g] = in_three(jnp.log2(sums[:, :1]))


def attend(qkv, starts, block):
    size, width = qkv.shape
    groups = (width - 2 * LANES) // LANES
    blocks = size // block
    return pl.pallas_call(
        functools.partial(attend_kernel, groups, block),
        name="attend",
        grid=(blocks,),
        in_specs=[whole_block((size, width)), whole_block((size, 1))],
        out_specs=[
            pl.BlockSpec((1, block, groups * LANES), lambda i: (i, 0, 0)),
            pl.BlockSpec((groups, 2 * block, LANES), lambda i: (0, i, 0)),
        ],
        out_shape=[
            jax.ShapeDtypeStruct((blocks, block, groups * LANES), BF16),
            jax.ShapeDtypeStruct((groups, 2 * size, LANES), BF16),
        ],
        scratch_shapes=[
            pltpu.VMEM((groups, size, LANES), BF16),
            pltpu.VMEM((groups, size, 2 * LANES), BF16),
            pltpu.VMEM((groups, 2 * block, 2 * LANES), F32),
        ],
        compiler_params=kernel_params(),
    )(qkv, starts)


def pair_of(bit):
    index = lax.axis_index("blk")
    mine = lax.rem(index // bit, 2)
    return mine, (lax.axis_index("dp"), index + bit * (1 - 2 * mine))


class Stream:
    def __init__(self, path, dims, block, line, kind=BF16):
        self.path, self.block, self.line, self.kind = path, block, line, kind
        self.dims = [tuple(dims)]
        left = list(dims)
        names = [name for name, unused in dims]
        for stage in path:
            if isinstance(stage, tuple):
                if stage[1] == line - 1:
                    at = [n for n, unused in left].index("z")
                    left = left[:at] + left[at + 1 :]
            else:
                at = [n for n, unused in left].index(stage)
                left = left[:at] + left[at + 1 :]
            self.dims.append(tuple(left))
        assert not left and "z" in names

    def is_hop(self, k):
        return isinstance(self.path[k], tuple)

    def starts_work(self, k):
        return k == 0 or not self.is_hop(k) or self.path[k][1] == 1

    def shape(self, dims):
        return tuple(count for unused, count in dims) + self.block

    def slots(self, k):
        return self.line if self.is_hop(k) else 2

    def scratch(self):
        shapes = []
        for k in range(len(self.path)):
            if self.starts_work(k):
                shapes.append(pltpu.VMEM((self.slots(k),) + self.shape(self.dims[k]), self.kind))
            if self.is_hop(k):
                rest = tuple(d for d in self.dims[k] if d[0] != "z")
                shapes.append(pltpu.VMEM((2, 2) + self.shape(rest), self.kind))
                shapes += [pltpu.SemaphoreType.DMA((2, 2))] * 2
            else:
                shapes.append(pltpu.VMEM((2,) + self.shape(self.dims[k + 1]), self.kind))
                shapes += [pltpu.SemaphoreType.DMA((2,))] * 2
        return shapes

    def bind(self, refs, units, finish, first_z=None):
        refs = list(refs)
        self.units, self.finish = units, finish
        self.first_z = 0 if first_z is None else first_z
        self.work, self.got, self.sent_sem, self.got_sem = [], [], [], []
        for k in range(len(self.path)):
            self.work.append(refs.pop(0) if self.starts_work(k) else self.work[-1])
            self.got.append(refs.pop(0))
            self.sent_sem.append(refs.pop(0))
            self.got_sem.append(refs.pop(0))
        self.source = self.work[0]

    def z_count(self, k):
        return dict(self.dims[k])["z"]

    def keeps(self, z, k):
        return (z >= self.first_z) & (z < self.first_z + self.z_count(k))

    def keeper(self, k):
        if "z" in [name for name, unused in self.dims[k]] or dict(self.dims[0])["z"] == self.line:
            return None
        z = lax.axis_index("dp")
        return (z >= self.first_z) & (z < self.first_z + dict(self.dims[0])["z"])

    def pair_copy(self, k, u):
        bit = self.path[k]
        mine, partner = pair_of(bit)
        at = [name for name, unused in self.dims[k]].index(bit)
        whole = (slice(None),) * at
        slot = lax.rem(u, 2)
        copy = pltpu.make_async_remote_copy(
            src_ref=self.work[k].at[(lax.rem(u, self.slots(k)),) + whole + (1 - mine,)],
            dst_ref=self.got[k].at[slot],
            send_sem=self.sent_sem[k].at[slot],
            recv_sem=self.got_sem[k].at[slot],
            device_id=partner,
            device_id_type=pl.DeviceIdType.MESH,
        )
        return copy, whole + (mine,)

    def hop_copy(self, k, u, way, block):
        z, index = lax.axis_index("dp"), lax.axis_index("blk")
        slot = lax.rem(u, 2)
        side = (1 - way) // 2
        return pltpu.make_async_remote_copy(
            src_ref=self.work[k].at[lax.rem(u, self.slots(k)), block],
            dst_ref=self.got[k].at[slot, side],
            send_sem=self.sent_sem[k].at[slot, side],
            recv_sem=self.got_sem[k].at[slot, side],
            device_id=(z + way, index),
            device_id_type=pl.DeviceIdType.MESH,
        )

    def hop_ends(self, k, way):
        z = lax.axis_index("dp")
        reach = way * (self.line - self.path[k][1])
        goes, comes = z + reach, z - way + reach
        sends = self.keeps(goes, k)
        takes = self.keeps(comes, k) & (z - way >= 0) & (z - way < self.line)
        return goes - self.first_z, sends, comes - self.first_z, takes

    def send(self, k, step):
        u = step - k - 1
        due = (u >= 0) & (u < self.units)
        if not self.is_hop(k):
            keeper = self.keeper(k)

            @pl.when(due if keeper is None else due & keeper)
            def _():
                self.pair_copy(k, u)[0].start()

            return
        for way in (1, -1):
            block, sends, unused, unused = self.hop_ends(k, way)

            @pl.when(due & sends)
            def _():
                self.hop_copy(k, u, way, block).start()

    def take(self, k, step):
        u = step - k - 2
        due = (u >= 0) & (u < self.units)
        keeper = self.keeper(k + 1)
        last = k == len(self.path) - 1

        def pass_on(value):
            if last:
                self.finish(u, value)
            else:
                self.work[k + 1][lax.rem(u, self.slots(k + 1))] = value

        if not self.is_hop(k):
            keeper = self.keeper(k)

            @pl.when(due if keeper is None else due & keeper)
            def _():
                copy, mine = self.pair_copy(k, u)
                copy.wait()
                own = self.work[k][(lax.rem(u, self.slots(k)),) + mine]
                pass_on(own + self.got[k][lax.rem(u, 2)])

            return
        slot = lax.rem(u, self.slots(k))
        for way in (1, -1):
            out_block, sends, in_block, takes = self.hop_ends(k, way)

            @pl.when(due & sends)
            def _():
                self.hop_copy(k, u, way, out_block).wait_send()

            @pl.when(due & takes)
            def _():
                self.hop_copy(k, u, way, in_block).wait_recv()
                self.work[k][slot, in_block] += self.got[k][lax.rem(u, 2), (1 - way) // 2]

        if self.path[k][1] == self.line - 1:
            own = lax.axis_index("dp") - self.first_z

            @pl.when(due if keeper is None else due & keeper)
            def _():
                pass_on(self.work[k][slot, own])


def hops(line):
    return [("z", t) for t in range(1, line)]


def greet(bits, line):
    barrier = pltpu.get_barrier_semaphore()
    z, index = lax.axis_index("dp"), lax.axis_index("blk")
    for bit in bits:
        pl.semaphore_signal(barrier, inc=1, device_id=pair_of(bit)[1], device_id_type=pl.DeviceIdType.MESH)
    for way in (1, -1):

        @pl.when((z + way >= 0) & (z + way < line))
        def _():
            pl.semaphore_signal(
                barrier, inc=1, device_id=(z + way, index), device_id_type=pl.DeviceIdType.MESH
            )

    beside = jnp.minimum(z, 1) + jnp.minimum(line - 1 - z, 1)
    pl.semaphore_wait(barrier, len(bits) + beside)


def step_streams(streams, step, steps, line, ready):
    longest = max(len(stream.path) for stream in streams)
    z, index = lax.axis_index("dp"), lax.axis_index("blk")
    for k in range(longest):
        for stream in streams:
            if k < len(stream.path):
                stream.take(k, step)
    for way in (1, -1):
        there = (z + way >= 0) & (z + way < line)

        @pl.when(there & (step >= 0) & (step < steps - 1))
        def _():
            pl.semaphore_signal(
                ready.at[(1 - way) // 2],
                inc=1,
                device_id=(z + way, index),
                device_id_type=pl.DeviceIdType.MESH,
            )

        @pl.when(there & (step > 0))
        def _():
            pl.semaphore_wait(ready.at[(1 + way) // 2], 1)

    for k in range(longest):
        for stream in streams:
            if k < len(stream.path):
                stream.send(k, step)


def greet_all(blk_count, line):
    barrier = pltpu.get_barrier_semaphore()
    z, index = lax.axis_index("dp"), lax.axis_index("blk")
    for step in range(1, blk_count):
        pl.semaphore_signal(
            barrier,
            inc=1,
            device_id=(z, lax.rem(index + step, blk_count)),
            device_id_type=pl.DeviceIdType.MESH,
        )
    for way in (1, -1):

        @pl.when((z + way >= 0) & (z + way < line))
        def _():
            pl.semaphore_signal(
                barrier, inc=1, device_id=(z + way, index), device_id_type=pl.DeviceIdType.MESH
            )

    beside = jnp.minimum(z, 1) + jnp.minimum(line - 1 - z, 1)
    pl.semaphore_wait(barrier, blk_count - 1 + beside)


def middle_kernel(
    line,
    bits,
    streams,
    units,
    tokens_ref,
    heads_ref,
    w_out_ref,
    gain_ref,
    dy_own_ref,
    dy_got_ref,
    w_gate_ref,
    w_up_ref,
    w_down_ref,
    output_ref,
    mid_ref,
    gain_grad_ref,
    w_grad_ref,
    grad_heads_ref,
    acts_ref,
    gate_out_ref,
    up_out_ref,
    hidden,
    flipped,
    dy,
    middle,
    out_sum,
    back_sum,
    gate_grads,
    up_grads,
    part_send,
    part_got,
    low_grad,
    do_send,
    do_got,
    hidden_sem,
    part_sent_sem,
    part_got_sem,
    do_sent_sem,
    do_got_sem,
    ready,
    *refs,
):
    n = pl.program_id(0)
    steps = pl.num_programs(0)
    z, index = lax.axis_index("dp"), lax.axis_index("blk")
    sibling = pair_of(1)[1]
    own_rows, width = tokens_ref.shape
    rows = 2 * own_rows
    blk_count, tok_count, head_lanes = heads_ref.shape
    chips = blk_count // 2
    chunk = 256
    gate_stream, up_stream, both_stream = streams
    gate_rows = gate_stream.block[0]
    own, other = pl.ds(0, own_rows), pl.ds(own_rows, own_rows)

    def finish_gate(u, value):
        gate_out_ref[:gate_rows, pl.ds(pl.multiple_of(u * FF_TILE, FF_TILE), FF_TILE)] = value

    def finish_up(u, value):
        up_out_ref[:gate_rows, pl.ds(pl.multiple_of(u * FF_TILE, FF_TILE), FF_TILE)] = value

    def finish_both(u, value):
        here = pl.ds(pl.multiple_of(u * FF_TILE, FF_TILE), FF_TILE)
        gate_out_ref[gate_rows:, here] = value[:, :FF_TILE]
        up_out_ref[gate_rows:, here] = value[:, FF_TILE:]

    at = 0
    for stream, finish in zip(streams, (finish_gate, finish_up, finish_both)):
        count = len(stream.scratch())
        stream.bind(refs[at : at + count], units, finish)
        at += count

    def hidden_copy():
        return pltpu.make_async_remote_copy(
            src_ref=hidden.at[own],
            dst_ref=hidden.at[other],
            send_sem=hidden_sem.at[0],
            recv_sem=hidden_sem.at[1],
            device_id=sibling,
            device_id_type=pl.DeviceIdType.MESH,
        )

    def part_copy(i):
        return pltpu.make_async_remote_copy(
            src_ref=part_send.at[i],
            dst_ref=part_got.at[i],
            send_sem=part_sent_sem.at[i],
            recv_sem=part_got_sem.at[i],
            device_id=sibling,
            device_id_type=pl.DeviceIdType.MESH,
        )

    def do_copy(target, source):
        return pltpu.make_async_remote_copy(
            src_ref=do_send.at[target],
            dst_ref=do_got.at[source],
            send_sem=do_sent_sem.at[target],
            recv_sem=do_got_sem.at[source],
            device_id=(z, target),
            device_id_type=pl.DeviceIdType.MESH,
        )

    def flip(start):
        for r in range(start, start + own_rows, chunk):
            for c in range(0, width, chunk):
                flipped[c : c + chunk, r : r + chunk] = hidden[r : r + chunk, c : c + chunk].T

    @pl.when(n == 0)
    def _():
        greet_all(blk_count, line)
        total = tokens_ref[...].astype(F32)
        for p in range(chips):
            block = jnp.concatenate([heads_ref[2 * p], heads_ref[2 * p + 1]], axis=0)
            total = total + nn_dot(block, w_out_ref[p * head_lanes : (p + 1) * head_lanes, :])
        middle[...] = total
        scale = lax.rsqrt(jnp.mean(total * total, axis=-1, keepdims=True) + EPSILON)
        hidden[own] = (total * scale * gain_ref[...]).astype(BF16)
        hidden_copy().start()
        dy[own] = dy_own_ref[...]
        dy[other] = dy_got_ref[...]
        out_sum[...] = jnp.zeros_like(out_sum)
        back_sum[...] = jnp.zeros_like(back_sum)
        flip(0)

    @pl.when(n == 1)
    def _():
        hidden_copy().wait()
        flip(own_rows)

    step_streams(streams, n - 1, steps - 1, line, ready)

    @pl.when((n >= 1) & (n <= units))
    def _():
        for m in range(rows // chunk):
            part = slice(m * chunk, (m + 1) * chunk)
            gate = nn_dot(hidden[part, :], w_gate_ref[...])
            up = nn_dot(hidden[part, :], w_up_ref[...])
            pushed = nt_dot(dy[part, :], w_down_ref[...])
            opened = jax.nn.sigmoid(gate)
            silu = gate * opened
            act = (silu * up).astype(BF16)
            gate_grad = (pushed * up * opened * (1.0 + gate * (1.0 - opened))).astype(BF16)
            up_grad = (pushed * silu).astype(BF16)
            acts_ref[:, part] = act.T
            gate_grads[part, :] = gate_grad
            up_grads[part, :] = up_grad
            out_sum[part, :] += nn_dot(act, w_down_ref[...])
            back_sum[part, :] += nt_dot(gate_grad, w_gate_ref[...]) + nt_dot(up_grad, w_up_ref[...])
        u = n - 1
        slot, long_slot = lax.rem(u, 2), lax.rem(u, both_stream.slots(0))
        each = width // line
        shape = gate_stream.shape(gate_stream.dims[0])[1:-2] + (-1, FF_TILE)
        for m in range(line):
            part = slice(m * each, (m + 1) * each)
            gate_part = nn_dot(flipped[part, :], gate_grads[...]).astype(BF16).reshape(shape)
            up_part = nn_dot(flipped[part, :], up_grads[...]).astype(BF16).reshape(shape)
            gate_stream.source[slot, m] = gate_part[..., :gate_rows, :]
            up_stream.source[slot, m] = up_part[..., :gate_rows, :]
            both_stream.source[long_slot, m, ..., :FF_TILE] = gate_part[..., gate_rows:, :]
            both_stream.source[long_slot, m, ..., FF_TILE:] = up_part[..., gate_rows:, :]

    @pl.when(n == units)
    def _():
        part_send[0] = back_sum[other].astype(BF16)
        part_copy(0).start()
        part_send[1] = out_sum[other].astype(BF16)
        part_copy(1).start()

    @pl.when(n == units + 1)
    def _():
        part_copy(0).wait()
        values = middle[...]
        scale = lax.rsqrt(jnp.mean(values * values, axis=-1, keepdims=True) + EPSILON)
        normal = values * scale
        back = back_sum[own] + part_got[0].astype(F32)
        gain_grad_ref[...] = jnp.sum(back * normal, axis=0, keepdims=True)
        pushed = back * gain_ref[...]
        inner = jnp.mean(pushed * normal, axis=-1, keepdims=True)
        mid = dy[own].astype(F32) + scale * (pushed - normal * inner)
        mid_ref[...] = mid
        low_grad[...] = mid.astype(BF16)
        part_copy(1).wait()
        output_ref[...] = (values + (out_sum[own] + part_got[1].astype(F32))).astype(BF16)

    @pl.when((n > units + 1) & (n <= units + 1 + chips))
    def _():
        p = n - units - 2
        grad = low_grad[...]
        lanes = pl.ds(pl.multiple_of(p * head_lanes, head_lanes), head_lanes)
        send = nt_dot(grad, w_out_ref[lanes, :]).astype(BF16)
        for half in range(2):
            target = 2 * p + half
            do_send[target] = send[half * tok_count : (half + 1) * tok_count]

            @pl.when(target != index)
            def _():
                do_copy(target, index).start()

            @pl.when(target == index)
            def _():
                do_got[target] = send[half * tok_count : (half + 1) * tok_count]

        heads = jnp.concatenate([heads_ref[2 * p], heads_ref[2 * p + 1]], axis=0)
        w_grad_ref[lanes, :] = tn_dot(heads, grad).astype(BF16)

    @pl.when(n == steps - 1)
    def _():
        for other_index in range(blk_count):

            @pl.when(other_index != index)
            def _():
                do_copy(other_index, other_index).wait()

        grad_heads_ref[...] = do_got[...]


def middle_layer(line, bits, tokens, heads, w_out, gain, dy_own, dy_got, w_gate, w_up, w_down):
    own_rows, width = tokens.shape
    rows = 2 * own_rows
    blk_count, tok_count, head_lanes = heads.shape
    units = w_gate.shape[1] // 2 // FF_TILE
    chips = line * 2 ** len(bits)
    each = width // chips
    late = each // 4
    dims = [("z", line)] + [(bit, 2) for bit in bits]
    streams = [
        Stream(bits[::-1] + hops(line), dims, (each - late, FF_TILE), line),
        Stream(bits + hops(line), dims, (each - late, FF_TILE), line),
        Stream(hops(line) + bits, dims, (late, 2 * FF_TILE), line),
    ]
    steps = max(units + 2 + max(len(stream.path) for stream in streams), units + 3 + blk_count // 2)

    def keep(shape):
        return pl.BlockSpec(shape, lambda n: (0,) * len(shape), pipeline_mode=pl.Buffered(1))

    def tile(n):
        return jnp.clip(n - 1, 0, units - 1)

    def mine(n):
        return lax.rem(lax.axis_index("blk"), 2) * units + tile(n)

    scratch = [
        pltpu.VMEM((rows, width), BF16),
        pltpu.VMEM((width, rows), BF16),
        pltpu.VMEM((rows, width), BF16),
        pltpu.VMEM((own_rows, width), F32),
        pltpu.VMEM((rows, width), F32),
        pltpu.VMEM((rows, width), F32),
        pltpu.VMEM((rows, FF_TILE), BF16),
        pltpu.VMEM((rows, FF_TILE), BF16),
        pltpu.VMEM((2, own_rows, width), BF16),
        pltpu.VMEM((2, own_rows, width), BF16),
        pltpu.VMEM((own_rows, width), BF16),
        pltpu.VMEM(heads.shape, BF16),
        pltpu.VMEM(heads.shape, BF16),
        pltpu.SemaphoreType.DMA((2,)),
        pltpu.SemaphoreType.DMA((2,)),
        pltpu.SemaphoreType.DMA((2,)),
        pltpu.SemaphoreType.DMA((blk_count,)),
        pltpu.SemaphoreType.DMA((blk_count,)),
        pltpu.SemaphoreType.REGULAR((2,)),
    ]
    for stream in streams:
        scratch += stream.scratch()
    outs = [
        ((own_rows, width), BF16),
        ((own_rows, width), F32),
        ((1, width), F32),
        (w_out.shape, BF16),
        (heads.shape, BF16),
        ((units * FF_TILE, rows), BF16),
        ((each, units * FF_TILE), BF16),
        ((each, units * FF_TILE), BF16),
    ]
    out_specs = [keep(shape) for shape, unused in outs]
    out_specs[5] = pl.BlockSpec((FF_TILE, rows), lambda n: (tile(n), 0))
    return pl.pallas_call(
        functools.partial(middle_kernel, line, bits, streams, units),
        name="middle",
        grid=(steps,),
        in_specs=[
            keep(tokens.shape),
            keep(heads.shape),
            keep(w_out.shape),
            keep(gain.shape),
            keep(dy_own.shape),
            keep(dy_got.shape),
            pl.BlockSpec((width, FF_TILE), lambda n: (0, mine(n))),
            pl.BlockSpec((width, FF_TILE), lambda n: (0, mine(n))),
            pl.BlockSpec((FF_TILE, width), lambda n: (mine(n), 0)),
        ],
        out_specs=out_specs,
        out_shape=[jax.ShapeDtypeStruct(shape, kind) for shape, kind in outs],
        scratch_shapes=scratch,
        compiler_params=kernel_params(collective_id=6, has_side_effects=True),
    )(tokens, heads, w_out, gain, dy_own, dy_got, w_gate, w_up, w_down)


def back_kernel(
    groups,
    block,
    line,
    bits,
    streams,
    units,
    qkv_ref,
    logs_ref,
    out_ref,
    grad_ref,
    starts_ref,
    dy_own_ref,
    dy_got_ref,
    acts_ref,
    result_ref,
    down_out_ref,
    queries,
    keys,
    values,
    grads,
    query_grad,
    pair_grad,
    ready,
    *refs,
):
    size = qkv_ref.shape[0]
    blocks = size // block
    q_width = groups * LANES
    n = pl.program_id(0)
    core = lax.rem(lax.axis_index("blk"), 2)
    half = down_out_ref.shape[1] // 2

    def finish_low(u, value):
        rows = value.shape[0]
        down_out_ref[pl.ds(pl.multiple_of(u * rows, rows), rows), :half] = value

    def finish_high(u, value):
        rows = value.shape[0]
        down_out_ref[pl.ds(pl.multiple_of(u * rows, rows), rows), half:] = value

    at = 0
    for stream, finish in zip(streams, (finish_low, finish_high)):
        count = len(stream.scratch())
        stream.bind(refs[at : at + count], units, finish, core * (line // 2))
        at += count

    @pl.when(n == 0)
    def _():
        greet(bits, line)
        down_out_ref[...] = jnp.zeros_like(down_out_ref)
        query_grad[...] = jnp.zeros_like(query_grad)
        pair_grad[...] = jnp.zeros_like(pair_grad)
        for g in range(groups):
            lanes = slice(g * LANES, (g + 1) * LANES)
            keys[g, :, :LANES] = doubled(qkv_ref[:, q_width : q_width + LANES], g)
            keys[g, :, LANES:] = minus_three(size)
            values[g, :, :LANES] = doubled(qkv_ref[:, q_width + LANES : q_width + 2 * LANES], g)
            values[g, :, LANES:] = minus_three(size)

            def fill(i, carry):
                at = pl.multiple_of(i * block, block)
                to = pl.multiple_of(i * 2 * block, 2 * block)
                queries[g, pl.ds(to, 2 * block), :LANES] = stacked_heads(qkv_ref[pl.ds(at, block), lanes])
                queries[g, pl.ds(to, 2 * block), LANES:] = logs_ref[g, pl.ds(to, 2 * block), :]
                grad = stacked_heads(grad_ref[pl.ds(at, block), lanes])
                mean = stacked_heads(out_ref[pl.ds(at, block), lanes])
                delta = jnp.sum(grad.astype(F32) * mean.astype(F32), axis=1, keepdims=True)
                grads[g, pl.ds(to, 2 * block), :LANES] = grad
                grads[g, pl.ds(to, 2 * block), LANES:] = in_three(delta)
                return carry

            lax.fori_loop(0, blocks, fill, 0)

    step_streams(streams, n, pl.num_programs(0), line, ready)

    @pl.when(n < units)
    def _():
        acts = acts_ref[...].reshape(-1, acts_ref.shape[-1])
        rows = dy_own_ref.shape[0]
        made = nn_dot(acts[:, :rows], dy_own_ref[...]) + nn_dot(acts[:, rows:], dy_got_ref[...])
        made = made.astype(BF16)
        for stream, part in zip(streams, (made[:, :half], made[:, half:])):
            shape = stream.shape(stream.dims[0])
            stream.source[lax.rem(n, stream.slots(0))] = part.reshape(shape)

    row = lax.broadcasted_iota(jnp.int32, (block, 2 * block), 0)
    column = lax.broadcasted_iota(jnp.int32, (block, 2 * block), 1) % block

    turn = n - (pl.num_programs(0) - blocks - 2)

    @pl.when((turn >= 0) & (turn < blocks + 1))
    def _():
        def pair(m, carry):
            late = (turn + m) // blocks
            j = m + late * (blocks - 1 - 2 * m)
            i = (1 - late) * (m + turn) + late * (turn - 1)
            key_at = pl.multiple_of(j * block, block)
            at = pl.multiple_of(i * 2 * block, 2 * block)
            key_rows = pl.ds(key_at, block)
            stack = pl.ds(at, 2 * block)
            allowed = (row >= starts_ref[:, stack] - key_at) & (row - column <= (i - j) * block)
            for g in range(groups):
                query = queries[g, stack, :]
                grad = grads[g, stack, :]
                key = keys[g, key_rows, :]
                scores = nt_dot(key, query)
                probs = jnp.exp2(jnp.where(allowed, scores, MASKED))
                pushed = (probs * nt_dot(values[g, key_rows, :], grad)).astype(BF16)
                pair_grad[g, key_rows, LANES:] += nn_dot(probs.astype(BF16), grad[:, :LANES])
                pair_grad[g, key_rows, :LANES] += nn_dot(pushed, query[:, :LANES])
                query_grad[g, stack, :] += tn_dot(pushed, key[:, :LANES])
            return carry

        lax.fori_loop(0, blocks // 2, pair, 0)

    @pl.when(turn == blocks + 1)
    def _():
        low = low_lanes((block, LANES))

        def finish(i, carry):
            at = pl.multiple_of(i * block, block)
            to = pl.multiple_of(i * 2 * block, 2 * block)
            here = pl.ds(at, block)
            for g in range(groups):
                first = query_grad[g, pl.ds(to, block), :]
                second = query_grad[g, pl.ds(to + block, block), :]
                joined = jnp.where(low, first, second) * HEAD_DIM ** (-0.5)
                result_ref[here, g * LANES : (g + 1) * LANES] = joined.astype(BF16)
            for part in range(2):
                sums = []
                for g in range(groups):
                    both = pair_grad[g, here, part * LANES : (part + 1) * LANES]
                    sums.append(both + pltpu.roll(both, HEAD_DIM, 1))
                joined = jnp.where(low, sums[0], sums[1])
                if part == 0:
                    joined = joined * (1.0 / LOG2_E)
                lane = q_width + part * LANES
                result_ref[here, lane : lane + LANES] = joined.astype(BF16)
            return carry

        lax.fori_loop(0, blocks, finish, 0)


def back(line, bits, qkv, logs, out, grad, starts, block, dy_own, dy_got, acts):
    size, width = qkv.shape
    groups = (width - 2 * LANES) // LANES
    model = dy_own.shape[1]
    rows = acts.shape[1]
    units = acts.shape[0] // FF_TILE
    chips = line * 2 ** len(bits)
    down_rows = acts.shape[0] // (chips // 2)
    down_block = (down_rows // units, model // 2)
    dims = [("z", line // 2)] + [(bit, 2) for bit in bits]
    streams = [
        Stream(hops(line) + bits[::-1], dims, down_block, line),
        Stream(bits + hops(line), dims, down_block, line),
    ]
    longest = max(len(stream.path) for stream in streams)
    steps = max(units + longest + 1, size // block + 2)

    def keep(shape):
        return pl.BlockSpec(shape, lambda n: (0,) * len(shape), pipeline_mode=pl.Buffered(1))

    acts = acts.reshape(chips // 2, down_rows, rows)
    scratch = [
        pltpu.VMEM((groups, 2 * size, 2 * LANES), BF16),
        pltpu.VMEM((groups, size, 2 * LANES), BF16),
        pltpu.VMEM((groups, size, 2 * LANES), BF16),
        pltpu.VMEM((groups, 2 * size, 2 * LANES), BF16),
        pltpu.VMEM((groups, 2 * size, LANES), F32),
        pltpu.VMEM((groups, size, 2 * LANES), F32),
        pltpu.SemaphoreType.REGULAR((2,)),
    ]
    for stream in streams:
        scratch += stream.scratch()
    return pl.pallas_call(
        functools.partial(back_kernel, groups, block, line, bits, streams, units),
        name="back",
        grid=(steps,),
        in_specs=[
            keep(qkv.shape),
            keep(logs.shape),
            keep(out.shape),
            keep(grad.shape),
            keep(starts.shape),
            keep(dy_own.shape),
            keep(dy_got.shape),
            pl.BlockSpec(
                (chips // 2, down_block[0], rows), lambda n: (0, jnp.minimum(n, units - 1), 0)
            ),
        ],
        out_specs=[keep(qkv.shape), keep((down_rows, model))],
        out_shape=[
            jax.ShapeDtypeStruct(qkv.shape, BF16),
            jax.ShapeDtypeStruct((down_rows, model), BF16),
        ],
        scratch_shapes=scratch,
        compiler_params=kernel_params(collective_id=4, has_side_effects=True),
    )(qkv, logs, out, grad, starts, dy_own, dy_got, acts)


def sum_gains(rounds, n, first, gains, gains_got, sent_sem, got_sem):
    for r, partner in enumerate(rounds):

        def copy():
            return pltpu.make_async_remote_copy(
                src_ref=gains.at[r],
                dst_ref=gains_got.at[r],
                send_sem=sent_sem.at[r],
                recv_sem=got_sem.at[r],
                device_id=partner,
                device_id_type=pl.DeviceIdType.MESH,
            )

        @pl.when(n == first + r + 1)
        def _():
            copy().wait()
            gains[r + 1] = gains[r] + gains_got[r]

    for r, partner in enumerate(rounds):

        @pl.when(n == first + r)
        def _():
            pltpu.make_async_remote_copy(
                src_ref=gains.at[r],
                dst_ref=gains_got.at[r],
                send_sem=sent_sem.at[r],
                recv_sem=got_sem.at[r],
                device_id=partner,
                device_id_type=pl.DeviceIdType.MESH,
            ).start()


def finish_kernel(
    line,
    bits,
    streams,
    units,
    got_ref,
    proj_ref,
    hidden_ref,
    tokens_ref,
    mid_ref,
    gain_ref,
    wq_ref,
    wk_ref,
    wv_ref,
    q_gain_ref,
    k_gain_ref,
    cos_ref,
    sin_ref,
    w_out_parts_ref,
    ffn_gain_ref,
    gate_ref,
    up_ref,
    down_ref,
    input_ref,
    gains_ref,
    gq_ref,
    gk_ref,
    gv_ref,
    go_ref,
    gate_out_ref,
    up_out_ref,
    down_out_ref,
    total,
    gains,
    gains_got,
    gains_sent_sem,
    gains_got_sem,
    half_got,
    down_got,
    half_sent_sem,
    half_got_sem,
    ready,
    *refs,
):
    n = pl.program_id(0)
    z, index = lax.axis_index("dp"), lax.axis_index("blk")
    core, sibling = pair_of(1)
    steps = pl.num_programs(0)
    qkv_stream, out_stream = streams
    q_width = wq_ref.shape[1]

    def finish_qkv(u, value):
        gq_ref[:, pl.ds(pl.multiple_of(u * q_width, q_width), q_width)] = value[:, :q_width]
        here = pl.ds(pl.multiple_of(u * LANES, LANES), LANES)
        gk_ref[:, here] = value[:, q_width : q_width + LANES]
        gv_ref[:, here] = value[:, q_width + LANES :]

    def finish_out(u, value):
        go_ref[:, pl.ds(pl.multiple_of(u * q_width, q_width), q_width)] = value

    at = 0
    for stream, finish in ((qkv_stream, finish_qkv), (out_stream, finish_out)):
        count = len(stream.scratch())
        stream.bind(refs[at : at + count], units, finish)
        at += count

    rounds = [pair_of(bit)[1] for bit in (1,) + tuple(bits)]
    reach = 1
    while reach < line:
        rounds.append((z + reach * (1 - 2 * lax.rem(z // reach, 2)), index))
        reach *= 2

    rows = gate_ref.shape[0] // 2
    columns = gate_ref.shape[1]
    down_rows = down_ref.shape[0] // 2
    give = pl.ds(pl.multiple_of((1 - core) * rows, rows), rows)
    keep = pl.ds(pl.multiple_of(core * rows, rows), rows)
    down_give = pl.ds(pl.multiple_of((1 - core) * down_rows, down_rows), down_rows)
    down_keep = pl.ds(pl.multiple_of(core * down_rows, down_rows), down_rows)

    def half_copies():
        sources = (gate_ref.at[give, :], up_ref.at[give, :], down_ref.at[down_give, :])
        targets = (half_got.at[0], half_got.at[1], down_got)
        return [
            pltpu.make_async_remote_copy(
                src_ref=source,
                dst_ref=target,
                send_sem=half_sent_sem.at[i],
                recv_sem=half_got_sem.at[i],
                device_id=sibling,
                device_id_type=pl.DeviceIdType.MESH,
            )
            for i, (source, target) in enumerate(zip(sources, targets))
        ]

    @pl.when(n == 0)
    def _():
        barrier = pltpu.get_barrier_semaphore()
        for peer in rounds:
            pl.semaphore_signal(barrier, inc=1, device_id=peer, device_id_type=pl.DeviceIdType.MESH)
        for way in (1, -1):

            @pl.when((z + way >= 0) & (z + way < line))
            def _():
                pl.semaphore_signal(
                    barrier, inc=1, device_id=(z + way, index), device_id_type=pl.DeviceIdType.MESH
                )

        beside = jnp.minimum(z, 1) + jnp.minimum(line - 1 - z, 1)
        pl.semaphore_wait(barrier, len(rounds) + beside)
        for copy in half_copies():
            copy.start()
        total[...] = jnp.zeros_like(total)
        gains[0] = jnp.zeros_like(gains[0])

    @pl.when(n == units)
    def _():
        for copy in half_copies():
            copy.wait()
        own = pl.ds(pl.multiple_of(core * columns, LANES), columns)
        other = pl.ds(pl.multiple_of((1 - core) * columns, LANES), columns)
        gate_out_ref[:, own] = gate_ref[keep, :]
        gate_out_ref[:, other] = half_got[0]
        up_out_ref[:, own] = up_ref[keep, :]
        up_out_ref[:, other] = half_got[1]
        holder = z // (line // 2)

        @pl.when(holder == core)
        def _():
            down_out_ref[...] = down_ref[down_keep, :]

        @pl.when(holder != core)
        def _():
            down_out_ref[...] = down_got[...]

    step_streams(streams, n, steps, line, ready)
    sum_gains(rounds, n, units, gains, gains_got, gains_sent_sem, gains_got_sem)

    @pl.when(n == steps - 1)
    def _():
        gains_ref[...] = gains[len(rounds)]

    @pl.when(n < units)
    def _():
        hidden = hidden_ref[...]

        def back(lane, head_gain, place):
            got = jnp.concatenate(
                [got_ref[0, :, lane : lane + LANES], got_ref[1, :, lane : lane + LANES]], axis=0
            ).astype(F32)
            turned = got * cos_ref[...] - half_partner(got) * sin_ref[...]
            block = proj_ref[0, :, lane : lane + LANES]
            scale = lax.rsqrt(head_means(block * block) + EPSILON)
            normal = block * scale
            gains[0, place : place + 1, :] += jnp.sum(turned * normal, axis=0, keepdims=True)
            pushed = turned * head_gain[...]
            inner = head_means(pushed * normal)
            return (scale * (pushed - normal * inner)).astype(BF16)

        width = tokens_ref.shape[1]
        lines = width // LANES
        query = jnp.concatenate(
            [back(at, q_gain_ref, 2 * lines) for at in range(0, q_width, LANES)], axis=1
        )
        key = back(q_width, k_gain_ref, 2 * lines + 1)
        lane = q_width + LANES
        value = jnp.concatenate(
            [got_ref[0, :, lane : lane + LANES], got_ref[1, :, lane : lane + LANES]], axis=0
        )
        slot = lax.rem(n, 2)
        shape = qkv_stream.shape(qkv_stream.dims[0])
        whole = (slot,) + (slice(None),) * (len(shape) - 1)
        both = jnp.concatenate([query, key, value], axis=1)
        made = tn_dot(hidden, both).astype(BF16)
        qkv_stream.source[whole] = made.reshape(shape)
        out_stream.source[slot] = w_out_parts_ref[...].reshape(out_stream.shape(out_stream.dims[0]))
        total[...] += (
            nt_dot(query, wq_ref[...]) + nt_dot(key, wk_ref[...]) + nt_dot(value, wv_ref[...])
        )

        @pl.when(n == units - 1)
        def _():
            inputs = tokens_ref[...].astype(F32)
            scale = lax.rsqrt(jnp.mean(inputs * inputs, axis=-1, keepdims=True) + EPSILON)
            normal = inputs * scale
            grad = total[...]
            gain_grad = jnp.sum(grad * normal, axis=0, keepdims=True)
            for i in range(lines):
                here = slice(i * LANES, (i + 1) * LANES)
                gains[0, i : i + 1, :] = gain_grad[:, here]
                gains[0, lines + i : lines + i + 1, :] = ffn_gain_ref[:, here]
            pushed = grad * gain_ref[...]
            inner = jnp.mean(pushed * normal, axis=-1, keepdims=True)
            input_ref[...] = (mid_ref[...] + scale * (pushed - normal * inner)).astype(BF16)


def finish(
    line,
    bits,
    got,
    proj,
    hidden,
    tokens,
    mid,
    gain,
    wq,
    wk,
    wv,
    q_gain,
    k_gain,
    cosine,
    sine,
    w_out_parts,
    ffn_gain,
    gate_sum,
    up_sum,
    down_sum,
):
    rows, width = tokens.shape
    count, half, lanes = got.shape
    units = count // 2
    q_width = wq.shape[1] // units
    chips = line * 2 ** len(bits)
    sides = [(bit, 2) for bit in bits]
    dims = [("z", line)] + sides + [(1, 2)]
    mine = width // chips // 2
    streams = [
        Stream([1] + bits[::-1] + hops(line), dims, (mine, lanes), line),
        Stream([1] + bits + hops(line), dims, (mine, q_width), line),
    ]
    rounds = 1 + len(bits) + (line - 1).bit_length()
    steps = units + max(len(stream.path) for stream in streams) + 1
    gain_rows = -(-(2 * width // LANES + 2) // 8) * 8
    half_rows = gate_sum.shape[0] // 2
    down_rows = down_sum.shape[0] // 2
    columns = gate_sum.shape[1]

    def keep(shape):
        return pl.BlockSpec(shape, lambda n: (0,) * len(shape), pipeline_mode=pl.Buffered(1))

    def at(n):
        return jnp.minimum(n, units - 1)

    scratch = [
        pltpu.VMEM((rows, width), F32),
        pltpu.VMEM((rounds + 1, gain_rows, LANES), F32),
        pltpu.VMEM((rounds, gain_rows, LANES), F32),
        pltpu.SemaphoreType.DMA((rounds,)),
        pltpu.SemaphoreType.DMA((rounds,)),
        pltpu.VMEM((2, half_rows, columns), BF16),
        pltpu.VMEM((down_rows, down_sum.shape[1]), BF16),
        pltpu.SemaphoreType.DMA((3,)),
        pltpu.SemaphoreType.DMA((3,)),
        pltpu.SemaphoreType.REGULAR((2,)),
    ]
    for stream in streams:
        scratch += stream.scratch()
    outs = [
        ((rows, width), BF16),
        ((gain_rows, LANES), F32),
        ((mine, wq.shape[1]), BF16),
        ((mine, wk.shape[1]), BF16),
        ((mine, wv.shape[1]), BF16),
        ((mine, width), BF16),
        ((half_rows, 2 * columns), BF16),
        ((half_rows, 2 * columns), BF16),
        ((down_rows, down_sum.shape[1]), BF16),
    ]
    return pl.pallas_call(
        functools.partial(finish_kernel, line, bits, streams, units),
        name="finish",
        grid=(steps,),
        in_specs=[
            pl.BlockSpec((2, half, lanes), lambda n: (at(n), 0, 0)),
            pl.BlockSpec((1, rows, q_width + LANES), lambda n: (at(n), 0, 0)),
            keep((rows, width)),
            keep((rows, width)),
            keep((rows, width)),
            keep((1, width)),
            pl.BlockSpec((width, q_width), lambda n: (0, at(n))),
            pl.BlockSpec((width, LANES), lambda n: (0, at(n))),
            pl.BlockSpec((width, LANES), lambda n: (0, at(n))),
            keep((1, LANES)),
            keep((1, LANES)),
            keep((rows, LANES)),
            keep((rows, LANES)),
            pl.BlockSpec((width, q_width), lambda n: (0, at(n))),
            keep((1, width)),
            keep(gate_sum.shape),
            keep(up_sum.shape),
            keep(down_sum.shape),
        ],
        out_specs=[keep(shape) for shape, unused in outs],
        out_shape=[jax.ShapeDtypeStruct(shape, kind) for shape, kind in outs],
        scratch_shapes=scratch,
        compiler_params=kernel_params(collective_id=5, has_side_effects=True),
    )(
        got,
        proj,
        hidden,
        tokens,
        mid,
        gain,
        wq,
        wk,
        wv,
        q_gain,
        k_gain,
        cosine,
        sine,
        w_out_parts,
        ffn_gain,
        gate_sum,
        up_sum,
        down_sum,
    )


def flip_pairs(count, bit):
    return [(i, i ^ bit) for i in range(count)]


def swap_core(block, blk_count):
    return lax.ppermute(block, "blk", flip_pairs(blk_count, 1))


def fast_local(
    dp_count,
    blk_count,
    tokens,
    doc_lengths,
    g_attn,
    w_query,
    w_key,
    w_value,
    q_gain,
    k_gain,
    w_out,
    g_ffn,
    w_gate,
    w_up,
    w_down,
    cotangent,
):
    row_count, tok_count, width = tokens.shape
    rows = row_count * tok_count
    chips = blk_count // 2
    size = tok_count * blk_count
    index = lax.axis_index("blk")
    core = index % 2
    bits = []
    bit = blk_count // 2
    while bit > 1:
        bits.append(bit)
        bit //= 2
    chip_dims = (dp_count,) + (2,) * len(bits)
    all_chips = dp_count * chips
    places = index * tok_count + jnp.arange(tok_count, dtype=jnp.int32)
    unused, positions = doc_layout(doc_lengths, places)
    cosine, sine = rope_angles(positions)
    cosine = jnp.tile(cosine.reshape(rows, -1), (1, 4))
    sine = sine.reshape(rows, -1)
    sine = jnp.concatenate([-sine, sine, -sine, sine], axis=1)
    q_gain2 = jnp.tile(q_gain, 2)[None]
    k_gain2 = jnp.tile(k_gain, 2)[None]
    all_places = jnp.arange(size, dtype=jnp.int32)
    row_lengths = lax.dynamic_slice_in_dim(doc_lengths, core, 1, axis=0)
    unused, all_positions = doc_layout(row_lengths, all_places)
    starts = all_places - all_positions[0]
    starts_two = jnp.broadcast_to(
        starts.reshape(blk_count, 1, tok_count), (blk_count, 2, tok_count)
    ).reshape(1, 2 * size)
    flat = tokens.reshape(rows, width)
    grad_own = cotangent.reshape(rows, width)
    grad_got = swap_core(grad_own, blk_count)

    hidden_in, proj, send = project(
        flat, g_attn[None], w_query, w_key, w_value, q_gain2, k_gain2, cosine, sine
    )
    qkv = swap_blocks(send, 0).reshape(size, -1)
    attended, logs = attend(qkv, starts[:, None], tok_count)
    heads = swap_blocks(attended, 1)
    output, mid, ffn_gain_grad, w_out_parts, grad_heads, acts, gate_sum, up_sum = middle_layer(
        dp_count,
        bits,
        flat,
        heads,
        w_out,
        g_ffn[None],
        grad_own,
        grad_got,
        w_gate,
        w_up,
        w_down,
    )
    qkv_grad, down_sum = back(
        dp_count,
        bits,
        qkv,
        logs,
        attended.reshape(size, -1),
        grad_heads.reshape(size, -1),
        starts_two,
        tok_count,
        grad_own,
        grad_got,
        acts,
    )
    got = swap_blocks(qkv_grad.reshape(blk_count, tok_count, -1), 3)
    input_grad, gains, *sums = finish(
        dp_count,
        bits,
        got,
        proj,
        hidden_in,
        flat,
        mid,
        g_attn[None],
        w_query,
        w_key,
        w_value,
        q_gain2,
        k_gain2,
        cosine,
        sine,
        w_out_parts,
        ffn_gain_grad,
        gate_sum,
        up_sum,
        down_sum,
    )
    grad_w_query, grad_w_key, grad_w_value, grad_w_out, grad_w_gate, grad_w_up, grad_w_down = [
        part.astype(F32) for part in sums
    ]
    lines = width // LANES
    gain_attn = gains[:lines].reshape(width)
    gain_ffn = gains[lines : 2 * lines].reshape(width)
    gain_query = gains[2 * lines, :HEAD_DIM] + gains[2 * lines, HEAD_DIM:]
    gain_key = gains[2 * lines + 1, :HEAD_DIM] + gains[2 * lines + 1, HEAD_DIM:]
    return (
        output.reshape(tokens.shape),
        input_grad.reshape(tokens.shape),
        gain_attn,
        grad_w_query,
        grad_w_key,
        grad_w_value,
        gain_query,
        gain_key,
        grad_w_out,
        gain_ffn,
        grad_w_gate,
        grad_w_up,
        grad_w_down,
    )


def fits(mesh):
    blk_count = mesh.shape["blk"]
    chips = blk_count // 2
    power = blk_count & (blk_count - 1) == 0
    return power and blk_count > 2 and (KV_HEADS * HEAD_DIM) == chips * LANES


def solution(mesh):
    if fits(mesh):
        body = functools.partial(fast_local, mesh.shape["dp"], mesh.shape["blk"])
    else:
        body = local
    return jax.shard_map(
        body,
        mesh=mesh,
        in_specs=(
            P("dp", "blk", None),
            P("dp", None),
            P(),
            P(),
            P(),
            P(),
            P(),
            P(),
            P(),
            P(),
            P(),
            P(),
            P(),
            P("dp", "blk", None),
        ),
        out_specs=(
            P("dp", "blk", None),
            P("dp", "blk", None),
            P(),
            P(("dp", "blk"), None),
            P(("dp", "blk"), None),
            P(("dp", "blk"), None),
            P(),
            P(),
            P(("dp", "blk"), None),
            P(),
            P(("dp", "blk"), None),
            P(("dp", "blk"), None),
            P(("dp", "blk"), None),
        ),
        check_vma=False,
    )
```

```python
import functools
import math

import jax
import jax.numpy as jnp
from jax import lax
from jax.experimental import pallas as pl
from jax.experimental.pallas import tpu as pltpu
from jax.sharding import PartitionSpec as P

HEADS = 16
KV_HEADS = 8
HEAD_DIM = 64


EPSILON = 1e-05
ROPE_BASE = 1000000.0
NEGATIVE = -1e30


def norm_rows(values, norm_gain):
    row_scale = lax.rsqrt(jnp.mean(values * values, axis=-1, keepdims=True) + EPSILON)
    normal = values * row_scale
    return (normal * norm_gain, normal, row_scale)


def norm_back(normal, row_scale, norm_gain, grad_out):
    pushed = grad_out * norm_gain
    inner = jnp.mean(pushed * normal, axis=-1, keepdims=True)
    grad_in = row_scale * (pushed - normal * inner)
    leading = tuple(range(grad_out.ndim - 1))
    return (grad_in, jnp.sum(grad_out * normal, axis=leading))


def doc_layout(lengths, places):
    ends = jnp.cumsum(lengths, axis=1)
    past = places[None, :, None] >= ends[:, None, :]
    docs = jnp.sum(past.astype(jnp.int32), axis=2)
    before = jnp.sum(jnp.where(past, lengths[:, None, :], 0), axis=2)
    return (docs, places[None, :] - before)


def rope_angles(positions):
    half = HEAD_DIM // 2
    freqs = ROPE_BASE ** (-jnp.arange(half, dtype=jnp.float32) / half)
    angles = positions.astype(jnp.float32)[..., None] * freqs
    return (jnp.cos(angles), jnp.sin(angles))


def rotate(values, cosine, sine):
    half = values.shape[-1] // 2
    first_half = values[..., :half]
    second_half = values[..., half:]
    cos_col = cosine[:, :, None, :]
    sin_col = sine[:, :, None, :]
    return jnp.concatenate(
        [
            first_half * cos_col - second_half * sin_col,
            second_half * cos_col + first_half * sin_col,
        ],
        axis=-1,
    )


def local(
    tokens,
    doc_lengths,
    g_attn,
    w_query,
    w_key,
    w_value,
    q_gain,
    k_gain,
    w_out,
    g_ffn,
    w_gate,
    w_up,
    w_down,
    cotangent,
):
    row_count, tok_count, width = tokens.shape
    grouping = HEADS // KV_HEADS
    flat_rows = row_count * tok_count
    kv_width = KV_HEADS * HEAD_DIM
    softmax_scale = HEAD_DIM ** (-0.5)
    places = lax.axis_index("blk") * tok_count + jnp.arange(tok_count, dtype=jnp.int32)
    query_docs, query_pos = doc_layout(doc_lengths, places)
    cosine, sine = rope_angles(query_pos)
    inputs = tokens.reshape(flat_rows, width).astype(jnp.float32)
    normed, normal_in, scale_in = norm_rows(inputs, g_attn)
    hidden_in = normed.astype(jnp.bfloat16)
    query_proj = jnp.dot(hidden_in, w_query, preferred_element_type=jnp.float32).reshape(
        row_count, tok_count, HEADS, HEAD_DIM
    )
    key_proj = jnp.dot(hidden_in, w_key, preferred_element_type=jnp.float32).reshape(
        row_count, tok_count, KV_HEADS, HEAD_DIM
    )
    value_b = (
        jnp.dot(hidden_in, w_value, preferred_element_type=jnp.float32)
        .astype(jnp.bfloat16)
        .reshape(row_count, tok_count, kv_width)
    )
    query_norm, query_normal, query_scale = norm_rows(query_proj, q_gain)
    key_norm, key_normal, key_scale = norm_rows(key_proj, k_gain)
    query_b = (
        rotate(query_norm, cosine, sine)
        .astype(jnp.bfloat16)
        .reshape(row_count, tok_count, KV_HEADS, grouping, HEAD_DIM)
    )
    key_b = (
        rotate(key_norm, cosine, sine).astype(jnp.bfloat16).reshape(row_count, tok_count, kv_width)
    )

    def piece_mask(size):
        key_places = jnp.arange(size, dtype=jnp.int32)
        key_docs, unused = doc_layout(doc_lengths, key_places)
        return (key_places[None, None, :] <= places[None, :, None]) & (
            key_docs[:, None, :] == query_docs[:, :, None]
        )

    def piece_scores(key_piece, allowed):
        key_heads = key_piece.reshape(row_count, key_piece.shape[1], KV_HEADS, HEAD_DIM)
        raw_scores = (
            jnp.einsum("rqkgd,rpkd->rkgqp", query_b, key_heads, preferred_element_type=jnp.float32)
            * softmax_scale
        )
        return (jnp.where(allowed[:, None, None], raw_scores, -jnp.inf), key_heads)

    stat_shape = (row_count, KV_HEADS, grouping, tok_count)
    key_piece = lax.all_gather(key_b, "blk", axis=1, tiled=True)
    value_piece = lax.all_gather(value_b, "blk", axis=1, tiled=True)
    allowed = piece_mask(key_piece.shape[1])
    running_max = jnp.full(stat_shape, NEGATIVE, jnp.float32)
    scores, key_heads = piece_scores(key_piece, allowed)
    new_max = jnp.maximum(running_max, jnp.max(scores, axis=-1))
    weights = jnp.exp(scores - new_max[..., None])
    value_heads = value_piece.reshape(row_count, value_piece.shape[1], KV_HEADS, HEAD_DIM)
    added = jnp.einsum(
        "rkgqp,rpkd->rkgqd",
        weights.astype(jnp.bfloat16),
        value_heads,
        preferred_element_type=jnp.float32,
    )
    running_sum = jnp.sum(weights, axis=-1)
    attended = added / running_sum[..., None]
    log_total = new_max + jnp.log(running_sum)
    attended_b = (
        jnp.transpose(attended, (0, 3, 1, 2, 4))
        .reshape(flat_rows, HEADS * HEAD_DIM)
        .astype(jnp.bfloat16)
    )
    middle = inputs + jnp.dot(attended_b, w_out, preferred_element_type=jnp.float32)
    normed_ffn, normal_ffn, scale_ffn = norm_rows(middle, g_ffn)
    hidden_ffn = normed_ffn.astype(jnp.bfloat16)
    gate = jnp.dot(hidden_ffn, w_gate, preferred_element_type=jnp.float32)
    up_proj = jnp.dot(hidden_ffn, w_up, preferred_element_type=jnp.float32)
    sigmoid_gate = jax.nn.sigmoid(gate)
    silu_gate = gate * sigmoid_gate
    hidden = (silu_gate * up_proj).astype(jnp.bfloat16)
    result = middle + jnp.dot(hidden, w_down, preferred_element_type=jnp.float32)
    output = result.astype(jnp.bfloat16).reshape(row_count, tok_count, width)
    grad_out = cotangent.reshape(flat_rows, width)
    grad_w_down = jnp.einsum("tf,td->fd", hidden, grad_out, preferred_element_type=jnp.float32)
    grad_hidden = jnp.einsum("td,fd->tf", grad_out, w_down, preferred_element_type=jnp.float32)
    grad_gate = (grad_hidden * up_proj * sigmoid_gate * (1.0 + gate * (1.0 - sigmoid_gate))).astype(
        jnp.bfloat16
    )
    grad_up = (grad_hidden * silu_gate).astype(jnp.bfloat16)
    grad_w_gate = jnp.einsum("td,tf->df", hidden_ffn, grad_gate, preferred_element_type=jnp.float32)
    grad_w_up = jnp.einsum("td,tf->df", hidden_ffn, grad_up, preferred_element_type=jnp.float32)
    grad_h2 = jnp.einsum(
        "tf,df->td", grad_gate, w_gate, preferred_element_type=jnp.float32
    ) + jnp.einsum("tf,df->td", grad_up, w_up, preferred_element_type=jnp.float32)
    grad_mid, grad_ffn_gain = norm_back(normal_ffn, scale_ffn, g_ffn, grad_h2)
    grad_mid = grad_out.astype(jnp.float32) + grad_mid
    grad_attn = grad_mid.astype(jnp.bfloat16)
    grad_w_out = jnp.einsum("tc,td->cd", attended_b, grad_attn, preferred_element_type=jnp.float32)
    grad_attended = jnp.einsum(
        "td,cd->tc", grad_attn, w_out, preferred_element_type=jnp.float32
    ).astype(jnp.bfloat16)
    grad_heads = grad_attended.reshape(row_count, tok_count, KV_HEADS, grouping, HEAD_DIM)
    deltas = jnp.einsum("rqkgd,rkgqd->rkgq", grad_heads.astype(jnp.float32), attended)
    key_piece = lax.all_gather(key_b, "blk", axis=1, tiled=True)
    value_piece = lax.all_gather(value_b, "blk", axis=1, tiled=True)
    size = key_piece.shape[1]
    allowed = piece_mask(size)
    scores, key_heads = piece_scores(key_piece, allowed)
    probs = jnp.exp(scores - log_total[..., None])
    value_heads = value_piece.reshape(row_count, size, KV_HEADS, HEAD_DIM)
    value_piece_grad = jnp.einsum(
        "rkgqp,rqkgd->rpkd",
        probs.astype(jnp.bfloat16),
        grad_heads,
        preferred_element_type=jnp.float32,
    )
    grad_probs = jnp.einsum(
        "rqkgd,rpkd->rkgqp", grad_heads, value_heads, preferred_element_type=jnp.float32
    )
    grad_scores = (probs * (grad_probs - deltas[..., None])).astype(jnp.bfloat16)
    grad_query = jnp.einsum(
        "rkgqp,rpkd->rkgqd", grad_scores, key_heads, preferred_element_type=jnp.float32
    )
    key_piece_grad = jnp.einsum(
        "rkgqp,rqkgd->rpkd", grad_scores, query_b, preferred_element_type=jnp.float32
    )
    grad_keys = key_piece_grad.reshape(row_count, size, kv_width)
    grad_values = value_piece_grad.reshape(row_count, size, kv_width)
    grad_query, grad_keys, grad_values = (grad_query, grad_keys, grad_values)
    key_grad_mine, value_grad_mine = (
        lax.psum_scatter(
            grad_keys.astype(jnp.bfloat16), "blk", scatter_dimension=1, tiled=True
        ).astype(jnp.float32),
        lax.psum_scatter(
            grad_values.astype(jnp.bfloat16), "blk", scatter_dimension=1, tiled=True
        ).astype(jnp.float32),
    )
    grad_q_rot = (jnp.transpose(grad_query, (0, 3, 1, 2, 4)) * softmax_scale).reshape(
        row_count, tok_count, HEADS, HEAD_DIM
    )
    grad_k_rot = (key_grad_mine * softmax_scale).reshape(row_count, tok_count, KV_HEADS, HEAD_DIM)
    grad_q_proj, grad_query_gain = norm_back(
        query_normal, query_scale, q_gain, rotate(grad_q_rot, cosine, -sine)
    )
    grad_k_proj, grad_key_gain = norm_back(
        key_normal, key_scale, k_gain, rotate(grad_k_rot, cosine, -sine)
    )
    grad_q_b = grad_q_proj.astype(jnp.bfloat16).reshape(flat_rows, HEADS * HEAD_DIM)
    grad_k_b = grad_k_proj.astype(jnp.bfloat16).reshape(flat_rows, kv_width)
    grad_v_b = value_grad_mine.astype(jnp.bfloat16).reshape(flat_rows, kv_width)
    grad_w_query = jnp.einsum("td,tc->dc", hidden_in, grad_q_b, preferred_element_type=jnp.float32)
    grad_w_key = jnp.einsum("td,tc->dc", hidden_in, grad_k_b, preferred_element_type=jnp.float32)
    grad_w_value = jnp.einsum("td,tc->dc", hidden_in, grad_v_b, preferred_element_type=jnp.float32)
    grad_h1 = jnp.einsum("tc,dc->td", grad_q_b, w_query, preferred_element_type=jnp.float32)
    grad_h1 = grad_h1 + jnp.einsum("tc,dc->td", grad_k_b, w_key, preferred_element_type=jnp.float32)
    grad_h1 = grad_h1 + jnp.einsum(
        "tc,dc->td", grad_v_b, w_value, preferred_element_type=jnp.float32
    )
    grad_base, grad_attn_gain = norm_back(normal_in, scale_in, g_attn, grad_h1)
    input_grad = (grad_mid + grad_base).astype(jnp.bfloat16).reshape(row_count, tok_count, width)
    gain_attn, gain_query, gain_key, gain_ffn = lax.psum(
        (grad_attn_gain, grad_query_gain, grad_key_gain, grad_ffn_gain), ("dp", "blk")
    )
    locals_all = (
        grad_w_query,
        grad_w_key,
        grad_w_value,
        grad_w_out,
        grad_w_gate,
        grad_w_up,
        grad_w_down,
    )
    shared = (
        lax.psum_scatter(locals_all[0], ("dp", "blk"), scatter_dimension=0, tiled=True),
        lax.psum_scatter(locals_all[1], ("dp", "blk"), scatter_dimension=0, tiled=True),
        lax.psum_scatter(locals_all[2], ("dp", "blk"), scatter_dimension=0, tiled=True),
        lax.psum_scatter(locals_all[3], ("dp", "blk"), scatter_dimension=0, tiled=True),
        lax.psum_scatter(locals_all[4], ("dp", "blk"), scatter_dimension=0, tiled=True),
        lax.psum_scatter(locals_all[5], ("dp", "blk"), scatter_dimension=0, tiled=True),
        lax.psum_scatter(locals_all[6], ("dp", "blk"), scatter_dimension=0, tiled=True),
    )
    return (
        output,
        input_grad,
        gain_attn,
        shared[0],
        shared[1],
        shared[2],
        gain_query,
        gain_key,
        shared[3],
        gain_ffn,
        shared[4],
        shared[5],
        shared[6],
    )


BF16 = jnp.bfloat16
F32 = jnp.float32
LANES = 128
FF_TILE = 256
LAG = 2
LAST_LAG = 1
ATTEND_PAIRS = 3
VMEM_BYTES = 60 * 1024 * 1024
LOG2_E = math.log2(math.e)
QUERY_SCALE = HEAD_DIM ** (-0.5) * LOG2_E
MASKED = -1e30


def nn_dot(left, right):
    return lax.dot_general(left, right, (((1,), (0,)), ((), ())), preferred_element_type=F32)


def nt_dot(left, right):
    return lax.dot_general(left, right, (((1,), (1,)), ((), ())), preferred_element_type=F32)


def tn_dot(left, right):
    return lax.dot_general(left, right, (((0,), (0,)), ((), ())), preferred_element_type=F32)


def kernel_params(**more):
    return pltpu.CompilerParams(vmem_limit_bytes=VMEM_BYTES, **more)


def whole_block(shape):
    return pl.BlockSpec(shape, lambda *ids: (0,) * len(shape))


def greet_blk(count):
    barrier = pltpu.get_barrier_semaphore()
    z, index = lax.axis_index("dp"), lax.axis_index("blk")
    for step in range(1, count):
        pl.semaphore_signal(
            barrier,
            inc=1,
            device_id=(z, lax.rem(index + step, count)),
            device_id_type=pl.DeviceIdType.MESH,
        )
    pl.semaphore_wait(barrier, count - 1)


def blk_copy(send, got, sent_sem, got_sem, target, source):
    return pltpu.make_async_remote_copy(
        src_ref=send.at[target],
        dst_ref=got.at[source],
        send_sem=sent_sem.at[target],
        recv_sem=got_sem.at[source],
        device_id=(lax.axis_index("dp"), target),
        device_id_type=pl.DeviceIdType.MESH,
    )


def blk_sems(count):
    return [pltpu.SemaphoreType.DMA((count,)), pltpu.SemaphoreType.DMA((count,))]


def head_means(values):
    rows = lax.broadcasted_iota(jnp.int32, (LANES, LANES), 0) // HEAD_DIM
    cols = lax.broadcasted_iota(jnp.int32, (LANES, LANES), 1) // HEAD_DIM
    spread = jnp.where(rows == cols, 1.0 / HEAD_DIM, 0.0).astype(BF16)
    high = values.astype(BF16)
    low = (values - high.astype(F32)).astype(BF16)
    return nn_dot(high, spread) + nn_dot(low, spread)


def half_partner(values):
    lane = lax.broadcasted_iota(jnp.int32, values.shape, 1)
    half = HEAD_DIM // 2
    ahead = pltpu.roll(values, LANES - half, 1)
    behind = pltpu.roll(values, half, 1)
    return jnp.where(lane % HEAD_DIM < half, ahead, behind)


def project_kernel(
    tokens_ref,
    gain_ref,
    wq_ref,
    wk_ref,
    wv_ref,
    q_gain_ref,
    k_gain_ref,
    cos_ref,
    sin_ref,
    hidden_ref,
    proj_ref,
    got_ref,
    send,
    got,
    sent_sem,
    got_sem,
):
    rows = tokens_ref.shape[0]
    n, chips = pl.program_id(0), pl.num_programs(0)
    count = send.shape[0]
    index = lax.axis_index("blk")
    p = lax.rem(index // 2 + 1 + n, chips)

    @pl.when(n == 0)
    def _():
        greet_blk(count)
        inputs = tokens_ref[...].astype(F32)
        scale = lax.rsqrt(jnp.mean(inputs * inputs, axis=-1, keepdims=True) + EPSILON)
        hidden_ref[...] = (inputs * scale * gain_ref[...]).astype(BF16)

    hidden = hidden_ref[...]
    half = rows // 2

    def put(block, lane):
        send[2 * p, :, lane : lane + LANES] = block[:half]
        send[2 * p + 1, :, lane : lane + LANES] = block[half:]

    queries = nn_dot(hidden, wq_ref[...])
    keys = nn_dot(hidden, wk_ref[...])
    values = nn_dot(hidden, wv_ref[...])
    q_width = queries.shape[1]
    blocks = [(queries[:, at : at + LANES], at, q_gain_ref, QUERY_SCALE) for at in range(0, q_width, LANES)]
    blocks.append((keys, q_width, k_gain_ref, 1.0))
    for block, lane, head_gain, factor in blocks:
        proj_ref[0, :, lane : lane + LANES] = block
        scale = lax.rsqrt(head_means(block * block) + EPSILON)
        normed = block * scale * head_gain[...]
        turned = normed * cos_ref[...] + half_partner(normed) * sin_ref[...]
        put((turned * factor).astype(BF16), lane)
    put(values.astype(BF16), q_width + LANES)
    for part in range(2):
        target = 2 * p + part

        @pl.when(target != index)
        def _():
            blk_copy(send, got, sent_sem, got_sem, target, index).start()

        @pl.when(target == index)
        def _():
            got[target] = send[target]

    @pl.when(n == chips - 1)
    def _():
        for step in range(1, count):
            other = lax.rem(index + step, count)
            blk_copy(send, got, sent_sem, got_sem, other, other).wait()
        got_ref[...] = got[...]


def project(tokens, gain, wq, wk, wv, q_gain, k_gain, cosine, sine):
    rows, width = tokens.shape
    chips = wk.shape[1] // LANES
    q_width = wq.shape[1] // chips
    block_width = q_width + 2 * LANES
    moved = (2 * chips, rows // 2, block_width)

    def at(n):
        return lax.rem(lax.axis_index("blk") // 2 + 1 + n, chips)

    return pl.pallas_call(
        project_kernel,
        name="project",
        grid=(chips,),
        in_specs=[
            whole_block((rows, width)),
            whole_block((1, width)),
            pl.BlockSpec((width, q_width), lambda n: (0, at(n))),
            pl.BlockSpec((width, LANES), lambda n: (0, at(n))),
            pl.BlockSpec((width, LANES), lambda n: (0, at(n))),
            whole_block((1, LANES)),
            whole_block((1, LANES)),
            whole_block((rows, LANES)),
            whole_block((rows, LANES)),
        ],
        out_specs=[
            whole_block((rows, width)),
            pl.BlockSpec((1, rows, q_width + LANES), lambda n: (at(n), 0, 0)),
            whole_block(moved),
        ],
        out_shape=[
            jax.ShapeDtypeStruct((rows, width), BF16),
            jax.ShapeDtypeStruct((chips, rows, q_width + LANES), F32),
            jax.ShapeDtypeStruct(moved, BF16),
        ],
        scratch_shapes=[pltpu.VMEM(moved, BF16), pltpu.VMEM(moved, BF16)] + blk_sems(2 * chips),
        compiler_params=kernel_params(collective_id=0, has_side_effects=True),
    )(tokens, gain, wq, wk, wv, q_gain, k_gain, cosine, sine)


def low_lanes(shape):
    return lax.broadcasted_iota(jnp.int32, shape, 1) < HEAD_DIM


def doubled(pair, group):
    turned = pltpu.roll(pair.astype(F32), HEAD_DIM, 1).astype(BF16)
    low = low_lanes(pair.shape)
    return jnp.where(low, pair, turned) if group == 0 else jnp.where(low, turned, pair)


def stacked_heads(pair):
    low = low_lanes(pair.shape)
    none = jnp.zeros_like(pair)
    return jnp.concatenate([jnp.where(low, pair, none), jnp.where(low, none, pair)], axis=0)


def in_three(column):
    lane = lax.broadcasted_iota(jnp.int32, (column.shape[0], LANES), 1)
    wide = jnp.broadcast_to(column, (column.shape[0], LANES))
    first = wide.astype(BF16).astype(F32)
    second = (wide - first).astype(BF16).astype(F32)
    third = wide - first - second
    return jnp.where(
        lane == 0, first, jnp.where(lane == 1, second, jnp.where(lane == 2, third, 0.0))
    ).astype(BF16)


def minus_three(rows):
    lane = lax.broadcasted_iota(jnp.int32, (rows, LANES), 1)
    return jnp.where(lane < 3, -1.0, 0.0).astype(BF16)


def attend_kernel(
    groups,
    block,
    qkv_ref,
    starts_ref,
    out_ref,
    logs_ref,
    heads_ref,
    keys,
    values,
    total,
    got,
    sent_sem,
    got_sem,
):
    size = qkv_ref.shape[0]
    blocks = size // block
    q_width = groups * LANES
    n = pl.program_id(0)
    index = lax.axis_index("blk")
    here = lax.rem(index + 1 + n, blocks)

    @pl.when(n == 0)
    def _():
        greet_blk(blocks)
        for g in range(groups):
            keys[g] = doubled(qkv_ref[:, q_width : q_width + LANES], g)
            values[g, :, :LANES] = doubled(qkv_ref[:, q_width + LANES : q_width + 2 * LANES], g)
            values[g, :, LANES:] = jnp.ones((size, LANES), BF16)

    at = pl.multiple_of(here * block, block)
    starts = jnp.concatenate([starts_ref[pl.ds(at, block), :]] * 2, axis=0)
    queries = [
        stacked_heads(qkv_ref[pl.ds(at, block), g * LANES : (g + 1) * LANES]) for g in range(groups)
    ]

    def step(key_at, width, diagonal):
        column = lax.broadcasted_iota(jnp.int32, (2 * block, width), 1)
        allowed = column >= starts - key_at
        if diagonal:
            row = lax.broadcasted_iota(jnp.int32, (2 * block, width), 0) % block
            allowed = allowed & (column <= row)
        for g in range(groups):
            scores = nt_dot(queries[g], keys[g, pl.ds(key_at, width), :])
            weights = jnp.exp2(jnp.where(allowed, scores, MASKED)).astype(BF16)
            part = nn_dot(weights, values[g, pl.ds(key_at, width), :])
            if diagonal:
                total[g] = part
            else:
                total[g] += part

    step(at, block, True)

    @pl.when(lax.rem(here, 2) == 1)
    def _():
        step(pl.multiple_of((here - 1) * block, block), block, False)

    def body(j, carry):
        step(pl.multiple_of(j * 2 * block, 2 * block), 2 * block, False)
        return carry

    lax.fori_loop(0, here // 2, body, 0)
    low = low_lanes((block, LANES))
    to = pl.multiple_of(here * 2 * block, 2 * block)
    for g in range(groups):
        sums = total[g, :, LANES:]
        mean = total[g, :, :LANES] / sums
        out_ref[here, :, g * LANES : (g + 1) * LANES] = jnp.where(low, mean[:block], mean[block:]).astype(BF16)
        logs_ref[g, pl.ds(to, 2 * block), :] = in_three(jnp.log2(sums[:, :1]))

    @pl.when(here != index)
    def _():
        blk_copy(out_ref, got, sent_sem, got_sem, here, index).start()

    @pl.when(n == blocks - 1)
    def _():
        got[index] = out_ref[index]
        for step in range(1, blocks):
            other = lax.rem(index + step, blocks)
            blk_copy(out_ref, got, sent_sem, got_sem, other, other).wait()
        heads_ref[...] = got[...]


def attend(qkv, starts, block):
    size, width = qkv.shape
    groups = (width - 2 * LANES) // LANES
    blocks = size // block
    heads = (blocks, block, groups * LANES)
    logs = (groups, 2 * size, LANES)

    def keep(shape):
        return pl.BlockSpec(shape, lambda n: (0,) * len(shape), pipeline_mode=pl.Buffered(1))

    return pl.pallas_call(
        functools.partial(attend_kernel, groups, block),
        name="attend",
        grid=(blocks,),
        in_specs=[keep((size, width)), keep((size, 1))],
        out_specs=[keep(heads), keep(logs), keep(heads)],
        out_shape=[jax.ShapeDtypeStruct(shape, BF16) for shape in (heads, logs, heads)],
        scratch_shapes=[
            pltpu.VMEM((groups, size, LANES), BF16),
            pltpu.VMEM((groups, size, 2 * LANES), BF16),
            pltpu.VMEM((groups, 2 * block, 2 * LANES), F32),
            pltpu.VMEM(heads, BF16),
        ]
        + blk_sems(blocks),
        compiler_params=kernel_params(collective_id=1, has_side_effects=True),
    )(qkv, starts)


def pair_of(bit):
    index = lax.axis_index("blk")
    mine = lax.rem(index // bit, 2)
    return mine, (lax.axis_index("dp"), index + bit * (1 - 2 * mine))


class Stream:
    def __init__(self, path, dims, block, line, lag, units, kind=BF16):
        self.path, self.block, self.line, self.lag, self.kind = path, block, line, lag, kind
        self.units = units
        self.got_slots = min(2 * lag, units)
        self.dims = [tuple(dims)]
        left = list(dims)
        names = [name for name, unused in dims]
        for stage in path:
            if isinstance(stage, tuple):
                if stage[1] == line - 1:
                    at = [n for n, unused in left].index("z")
                    left = left[:at] + left[at + 1 :]
            else:
                at = [n for n, unused in left].index(stage)
                left = left[:at] + left[at + 1 :]
            self.dims.append(tuple(left))
        assert not left and "z" in names

    def is_hop(self, k):
        return isinstance(self.path[k], tuple)

    def starts_work(self, k):
        return k == 0 or not self.is_hop(k) or self.path[k][1] == 1

    def shape(self, dims):
        return tuple(count for unused, count in dims) + self.block

    def slots(self, k):
        return min(((self.line - 1) if self.is_hop(k) else 1) * self.lag + 1, self.units)

    def steps(self):
        return self.units + self.lag * len(self.path) + 1

    def got_slot(self, u):
        return lax.rem(u, self.got_slots)

    def scratch(self):
        shapes = []
        for k in range(len(self.path)):
            if self.starts_work(k):
                shapes.append(pltpu.VMEM((self.slots(k),) + self.shape(self.dims[k]), self.kind))
            if self.is_hop(k):
                rest = tuple(d for d in self.dims[k] if d[0] != "z")
                shapes.append(pltpu.VMEM((self.got_slots, 2) + self.shape(rest), self.kind))
                shapes += [pltpu.SemaphoreType.DMA((self.got_slots, 2))] * 2
            else:
                shapes.append(pltpu.VMEM((self.got_slots,) + self.shape(self.dims[k + 1]), self.kind))
                shapes += [pltpu.SemaphoreType.DMA((self.got_slots,))] * 2
        return shapes

    def bind(self, refs, finish, first_z=None, begin=0):
        refs = list(refs)
        self.finish, self.begin = finish, begin
        self.first_z = 0 if first_z is None else first_z
        self.work, self.got, self.sent_sem, self.got_sem = [], [], [], []
        for k in range(len(self.path)):
            self.work.append(refs.pop(0) if self.starts_work(k) else self.work[-1])
            self.got.append(refs.pop(0))
            self.sent_sem.append(refs.pop(0))
            self.got_sem.append(refs.pop(0))
        self.source = self.work[0]

    def z_count(self, k):
        return dict(self.dims[k])["z"]

    def keeps(self, z, k):
        return (z >= self.first_z) & (z < self.first_z + self.z_count(k))

    def keeper(self, k):
        if "z" in [name for name, unused in self.dims[k]] or dict(self.dims[0])["z"] == self.line:
            return None
        z = lax.axis_index("dp")
        return (z >= self.first_z) & (z < self.first_z + dict(self.dims[0])["z"])

    def pair_copy(self, k, u):
        bit = self.path[k]
        mine, partner = pair_of(bit)
        at = [name for name, unused in self.dims[k]].index(bit)
        whole = (slice(None),) * at
        slot = self.got_slot(u)
        copy = pltpu.make_async_remote_copy(
            src_ref=self.work[k].at[(lax.rem(u, self.slots(k)),) + whole + (1 - mine,)],
            dst_ref=self.got[k].at[slot],
            send_sem=self.sent_sem[k].at[slot],
            recv_sem=self.got_sem[k].at[slot],
            device_id=partner,
            device_id_type=pl.DeviceIdType.MESH,
        )
        return copy, whole + (mine,)

    def hop_copy(self, k, u, way, block):
        z, index = lax.axis_index("dp"), lax.axis_index("blk")
        slot = self.got_slot(u)
        side = (1 - way) // 2
        return pltpu.make_async_remote_copy(
            src_ref=self.work[k].at[lax.rem(u, self.slots(k)), block],
            dst_ref=self.got[k].at[slot, side],
            send_sem=self.sent_sem[k].at[slot, side],
            recv_sem=self.got_sem[k].at[slot, side],
            device_id=(z + way, index),
            device_id_type=pl.DeviceIdType.MESH,
        )

    def hop_ends(self, k, way):
        z = lax.axis_index("dp")
        reach = way * (self.line - self.path[k][1])
        goes, comes = z + reach, z - way + reach
        sends = self.keeps(goes, k)
        takes = self.keeps(comes, k) & (z - way >= 0) & (z - way < self.line)
        return goes - self.first_z, sends, comes - self.first_z, takes

    def send(self, k, step):
        u = step - self.begin - self.lag * k - 1
        due = (u >= 0) & (u < self.units)
        if not self.is_hop(k):
            keeper = self.keeper(k)

            @pl.when(due if keeper is None else due & keeper)
            def _():
                self.pair_copy(k, u)[0].start()

            return
        for way in (1, -1):
            block, sends, unused, unused = self.hop_ends(k, way)

            @pl.when(due & sends)
            def _():
                self.hop_copy(k, u, way, block).start()

    def take(self, k, step):
        u = step - self.begin - self.lag * (k + 1) - 1
        due = (u >= 0) & (u < self.units)
        keeper = self.keeper(k + 1)
        last = k == len(self.path) - 1

        def pass_on(value):
            if last:
                self.finish(u, value)
            else:
                self.work[k + 1][lax.rem(u, self.slots(k + 1))] = value

        if not self.is_hop(k):
            keeper = self.keeper(k)

            @pl.when(due if keeper is None else due & keeper)
            def _():
                copy, mine = self.pair_copy(k, u)
                copy.wait()
                own = self.work[k][(lax.rem(u, self.slots(k)),) + mine]
                pass_on(own + self.got[k][self.got_slot(u)])

            return
        slot = lax.rem(u, self.slots(k))
        for way in (1, -1):
            out_block, sends, in_block, takes = self.hop_ends(k, way)

            @pl.when(due & sends)
            def _():
                self.hop_copy(k, u, way, out_block).wait_send()

            @pl.when(due & takes)
            def _():
                self.hop_copy(k, u, way, in_block).wait_recv()
                self.work[k][slot, in_block] += self.got[k][self.got_slot(u), (1 - way) // 2]

        if self.path[k][1] == self.line - 1:
            own = lax.axis_index("dp") - self.first_z

            @pl.when(due if keeper is None else due & keeper)
            def _():
                pass_on(self.work[k][slot, own])


def hops(line):
    return [("z", t) for t in range(1, line)]


def greet(bits, line):
    barrier = pltpu.get_barrier_semaphore()
    z, index = lax.axis_index("dp"), lax.axis_index("blk")
    for bit in bits:
        pl.semaphore_signal(barrier, inc=1, device_id=pair_of(bit)[1], device_id_type=pl.DeviceIdType.MESH)
    for way in (1, -1):

        @pl.when((z + way >= 0) & (z + way < line))
        def _():
            pl.semaphore_signal(
                barrier, inc=1, device_id=(z + way, index), device_id_type=pl.DeviceIdType.MESH
            )

    beside = jnp.minimum(z, 1) + jnp.minimum(line - 1 - z, 1)
    pl.semaphore_wait(barrier, len(bits) + beside)


def step_streams(streams, step, steps, line, ready):
    longest = max(len(stream.path) for stream in streams)
    z, index = lax.axis_index("dp"), lax.axis_index("blk")
    for k in range(longest):
        for stream in streams:
            if k < len(stream.path):
                stream.take(k, step)
    for way in (1, -1):
        there = (z + way >= 0) & (z + way < line)

        @pl.when(there & (step >= 0) & (step < steps - 1))
        def _():
            pl.semaphore_signal(
                ready.at[(1 - way) // 2],
                inc=1,
                device_id=(z + way, index),
                device_id_type=pl.DeviceIdType.MESH,
            )

        @pl.when(there & (step > 0))
        def _():
            pl.semaphore_wait(ready.at[(1 + way) // 2], 1)

    for k in range(longest):
        for stream in streams:
            if k < len(stream.path):
                stream.send(k, step)


def greet_all(blk_count, line):
    barrier = pltpu.get_barrier_semaphore()
    z, index = lax.axis_index("dp"), lax.axis_index("blk")
    for step in range(1, blk_count):
        pl.semaphore_signal(
            barrier,
            inc=1,
            device_id=(z, lax.rem(index + step, blk_count)),
            device_id_type=pl.DeviceIdType.MESH,
        )
    for way in (1, -1):

        @pl.when((z + way >= 0) & (z + way < line))
        def _():
            pl.semaphore_signal(
                barrier, inc=1, device_id=(z + way, index), device_id_type=pl.DeviceIdType.MESH
            )

    beside = jnp.minimum(z, 1) + jnp.minimum(line - 1 - z, 1)
    pl.semaphore_wait(barrier, blk_count - 1 + beside)


def middle_kernel(
    line,
    bits,
    streams,
    units,
    tokens_ref,
    heads_ref,
    w_out_ref,
    gain_ref,
    dy_own_ref,
    dy_got_ref,
    w_gate_ref,
    w_up_ref,
    w_down_ref,
    output_ref,
    mid_ref,
    gain_grad_ref,
    w_grad_ref,
    grad_heads_ref,
    acts_ref,
    gate_out_ref,
    up_out_ref,
    hidden,
    flipped,
    out_sum,
    back_sum,
    gate_grads,
    up_grads,
    part_send,
    part_got,
    low_grad,
    do_send,
    do_got,
    hidden_sem,
    part_sent_sem,
    part_got_sem,
    do_sent_sem,
    do_got_sem,
    ready,
    *refs,
):
    n = pl.program_id(0)
    steps = pl.num_programs(0)
    z, index = lax.axis_index("dp"), lax.axis_index("blk")
    sibling = pair_of(1)[1]
    own_rows, width = tokens_ref.shape
    rows = 2 * own_rows
    blk_count, tok_count, head_lanes = heads_ref.shape
    chips = blk_count // 2
    chunk = 256
    gate_stream, up_stream, both_stream = streams
    gate_rows = gate_stream.block[0]
    own, other = pl.ds(0, own_rows), pl.ds(own_rows, own_rows)

    def finish_gate(u, value):
        gate_out_ref[:gate_rows, pl.ds(pl.multiple_of(u * FF_TILE, FF_TILE), FF_TILE)] = value

    def finish_up(u, value):
        up_out_ref[:gate_rows, pl.ds(pl.multiple_of(u * FF_TILE, FF_TILE), FF_TILE)] = value

    def finish_both(u, value):
        here = pl.ds(pl.multiple_of(u * FF_TILE, FF_TILE), FF_TILE)
        gate_out_ref[gate_rows:, here] = value[:, :FF_TILE]
        up_out_ref[gate_rows:, here] = value[:, FF_TILE:]

    at = 0
    for stream, finish in zip(streams, (finish_gate, finish_up, finish_both)):
        count = len(stream.scratch())
        stream.bind(refs[at : at + count], finish)
        at += count

    def hidden_copy():
        return pltpu.make_async_remote_copy(
            src_ref=hidden.at[own],
            dst_ref=hidden.at[other],
            send_sem=hidden_sem.at[0],
            recv_sem=hidden_sem.at[1],
            device_id=sibling,
            device_id_type=pl.DeviceIdType.MESH,
        )

    def part_copy(i):
        return pltpu.make_async_remote_copy(
            src_ref=part_send.at[i],
            dst_ref=part_got.at[i],
            send_sem=part_sent_sem.at[i],
            recv_sem=part_got_sem.at[i],
            device_id=sibling,
            device_id_type=pl.DeviceIdType.MESH,
        )

    def do_copy(target, source):
        return pltpu.make_async_remote_copy(
            src_ref=do_send.at[target],
            dst_ref=do_got.at[source],
            send_sem=do_sent_sem.at[target],
            recv_sem=do_got_sem.at[source],
            device_id=(z, target),
            device_id_type=pl.DeviceIdType.MESH,
        )

    def flip(start):
        for r in range(start, start + own_rows, chunk):
            for c in range(0, width, chunk):
                flipped[c : c + chunk, r : r + chunk] = hidden[r : r + chunk, c : c + chunk].T

    @pl.when(n == 0)
    def _():
        greet_all(blk_count, line)
        total = tokens_ref[...].astype(F32)
        for p in range(chips):
            block = jnp.concatenate([heads_ref[2 * p], heads_ref[2 * p + 1]], axis=0)
            total = total + nn_dot(block, w_out_ref[p * head_lanes : (p + 1) * head_lanes, :])
        mid_ref[...] = total
        scale = lax.rsqrt(jnp.mean(total * total, axis=-1, keepdims=True) + EPSILON)
        hidden[own] = (total * scale * gain_ref[...]).astype(BF16)
        hidden_copy().start()
        out_sum[...] = jnp.zeros_like(out_sum)
        back_sum[...] = jnp.zeros_like(back_sum)
        flip(0)

    @pl.when(n == 1)
    def _():
        hidden_copy().wait()
        flip(own_rows)

    step_streams(streams, n - 1, steps - 1, line, ready)

    @pl.when((n >= 1) & (n <= units))
    def _():
        for m in range(rows // chunk):
            part = slice(m * chunk, (m + 1) * chunk)
            gate = nn_dot(hidden[part, :], w_gate_ref[...])
            up = nn_dot(hidden[part, :], w_up_ref[...])
            at = m * chunk % own_rows
            dy_ref = dy_own_ref if m * chunk < own_rows else dy_got_ref
            pushed = nt_dot(dy_ref[at : at + chunk, :], w_down_ref[...])
            opened = jax.nn.sigmoid(gate)
            silu = gate * opened
            act = (silu * up).astype(BF16)
            gate_grad = (pushed * up * opened * (1.0 + gate * (1.0 - opened))).astype(BF16)
            up_grad = (pushed * silu).astype(BF16)
            acts_ref[:, part] = act.T
            gate_grads[part, :] = gate_grad
            up_grads[part, :] = up_grad
            out_sum[part, :] += nn_dot(act, w_down_ref[...])
            back_sum[part, :] += nt_dot(gate_grad, w_gate_ref[...]) + nt_dot(up_grad, w_up_ref[...])
        u = n - 1
        slot, long_slot = lax.rem(u, gate_stream.slots(0)), lax.rem(u, both_stream.slots(0))
        each = width // line
        shape = gate_stream.shape(gate_stream.dims[0])[1:-2] + (-1, FF_TILE)
        for m in range(line):
            part = slice(m * each, (m + 1) * each)
            gate_part = nn_dot(flipped[part, :], gate_grads[...]).astype(BF16)
            up_part = nn_dot(flipped[part, :], up_grads[...]).astype(BF16)
            gate_part, up_part = gate_part.reshape(shape), up_part.reshape(shape)
            gate_stream.source[slot, m] = gate_part[..., :gate_rows, :]
            up_stream.source[slot, m] = up_part[..., :gate_rows, :]
            both_stream.source[long_slot, m, ..., :FF_TILE] = gate_part[..., gate_rows:, :]
            both_stream.source[long_slot, m, ..., FF_TILE:] = up_part[..., gate_rows:, :]

    @pl.when(n == units)
    def _():
        part_send[0] = back_sum[other].astype(BF16)
        part_copy(0).start()
        part_send[1] = out_sum[other].astype(BF16)
        part_copy(1).start()

    @pl.when(n == units + 1)
    def _():
        part_copy(0).wait()
        values = mid_ref[...]
        scale = lax.rsqrt(jnp.mean(values * values, axis=-1, keepdims=True) + EPSILON)
        normal = values * scale
        back = back_sum[own] + part_got[0].astype(F32)
        gain_grad_ref[...] = jnp.sum(back * normal, axis=0, keepdims=True)
        pushed = back * gain_ref[...]
        inner = jnp.mean(pushed * normal, axis=-1, keepdims=True)
        mid = dy_own_ref[...].astype(F32) + scale * (pushed - normal * inner)
        part_copy(1).wait()
        mid_ref[...] = mid
        low_grad[...] = mid.astype(BF16)
        output_ref[...] = (values + (out_sum[own] + part_got[1].astype(F32))).astype(BF16)

    @pl.when((n > units + 1) & (n <= units + 1 + chips))
    def _():
        p = n - units - 2
        grad = low_grad[...]
        lanes = pl.ds(pl.multiple_of(p * head_lanes, head_lanes), head_lanes)
        send = nt_dot(grad, w_out_ref[lanes, :]).astype(BF16)
        for half in range(2):
            target = 2 * p + half
            do_send[target] = send[half * tok_count : (half + 1) * tok_count]

            @pl.when(target != index)
            def _():
                do_copy(target, index).start()

            @pl.when(target == index)
            def _():
                do_got[target] = send[half * tok_count : (half + 1) * tok_count]

        heads = jnp.concatenate([heads_ref[2 * p], heads_ref[2 * p + 1]], axis=0)
        w_grad_ref[lanes, :] = tn_dot(heads, grad).astype(BF16)

    @pl.when(n == steps - 1)
    def _():
        for other_index in range(blk_count):

            @pl.when(other_index != index)
            def _():
                do_copy(other_index, other_index).wait()

        grad_heads_ref[...] = do_got[...]


def column_streams(line, bits, each, units):
    late = each // 4
    dims = [("z", line)] + [(bit, 2) for bit in bits]
    return [
        Stream(bits[::-1] + hops(line), dims, (each - late, FF_TILE), line, LAG, units),
        Stream(bits + hops(line), dims, (each - late, FF_TILE), line, LAG, units),
        Stream(hops(line) + bits, dims, (late, 2 * FF_TILE), line, LAG, units),
    ]


def middle_layer(line, bits, tokens, heads, w_out, gain, dy_own, dy_got, w_gate, w_up, w_down):
    own_rows, width = tokens.shape
    rows = 2 * own_rows
    blk_count, tok_count, head_lanes = heads.shape
    units = w_gate.shape[1] // 2 // FF_TILE
    chips = line * 2 ** len(bits)
    each = width // chips
    streams = column_streams(line, bits, each, units)
    steps = max([1 + stream.steps() for stream in streams] + [units + 3 + blk_count // 2])

    def keep(shape):
        return pl.BlockSpec(shape, lambda n: (0,) * len(shape), pipeline_mode=pl.Buffered(1))

    def tile(n):
        return jnp.clip(n - 1, 0, units - 1)

    def mine(n):
        return lax.rem(lax.axis_index("blk"), 2) * units + tile(n)

    scratch = [
        pltpu.VMEM((rows, width), BF16),
        pltpu.VMEM((width, rows), BF16),
        pltpu.VMEM((rows, width), F32),
        pltpu.VMEM((rows, width), F32),
        pltpu.VMEM((rows, FF_TILE), BF16),
        pltpu.VMEM((rows, FF_TILE), BF16),
        pltpu.VMEM((2, own_rows, width), BF16),
        pltpu.VMEM((2, own_rows, width), BF16),
        pltpu.VMEM((own_rows, width), BF16),
        pltpu.VMEM(heads.shape, BF16),
        pltpu.VMEM(heads.shape, BF16),
        pltpu.SemaphoreType.DMA((2,)),
        pltpu.SemaphoreType.DMA((2,)),
        pltpu.SemaphoreType.DMA((2,)),
        pltpu.SemaphoreType.DMA((blk_count,)),
        pltpu.SemaphoreType.DMA((blk_count,)),
        pltpu.SemaphoreType.REGULAR((2,)),
    ]
    for stream in streams:
        scratch += stream.scratch()
    outs = [
        ((own_rows, width), BF16),
        ((own_rows, width), F32),
        ((1, width), F32),
        (w_out.shape, BF16),
        (heads.shape, BF16),
        ((units * FF_TILE, rows), BF16),
        ((each, units * FF_TILE), BF16),
        ((each, units * FF_TILE), BF16),
    ]
    out_specs = [keep(shape) for shape, unused in outs]
    out_specs[5] = pl.BlockSpec((FF_TILE, rows), lambda n: (tile(n), 0))
    return pl.pallas_call(
        functools.partial(middle_kernel, line, bits, streams, units),
        name="middle",
        grid=(steps,),
        in_specs=[
            keep(tokens.shape),
            keep(heads.shape),
            keep(w_out.shape),
            keep(gain.shape),
            keep(dy_own.shape),
            keep(dy_got.shape),
            pl.BlockSpec((width, FF_TILE), lambda n: (0, mine(n))),
            pl.BlockSpec((width, FF_TILE), lambda n: (0, mine(n))),
            pl.BlockSpec((FF_TILE, width), lambda n: (mine(n), 0)),
        ],
        out_specs=out_specs,
        out_shape=[jax.ShapeDtypeStruct(shape, kind) for shape, kind in outs],
        scratch_shapes=scratch,
        compiler_params=kernel_params(collective_id=6, has_side_effects=True),
    )(tokens, heads, w_out, gain, dy_own, dy_got, w_gate, w_up, w_down)


def back_kernel(
    groups,
    block,
    line,
    bits,
    streams,
    units,
    qkv_ref,
    logs_ref,
    out_ref,
    grad_ref,
    starts_ref,
    dy_own_ref,
    dy_got_ref,
    acts_ref,
    w_out_parts_ref,
    moved_ref,
    down_out_ref,
    w_out_ref,
    queries,
    keys,
    values,
    grads,
    query_grad,
    pair_grad,
    result,
    moved,
    sent_sem,
    got_sem,
    ready,
    *refs,
):
    size = qkv_ref.shape[0]
    blocks = size // block
    q_width = groups * LANES
    n = pl.program_id(0)
    index = lax.axis_index("blk")
    core = lax.rem(index, 2)

    def move(target, source):
        return pltpu.make_async_remote_copy(
            src_ref=result.at[target],
            dst_ref=moved.at[source],
            send_sem=sent_sem.at[target],
            recv_sem=got_sem.at[source],
            device_id=(lax.axis_index("dp"), target),
            device_id_type=pl.DeviceIdType.MESH,
        )

    low_half = streams[0].block[1]
    mid_half = low_half + streams[1].block[1]

    def finish_down(lanes):
        def put(u, value):
            rows = value.shape[0]
            down_out_ref[pl.ds(pl.multiple_of(u * rows, rows), rows), lanes] = value

        return put

    def finish_w_out(u, value):
        w_out_ref[:, pl.ds(pl.multiple_of(u * LANES, LANES), LANES)] = value

    at = 0
    columns = w_out_ref.shape[1] // LANES
    first_z = core * (line // 2)
    for stream, finish, first, begin in (
        (streams[0], finish_down(slice(0, low_half)), first_z, 0),
        (streams[1], finish_down(slice(low_half, mid_half)), first_z, 0),
        (streams[2], finish_down(slice(mid_half, None)), first_z, 0),
        (streams[3], finish_w_out, None, 0),
    ):
        size_of = len(stream.scratch())
        stream.bind(refs[at : at + size_of], finish, first, begin)
        at += size_of

    @pl.when(n == 0)
    def _():
        greet_all(blocks, line)
        down_out_ref[...] = jnp.zeros_like(down_out_ref)

    step_streams(streams, n, pl.num_programs(0), line, ready)

    @pl.when(n == 1)
    def _():
        query_grad[...] = jnp.zeros_like(query_grad)
        pair_grad[...] = jnp.zeros_like(pair_grad)
        for g in range(groups):
            lanes = slice(g * LANES, (g + 1) * LANES)
            keys[g, :, :LANES] = doubled(qkv_ref[:, q_width : q_width + LANES], g)
            keys[g, :, LANES:] = minus_three(size)
            values[g, :, :LANES] = doubled(qkv_ref[:, q_width + LANES : q_width + 2 * LANES], g)
            values[g, :, LANES:] = minus_three(size)

            def fill(i, carry):
                at = pl.multiple_of(i * block, block)
                to = pl.multiple_of(i * 2 * block, 2 * block)
                queries[g, pl.ds(to, 2 * block), :LANES] = stacked_heads(qkv_ref[pl.ds(at, block), lanes])
                queries[g, pl.ds(to, 2 * block), LANES:] = logs_ref[g, pl.ds(to, 2 * block), :]
                grad = stacked_heads(grad_ref[pl.ds(at, block), lanes])
                mean = stacked_heads(out_ref[pl.ds(at, block), lanes])
                delta = jnp.sum(grad.astype(F32) * mean.astype(F32), axis=1, keepdims=True)
                grads[g, pl.ds(to, 2 * block), :LANES] = grad
                grads[g, pl.ds(to, 2 * block), LANES:] = in_three(delta)
                return carry

            lax.fori_loop(0, blocks, fill, 0)

    @pl.when(n < units)
    def _():
        acts = acts_ref[...].reshape(-1, acts_ref.shape[-1])
        rows = dy_own_ref.shape[0]
        made = nn_dot(acts[:, :rows], dy_own_ref[...]) + nn_dot(acts[:, rows:], dy_got_ref[...])
        made = made.astype(BF16)
        parts = (made[:, :low_half], made[:, low_half:mid_half], made[:, mid_half:])
        for stream, part in zip(streams[:3], parts):
            shape = stream.shape(stream.dims[0])
            stream.source[lax.rem(n, stream.slots(0))] = part.reshape(shape)

    @pl.when(n < columns)
    def _():
        stream = streams[3]
        part = w_out_parts_ref[...].reshape(stream.shape(stream.dims[0]))
        stream.source[lax.rem(n, stream.slots(0))] = part

    row = lax.broadcasted_iota(jnp.int32, (block, 2 * block), 0)
    column = lax.broadcasted_iota(jnp.int32, (block, 2 * block), 1) % block

    pairs = (blocks + 1) * (blocks // 2)
    each = ATTEND_PAIRS
    rounds = pairs // each

    @pl.when((n >= 1) & (n <= rounds))
    def _():
        def pair(at, carry):
            place = (n - 1) * each + at
            turn = place // (blocks // 2)
            m = lax.rem(place, blocks // 2)
            late = (turn + m) // blocks
            j = m + late * (blocks - 1 - 2 * m)
            i = (1 - late) * (m + turn) + late * (turn - 1)
            key_at = pl.multiple_of(j * block, block)
            at = pl.multiple_of(i * 2 * block, 2 * block)
            key_rows = pl.ds(key_at, block)
            stack = pl.ds(at, 2 * block)
            allowed = (row >= starts_ref[:, stack] - key_at) & (row - column <= (i - j) * block)
            for g in range(groups):
                query = queries[g, stack, :]
                grad = grads[g, stack, :]
                key = keys[g, key_rows, :]
                scores = nt_dot(key, query)
                probs = jnp.exp2(jnp.where(allowed, scores, MASKED))
                pushed = (probs * nt_dot(values[g, key_rows, :], grad)).astype(BF16)
                pair_grad[g, key_rows, LANES:] += nn_dot(probs.astype(BF16), grad[:, :LANES])
                pair_grad[g, key_rows, :LANES] += nn_dot(pushed, query[:, :LANES])
                query_grad[g, stack, :] += tn_dot(pushed, key[:, :LANES])
            return carry

        lax.fori_loop(0, each, pair, 0, unroll=True)

    @pl.when(n == rounds + 1)
    def _():
        low = low_lanes((block, LANES))

        def finish(i, carry):
            at = pl.multiple_of(i * block, block)
            to = pl.multiple_of(i * 2 * block, 2 * block)
            here = pl.ds(at, block)
            for g in range(groups):
                first = query_grad[g, pl.ds(to, block), :]
                second = query_grad[g, pl.ds(to + block, block), :]
                joined = jnp.where(low, first, second) * HEAD_DIM ** (-0.5)
                result[i, :, g * LANES : (g + 1) * LANES] = joined.astype(BF16)
            for part in range(2):
                sums = []
                for g in range(groups):
                    both = pair_grad[g, here, part * LANES : (part + 1) * LANES]
                    sums.append(both + pltpu.roll(both, HEAD_DIM, 1))
                joined = jnp.where(low, sums[0], sums[1])
                if part == 0:
                    joined = joined * (1.0 / LOG2_E)
                lane = q_width + part * LANES
                result[i, :, lane : lane + LANES] = joined.astype(BF16)
            return carry

        lax.fori_loop(0, blocks, finish, 0)
        for step in range(blocks - 1, 0, -1):
            move(lax.rem(index + step, blocks), index).start()
        moved[index] = result[index]

    @pl.when(n == pl.num_programs(0) - 1)
    def _():
        for step in range(1, blocks):
            other = lax.rem(index + step, blocks)
            move(other, other).wait()
        moved_ref[...] = moved[...]


def back(line, bits, qkv, logs, out, grad, starts, block, dy_own, dy_got, acts, w_out_parts):
    size, width = qkv.shape
    groups = (width - 2 * LANES) // LANES
    model = dy_own.shape[1]
    rows = acts.shape[1]
    units = acts.shape[0] // FF_TILE
    chips = line * 2 ** len(bits)
    down_rows = acts.shape[0] // (chips // 2)
    down_each = down_rows // units
    dims = [("z", line // 2)] + [(bit, 2) for bit in bits]
    quarter = model // 4
    w_rows = w_out_parts.shape[0] // chips // 2
    columns = w_out_parts.shape[1] // LANES
    streams = [
        Stream(hops(line) + bits[::-1], dims, (down_each, quarter), line, LAG, units),
        Stream(bits + hops(line), dims, (down_each, quarter * 3 // 2), line, LAG, units),
        Stream(bits[::-1] + hops(line), dims, (down_each, quarter * 3 // 2), line, LAG, units),
        Stream(
            [1] + bits[::-1] + hops(line),
            [("z", line)] + [(bit, 2) for bit in bits] + [(1, 2)],
            (w_rows, LANES),
            line,
            LAG,
            columns,
        ),
    ]
    steps = max(
        [stream.steps() for stream in streams]
        + [(size // block + 1) * (size // block // 2) // ATTEND_PAIRS + 3]
    )

    def keep(shape):
        return pl.BlockSpec(shape, lambda n: (0,) * len(shape), pipeline_mode=pl.Buffered(1))

    acts = acts.reshape(chips // 2, down_rows, rows)
    scratch = [
        pltpu.VMEM((groups, 2 * size, 2 * LANES), BF16),
        pltpu.VMEM((groups, size, 2 * LANES), BF16),
        pltpu.VMEM((groups, size, 2 * LANES), BF16),
        pltpu.VMEM((groups, 2 * size, 2 * LANES), BF16),
        pltpu.VMEM((groups, 2 * size, LANES), F32),
        pltpu.VMEM((groups, size, 2 * LANES), F32),
        pltpu.VMEM((size // block, block, width), BF16),
        pltpu.VMEM((size // block, block, width), BF16),
        pltpu.SemaphoreType.DMA((size // block,)),
        pltpu.SemaphoreType.DMA((size // block,)),
        pltpu.SemaphoreType.REGULAR((2,)),
    ]
    for stream in streams:
        scratch += stream.scratch()

    outs = [
        (size // block, block, width),
        (down_rows, model),
        (w_rows, w_out_parts.shape[1]),
    ]
    return pl.pallas_call(
        functools.partial(back_kernel, groups, block, line, bits, streams, units),
        name="back",
        grid=(steps,),
        in_specs=[
            keep(qkv.shape),
            keep(logs.shape),
            keep(out.shape),
            keep(grad.shape),
            keep(starts.shape),
            keep(dy_own.shape),
            keep(dy_got.shape),
            pl.BlockSpec(
                (chips // 2, down_each, rows), lambda n: (0, jnp.minimum(n, units - 1), 0)
            ),
            pl.BlockSpec((w_out_parts.shape[0], LANES), lambda n: (0, jnp.minimum(n, columns - 1))),
        ],
        out_specs=[keep(shape) for shape in outs],
        out_shape=[jax.ShapeDtypeStruct(shape, BF16) for shape in outs],
        scratch_shapes=scratch,
        compiler_params=kernel_params(collective_id=4, has_side_effects=True),
    )(qkv, logs, out, grad, starts, dy_own, dy_got, acts, w_out_parts)


def sum_gains(rounds, n, first, gains, gains_got, sent_sem, got_sem):
    for r, partner in enumerate(rounds):

        def copy():
            return pltpu.make_async_remote_copy(
                src_ref=gains.at[r],
                dst_ref=gains_got.at[r],
                send_sem=sent_sem.at[r],
                recv_sem=got_sem.at[r],
                device_id=partner,
                device_id_type=pl.DeviceIdType.MESH,
            )

        @pl.when(n == first + r + 1)
        def _():
            copy().wait()
            gains[r + 1] = gains[r] + gains_got[r]

    for r, partner in enumerate(rounds):

        @pl.when(n == first + r)
        def _():
            pltpu.make_async_remote_copy(
                src_ref=gains.at[r],
                dst_ref=gains_got.at[r],
                send_sem=sent_sem.at[r],
                recv_sem=got_sem.at[r],
                device_id=partner,
                device_id_type=pl.DeviceIdType.MESH,
            ).start()


def finish_kernel(
    line,
    bits,
    streams,
    units,
    got_ref,
    proj_ref,
    hidden_ref,
    tokens_ref,
    mid_ref,
    gain_ref,
    wq_ref,
    wk_ref,
    wv_ref,
    q_gain_ref,
    k_gain_ref,
    cos_ref,
    sin_ref,
    ffn_gain_ref,
    gate_ref,
    up_ref,
    down_ref,
    input_ref,
    gains_ref,
    gq_ref,
    gk_ref,
    gv_ref,
    gate_out_ref,
    up_out_ref,
    down_out_ref,
    total,
    gains,
    gains_got,
    gains_sent_sem,
    gains_got_sem,
    half_got,
    down_got,
    half_sent_sem,
    half_got_sem,
    ready,
    *refs,
):
    n = pl.program_id(0)
    z, index = lax.axis_index("dp"), lax.axis_index("blk")
    core, sibling = pair_of(1)
    steps = pl.num_programs(0)
    query_stream, pair_stream = streams
    q_width = wq_ref.shape[1]

    def finish_query(u, value):
        gq_ref[:, pl.ds(pl.multiple_of(u * q_width, q_width), q_width)] = value

    def finish_pair(u, value):
        here = pl.ds(pl.multiple_of(u * LANES, LANES), LANES)
        gk_ref[:, here] = value[:, :LANES]
        gv_ref[:, here] = value[:, LANES:]

    at = 0
    for stream, finish in ((query_stream, finish_query), (pair_stream, finish_pair)):
        count = len(stream.scratch())
        stream.bind(refs[at : at + count], finish)
        at += count

    rounds = [pair_of(bit)[1] for bit in (1,) + tuple(bits)]
    reach = 1
    while reach < line:
        rounds.append((z + reach * (1 - 2 * lax.rem(z // reach, 2)), index))
        reach *= 2

    rows = gate_ref.shape[0] // 2
    columns = gate_ref.shape[1]
    down_rows = down_ref.shape[0] // 2
    give = pl.ds(pl.multiple_of((1 - core) * rows, rows), rows)
    keep = pl.ds(pl.multiple_of(core * rows, rows), rows)
    down_give = pl.ds(pl.multiple_of((1 - core) * down_rows, down_rows), down_rows)
    down_keep = pl.ds(pl.multiple_of(core * down_rows, down_rows), down_rows)

    def half_copies():
        sources = (gate_ref.at[give, :], up_ref.at[give, :], down_ref.at[down_give, :])
        targets = (half_got.at[0], half_got.at[1], down_got)
        return [
            pltpu.make_async_remote_copy(
                src_ref=source,
                dst_ref=target,
                send_sem=half_sent_sem.at[i],
                recv_sem=half_got_sem.at[i],
                device_id=sibling,
                device_id_type=pl.DeviceIdType.MESH,
            )
            for i, (source, target) in enumerate(zip(sources, targets))
        ]

    @pl.when(n == 0)
    def _():
        barrier = pltpu.get_barrier_semaphore()
        for peer in rounds:
            pl.semaphore_signal(barrier, inc=1, device_id=peer, device_id_type=pl.DeviceIdType.MESH)
        for way in (1, -1):

            @pl.when((z + way >= 0) & (z + way < line))
            def _():
                pl.semaphore_signal(
                    barrier, inc=1, device_id=(z + way, index), device_id_type=pl.DeviceIdType.MESH
                )

        beside = jnp.minimum(z, 1) + jnp.minimum(line - 1 - z, 1)
        pl.semaphore_wait(barrier, len(rounds) + beside)
        for copy in half_copies():
            copy.start()
        total[...] = jnp.zeros_like(total)
        gains[0] = jnp.zeros_like(gains[0])

    @pl.when(n == units)
    def _():
        for copy in half_copies():
            copy.wait()
        own = pl.ds(pl.multiple_of(core * columns, LANES), columns)
        other = pl.ds(pl.multiple_of((1 - core) * columns, LANES), columns)
        gate_out_ref[:, own] = gate_ref[keep, :]
        gate_out_ref[:, other] = half_got[0]
        up_out_ref[:, own] = up_ref[keep, :]
        up_out_ref[:, other] = half_got[1]
        holder = z // (line // 2)

        @pl.when(holder == core)
        def _():
            down_out_ref[...] = down_ref[down_keep, :]

        @pl.when(holder != core)
        def _():
            down_out_ref[...] = down_got[...]

    step_streams(streams, n, steps, line, ready)
    sum_gains(rounds, n, units, gains, gains_got, gains_sent_sem, gains_got_sem)

    @pl.when(n == steps - 1)
    def _():
        gains_ref[...] = gains[len(rounds)]

    @pl.when(n < units)
    def _():
        hidden = hidden_ref[...]

        def back(lane, head_gain, place):
            got = jnp.concatenate(
                [got_ref[0, :, lane : lane + LANES], got_ref[1, :, lane : lane + LANES]], axis=0
            ).astype(F32)
            turned = got * cos_ref[...] - half_partner(got) * sin_ref[...]
            block = proj_ref[0, :, lane : lane + LANES]
            scale = lax.rsqrt(head_means(block * block) + EPSILON)
            normal = block * scale
            gains[0, place : place + 1, :] += jnp.sum(turned * normal, axis=0, keepdims=True)
            pushed = turned * head_gain[...]
            inner = head_means(pushed * normal)
            return (scale * (pushed - normal * inner)).astype(BF16)

        width = tokens_ref.shape[1]
        lines = width // LANES
        query = jnp.concatenate(
            [back(at, q_gain_ref, 2 * lines) for at in range(0, q_width, LANES)], axis=1
        )
        key = back(q_width, k_gain_ref, 2 * lines + 1)
        lane = q_width + LANES
        value = jnp.concatenate(
            [got_ref[0, :, lane : lane + LANES], got_ref[1, :, lane : lane + LANES]], axis=0
        )
        for stream, part in ((query_stream, query), (pair_stream, jnp.concatenate([key, value], axis=1))):
            shape = stream.shape(stream.dims[0])
            stream.source[lax.rem(n, stream.slots(0))] = tn_dot(hidden, part).astype(BF16).reshape(shape)

        total[...] += (
            nt_dot(query, wq_ref[...]) + nt_dot(key, wk_ref[...]) + nt_dot(value, wv_ref[...])
        )

        @pl.when(n == units - 1)
        def _():
            inputs = tokens_ref[...].astype(F32)
            scale = lax.rsqrt(jnp.mean(inputs * inputs, axis=-1, keepdims=True) + EPSILON)
            normal = inputs * scale
            grad = total[...]
            gain_grad = jnp.sum(grad * normal, axis=0, keepdims=True)
            for i in range(lines):
                here = slice(i * LANES, (i + 1) * LANES)
                gains[0, i : i + 1, :] = gain_grad[:, here]
                gains[0, lines + i : lines + i + 1, :] = ffn_gain_ref[:, here]
            pushed = grad * gain_ref[...]
            inner = jnp.mean(pushed * normal, axis=-1, keepdims=True)
            input_ref[...] = (mid_ref[...] + scale * (pushed - normal * inner)).astype(BF16)


def finish(
    line,
    bits,
    got,
    proj,
    hidden,
    tokens,
    mid,
    gain,
    wq,
    wk,
    wv,
    q_gain,
    k_gain,
    cosine,
    sine,
    ffn_gain,
    gate_sum,
    up_sum,
    down_sum,
):
    rows, width = tokens.shape
    count, half, lanes = got.shape
    units = count // 2
    q_width = wq.shape[1] // units
    chips = line * 2 ** len(bits)
    sides = [(bit, 2) for bit in bits]
    dims = [("z", line)] + sides + [(1, 2)]
    mine = width // chips // 2
    streams = [
        Stream([1] + bits[::-1] + hops(line), dims, (mine, q_width), line, LAST_LAG, units),
        Stream([1] + bits + hops(line), dims, (mine, 2 * LANES), line, LAST_LAG, units),
    ]
    rounds = 1 + len(bits) + (line - 1).bit_length()
    steps = max([stream.steps() for stream in streams] + [units + rounds + 2])
    gain_rows = -(-(2 * width // LANES + 2) // 8) * 8
    half_rows = gate_sum.shape[0] // 2
    down_rows = down_sum.shape[0] // 2
    columns = gate_sum.shape[1]

    def keep(shape):
        return pl.BlockSpec(shape, lambda n: (0,) * len(shape), pipeline_mode=pl.Buffered(1))

    def at(n):
        return jnp.minimum(n, units - 1)

    scratch = [
        pltpu.VMEM((rows, width), F32),
        pltpu.VMEM((rounds + 1, gain_rows, LANES), F32),
        pltpu.VMEM((rounds, gain_rows, LANES), F32),
        pltpu.SemaphoreType.DMA((rounds,)),
        pltpu.SemaphoreType.DMA((rounds,)),
        pltpu.VMEM((2, half_rows, columns), BF16),
        pltpu.VMEM((down_rows, down_sum.shape[1]), BF16),
        pltpu.SemaphoreType.DMA((3,)),
        pltpu.SemaphoreType.DMA((3,)),
        pltpu.SemaphoreType.REGULAR((2,)),
    ]
    for stream in streams:
        scratch += stream.scratch()
    outs = [
        ((rows, width), BF16),
        ((gain_rows, LANES), F32),
        ((mine, wq.shape[1]), BF16),
        ((mine, wk.shape[1]), BF16),
        ((mine, wv.shape[1]), BF16),
        ((half_rows, 2 * columns), BF16),
        ((half_rows, 2 * columns), BF16),
        ((down_rows, down_sum.shape[1]), BF16),
    ]
    return pl.pallas_call(
        functools.partial(finish_kernel, line, bits, streams, units),
        name="finish",
        grid=(steps,),
        in_specs=[
            pl.BlockSpec((2, half, lanes), lambda n: (at(n), 0, 0)),
            pl.BlockSpec((1, rows, q_width + LANES), lambda n: (at(n), 0, 0)),
            keep((rows, width)),
            keep((rows, width)),
            keep((rows, width)),
            keep((1, width)),
            pl.BlockSpec((width, q_width), lambda n: (0, at(n))),
            pl.BlockSpec((width, LANES), lambda n: (0, at(n))),
            pl.BlockSpec((width, LANES), lambda n: (0, at(n))),
            keep((1, LANES)),
            keep((1, LANES)),
            keep((rows, LANES)),
            keep((rows, LANES)),
            keep((1, width)),
            keep(gate_sum.shape),
            keep(up_sum.shape),
            keep(down_sum.shape),
        ],
        out_specs=[keep(shape) for shape, unused in outs],
        out_shape=[jax.ShapeDtypeStruct(shape, kind) for shape, kind in outs],
        scratch_shapes=scratch,
        compiler_params=kernel_params(collective_id=5, has_side_effects=True),
    )(
        got,
        proj,
        hidden,
        tokens,
        mid,
        gain,
        wq,
        wk,
        wv,
        q_gain,
        k_gain,
        cosine,
        sine,
        ffn_gain,
        gate_sum,
        up_sum,
        down_sum,
    )


def widen_kernel(*refs):
    count = len(refs) // 2
    for source, target in zip(refs[:count], refs[count:]):
        target[...] = source[...].astype(F32)


def widen(parts):
    return pl.pallas_call(
        widen_kernel,
        name="widen",
        out_shape=[jax.ShapeDtypeStruct(part.shape, F32) for part in parts],
        compiler_params=kernel_params(),
    )(*parts)


def flip_pairs(count, bit):
    return [(i, i ^ bit) for i in range(count)]


def swap_core(block, blk_count):
    return lax.ppermute(block, "blk", flip_pairs(blk_count, 1))


def fast_local(
    dp_count,
    blk_count,
    tokens,
    doc_lengths,
    g_attn,
    w_query,
    w_key,
    w_value,
    q_gain,
    k_gain,
    w_out,
    g_ffn,
    w_gate,
    w_up,
    w_down,
    cotangent,
):
    row_count, tok_count, width = tokens.shape
    rows = row_count * tok_count
    chips = blk_count // 2
    size = tok_count * blk_count
    index = lax.axis_index("blk")
    core = index % 2
    bits = []
    bit = blk_count // 2
    while bit > 1:
        bits.append(bit)
        bit //= 2
    chip_dims = (dp_count,) + (2,) * len(bits)
    all_chips = dp_count * chips
    places = index * tok_count + jnp.arange(tok_count, dtype=jnp.int32)
    unused, positions = doc_layout(doc_lengths, places)
    cosine, sine = rope_angles(positions)
    cosine = jnp.tile(cosine.reshape(rows, -1), (1, 4))
    sine = sine.reshape(rows, -1)
    sine = jnp.concatenate([-sine, sine, -sine, sine], axis=1)
    q_gain2 = jnp.tile(q_gain, 2)[None]
    k_gain2 = jnp.tile(k_gain, 2)[None]
    all_places = jnp.arange(size, dtype=jnp.int32)
    row_lengths = lax.dynamic_slice_in_dim(doc_lengths, core, 1, axis=0)
    unused, all_positions = doc_layout(row_lengths, all_places)
    starts = all_places - all_positions[0]
    starts_two = jnp.broadcast_to(
        starts.reshape(blk_count, 1, tok_count), (blk_count, 2, tok_count)
    ).reshape(1, 2 * size)
    flat = tokens.reshape(rows, width)
    grad_own = cotangent.reshape(rows, width)
    grad_got = swap_core(grad_own, blk_count)

    hidden_in, proj, qkv = project(
        flat, g_attn[None], w_query, w_key, w_value, q_gain2, k_gain2, cosine, sine
    )
    qkv = qkv.reshape(size, -1)
    attended, logs, heads = attend(qkv, starts[:, None], tok_count)
    output, mid, ffn_gain_grad, w_out_parts, grad_heads, acts, gate_sum, up_sum = middle_layer(
        dp_count,
        bits,
        flat,
        heads,
        w_out,
        g_ffn[None],
        grad_own,
        grad_got,
        w_gate,
        w_up,
        w_down,
    )
    got, down_sum, w_out_sum = back(
        dp_count,
        bits,
        qkv,
        logs,
        attended.reshape(size, -1),
        grad_heads.reshape(size, -1),
        starts_two,
        tok_count,
        grad_own,
        grad_got,
        acts,
        w_out_parts,
    )
    input_grad, gains, *sums = finish(
        dp_count,
        bits,
        got,
        proj,
        hidden_in,
        flat,
        mid,
        g_attn[None],
        w_query,
        w_key,
        w_value,
        q_gain2,
        k_gain2,
        cosine,
        sine,
        ffn_gain_grad,
        gate_sum,
        up_sum,
        down_sum,
    )
    sums = widen(sums + [w_out_sum])
    grad_w_query, grad_w_key, grad_w_value, grad_w_gate, grad_w_up, grad_w_down, grad_w_out = sums
    lines = width // LANES
    gain_attn = gains[:lines].reshape(width)
    gain_ffn = gains[lines : 2 * lines].reshape(width)
    gain_query = gains[2 * lines, :HEAD_DIM] + gains[2 * lines, HEAD_DIM:]
    gain_key = gains[2 * lines + 1, :HEAD_DIM] + gains[2 * lines + 1, HEAD_DIM:]
    return (
        output.reshape(tokens.shape),
        input_grad.reshape(tokens.shape),
        gain_attn,
        grad_w_query,
        grad_w_key,
        grad_w_value,
        gain_query,
        gain_key,
        grad_w_out,
        gain_ffn,
        grad_w_gate,
        grad_w_up,
        grad_w_down,
    )


def fits(mesh):
    blk_count = mesh.shape["blk"]
    chips = blk_count // 2
    power = blk_count & (blk_count - 1) == 0
    return power and blk_count > 2 and (KV_HEADS * HEAD_DIM) == chips * LANES


def solution(mesh):
    if fits(mesh):
        body = functools.partial(fast_local, mesh.shape["dp"], mesh.shape["blk"])
    else:
        body = local
    return jax.shard_map(
        body,
        mesh=mesh,
        in_specs=(
            P("dp", "blk", None),
            P("dp", None),
            P(),
            P(),
            P(),
            P(),
            P(),
            P(),
            P(),
            P(),
            P(),
            P(),
            P(),
            P("dp", "blk", None),
        ),
        out_specs=(
            P("dp", "blk", None),
            P("dp", "blk", None),
            P(),
            P(("dp", "blk"), None),
            P(("dp", "blk"), None),
            P(("dp", "blk"), None),
            P(),
            P(),
            P(("dp", "blk"), None),
            P(),
            P(("dp", "blk"), None),
            P(("dp", "blk"), None),
            P(("dp", "blk"), None),
        ),
        check_vma=False,
    )
```

```python
import functools
import math

import jax
import jax.numpy as jnp
from jax import lax
from jax.experimental import pallas as pl
from jax.experimental.pallas import tpu as pltpu
from jax.sharding import PartitionSpec as P

HEADS = 16
KV_HEADS = 8
HEAD_DIM = 64


EPSILON = 1e-05
ROPE_BASE = 1000000.0
NEGATIVE = -1e30


def norm_rows(values, norm_gain):
    row_scale = lax.rsqrt(jnp.mean(values * values, axis=-1, keepdims=True) + EPSILON)
    normal = values * row_scale
    return (normal * norm_gain, normal, row_scale)


def norm_back(normal, row_scale, norm_gain, grad_out):
    pushed = grad_out * norm_gain
    inner = jnp.mean(pushed * normal, axis=-1, keepdims=True)
    grad_in = row_scale * (pushed - normal * inner)
    leading = tuple(range(grad_out.ndim - 1))
    return (grad_in, jnp.sum(grad_out * normal, axis=leading))


def doc_layout(lengths, places):
    ends = jnp.cumsum(lengths, axis=1)
    past = places[None, :, None] >= ends[:, None, :]
    docs = jnp.sum(past.astype(jnp.int32), axis=2)
    before = jnp.sum(jnp.where(past, lengths[:, None, :], 0), axis=2)
    return (docs, places[None, :] - before)


def rope_angles(positions):
    half = HEAD_DIM // 2
    freqs = ROPE_BASE ** (-jnp.arange(half, dtype=jnp.float32) / half)
    angles = positions.astype(jnp.float32)[..., None] * freqs
    return (jnp.cos(angles), jnp.sin(angles))


def rotate(values, cosine, sine):
    half = values.shape[-1] // 2
    first_half = values[..., :half]
    second_half = values[..., half:]
    cos_col = cosine[:, :, None, :]
    sin_col = sine[:, :, None, :]
    return jnp.concatenate(
        [
            first_half * cos_col - second_half * sin_col,
            second_half * cos_col + first_half * sin_col,
        ],
        axis=-1,
    )


def local(
    tokens,
    doc_lengths,
    g_attn,
    w_query,
    w_key,
    w_value,
    q_gain,
    k_gain,
    w_out,
    g_ffn,
    w_gate,
    w_up,
    w_down,
    cotangent,
):
    row_count, tok_count, width = tokens.shape
    grouping = HEADS // KV_HEADS
    flat_rows = row_count * tok_count
    kv_width = KV_HEADS * HEAD_DIM
    softmax_scale = HEAD_DIM ** (-0.5)
    places = lax.axis_index("blk") * tok_count + jnp.arange(tok_count, dtype=jnp.int32)
    query_docs, query_pos = doc_layout(doc_lengths, places)
    cosine, sine = rope_angles(query_pos)
    inputs = tokens.reshape(flat_rows, width).astype(jnp.float32)
    normed, normal_in, scale_in = norm_rows(inputs, g_attn)
    hidden_in = normed.astype(jnp.bfloat16)
    query_proj = jnp.dot(hidden_in, w_query, preferred_element_type=jnp.float32).reshape(
        row_count, tok_count, HEADS, HEAD_DIM
    )
    key_proj = jnp.dot(hidden_in, w_key, preferred_element_type=jnp.float32).reshape(
        row_count, tok_count, KV_HEADS, HEAD_DIM
    )
    value_b = (
        jnp.dot(hidden_in, w_value, preferred_element_type=jnp.float32)
        .astype(jnp.bfloat16)
        .reshape(row_count, tok_count, kv_width)
    )
    query_norm, query_normal, query_scale = norm_rows(query_proj, q_gain)
    key_norm, key_normal, key_scale = norm_rows(key_proj, k_gain)
    query_b = (
        rotate(query_norm, cosine, sine)
        .astype(jnp.bfloat16)
        .reshape(row_count, tok_count, KV_HEADS, grouping, HEAD_DIM)
    )
    key_b = (
        rotate(key_norm, cosine, sine).astype(jnp.bfloat16).reshape(row_count, tok_count, kv_width)
    )

    def piece_mask(size):
        key_places = jnp.arange(size, dtype=jnp.int32)
        key_docs, unused = doc_layout(doc_lengths, key_places)
        return (key_places[None, None, :] <= places[None, :, None]) & (
            key_docs[:, None, :] == query_docs[:, :, None]
        )

    def piece_scores(key_piece, allowed):
        key_heads = key_piece.reshape(row_count, key_piece.shape[1], KV_HEADS, HEAD_DIM)
        raw_scores = (
            jnp.einsum("rqkgd,rpkd->rkgqp", query_b, key_heads, preferred_element_type=jnp.float32)
            * softmax_scale
        )
        return (jnp.where(allowed[:, None, None], raw_scores, -jnp.inf), key_heads)

    stat_shape = (row_count, KV_HEADS, grouping, tok_count)
    key_piece = lax.all_gather(key_b, "blk", axis=1, tiled=True)
    value_piece = lax.all_gather(value_b, "blk", axis=1, tiled=True)
    allowed = piece_mask(key_piece.shape[1])
    running_max = jnp.full(stat_shape, NEGATIVE, jnp.float32)
    scores, key_heads = piece_scores(key_piece, allowed)
    new_max = jnp.maximum(running_max, jnp.max(scores, axis=-1))
    weights = jnp.exp(scores - new_max[..., None])
    value_heads = value_piece.reshape(row_count, value_piece.shape[1], KV_HEADS, HEAD_DIM)
    added = jnp.einsum(
        "rkgqp,rpkd->rkgqd",
        weights.astype(jnp.bfloat16),
        value_heads,
        preferred_element_type=jnp.float32,
    )
    running_sum = jnp.sum(weights, axis=-1)
    attended = added / running_sum[..., None]
    log_total = new_max + jnp.log(running_sum)
    attended_b = (
        jnp.transpose(attended, (0, 3, 1, 2, 4))
        .reshape(flat_rows, HEADS * HEAD_DIM)
        .astype(jnp.bfloat16)
    )
    middle = inputs + jnp.dot(attended_b, w_out, preferred_element_type=jnp.float32)
    normed_ffn, normal_ffn, scale_ffn = norm_rows(middle, g_ffn)
    hidden_ffn = normed_ffn.astype(jnp.bfloat16)
    gate = jnp.dot(hidden_ffn, w_gate, preferred_element_type=jnp.float32)
    up_proj = jnp.dot(hidden_ffn, w_up, preferred_element_type=jnp.float32)
    sigmoid_gate = jax.nn.sigmoid(gate)
    silu_gate = gate * sigmoid_gate
    hidden = (silu_gate * up_proj).astype(jnp.bfloat16)
    result = middle + jnp.dot(hidden, w_down, preferred_element_type=jnp.float32)
    output = result.astype(jnp.bfloat16).reshape(row_count, tok_count, width)
    grad_out = cotangent.reshape(flat_rows, width)
    grad_w_down = jnp.einsum("tf,td->fd", hidden, grad_out, preferred_element_type=jnp.float32)
    grad_hidden = jnp.einsum("td,fd->tf", grad_out, w_down, preferred_element_type=jnp.float32)
    grad_gate = (grad_hidden * up_proj * sigmoid_gate * (1.0 + gate * (1.0 - sigmoid_gate))).astype(
        jnp.bfloat16
    )
    grad_up = (grad_hidden * silu_gate).astype(jnp.bfloat16)
    grad_w_gate = jnp.einsum("td,tf->df", hidden_ffn, grad_gate, preferred_element_type=jnp.float32)
    grad_w_up = jnp.einsum("td,tf->df", hidden_ffn, grad_up, preferred_element_type=jnp.float32)
    grad_h2 = jnp.einsum(
        "tf,df->td", grad_gate, w_gate, preferred_element_type=jnp.float32
    ) + jnp.einsum("tf,df->td", grad_up, w_up, preferred_element_type=jnp.float32)
    grad_mid, grad_ffn_gain = norm_back(normal_ffn, scale_ffn, g_ffn, grad_h2)
    grad_mid = grad_out.astype(jnp.float32) + grad_mid
    grad_attn = grad_mid.astype(jnp.bfloat16)
    grad_w_out = jnp.einsum("tc,td->cd", attended_b, grad_attn, preferred_element_type=jnp.float32)
    grad_attended = jnp.einsum(
        "td,cd->tc", grad_attn, w_out, preferred_element_type=jnp.float32
    ).astype(jnp.bfloat16)
    grad_heads = grad_attended.reshape(row_count, tok_count, KV_HEADS, grouping, HEAD_DIM)
    deltas = jnp.einsum("rqkgd,rkgqd->rkgq", grad_heads.astype(jnp.float32), attended)
    key_piece = lax.all_gather(key_b, "blk", axis=1, tiled=True)
    value_piece = lax.all_gather(value_b, "blk", axis=1, tiled=True)
    size = key_piece.shape[1]
    allowed = piece_mask(size)
    scores, key_heads = piece_scores(key_piece, allowed)
    probs = jnp.exp(scores - log_total[..., None])
    value_heads = value_piece.reshape(row_count, size, KV_HEADS, HEAD_DIM)
    value_piece_grad = jnp.einsum(
        "rkgqp,rqkgd->rpkd",
        probs.astype(jnp.bfloat16),
        grad_heads,
        preferred_element_type=jnp.float32,
    )
    grad_probs = jnp.einsum(
        "rqkgd,rpkd->rkgqp", grad_heads, value_heads, preferred_element_type=jnp.float32
    )
    grad_scores = (probs * (grad_probs - deltas[..., None])).astype(jnp.bfloat16)
    grad_query = jnp.einsum(
        "rkgqp,rpkd->rkgqd", grad_scores, key_heads, preferred_element_type=jnp.float32
    )
    key_piece_grad = jnp.einsum(
        "rkgqp,rqkgd->rpkd", grad_scores, query_b, preferred_element_type=jnp.float32
    )
    grad_keys = key_piece_grad.reshape(row_count, size, kv_width)
    grad_values = value_piece_grad.reshape(row_count, size, kv_width)
    grad_query, grad_keys, grad_values = (grad_query, grad_keys, grad_values)
    key_grad_mine, value_grad_mine = (
        lax.psum_scatter(
            grad_keys.astype(jnp.bfloat16), "blk", scatter_dimension=1, tiled=True
        ).astype(jnp.float32),
        lax.psum_scatter(
            grad_values.astype(jnp.bfloat16), "blk", scatter_dimension=1, tiled=True
        ).astype(jnp.float32),
    )
    grad_q_rot = (jnp.transpose(grad_query, (0, 3, 1, 2, 4)) * softmax_scale).reshape(
        row_count, tok_count, HEADS, HEAD_DIM
    )
    grad_k_rot = (key_grad_mine * softmax_scale).reshape(row_count, tok_count, KV_HEADS, HEAD_DIM)
    grad_q_proj, grad_query_gain = norm_back(
        query_normal, query_scale, q_gain, rotate(grad_q_rot, cosine, -sine)
    )
    grad_k_proj, grad_key_gain = norm_back(
        key_normal, key_scale, k_gain, rotate(grad_k_rot, cosine, -sine)
    )
    grad_q_b = grad_q_proj.astype(jnp.bfloat16).reshape(flat_rows, HEADS * HEAD_DIM)
    grad_k_b = grad_k_proj.astype(jnp.bfloat16).reshape(flat_rows, kv_width)
    grad_v_b = value_grad_mine.astype(jnp.bfloat16).reshape(flat_rows, kv_width)
    grad_w_query = jnp.einsum("td,tc->dc", hidden_in, grad_q_b, preferred_element_type=jnp.float32)
    grad_w_key = jnp.einsum("td,tc->dc", hidden_in, grad_k_b, preferred_element_type=jnp.float32)
    grad_w_value = jnp.einsum("td,tc->dc", hidden_in, grad_v_b, preferred_element_type=jnp.float32)
    grad_h1 = jnp.einsum("tc,dc->td", grad_q_b, w_query, preferred_element_type=jnp.float32)
    grad_h1 = grad_h1 + jnp.einsum("tc,dc->td", grad_k_b, w_key, preferred_element_type=jnp.float32)
    grad_h1 = grad_h1 + jnp.einsum(
        "tc,dc->td", grad_v_b, w_value, preferred_element_type=jnp.float32
    )
    grad_base, grad_attn_gain = norm_back(normal_in, scale_in, g_attn, grad_h1)
    input_grad = (grad_mid + grad_base).astype(jnp.bfloat16).reshape(row_count, tok_count, width)
    gain_attn, gain_query, gain_key, gain_ffn = lax.psum(
        (grad_attn_gain, grad_query_gain, grad_key_gain, grad_ffn_gain), ("dp", "blk")
    )
    locals_all = (
        grad_w_query,
        grad_w_key,
        grad_w_value,
        grad_w_out,
        grad_w_gate,
        grad_w_up,
        grad_w_down,
    )
    shared = (
        lax.psum_scatter(locals_all[0], ("dp", "blk"), scatter_dimension=0, tiled=True),
        lax.psum_scatter(locals_all[1], ("dp", "blk"), scatter_dimension=0, tiled=True),
        lax.psum_scatter(locals_all[2], ("dp", "blk"), scatter_dimension=0, tiled=True),
        lax.psum_scatter(locals_all[3], ("dp", "blk"), scatter_dimension=0, tiled=True),
        lax.psum_scatter(locals_all[4], ("dp", "blk"), scatter_dimension=0, tiled=True),
        lax.psum_scatter(locals_all[5], ("dp", "blk"), scatter_dimension=0, tiled=True),
        lax.psum_scatter(locals_all[6], ("dp", "blk"), scatter_dimension=0, tiled=True),
    )
    return (
        output,
        input_grad,
        gain_attn,
        shared[0],
        shared[1],
        shared[2],
        gain_query,
        gain_key,
        shared[3],
        gain_ffn,
        shared[4],
        shared[5],
        shared[6],
    )


BF16 = jnp.bfloat16
F32 = jnp.float32
LANES = 128
FF_TILE = 256
LAG = 2
LAST_LAG = 1
ATTEND_PAIRS = 6
VMEM_BYTES = 60 * 1024 * 1024
LOG2_E = math.log2(math.e)
QUERY_SCALE = HEAD_DIM ** (-0.5) * LOG2_E
MASKED = -1e30


def nn_dot(left, right):
    return lax.dot_general(left, right, (((1,), (0,)), ((), ())), preferred_element_type=F32)


def nt_dot(left, right):
    return lax.dot_general(left, right, (((1,), (1,)), ((), ())), preferred_element_type=F32)


def tn_dot(left, right):
    return lax.dot_general(left, right, (((0,), (0,)), ((), ())), preferred_element_type=F32)


def kernel_params(**more):
    return pltpu.CompilerParams(vmem_limit_bytes=VMEM_BYTES, **more)


def whole_block(shape):
    return pl.BlockSpec(shape, lambda *ids: (0,) * len(shape))


def greet_blk(count):
    barrier = pltpu.get_barrier_semaphore()
    z, index = lax.axis_index("dp"), lax.axis_index("blk")
    for step in range(1, count):
        pl.semaphore_signal(
            barrier,
            inc=1,
            device_id=(z, lax.rem(index + step, count)),
            device_id_type=pl.DeviceIdType.MESH,
        )
    pl.semaphore_wait(barrier, count - 1)


def blk_copy(send, got, sent_sem, got_sem, target, source):
    return pltpu.make_async_remote_copy(
        src_ref=send.at[target],
        dst_ref=got.at[source],
        send_sem=sent_sem.at[target],
        recv_sem=got_sem.at[source],
        device_id=(lax.axis_index("dp"), target),
        device_id_type=pl.DeviceIdType.MESH,
    )


def blk_sems(count):
    return [pltpu.SemaphoreType.DMA((count,)), pltpu.SemaphoreType.DMA((count,))]


def head_means(values):
    rows = lax.broadcasted_iota(jnp.int32, (LANES, LANES), 0) // HEAD_DIM
    cols = lax.broadcasted_iota(jnp.int32, (LANES, LANES), 1) // HEAD_DIM
    spread = jnp.where(rows == cols, 1.0 / HEAD_DIM, 0.0).astype(BF16)
    high = values.astype(BF16)
    low = (values - high.astype(F32)).astype(BF16)
    return nn_dot(high, spread) + nn_dot(low, spread)


def half_partner(values):
    lane = lax.broadcasted_iota(jnp.int32, values.shape, 1)
    half = HEAD_DIM // 2
    ahead = pltpu.roll(values, LANES - half, 1)
    behind = pltpu.roll(values, half, 1)
    return jnp.where(lane % HEAD_DIM < half, ahead, behind)


def project_kernel(
    tokens_ref,
    gain_ref,
    wq_ref,
    wk_ref,
    wv_ref,
    q_gain_ref,
    k_gain_ref,
    cos_ref,
    sin_ref,
    hidden_ref,
    proj_ref,
    got_ref,
    send,
    got,
    sent_sem,
    got_sem,
):
    rows = tokens_ref.shape[0]
    n, chips = pl.program_id(0), pl.num_programs(0)
    count = send.shape[0]
    index = lax.axis_index("blk")
    p = lax.rem(index // 2 + 1 + n, chips)

    @pl.when(n == 0)
    def _():
        greet_blk(count)
        inputs = tokens_ref[...].astype(F32)
        scale = lax.rsqrt(jnp.mean(inputs * inputs, axis=-1, keepdims=True) + EPSILON)
        hidden_ref[...] = (inputs * scale * gain_ref[...]).astype(BF16)

    hidden = hidden_ref[...]
    half = rows // 2

    def put(block, lane):
        send[2 * p, :, lane : lane + LANES] = block[:half]
        send[2 * p + 1, :, lane : lane + LANES] = block[half:]

    queries = nn_dot(hidden, wq_ref[...])
    keys = nn_dot(hidden, wk_ref[...])
    values = nn_dot(hidden, wv_ref[...])
    q_width = queries.shape[1]
    blocks = [(queries[:, at : at + LANES], at, q_gain_ref, QUERY_SCALE) for at in range(0, q_width, LANES)]
    blocks.append((keys, q_width, k_gain_ref, 1.0))
    for block, lane, head_gain, factor in blocks:
        proj_ref[0, :, lane : lane + LANES] = block
        scale = lax.rsqrt(head_means(block * block) + EPSILON)
        normed = block * scale * head_gain[...]
        turned = normed * cos_ref[...] + half_partner(normed) * sin_ref[...]
        put((turned * factor).astype(BF16), lane)
    put(values.astype(BF16), q_width + LANES)
    for part in range(2):
        target = 2 * p + part

        @pl.when(target != index)
        def _():
            blk_copy(send, got, sent_sem, got_sem, target, index).start()

        @pl.when(target == index)
        def _():
            got[target] = send[target]

    @pl.when(n == chips - 1)
    def _():
        for step in range(1, count):
            other = lax.rem(index + step, count)
            blk_copy(send, got, sent_sem, got_sem, other, other).wait()
        got_ref[...] = got[...]


def project(tokens, gain, wq, wk, wv, q_gain, k_gain, cosine, sine):
    rows, width = tokens.shape
    chips = wk.shape[1] // LANES
    q_width = wq.shape[1] // chips
    block_width = q_width + 2 * LANES
    moved = (2 * chips, rows // 2, block_width)

    def at(n):
        return lax.rem(lax.axis_index("blk") // 2 + 1 + n, chips)

    return pl.pallas_call(
        project_kernel,
        name="project",
        grid=(chips,),
        in_specs=[
            whole_block((rows, width)),
            whole_block((1, width)),
            pl.BlockSpec((width, q_width), lambda n: (0, at(n))),
            pl.BlockSpec((width, LANES), lambda n: (0, at(n))),
            pl.BlockSpec((width, LANES), lambda n: (0, at(n))),
            whole_block((1, LANES)),
            whole_block((1, LANES)),
            whole_block((rows, LANES)),
            whole_block((rows, LANES)),
        ],
        out_specs=[
            whole_block((rows, width)),
            pl.BlockSpec((1, rows, q_width + LANES), lambda n: (at(n), 0, 0)),
            whole_block(moved),
        ],
        out_shape=[
            jax.ShapeDtypeStruct((rows, width), BF16),
            jax.ShapeDtypeStruct((chips, rows, q_width + LANES), F32),
            jax.ShapeDtypeStruct(moved, BF16),
        ],
        scratch_shapes=[pltpu.VMEM(moved, BF16), pltpu.VMEM(moved, BF16)] + blk_sems(2 * chips),
        compiler_params=kernel_params(collective_id=0, has_side_effects=True),
    )(tokens, gain, wq, wk, wv, q_gain, k_gain, cosine, sine)


def low_lanes(shape):
    return lax.broadcasted_iota(jnp.int32, shape, 1) < HEAD_DIM


def doubled(pair, group):
    turned = pltpu.roll(pair.astype(F32), HEAD_DIM, 1).astype(BF16)
    low = low_lanes(pair.shape)
    return jnp.where(low, pair, turned) if group == 0 else jnp.where(low, turned, pair)


def stacked_heads(pair):
    low = low_lanes(pair.shape)
    none = jnp.zeros_like(pair)
    return jnp.concatenate([jnp.where(low, pair, none), jnp.where(low, none, pair)], axis=0)


def in_three(column):
    lane = lax.broadcasted_iota(jnp.int32, (column.shape[0], LANES), 1)
    wide = jnp.broadcast_to(column, (column.shape[0], LANES))
    first = wide.astype(BF16).astype(F32)
    second = (wide - first).astype(BF16).astype(F32)
    third = wide - first - second
    return jnp.where(
        lane == 0, first, jnp.where(lane == 1, second, jnp.where(lane == 2, third, 0.0))
    ).astype(BF16)


def minus_three(rows):
    lane = lax.broadcasted_iota(jnp.int32, (rows, LANES), 1)
    return jnp.where(lane < 3, -1.0, 0.0).astype(BF16)


def attend_kernel(
    groups,
    block,
    qkv_ref,
    starts_ref,
    out_ref,
    logs_ref,
    heads_ref,
    keys,
    values,
    total,
    got,
    sent_sem,
    got_sem,
):
    size = qkv_ref.shape[0]
    blocks = size // block
    q_width = groups * LANES
    n = pl.program_id(0)
    index = lax.axis_index("blk")
    here = lax.rem(index + 1 + n, blocks)

    @pl.when(n == 0)
    def _():
        greet_blk(blocks)
        for g in range(groups):
            keys[g] = doubled(qkv_ref[:, q_width : q_width + LANES], g)
            values[g, :, :LANES] = doubled(qkv_ref[:, q_width + LANES : q_width + 2 * LANES], g)
            values[g, :, LANES:] = jnp.ones((size, LANES), BF16)

    at = pl.multiple_of(here * block, block)
    starts = jnp.concatenate([starts_ref[pl.ds(at, block), :]] * 2, axis=0)
    queries = [
        stacked_heads(qkv_ref[pl.ds(at, block), g * LANES : (g + 1) * LANES]) for g in range(groups)
    ]

    def step(key_at, width, diagonal):
        column = lax.broadcasted_iota(jnp.int32, (2 * block, width), 1)
        allowed = column >= starts - key_at
        if diagonal:
            row = lax.broadcasted_iota(jnp.int32, (2 * block, width), 0) % block
            allowed = allowed & (column <= row)
        for g in range(groups):
            scores = nt_dot(queries[g], keys[g, pl.ds(key_at, width), :])
            weights = jnp.exp2(jnp.where(allowed, scores, MASKED)).astype(BF16)
            part = nn_dot(weights, values[g, pl.ds(key_at, width), :])
            if diagonal:
                total[g] = part
            else:
                total[g] += part

    step(at, block, True)

    @pl.when(lax.rem(here, 2) == 1)
    def _():
        step(pl.multiple_of((here - 1) * block, block), block, False)

    def body(j, carry):
        step(pl.multiple_of(j * 2 * block, 2 * block), 2 * block, False)
        return carry

    lax.fori_loop(0, here // 2, body, 0)
    low = low_lanes((block, LANES))
    to = pl.multiple_of(here * 2 * block, 2 * block)
    for g in range(groups):
        sums = total[g, :, LANES:]
        mean = total[g, :, :LANES] / sums
        out_ref[here, :, g * LANES : (g + 1) * LANES] = jnp.where(low, mean[:block], mean[block:]).astype(BF16)
        logs_ref[g, pl.ds(to, 2 * block), :] = in_three(jnp.log2(sums[:, :1]))

    @pl.when(here != index)
    def _():
        blk_copy(out_ref, got, sent_sem, got_sem, here, index).start()

    @pl.when(n == blocks - 1)
    def _():
        got[index] = out_ref[index]
        for step in range(1, blocks):
            other = lax.rem(index + step, blocks)
            blk_copy(out_ref, got, sent_sem, got_sem, other, other).wait()
        heads_ref[...] = got[...]


def attend(qkv, starts, block):
    size, width = qkv.shape
    groups = (width - 2 * LANES) // LANES
    blocks = size // block
    heads = (blocks, block, groups * LANES)
    logs = (groups, 2 * size, LANES)

    def keep(shape):
        return pl.BlockSpec(shape, lambda n: (0,) * len(shape), pipeline_mode=pl.Buffered(1))

    return pl.pallas_call(
        functools.partial(attend_kernel, groups, block),
        name="attend",
        grid=(blocks,),
        in_specs=[keep((size, width)), keep((size, 1))],
        out_specs=[keep(heads), keep(logs), keep(heads)],
        out_shape=[jax.ShapeDtypeStruct(shape, BF16) for shape in (heads, logs, heads)],
        scratch_shapes=[
            pltpu.VMEM((groups, size, LANES), BF16),
            pltpu.VMEM((groups, size, 2 * LANES), BF16),
            pltpu.VMEM((groups, 2 * block, 2 * LANES), F32),
            pltpu.VMEM(heads, BF16),
        ]
        + blk_sems(blocks),
        compiler_params=kernel_params(collective_id=1, has_side_effects=True),
    )(qkv, starts)


def pair_of(name):
    z, index = lax.axis_index("dp"), lax.axis_index("blk")
    if isinstance(name, tuple):
        mine = lax.rem(z // name[1], 2)
        return mine, (z + name[1] * (1 - 2 * mine), index)
    mine = lax.rem(index // name, 2)
    return mine, (z, index + name * (1 - 2 * mine))


class Stream:
    def __init__(self, path, names, block, lag, units, swap=None):
        self.path, self.block, self.lag, self.units, self.swap = path, block, lag, units, swap
        self.slots = min(2 * lag, units)
        self.names = [tuple(names)]
        for k, stage in enumerate(path):
            left = tuple(name for name in self.names[-1] if name != stage)
            self.names.append((swap,) + left if swap is not None and k == 0 else left)
        assert not self.names[-1]

    def shape(self, names):
        return (2,) * len(names) + self.block

    def steps(self):
        return self.units + self.lag * len(self.path) + 1

    def slot(self, u):
        return lax.rem(u, self.slots)

    def scratch(self):
        shapes = []
        for k, stage in enumerate(self.path):
            left = tuple(name for name in self.names[k] if name != stage)
            shapes.append(pltpu.VMEM((self.slots,) + self.shape(self.names[k]), BF16))
            shapes.append(pltpu.VMEM((self.slots,) + self.shape(left), BF16))
            shapes += [pltpu.SemaphoreType.DMA((self.slots,))] * 2
        return shapes

    def bind(self, refs, finish, begin=0):
        self.finish, self.begin = finish, begin
        self.work, self.got, self.sent_sem, self.got_sem = refs[::4], refs[1::4], refs[2::4], refs[3::4]
        self.source = self.work[0]

    def copy(self, k, u):
        mine, partner = pair_of(self.path[k])
        whole = (slice(None),) * self.names[k].index(self.path[k])
        slot = self.slot(u)
        copy = pltpu.make_async_remote_copy(
            src_ref=self.work[k].at[(slot,) + whole + (1 - mine,)],
            dst_ref=self.got[k].at[slot],
            send_sem=self.sent_sem[k].at[slot],
            recv_sem=self.got_sem[k].at[slot],
            device_id=partner,
            device_id_type=pl.DeviceIdType.MESH,
        )
        return copy, (slot,) + whole + (mine,), mine

    def send(self, k, step):
        u = step - self.begin - self.lag * k - 1

        @pl.when((u >= 0) & (u < self.units))
        def _():
            self.copy(k, u)[0].start()

    def take(self, k, step):
        u = step - self.begin - self.lag * (k + 1) - 1

        @pl.when((u >= 0) & (u < self.units))
        def _():
            copy, own, mine = self.copy(k, u)
            copy.wait()
            slot = self.slot(u)
            if self.swap is not None and k == 0:
                self.work[1][slot, mine] = self.work[0][own]
                self.work[1][slot, 1 - mine] = self.got[0][slot]
            elif k == len(self.path) - 1:
                self.finish(u, self.work[k][own] + self.got[k][slot])
            else:
                self.work[k + 1][slot] = self.work[k][own] + self.got[k][slot]


def step_streams(streams, step):
    longest = max(len(stream.path) for stream in streams)
    for k in range(longest):
        for stream in streams:
            if k < len(stream.path):
                stream.take(k, step)
    for k in range(longest):
        for stream in streams:
            if k < len(stream.path):
                stream.send(k, step)


def line_bits(line):
    return [("z", 1 << i) for i in range(line.bit_length() - 1)]


def greet_all(blk_count, line):
    barrier = pltpu.get_barrier_semaphore()
    z, index = lax.axis_index("dp"), lax.axis_index("blk")
    peers = [(z, lax.rem(index + step, blk_count)) for step in range(1, blk_count)]
    peers += [pair_of(name)[1] for name in line_bits(line)]
    for peer in peers:
        pl.semaphore_signal(barrier, inc=1, device_id=peer, device_id_type=pl.DeviceIdType.MESH)
    pl.semaphore_wait(barrier, len(peers))


def middle_kernel(
    line,
    bits,
    streams,
    units,
    tokens_ref,
    heads_ref,
    w_out_ref,
    gain_ref,
    dy_own_ref,
    dy_got_ref,
    w_gate_ref,
    w_up_ref,
    w_down_ref,
    output_ref,
    mid_ref,
    gain_grad_ref,
    w_grad_ref,
    grad_heads_ref,
    acts_ref,
    gate_out_ref,
    up_out_ref,
    hidden,
    flipped,
    out_sum,
    back_sum,
    gate_grads,
    up_grads,
    part_send,
    part_got,
    low_grad,
    do_send,
    do_got,
    hidden_sem,
    part_sent_sem,
    part_got_sem,
    do_sent_sem,
    do_got_sem,
    *refs,
):
    n = pl.program_id(0)
    steps = pl.num_programs(0)
    z, index = lax.axis_index("dp"), lax.axis_index("blk")
    sibling = pair_of(1)[1]
    own_rows, width = tokens_ref.shape
    rows = 2 * own_rows
    blk_count, tok_count, head_lanes = heads_ref.shape
    chips = blk_count // 2
    chunk = 256
    gate_stream, up_stream, both_stream = streams
    gate_rows = gate_stream.block[0]
    own, other = pl.ds(0, own_rows), pl.ds(own_rows, own_rows)

    def finish_gate(u, value):
        gate_out_ref[:gate_rows, pl.ds(pl.multiple_of(u * FF_TILE, FF_TILE), FF_TILE)] = value

    def finish_up(u, value):
        up_out_ref[:gate_rows, pl.ds(pl.multiple_of(u * FF_TILE, FF_TILE), FF_TILE)] = value

    def finish_both(u, value):
        here = pl.ds(pl.multiple_of(u * FF_TILE, FF_TILE), FF_TILE)
        gate_out_ref[gate_rows:, here] = value[:, :FF_TILE]
        up_out_ref[gate_rows:, here] = value[:, FF_TILE:]

    at = 0
    for stream, finish in zip(streams, (finish_gate, finish_up, finish_both)):
        count = len(stream.scratch())
        stream.bind(refs[at : at + count], finish)
        at += count

    def hidden_copy():
        return pltpu.make_async_remote_copy(
            src_ref=hidden.at[own],
            dst_ref=hidden.at[other],
            send_sem=hidden_sem.at[0],
            recv_sem=hidden_sem.at[1],
            device_id=sibling,
            device_id_type=pl.DeviceIdType.MESH,
        )

    def part_copy(i):
        return pltpu.make_async_remote_copy(
            src_ref=part_send.at[i],
            dst_ref=part_got.at[i],
            send_sem=part_sent_sem.at[i],
            recv_sem=part_got_sem.at[i],
            device_id=sibling,
            device_id_type=pl.DeviceIdType.MESH,
        )

    def do_copy(target, source):
        return pltpu.make_async_remote_copy(
            src_ref=do_send.at[target],
            dst_ref=do_got.at[source],
            send_sem=do_sent_sem.at[target],
            recv_sem=do_got_sem.at[source],
            device_id=(z, target),
            device_id_type=pl.DeviceIdType.MESH,
        )

    def flip(start):
        for r in range(start, start + own_rows, chunk):
            for c in range(0, width, chunk):
                flipped[c : c + chunk, r : r + chunk] = hidden[r : r + chunk, c : c + chunk].T

    @pl.when(n == 0)
    def _():
        greet_all(blk_count, line)
        total = tokens_ref[...].astype(F32)
        for p in range(chips):
            block = jnp.concatenate([heads_ref[2 * p], heads_ref[2 * p + 1]], axis=0)
            total = total + nn_dot(block, w_out_ref[p * head_lanes : (p + 1) * head_lanes, :])
        mid_ref[...] = total
        scale = lax.rsqrt(jnp.mean(total * total, axis=-1, keepdims=True) + EPSILON)
        hidden[own] = (total * scale * gain_ref[...]).astype(BF16)
        hidden_copy().start()
        out_sum[...] = jnp.zeros_like(out_sum)
        back_sum[...] = jnp.zeros_like(back_sum)
        flip(0)

    @pl.when(n == 1)
    def _():
        hidden_copy().wait()
        flip(own_rows)

    step_streams(streams, n - 1)

    @pl.when((n >= 1) & (n <= units))
    def _():
        for m in range(rows // chunk):
            part = slice(m * chunk, (m + 1) * chunk)
            gate = nn_dot(hidden[part, :], w_gate_ref[...])
            up = nn_dot(hidden[part, :], w_up_ref[...])
            at = m * chunk % own_rows
            dy_ref = dy_own_ref if m * chunk < own_rows else dy_got_ref
            pushed = nt_dot(dy_ref[at : at + chunk, :], w_down_ref[...])
            opened = jax.nn.sigmoid(gate)
            silu = gate * opened
            act = (silu * up).astype(BF16)
            gate_grad = (pushed * up * opened * (1.0 + gate * (1.0 - opened))).astype(BF16)
            up_grad = (pushed * silu).astype(BF16)
            acts_ref[:, part] = act.T
            gate_grads[part, :] = gate_grad
            up_grads[part, :] = up_grad
            out_sum[part, :] += nn_dot(act, w_down_ref[...])
            back_sum[part, :] += nt_dot(gate_grad, w_gate_ref[...]) + nt_dot(up_grad, w_up_ref[...])
        u = n - 1
        slot = gate_stream.slot(u)
        each = width // line
        zs = line.bit_length() - 1
        shape = gate_stream.shape(gate_stream.names[0])[zs:-2] + (-1, FF_TILE)
        for m in range(line):
            at = (slot,) + tuple(m >> i & 1 for i in reversed(range(zs)))
            part = slice(m * each, (m + 1) * each)
            gate_part = nn_dot(flipped[part, :], gate_grads[...]).astype(BF16)
            up_part = nn_dot(flipped[part, :], up_grads[...]).astype(BF16)
            gate_part, up_part = gate_part.reshape(shape), up_part.reshape(shape)
            gate_stream.source[at] = gate_part[..., :gate_rows, :]
            up_stream.source[at] = up_part[..., :gate_rows, :]
            both_stream.source[at + (..., slice(0, FF_TILE))] = gate_part[..., gate_rows:, :]
            both_stream.source[at + (..., slice(FF_TILE, None))] = up_part[..., gate_rows:, :]

    @pl.when(n == units)
    def _():
        part_send[0] = back_sum[other].astype(BF16)
        part_copy(0).start()
        part_send[1] = out_sum[other].astype(BF16)
        part_copy(1).start()

    @pl.when(n == units + 1)
    def _():
        part_copy(0).wait()
        values = mid_ref[...]
        scale = lax.rsqrt(jnp.mean(values * values, axis=-1, keepdims=True) + EPSILON)
        normal = values * scale
        back = back_sum[own] + part_got[0].astype(F32)
        gain_grad_ref[...] = jnp.sum(back * normal, axis=0, keepdims=True)
        pushed = back * gain_ref[...]
        inner = jnp.mean(pushed * normal, axis=-1, keepdims=True)
        mid = dy_own_ref[...].astype(F32) + scale * (pushed - normal * inner)
        part_copy(1).wait()
        mid_ref[...] = mid
        low_grad[...] = mid.astype(BF16)
        output_ref[...] = (values + (out_sum[own] + part_got[1].astype(F32))).astype(BF16)

    @pl.when((n > units + 1) & (n <= units + 1 + chips))
    def _():
        p = n - units - 2
        grad = low_grad[...]
        lanes = pl.ds(pl.multiple_of(p * head_lanes, head_lanes), head_lanes)
        send = nt_dot(grad, w_out_ref[lanes, :]).astype(BF16)
        for half in range(2):
            target = 2 * p + half
            do_send[target] = send[half * tok_count : (half + 1) * tok_count]

            @pl.when(target != index)
            def _():
                do_copy(target, index).start()

            @pl.when(target == index)
            def _():
                do_got[target] = send[half * tok_count : (half + 1) * tok_count]

        heads = jnp.concatenate([heads_ref[2 * p], heads_ref[2 * p + 1]], axis=0)
        w_grad_ref[lanes, :] = tn_dot(heads, grad).astype(BF16)

    @pl.when(n == steps - 1)
    def _():
        for other_index in range(blk_count):

            @pl.when(other_index != index)
            def _():
                do_copy(other_index, other_index).wait()

        grad_heads_ref[...] = do_got[...]


def column_streams(line, bits, each, units):
    late = each // 4
    zs = line_bits(line)
    names = zs[::-1] + bits
    return [
        Stream(bits[::-1] + zs, names, (each - late, FF_TILE), LAG, units),
        Stream(bits + zs, names, (each - late, FF_TILE), LAG, units),
        Stream(zs + bits, names, (late, 2 * FF_TILE), LAG, units),
    ]


def middle_layer(line, bits, tokens, heads, w_out, gain, dy_own, dy_got, w_gate, w_up, w_down):
    own_rows, width = tokens.shape
    rows = 2 * own_rows
    blk_count, tok_count, head_lanes = heads.shape
    units = w_gate.shape[1] // 2 // FF_TILE
    chips = line * 2 ** len(bits)
    each = width // chips
    streams = column_streams(line, bits, each, units)
    steps = max([1 + stream.steps() for stream in streams] + [units + 3 + blk_count // 2])

    def keep(shape):
        return pl.BlockSpec(shape, lambda n: (0,) * len(shape), pipeline_mode=pl.Buffered(1))

    def tile(n):
        return jnp.clip(n - 1, 0, units - 1)

    def mine(n):
        return lax.rem(lax.axis_index("blk"), 2) * units + tile(n)

    scratch = [
        pltpu.VMEM((rows, width), BF16),
        pltpu.VMEM((width, rows), BF16),
        pltpu.VMEM((rows, width), F32),
        pltpu.VMEM((rows, width), F32),
        pltpu.VMEM((rows, FF_TILE), BF16),
        pltpu.VMEM((rows, FF_TILE), BF16),
        pltpu.VMEM((2, own_rows, width), BF16),
        pltpu.VMEM((2, own_rows, width), BF16),
        pltpu.VMEM((own_rows, width), BF16),
        pltpu.VMEM(heads.shape, BF16),
        pltpu.VMEM(heads.shape, BF16),
        pltpu.SemaphoreType.DMA((2,)),
        pltpu.SemaphoreType.DMA((2,)),
        pltpu.SemaphoreType.DMA((2,)),
        pltpu.SemaphoreType.DMA((blk_count,)),
        pltpu.SemaphoreType.DMA((blk_count,)),
    ]
    for stream in streams:
        scratch += stream.scratch()
    outs = [
        ((own_rows, width), BF16),
        ((own_rows, width), F32),
        ((1, width), F32),
        (w_out.shape, BF16),
        (heads.shape, BF16),
        ((units * FF_TILE, rows), BF16),
        ((each, units * FF_TILE), BF16),
        ((each, units * FF_TILE), BF16),
    ]
    out_specs = [keep(shape) for shape, unused in outs]
    out_specs[5] = pl.BlockSpec((FF_TILE, rows), lambda n: (tile(n), 0))
    return pl.pallas_call(
        functools.partial(middle_kernel, line, bits, streams, units),
        name="middle",
        grid=(steps,),
        in_specs=[
            keep(tokens.shape),
            keep(heads.shape),
            keep(w_out.shape),
            keep(gain.shape),
            keep(dy_own.shape),
            keep(dy_got.shape),
            pl.BlockSpec((width, FF_TILE), lambda n: (0, mine(n))),
            pl.BlockSpec((width, FF_TILE), lambda n: (0, mine(n))),
            pl.BlockSpec((FF_TILE, width), lambda n: (mine(n), 0)),
        ],
        out_specs=out_specs,
        out_shape=[jax.ShapeDtypeStruct(shape, kind) for shape, kind in outs],
        scratch_shapes=scratch,
        compiler_params=kernel_params(collective_id=6, has_side_effects=True),
    )(tokens, heads, w_out, gain, dy_own, dy_got, w_gate, w_up, w_down)


def back_kernel(
    groups,
    block,
    line,
    bits,
    streams,
    units,
    qkv_ref,
    logs_ref,
    out_ref,
    grad_ref,
    starts_ref,
    dy_own_ref,
    dy_got_ref,
    acts_ref,
    w_out_parts_ref,
    moved_ref,
    down_out_ref,
    w_out_ref,
    queries,
    keys,
    values,
    grads,
    query_grad,
    pair_grad,
    result,
    moved,
    sent_sem,
    got_sem,
    *refs,
):
    size = qkv_ref.shape[0]
    blocks = size // block
    q_width = groups * LANES
    n = pl.program_id(0)
    index = lax.axis_index("blk")
    core = lax.rem(index, 2)

    def move(g, target, source):
        return blk_copy(result.at[g], moved.at[g], sent_sem.at[g], got_sem.at[g], target, source)

    half = streams[0].block[1]

    def finish_low(u, value):
        rows = value.shape[0]
        down_out_ref[pl.ds(pl.multiple_of(u * rows, rows), rows), :half] = value

    def finish_high(u, value):
        rows = value.shape[0]
        down_out_ref[pl.ds(pl.multiple_of(u * rows, rows), rows), half:] = value

    def finish_w_out(u, value):
        w_out_ref[:, pl.ds(pl.multiple_of(u * LANES, LANES), LANES)] = value

    columns = w_out_ref.shape[1] // LANES
    at = 0
    for stream, finish in zip(streams, (finish_low, finish_high, finish_w_out)):
        size_of = len(stream.scratch())
        stream.bind(refs[at : at + size_of], finish)
        at += size_of

    @pl.when(n == 0)
    def _():
        greet_all(blocks, line)

    step_streams(streams, n)

    @pl.when(n == 1)
    def _():
        query_grad[...] = jnp.zeros_like(query_grad)
        pair_grad[...] = jnp.zeros_like(pair_grad)
        for g in range(groups):
            lanes = slice(g * LANES, (g + 1) * LANES)
            keys[g, :, :LANES] = doubled(qkv_ref[:, q_width : q_width + LANES], g)
            keys[g, :, LANES:] = minus_three(size)
            values[g, :, :LANES] = doubled(qkv_ref[:, q_width + LANES : q_width + 2 * LANES], g)
            values[g, :, LANES:] = minus_three(size)

            def fill(i, carry):
                at = pl.multiple_of(i * block, block)
                to = pl.multiple_of(i * 2 * block, 2 * block)
                queries[g, pl.ds(to, 2 * block), :LANES] = stacked_heads(qkv_ref[pl.ds(at, block), lanes])
                queries[g, pl.ds(to, 2 * block), LANES:] = logs_ref[g, pl.ds(to, 2 * block), :]
                grad = stacked_heads(grad_ref[pl.ds(at, block), lanes])
                mean = stacked_heads(out_ref[pl.ds(at, block), lanes])
                delta = jnp.sum(grad.astype(F32) * mean.astype(F32), axis=1, keepdims=True)
                grads[g, pl.ds(to, 2 * block), :LANES] = grad
                grads[g, pl.ds(to, 2 * block), LANES:] = in_three(delta)
                return carry

            lax.fori_loop(0, blocks, fill, 0)

    @pl.when(n < units)
    def _():
        acts = acts_ref[...].reshape(-1, acts_ref.shape[-1])
        rows = dy_own_ref.shape[0]
        made = nn_dot(acts[:, :rows], dy_own_ref[...]) + nn_dot(acts[:, rows:], dy_got_ref[...])
        made = made.astype(BF16)
        for i, stream in enumerate(streams[:2]):
            shape = stream.shape(stream.names[0])[1:]
            for side in range(2):
                at = (2 * side + i) * half
                stream.source[stream.slot(n), side] = made[:, at : at + half].reshape(shape)

    @pl.when(n < columns)
    def _():
        stream = streams[2]
        stream.source[stream.slot(n)] = w_out_parts_ref[...].reshape(stream.shape(stream.names[0]))

    row = lax.broadcasted_iota(jnp.int32, (block, 2 * block), 0)
    column = lax.broadcasted_iota(jnp.int32, (block, 2 * block), 1) % block

    pairs = (blocks + 1) * (blocks // 2)
    each = ATTEND_PAIRS
    rounds = groups * pairs // each

    @pl.when((n >= 1) & (n <= rounds))
    def _():
        def pair(at, carry):
            number = (n - 1) * each + at
            g = number // pairs
            place = lax.rem(number, pairs)
            turn = place // (blocks // 2)
            m = lax.rem(place, blocks // 2)
            late = (turn + m) // blocks
            j = m + late * (blocks - 1 - 2 * m)
            i = (1 - late) * (m + turn) + late * (turn - 1)
            key_at = pl.multiple_of(j * block, block)
            at = pl.multiple_of(i * 2 * block, 2 * block)
            key_rows = pl.ds(key_at, block)
            stack = pl.ds(at, 2 * block)
            allowed = (row >= starts_ref[:, stack] - key_at) & (row - column <= (i - j) * block)
            query = queries[g, stack, :]
            grad = grads[g, stack, :]
            key = keys[g, key_rows, :]
            scores = nt_dot(key, query)
            probs = jnp.exp2(jnp.where(allowed, scores, MASKED))
            pushed = (probs * nt_dot(values[g, key_rows, :], grad)).astype(BF16)
            pair_grad[g, key_rows, LANES:] += nn_dot(probs.astype(BF16), grad[:, :LANES])
            pair_grad[g, key_rows, :LANES] += nn_dot(pushed, query[:, :LANES])
            query_grad[g, stack, :] += tn_dot(pushed, key[:, :LANES])
            return carry

        lax.fori_loop(0, each, pair, 0, unroll=True)

    for g in range(groups):

        @pl.when(n == (g + 1) * rounds // groups + 1)
        def _():
            low = low_lanes((block, LANES))

            def finish(i, carry):
                at = pl.multiple_of(i * block, block)
                to = pl.multiple_of(i * 2 * block, 2 * block)
                here = pl.ds(at, block)
                first = query_grad[g, pl.ds(to, block), :]
                second = query_grad[g, pl.ds(to + block, block), :]
                joined = jnp.where(low, first, second) * HEAD_DIM ** (-0.5)
                result[g, i, :, :LANES] = joined.astype(BF16)
                key = pair_grad[g, here, :LANES] * (1.0 / LOG2_E)
                value = pair_grad[g, here, LANES:]
                key = key + pltpu.roll(key, HEAD_DIM, 1)
                value = value + pltpu.roll(value, HEAD_DIM, 1)
                result[g, i, :, LANES:] = jnp.where(low, key, value).astype(BF16)
                return carry

            lax.fori_loop(0, blocks, finish, 0)
            for step in range(blocks - 1, 0, -1):
                move(g, lax.rem(index + step, blocks), index).start()
            moved[g, index] = result[g, index]

    @pl.when(n == pl.num_programs(0) - 1)
    def _():
        for g in range(groups):
            for step in range(1, blocks):
                other = lax.rem(index + step, blocks)
                move(g, other, other).wait()
            moved_ref[:, :, 2 * g * LANES : 2 * (g + 1) * LANES] = moved[g]


def back(line, bits, qkv, logs, out, grad, starts, block, dy_own, dy_got, acts, w_out_parts):
    size, width = qkv.shape
    groups = (width - 2 * LANES) // LANES
    model = dy_own.shape[1]
    rows = acts.shape[1]
    units = acts.shape[0] // FF_TILE
    chips = line * 2 ** len(bits)
    down_rows = acts.shape[0] // (chips // 2)
    down_each = down_rows // units
    w_rows = w_out_parts.shape[0] // chips // 2
    columns = w_out_parts.shape[1] // LANES
    zs = line_bits(line)
    names = [1] + zs[-2::-1] + bits
    streams = [
        Stream([1] + bits[::-1] + zs, names, (down_each, model // 4), LAG, units, swap=zs[-1]),
        Stream([1] + bits + zs, names, (down_each, model // 4), LAG, units, swap=zs[-1]),
        Stream([1] + zs + bits, zs[::-1] + bits + [1], (w_rows, LANES), LAG, columns),
    ]
    steps = max(
        [stream.steps() for stream in streams]
        + [groups * (size // block + 1) * (size // block // 2) // ATTEND_PAIRS + 3]
    )

    def keep(shape):
        return pl.BlockSpec(shape, lambda n: (0,) * len(shape), pipeline_mode=pl.Buffered(1))

    acts = acts.reshape(chips // 2, down_rows, rows)
    scratch = [
        pltpu.VMEM((groups, 2 * size, 2 * LANES), BF16),
        pltpu.VMEM((groups, size, 2 * LANES), BF16),
        pltpu.VMEM((groups, size, 2 * LANES), BF16),
        pltpu.VMEM((groups, 2 * size, 2 * LANES), BF16),
        pltpu.VMEM((groups, 2 * size, LANES), F32),
        pltpu.VMEM((groups, size, 2 * LANES), F32),
        pltpu.VMEM((groups, size // block, block, 2 * LANES), BF16),
        pltpu.VMEM((groups, size // block, block, 2 * LANES), BF16),
        pltpu.SemaphoreType.DMA((groups, size // block)),
        pltpu.SemaphoreType.DMA((groups, size // block)),
    ]
    for stream in streams:
        scratch += stream.scratch()

    outs = [
        (size // block, block, width),
        (down_rows, model // 2),
        (w_rows, w_out_parts.shape[1]),
    ]
    return pl.pallas_call(
        functools.partial(back_kernel, groups, block, line, bits, streams, units),
        name="back",
        grid=(steps,),
        in_specs=[
            keep(qkv.shape),
            keep(logs.shape),
            keep(out.shape),
            keep(grad.shape),
            keep(starts.shape),
            keep(dy_own.shape),
            keep(dy_got.shape),
            pl.BlockSpec(
                (chips // 2, down_each, rows), lambda n: (0, jnp.minimum(n, units - 1), 0)
            ),
            pl.BlockSpec((w_out_parts.shape[0], LANES), lambda n: (0, jnp.minimum(n, columns - 1))),
        ],
        out_specs=[keep(shape) for shape in outs],
        out_shape=[jax.ShapeDtypeStruct(shape, BF16) for shape in outs],
        scratch_shapes=scratch,
        compiler_params=kernel_params(collective_id=4, has_side_effects=True),
    )(qkv, logs, out, grad, starts, dy_own, dy_got, acts, w_out_parts)


def sum_gains(rounds, n, first, gains, gains_got, sent_sem, got_sem):
    for r, partner in enumerate(rounds):

        def copy():
            return pltpu.make_async_remote_copy(
                src_ref=gains.at[r],
                dst_ref=gains_got.at[r],
                send_sem=sent_sem.at[r],
                recv_sem=got_sem.at[r],
                device_id=partner,
                device_id_type=pl.DeviceIdType.MESH,
            )

        @pl.when(n == first + r + 1)
        def _():
            copy().wait()
            gains[r + 1] = gains[r] + gains_got[r]

    for r, partner in enumerate(rounds):

        @pl.when(n == first + r)
        def _():
            pltpu.make_async_remote_copy(
                src_ref=gains.at[r],
                dst_ref=gains_got.at[r],
                send_sem=sent_sem.at[r],
                recv_sem=got_sem.at[r],
                device_id=partner,
                device_id_type=pl.DeviceIdType.MESH,
            ).start()


def finish_kernel(
    line,
    bits,
    streams,
    units,
    got_ref,
    proj_ref,
    hidden_ref,
    tokens_ref,
    mid_ref,
    gain_ref,
    wq_ref,
    wk_ref,
    wv_ref,
    q_gain_ref,
    k_gain_ref,
    cos_ref,
    sin_ref,
    ffn_gain_ref,
    gate_ref,
    up_ref,
    down_ref,
    input_ref,
    gains_ref,
    gq_ref,
    gk_ref,
    gv_ref,
    gate_out_ref,
    up_out_ref,
    down_out_ref,
    total,
    gains,
    gains_got,
    gains_sent_sem,
    gains_got_sem,
    half_got,
    down_got,
    half_sent_sem,
    half_got_sem,
    *refs,
):
    n = pl.program_id(0)
    z, index = lax.axis_index("dp"), lax.axis_index("blk")
    core, sibling = pair_of(1)
    steps = pl.num_programs(0)
    query_stream, pair_stream = streams
    q_width = wq_ref.shape[1]

    def finish_query(u, value):
        gq_ref[:, pl.ds(pl.multiple_of(u * q_width, q_width), q_width)] = value

    def finish_pair(u, value):
        here = pl.ds(pl.multiple_of(u * LANES, LANES), LANES)
        gk_ref[:, here] = value[:, :LANES]
        gv_ref[:, here] = value[:, LANES:]

    at = 0
    for stream, finish in ((query_stream, finish_query), (pair_stream, finish_pair)):
        count = len(stream.scratch())
        stream.bind(refs[at : at + count], finish)
        at += count

    rounds = [pair_of(name)[1] for name in [1] + list(bits) + line_bits(line)]

    rows = gate_ref.shape[0] // 2
    columns = gate_ref.shape[1]
    down_rows = down_ref.shape[0] // 2
    give = pl.ds(pl.multiple_of((1 - core) * rows, rows), rows)
    keep = pl.ds(pl.multiple_of(core * rows, rows), rows)
    down_give = pl.ds(pl.multiple_of((1 - core) * down_rows, down_rows), down_rows)
    down_keep = pl.ds(pl.multiple_of(core * down_rows, down_rows), down_rows)

    def half_copies():
        sources = (gate_ref.at[give, :], up_ref.at[give, :], down_ref.at[down_give, :])
        targets = (half_got.at[0], half_got.at[1], down_got)
        return [
            pltpu.make_async_remote_copy(
                src_ref=source,
                dst_ref=target,
                send_sem=half_sent_sem.at[i],
                recv_sem=half_got_sem.at[i],
                device_id=sibling,
                device_id_type=pl.DeviceIdType.MESH,
            )
            for i, (source, target) in enumerate(zip(sources, targets))
        ]

    @pl.when(n == 0)
    def _():
        barrier = pltpu.get_barrier_semaphore()
        for peer in rounds:
            pl.semaphore_signal(barrier, inc=1, device_id=peer, device_id_type=pl.DeviceIdType.MESH)
        pl.semaphore_wait(barrier, len(rounds))
        for copy in half_copies():
            copy.start()
        total[...] = jnp.zeros_like(total)
        gains[0] = jnp.zeros_like(gains[0])

    @pl.when(n == units)
    def _():
        for copy in half_copies():
            copy.wait()
        own = pl.ds(pl.multiple_of(core * columns, LANES), columns)
        other = pl.ds(pl.multiple_of((1 - core) * columns, LANES), columns)
        gate_out_ref[:, own] = gate_ref[keep, :]
        gate_out_ref[:, other] = half_got[0]
        up_out_ref[:, own] = up_ref[keep, :]
        up_out_ref[:, other] = half_got[1]
        half = down_ref.shape[1]
        down_out_ref[:, pl.ds(pl.multiple_of(core * half, LANES), half)] = down_ref[down_keep, :]
        down_out_ref[:, pl.ds(pl.multiple_of((1 - core) * half, LANES), half)] = down_got[...]

    step_streams(streams, n)
    sum_gains(rounds, n, units, gains, gains_got, gains_sent_sem, gains_got_sem)

    @pl.when(n == steps - 1)
    def _():
        gains_ref[...] = gains[len(rounds)]

    @pl.when(n < units)
    def _():
        hidden = hidden_ref[...]

        def got_lanes(lane):
            return jnp.concatenate(
                [got_ref[0, :, lane : lane + LANES], got_ref[1, :, lane : lane + LANES]], axis=0
            ).astype(F32)

        def back(got, lane, head_gain, place):
            turned = got * cos_ref[...] - half_partner(got) * sin_ref[...]
            block = proj_ref[0, :, lane : lane + LANES]
            scale = lax.rsqrt(head_means(block * block) + EPSILON)
            normal = block * scale
            gains[0, place : place + 1, :] += jnp.sum(turned * normal, axis=0, keepdims=True)
            pushed = turned * head_gain[...]
            inner = head_means(pushed * normal)
            return (scale * (pushed - normal * inner)).astype(BF16)

        width = tokens_ref.shape[1]
        lines = width // LANES
        query = jnp.concatenate(
            [back(got_lanes(2 * at), at, q_gain_ref, 2 * lines) for at in range(0, q_width, LANES)],
            axis=1,
        )
        first, second = got_lanes(LANES), got_lanes(3 * LANES)
        low = low_lanes(first.shape)
        key = jnp.where(low, first, pltpu.roll(second, HEAD_DIM, 1))
        key = back(key, q_width, k_gain_ref, 2 * lines + 1)
        value = jnp.where(low, pltpu.roll(first, HEAD_DIM, 1), second).astype(BF16)
        for stream, part in ((query_stream, query), (pair_stream, jnp.concatenate([key, value], axis=1))):
            shape = stream.shape(stream.names[0])
            stream.source[stream.slot(n)] = tn_dot(hidden, part).astype(BF16).reshape(shape)

        total[...] += (
            nt_dot(query, wq_ref[...]) + nt_dot(key, wk_ref[...]) + nt_dot(value, wv_ref[...])
        )

        @pl.when(n == units - 1)
        def _():
            inputs = tokens_ref[...].astype(F32)
            scale = lax.rsqrt(jnp.mean(inputs * inputs, axis=-1, keepdims=True) + EPSILON)
            normal = inputs * scale
            grad = total[...]
            gain_grad = jnp.sum(grad * normal, axis=0, keepdims=True)
            for i in range(lines):
                here = slice(i * LANES, (i + 1) * LANES)
                gains[0, i : i + 1, :] = gain_grad[:, here]
                gains[0, lines + i : lines + i + 1, :] = ffn_gain_ref[:, here]
            pushed = grad * gain_ref[...]
            inner = jnp.mean(pushed * normal, axis=-1, keepdims=True)
            input_ref[...] = (mid_ref[...] + scale * (pushed - normal * inner)).astype(BF16)


def finish(
    line,
    bits,
    got,
    proj,
    hidden,
    tokens,
    mid,
    gain,
    wq,
    wk,
    wv,
    q_gain,
    k_gain,
    cosine,
    sine,
    ffn_gain,
    gate_sum,
    up_sum,
    down_sum,
):
    rows, width = tokens.shape
    count, half, lanes = got.shape
    units = count // 2
    q_width = wq.shape[1] // units
    chips = line * 2 ** len(bits)
    mine = width // chips // 2
    zs = line_bits(line)
    names = zs[::-1] + bits + [1]
    streams = [
        Stream([1] + bits[::-1] + zs, names, (mine, q_width), LAST_LAG, units),
        Stream([1] + bits + zs, names, (mine, 2 * LANES), LAST_LAG, units),
    ]
    rounds = 1 + len(bits) + (line - 1).bit_length()
    steps = max([stream.steps() for stream in streams] + [units + rounds + 2])
    gain_rows = -(-(2 * width // LANES + 2) // 8) * 8
    half_rows = gate_sum.shape[0] // 2
    down_rows = down_sum.shape[0] // 2
    columns = gate_sum.shape[1]

    def keep(shape):
        return pl.BlockSpec(shape, lambda n: (0,) * len(shape), pipeline_mode=pl.Buffered(1))

    def at(n):
        return jnp.minimum(n, units - 1)

    scratch = [
        pltpu.VMEM((rows, width), F32),
        pltpu.VMEM((rounds + 1, gain_rows, LANES), F32),
        pltpu.VMEM((rounds, gain_rows, LANES), F32),
        pltpu.SemaphoreType.DMA((rounds,)),
        pltpu.SemaphoreType.DMA((rounds,)),
        pltpu.VMEM((2, half_rows, columns), BF16),
        pltpu.VMEM((down_rows, down_sum.shape[1]), BF16),
        pltpu.SemaphoreType.DMA((3,)),
        pltpu.SemaphoreType.DMA((3,)),
    ]
    for stream in streams:
        scratch += stream.scratch()
    outs = [
        ((rows, width), BF16),
        ((gain_rows, LANES), F32),
        ((mine, wq.shape[1]), BF16),
        ((mine, wk.shape[1]), BF16),
        ((mine, wv.shape[1]), BF16),
        ((half_rows, 2 * columns), BF16),
        ((half_rows, 2 * columns), BF16),
        ((down_rows, 2 * down_sum.shape[1]), BF16),
    ]
    return pl.pallas_call(
        functools.partial(finish_kernel, line, bits, streams, units),
        name="finish",
        grid=(steps,),
        in_specs=[
            pl.BlockSpec((2, half, lanes), lambda n: (at(n), 0, 0)),
            pl.BlockSpec((1, rows, q_width + LANES), lambda n: (at(n), 0, 0)),
            keep((rows, width)),
            keep((rows, width)),
            keep((rows, width)),
            keep((1, width)),
            pl.BlockSpec((width, q_width), lambda n: (0, at(n))),
            pl.BlockSpec((width, LANES), lambda n: (0, at(n))),
            pl.BlockSpec((width, LANES), lambda n: (0, at(n))),
            keep((1, LANES)),
            keep((1, LANES)),
            keep((rows, LANES)),
            keep((rows, LANES)),
            keep((1, width)),
            keep(gate_sum.shape),
            keep(up_sum.shape),
            keep(down_sum.shape),
        ],
        out_specs=[keep(shape) for shape, unused in outs],
        out_shape=[jax.ShapeDtypeStruct(shape, kind) for shape, kind in outs],
        scratch_shapes=scratch,
        compiler_params=kernel_params(collective_id=5, has_side_effects=True),
    )(
        got,
        proj,
        hidden,
        tokens,
        mid,
        gain,
        wq,
        wk,
        wv,
        q_gain,
        k_gain,
        cosine,
        sine,
        ffn_gain,
        gate_sum,
        up_sum,
        down_sum,
    )


def widen_kernel(count, gains_ref, *refs):
    for source, target in zip(refs[:count], refs[count : 2 * count]):
        target[...] = source[...].astype(F32)
    attn_ref, ffn_ref, heads_ref = refs[2 * count :]
    lines = attn_ref.shape[0]
    attn_ref[...] = gains_ref[:lines, :]
    ffn_ref[...] = gains_ref[lines : 2 * lines, :]
    both = gains_ref[2 * lines : 2 * lines + 2, :]
    heads_ref[...] = both + pltpu.roll(both, HEAD_DIM, 1)


def widen(gains, lines, parts):
    shapes = [part.shape for part in parts] + [(lines, LANES), (lines, LANES), (2, LANES)]
    return pl.pallas_call(
        functools.partial(widen_kernel, len(parts)),
        name="widen",
        out_shape=[jax.ShapeDtypeStruct(shape, F32) for shape in shapes],
        compiler_params=kernel_params(),
    )(gains, *parts)


def flip_pairs(count, bit):
    return [(i, i ^ bit) for i in range(count)]


def swap_core(block, blk_count):
    return lax.ppermute(block, "blk", flip_pairs(blk_count, 1))


def fast_local(
    dp_count,
    blk_count,
    tokens,
    doc_lengths,
    g_attn,
    w_query,
    w_key,
    w_value,
    q_gain,
    k_gain,
    w_out,
    g_ffn,
    w_gate,
    w_up,
    w_down,
    cotangent,
):
    row_count, tok_count, width = tokens.shape
    rows = row_count * tok_count
    chips = blk_count // 2
    size = tok_count * blk_count
    index = lax.axis_index("blk")
    core = index % 2
    bits = []
    bit = blk_count // 2
    while bit > 1:
        bits.append(bit)
        bit //= 2
    chip_dims = (dp_count,) + (2,) * len(bits)
    all_chips = dp_count * chips
    which = jnp.arange(doc_lengths.shape[1])
    ends = jnp.sum(jnp.where(which[:, None] <= which[None, :], doc_lengths[:, :, None], 0), axis=1)
    places = index * tok_count + jnp.arange(tok_count, dtype=jnp.int32)[None]
    begins = jnp.max(jnp.where(places[:, :, None] >= ends[:, None, :], ends[:, None, :], 0), axis=2)
    positions = (places - begins).reshape(rows, 1).astype(F32)
    half_head = HEAD_DIM // 2
    lane = jnp.arange(LANES)
    freqs = ROPE_BASE ** (-(lane % half_head).astype(F32) / half_head)
    angles = positions * freqs
    cosine = jnp.cos(angles)
    sine = jnp.sin(angles) * jnp.where(lane % HEAD_DIM < half_head, -1.0, 1.0)
    q_gain2 = jnp.tile(q_gain, 2)[None]
    k_gain2 = jnp.tile(k_gain, 2)[None]
    all_places = jnp.arange(size, dtype=jnp.int32)
    own_ends = lax.dynamic_slice_in_dim(ends, core, 1, axis=0)
    starts = jnp.max(jnp.where(all_places[:, None] >= own_ends, own_ends, 0), axis=1)
    starts_two = jnp.broadcast_to(
        starts.reshape(blk_count, 1, tok_count), (blk_count, 2, tok_count)
    ).reshape(1, 2 * size)
    flat = tokens.reshape(rows, width)
    grad_own = cotangent.reshape(rows, width)
    grad_got = swap_core(grad_own, blk_count)

    hidden_in, proj, qkv = project(
        flat, g_attn[None], w_query, w_key, w_value, q_gain2, k_gain2, cosine, sine
    )
    qkv = qkv.reshape(size, -1)
    attended, logs, heads = attend(qkv, starts[:, None], tok_count)
    output, mid, ffn_gain_grad, w_out_parts, grad_heads, acts, gate_sum, up_sum = middle_layer(
        dp_count,
        bits,
        flat,
        heads,
        w_out,
        g_ffn[None],
        grad_own,
        grad_got,
        w_gate,
        w_up,
        w_down,
    )
    got, down_sum, w_out_sum = back(
        dp_count,
        bits,
        qkv,
        logs,
        attended.reshape(size, -1),
        grad_heads.reshape(size, -1),
        starts_two,
        tok_count,
        grad_own,
        grad_got,
        acts,
        w_out_parts,
    )
    input_grad, gains, *sums = finish(
        dp_count,
        bits,
        got,
        proj,
        hidden_in,
        flat,
        mid,
        g_attn[None],
        w_query,
        w_key,
        w_value,
        q_gain2,
        k_gain2,
        cosine,
        sine,
        ffn_gain_grad,
        gate_sum,
        up_sum,
        down_sum,
    )
    *sums, gain_attn, gain_ffn, gain_heads = widen(gains, width // LANES, sums + [w_out_sum])
    grad_w_query, grad_w_key, grad_w_value, grad_w_gate, grad_w_up, grad_w_down, grad_w_out = sums
    gain_attn, gain_ffn = gain_attn.reshape(width), gain_ffn.reshape(width)
    gain_query, gain_key = gain_heads[0, :HEAD_DIM], gain_heads[1, :HEAD_DIM]
    return (
        output.reshape(tokens.shape),
        input_grad.reshape(tokens.shape),
        gain_attn,
        grad_w_query,
        grad_w_key,
        grad_w_value,
        gain_query,
        gain_key,
        grad_w_out,
        gain_ffn,
        grad_w_gate,
        grad_w_up,
        grad_w_down,
    )


def fits(mesh):
    blk_count = mesh.shape["blk"]
    chips = blk_count // 2
    line = mesh.shape["dp"]
    power = blk_count & (blk_count - 1) == 0 and line & (line - 1) == 0
    return power and blk_count > 2 and line > 1 and (KV_HEADS * HEAD_DIM) == chips * LANES


def solution(mesh):
    if fits(mesh):
        body = functools.partial(fast_local, mesh.shape["dp"], mesh.shape["blk"])
    else:
        body = local
    return jax.shard_map(
        body,
        mesh=mesh,
        in_specs=(
            P("dp", "blk", None),
            P("dp", None),
            P(),
            P(),
            P(),
            P(),
            P(),
            P(),
            P(),
            P(),
            P(),
            P(),
            P(),
            P("dp", "blk", None),
        ),
        out_specs=(
            P("dp", "blk", None),
            P("dp", "blk", None),
            P(),
            P(("dp", "blk"), None),
            P(("dp", "blk"), None),
            P(("dp", "blk"), None),
            P(),
            P(),
            P(("dp", "blk"), None),
            P(),
            P(("dp", "blk"), None),
            P(("dp", "blk"), None),
            P(("dp", "blk"), None),
        ),
        check_vma=False,
    )
```

```python
import functools
import math

import jax
import jax.numpy as jnp
from jax import lax
from jax.experimental import pallas as pl
from jax.experimental.pallas import tpu as pltpu
from jax.sharding import PartitionSpec as P

HEADS = 16
KV_HEADS = 8
HEAD_DIM = 64


EPSILON = 1e-05
ROPE_BASE = 1000000.0
NEGATIVE = -1e30


def norm_rows(values, norm_gain):
    row_scale = lax.rsqrt(jnp.mean(values * values, axis=-1, keepdims=True) + EPSILON)
    normal = values * row_scale
    return (normal * norm_gain, normal, row_scale)


def norm_back(normal, row_scale, norm_gain, grad_out):
    pushed = grad_out * norm_gain
    inner = jnp.mean(pushed * normal, axis=-1, keepdims=True)
    grad_in = row_scale * (pushed - normal * inner)
    leading = tuple(range(grad_out.ndim - 1))
    return (grad_in, jnp.sum(grad_out * normal, axis=leading))


def doc_layout(lengths, places):
    ends = jnp.cumsum(lengths, axis=1)
    past = places[None, :, None] >= ends[:, None, :]
    docs = jnp.sum(past.astype(jnp.int32), axis=2)
    before = jnp.sum(jnp.where(past, lengths[:, None, :], 0), axis=2)
    return (docs, places[None, :] - before)


def rope_angles(positions):
    half = HEAD_DIM // 2
    freqs = ROPE_BASE ** (-jnp.arange(half, dtype=jnp.float32) / half)
    angles = positions.astype(jnp.float32)[..., None] * freqs
    return (jnp.cos(angles), jnp.sin(angles))


def rotate(values, cosine, sine):
    half = values.shape[-1] // 2
    first_half = values[..., :half]
    second_half = values[..., half:]
    cos_col = cosine[:, :, None, :]
    sin_col = sine[:, :, None, :]
    return jnp.concatenate(
        [
            first_half * cos_col - second_half * sin_col,
            second_half * cos_col + first_half * sin_col,
        ],
        axis=-1,
    )


def local(
    tokens,
    doc_lengths,
    g_attn,
    w_query,
    w_key,
    w_value,
    q_gain,
    k_gain,
    w_out,
    g_ffn,
    w_gate,
    w_up,
    w_down,
    cotangent,
):
    row_count, tok_count, width = tokens.shape
    grouping = HEADS // KV_HEADS
    flat_rows = row_count * tok_count
    kv_width = KV_HEADS * HEAD_DIM
    softmax_scale = HEAD_DIM ** (-0.5)
    places = lax.axis_index("blk") * tok_count + jnp.arange(tok_count, dtype=jnp.int32)
    query_docs, query_pos = doc_layout(doc_lengths, places)
    cosine, sine = rope_angles(query_pos)
    inputs = tokens.reshape(flat_rows, width).astype(jnp.float32)
    normed, normal_in, scale_in = norm_rows(inputs, g_attn)
    hidden_in = normed.astype(jnp.bfloat16)
    query_proj = jnp.dot(hidden_in, w_query, preferred_element_type=jnp.float32).reshape(
        row_count, tok_count, HEADS, HEAD_DIM
    )
    key_proj = jnp.dot(hidden_in, w_key, preferred_element_type=jnp.float32).reshape(
        row_count, tok_count, KV_HEADS, HEAD_DIM
    )
    value_b = (
        jnp.dot(hidden_in, w_value, preferred_element_type=jnp.float32)
        .astype(jnp.bfloat16)
        .reshape(row_count, tok_count, kv_width)
    )
    query_norm, query_normal, query_scale = norm_rows(query_proj, q_gain)
    key_norm, key_normal, key_scale = norm_rows(key_proj, k_gain)
    query_b = (
        rotate(query_norm, cosine, sine)
        .astype(jnp.bfloat16)
        .reshape(row_count, tok_count, KV_HEADS, grouping, HEAD_DIM)
    )
    key_b = (
        rotate(key_norm, cosine, sine).astype(jnp.bfloat16).reshape(row_count, tok_count, kv_width)
    )

    def piece_mask(size):
        key_places = jnp.arange(size, dtype=jnp.int32)
        key_docs, unused = doc_layout(doc_lengths, key_places)
        return (key_places[None, None, :] <= places[None, :, None]) & (
            key_docs[:, None, :] == query_docs[:, :, None]
        )

    def piece_scores(key_piece, allowed):
        key_heads = key_piece.reshape(row_count, key_piece.shape[1], KV_HEADS, HEAD_DIM)
        raw_scores = (
            jnp.einsum("rqkgd,rpkd->rkgqp", query_b, key_heads, preferred_element_type=jnp.float32)
            * softmax_scale
        )
        return (jnp.where(allowed[:, None, None], raw_scores, -jnp.inf), key_heads)

    stat_shape = (row_count, KV_HEADS, grouping, tok_count)
    key_piece = lax.all_gather(key_b, "blk", axis=1, tiled=True)
    value_piece = lax.all_gather(value_b, "blk", axis=1, tiled=True)
    allowed = piece_mask(key_piece.shape[1])
    running_max = jnp.full(stat_shape, NEGATIVE, jnp.float32)
    scores, key_heads = piece_scores(key_piece, allowed)
    new_max = jnp.maximum(running_max, jnp.max(scores, axis=-1))
    weights = jnp.exp(scores - new_max[..., None])
    value_heads = value_piece.reshape(row_count, value_piece.shape[1], KV_HEADS, HEAD_DIM)
    added = jnp.einsum(
        "rkgqp,rpkd->rkgqd",
        weights.astype(jnp.bfloat16),
        value_heads,
        preferred_element_type=jnp.float32,
    )
    running_sum = jnp.sum(weights, axis=-1)
    attended = added / running_sum[..., None]
    log_total = new_max + jnp.log(running_sum)
    attended_b = (
        jnp.transpose(attended, (0, 3, 1, 2, 4))
        .reshape(flat_rows, HEADS * HEAD_DIM)
        .astype(jnp.bfloat16)
    )
    middle = inputs + jnp.dot(attended_b, w_out, preferred_element_type=jnp.float32)
    normed_ffn, normal_ffn, scale_ffn = norm_rows(middle, g_ffn)
    hidden_ffn = normed_ffn.astype(jnp.bfloat16)
    gate = jnp.dot(hidden_ffn, w_gate, preferred_element_type=jnp.float32)
    up_proj = jnp.dot(hidden_ffn, w_up, preferred_element_type=jnp.float32)
    sigmoid_gate = jax.nn.sigmoid(gate)
    silu_gate = gate * sigmoid_gate
    hidden = (silu_gate * up_proj).astype(jnp.bfloat16)
    result = middle + jnp.dot(hidden, w_down, preferred_element_type=jnp.float32)
    output = result.astype(jnp.bfloat16).reshape(row_count, tok_count, width)
    grad_out = cotangent.reshape(flat_rows, width)
    grad_w_down = jnp.einsum("tf,td->fd", hidden, grad_out, preferred_element_type=jnp.float32)
    grad_hidden = jnp.einsum("td,fd->tf", grad_out, w_down, preferred_element_type=jnp.float32)
    grad_gate = (grad_hidden * up_proj * sigmoid_gate * (1.0 + gate * (1.0 - sigmoid_gate))).astype(
        jnp.bfloat16
    )
    grad_up = (grad_hidden * silu_gate).astype(jnp.bfloat16)
    grad_w_gate = jnp.einsum("td,tf->df", hidden_ffn, grad_gate, preferred_element_type=jnp.float32)
    grad_w_up = jnp.einsum("td,tf->df", hidden_ffn, grad_up, preferred_element_type=jnp.float32)
    grad_h2 = jnp.einsum(
        "tf,df->td", grad_gate, w_gate, preferred_element_type=jnp.float32
    ) + jnp.einsum("tf,df->td", grad_up, w_up, preferred_element_type=jnp.float32)
    grad_mid, grad_ffn_gain = norm_back(normal_ffn, scale_ffn, g_ffn, grad_h2)
    grad_mid = grad_out.astype(jnp.float32) + grad_mid
    grad_attn = grad_mid.astype(jnp.bfloat16)
    grad_w_out = jnp.einsum("tc,td->cd", attended_b, grad_attn, preferred_element_type=jnp.float32)
    grad_attended = jnp.einsum(
        "td,cd->tc", grad_attn, w_out, preferred_element_type=jnp.float32
    ).astype(jnp.bfloat16)
    grad_heads = grad_attended.reshape(row_count, tok_count, KV_HEADS, grouping, HEAD_DIM)
    deltas = jnp.einsum("rqkgd,rkgqd->rkgq", grad_heads.astype(jnp.float32), attended)
    key_piece = lax.all_gather(key_b, "blk", axis=1, tiled=True)
    value_piece = lax.all_gather(value_b, "blk", axis=1, tiled=True)
    size = key_piece.shape[1]
    allowed = piece_mask(size)
    scores, key_heads = piece_scores(key_piece, allowed)
    probs = jnp.exp(scores - log_total[..., None])
    value_heads = value_piece.reshape(row_count, size, KV_HEADS, HEAD_DIM)
    value_piece_grad = jnp.einsum(
        "rkgqp,rqkgd->rpkd",
        probs.astype(jnp.bfloat16),
        grad_heads,
        preferred_element_type=jnp.float32,
    )
    grad_probs = jnp.einsum(
        "rqkgd,rpkd->rkgqp", grad_heads, value_heads, preferred_element_type=jnp.float32
    )
    grad_scores = (probs * (grad_probs - deltas[..., None])).astype(jnp.bfloat16)
    grad_query = jnp.einsum(
        "rkgqp,rpkd->rkgqd", grad_scores, key_heads, preferred_element_type=jnp.float32
    )
    key_piece_grad = jnp.einsum(
        "rkgqp,rqkgd->rpkd", grad_scores, query_b, preferred_element_type=jnp.float32
    )
    grad_keys = key_piece_grad.reshape(row_count, size, kv_width)
    grad_values = value_piece_grad.reshape(row_count, size, kv_width)
    grad_query, grad_keys, grad_values = (grad_query, grad_keys, grad_values)
    key_grad_mine, value_grad_mine = (
        lax.psum_scatter(
            grad_keys.astype(jnp.bfloat16), "blk", scatter_dimension=1, tiled=True
        ).astype(jnp.float32),
        lax.psum_scatter(
            grad_values.astype(jnp.bfloat16), "blk", scatter_dimension=1, tiled=True
        ).astype(jnp.float32),
    )
    grad_q_rot = (jnp.transpose(grad_query, (0, 3, 1, 2, 4)) * softmax_scale).reshape(
        row_count, tok_count, HEADS, HEAD_DIM
    )
    grad_k_rot = (key_grad_mine * softmax_scale).reshape(row_count, tok_count, KV_HEADS, HEAD_DIM)
    grad_q_proj, grad_query_gain = norm_back(
        query_normal, query_scale, q_gain, rotate(grad_q_rot, cosine, -sine)
    )
    grad_k_proj, grad_key_gain = norm_back(
        key_normal, key_scale, k_gain, rotate(grad_k_rot, cosine, -sine)
    )
    grad_q_b = grad_q_proj.astype(jnp.bfloat16).reshape(flat_rows, HEADS * HEAD_DIM)
    grad_k_b = grad_k_proj.astype(jnp.bfloat16).reshape(flat_rows, kv_width)
    grad_v_b = value_grad_mine.astype(jnp.bfloat16).reshape(flat_rows, kv_width)
    grad_w_query = jnp.einsum("td,tc->dc", hidden_in, grad_q_b, preferred_element_type=jnp.float32)
    grad_w_key = jnp.einsum("td,tc->dc", hidden_in, grad_k_b, preferred_element_type=jnp.float32)
    grad_w_value = jnp.einsum("td,tc->dc", hidden_in, grad_v_b, preferred_element_type=jnp.float32)
    grad_h1 = jnp.einsum("tc,dc->td", grad_q_b, w_query, preferred_element_type=jnp.float32)
    grad_h1 = grad_h1 + jnp.einsum("tc,dc->td", grad_k_b, w_key, preferred_element_type=jnp.float32)
    grad_h1 = grad_h1 + jnp.einsum(
        "tc,dc->td", grad_v_b, w_value, preferred_element_type=jnp.float32
    )
    grad_base, grad_attn_gain = norm_back(normal_in, scale_in, g_attn, grad_h1)
    input_grad = (grad_mid + grad_base).astype(jnp.bfloat16).reshape(row_count, tok_count, width)
    gain_attn, gain_query, gain_key, gain_ffn = lax.psum(
        (grad_attn_gain, grad_query_gain, grad_key_gain, grad_ffn_gain), ("dp", "blk")
    )
    locals_all = (
        grad_w_query,
        grad_w_key,
        grad_w_value,
        grad_w_out,
        grad_w_gate,
        grad_w_up,
        grad_w_down,
    )
    shared = (
        lax.psum_scatter(locals_all[0], ("dp", "blk"), scatter_dimension=0, tiled=True),
        lax.psum_scatter(locals_all[1], ("dp", "blk"), scatter_dimension=0, tiled=True),
        lax.psum_scatter(locals_all[2], ("dp", "blk"), scatter_dimension=0, tiled=True),
        lax.psum_scatter(locals_all[3], ("dp", "blk"), scatter_dimension=0, tiled=True),
        lax.psum_scatter(locals_all[4], ("dp", "blk"), scatter_dimension=0, tiled=True),
        lax.psum_scatter(locals_all[5], ("dp", "blk"), scatter_dimension=0, tiled=True),
        lax.psum_scatter(locals_all[6], ("dp", "blk"), scatter_dimension=0, tiled=True),
    )
    return (
        output,
        input_grad,
        gain_attn,
        shared[0],
        shared[1],
        shared[2],
        gain_query,
        gain_key,
        shared[3],
        gain_ffn,
        shared[4],
        shared[5],
        shared[6],
    )


BF16 = jnp.bfloat16
F32 = jnp.float32
LANES = 128
FF_TILE = 256
LAG = 2
LAST_LAG = 1
ATTEND_PAIRS = 6
VMEM_BYTES = 60 * 1024 * 1024
LOG2_E = math.log2(math.e)
QUERY_SCALE = HEAD_DIM ** (-0.5) * LOG2_E
MASKED = -1e30


def nn_dot(left, right):
    return lax.dot_general(left, right, (((1,), (0,)), ((), ())), preferred_element_type=F32)


def nt_dot(left, right):
    return lax.dot_general(left, right, (((1,), (1,)), ((), ())), preferred_element_type=F32)


def tn_dot(left, right):
    return lax.dot_general(left, right, (((0,), (0,)), ((), ())), preferred_element_type=F32)


def kernel_params(**more):
    return pltpu.CompilerParams(vmem_limit_bytes=VMEM_BYTES, **more)


def whole_block(shape):
    return pl.BlockSpec(shape, lambda *ids: (0,) * len(shape))


def greet_blk(count):
    barrier = pltpu.get_barrier_semaphore()
    z, index = lax.axis_index("dp"), lax.axis_index("blk")
    for step in range(1, count):
        pl.semaphore_signal(
            barrier,
            inc=1,
            device_id=(z, lax.rem(index + step, count)),
            device_id_type=pl.DeviceIdType.MESH,
        )
    pl.semaphore_wait(barrier, count - 1)


def blk_copy(send, got, sent_sem, got_sem, target, source):
    return pltpu.make_async_remote_copy(
        src_ref=send.at[target],
        dst_ref=got.at[source],
        send_sem=sent_sem.at[target],
        recv_sem=got_sem.at[source],
        device_id=(lax.axis_index("dp"), target),
        device_id_type=pl.DeviceIdType.MESH,
    )


def head_means(values):
    rows = lax.broadcasted_iota(jnp.int32, (LANES, LANES), 0) // HEAD_DIM
    cols = lax.broadcasted_iota(jnp.int32, (LANES, LANES), 1) // HEAD_DIM
    spread = jnp.where(rows == cols, 1.0 / HEAD_DIM, 0.0).astype(BF16)
    high = values.astype(BF16)
    low = (values - high.astype(F32)).astype(BF16)
    return nn_dot(high, spread) + nn_dot(low, spread)


def half_partner(values):
    lane = lax.broadcasted_iota(jnp.int32, values.shape, 1)
    half = HEAD_DIM // 2
    ahead = pltpu.roll(values, LANES - half, 1)
    behind = pltpu.roll(values, half, 1)
    return jnp.where(lane % HEAD_DIM < half, ahead, behind)


def low_lanes(shape):
    return lax.broadcasted_iota(jnp.int32, shape, 1) < HEAD_DIM


def parted(packed):
    turned = pltpu.roll(packed.astype(F32), HEAD_DIM, 1).astype(BF16)
    low = low_lanes(packed.shape)
    return jnp.where(low, packed, turned), jnp.where(low, turned, packed)


def stacked_heads(pair):
    low = low_lanes(pair.shape)
    none = jnp.zeros_like(pair)
    return jnp.concatenate([jnp.where(low, pair, none), jnp.where(low, none, pair)], axis=0)


def in_three(column):
    lane = lax.broadcasted_iota(jnp.int32, (column.shape[0], LANES), 1)
    wide = jnp.broadcast_to(column, (column.shape[0], LANES))
    first = wide.astype(BF16).astype(F32)
    second = (wide - first).astype(BF16).astype(F32)
    third = wide - first - second
    return jnp.where(
        lane == 0, first, jnp.where(lane == 1, second, jnp.where(lane == 2, third, 0.0))
    ).astype(BF16)


def minus_three(rows):
    lane = lax.broadcasted_iota(jnp.int32, (rows, LANES), 1)
    return jnp.where(lane < 3, -1.0, 0.0).astype(BF16)


def forward_kernel(
    chips,
    groups,
    tokens_ref,
    gain_ref,
    wq_ref,
    wk_ref,
    wv_ref,
    q_gain_ref,
    k_gain_ref,
    cos_ref,
    sin_ref,
    starts_ref,
    hidden_ref,
    proj_ref,
    qkv_ref,
    out_ref,
    logs_ref,
    heads_ref,
    send,
    got,
    keys,
    values,
    total,
    out_send,
    out_got,
    sent_sem,
    got_sem,
    out_sent_sem,
    out_got_sem,
):
    n = pl.program_id(0)
    blocks, block = send.shape[1:3]
    size = blocks * block
    index = lax.axis_index("blk")
    p = lax.rem(index // 2 + 1 + n, chips)

    def give(g, p):
        for part in range(2):
            target = 2 * p + part

            @pl.when(target != index)
            def _():
                blk_copy(send.at[g], got.at[g], sent_sem.at[g], got_sem.at[g], target, index).start()

            @pl.when(target == index)
            def _():
                got[g, target] = send[g, target]

    @pl.when(n == 0)
    def _():
        greet_blk(blocks)
        inputs = tokens_ref[...].astype(F32)
        scale = lax.rsqrt(jnp.mean(inputs * inputs, axis=-1, keepdims=True) + EPSILON)
        hidden_ref[...] = (inputs * scale * gain_ref[...]).astype(BF16)

    @pl.when(n < chips)
    def _():
        hidden = hidden_ref[...]
        queries = nn_dot(hidden, wq_ref[...])
        keys_of = nn_dot(hidden, wk_ref[...])
        values_of = nn_dot(hidden, wv_ref[...])

        def turn(part, lane, head_gain):
            proj_ref[0, :, lane : lane + LANES] = part
            scale = lax.rsqrt(head_means(part * part) + EPSILON)
            normed = part * scale * head_gain[...]
            return normed * cos_ref[...] + half_partner(normed) * sin_ref[...]

        def put(g, lane, part):
            for half in range(2):
                send[g, 2 * p + half, :, lane : lane + LANES] = part[half * block : (half + 1) * block].astype(BF16)

        key = turn(keys_of, groups * LANES, k_gain_ref)
        low = low_lanes(key.shape)
        for g in range(groups):
            lanes = slice(g * LANES, (g + 1) * LANES)
            put(g, 0, turn(queries[:, lanes], g * LANES, q_gain_ref) * QUERY_SCALE)
            if g == 0:
                put(g, LANES, jnp.where(low, key, pltpu.roll(values_of, HEAD_DIM, 1)))
            else:
                put(g, LANES, jnp.where(low, pltpu.roll(key, HEAD_DIM, 1), values_of))
        give(0, p)

    @pl.when(n == chips - 1)
    def _():
        for step in range(chips):
            give(1, lax.rem(index // 2 + 1 + step, chips))

    for g in range(groups):

        @pl.when(n == chips + g * blocks)
        def _():
            for step in range(1, blocks):
                other = lax.rem(index + step, blocks)
                blk_copy(send.at[g], got.at[g], sent_sem.at[g], got_sem.at[g], other, other).wait()
            for i in range(blocks):
                here = slice(i * block, (i + 1) * block)
                qkv_ref[g, here, :] = got[g, i]
                keys[here, :], values[here, :LANES] = parted(got[g, i, :, LANES:])
                values[here, LANES:] = jnp.ones((block, LANES), BF16)

    @pl.when(n >= chips)
    def _():
        g = (n - chips) // blocks
        here = lax.rem(index + 1 + lax.rem(n - chips, blocks), blocks)
        at = pl.multiple_of(here * block, block)
        starts = jnp.concatenate([starts_ref[pl.ds(at, block), :]] * 2, axis=0)
        query = stacked_heads(got[g, here, :, :LANES])

        def step(key_at, width, diagonal):
            column = lax.broadcasted_iota(jnp.int32, (2 * block, width), 1)
            allowed = column >= starts - key_at
            if diagonal:
                row = lax.broadcasted_iota(jnp.int32, (2 * block, width), 0) % block
                allowed = allowed & (column <= row)
            scores = nt_dot(query, keys[pl.ds(key_at, width), :])
            weights = jnp.exp2(jnp.where(allowed, scores, MASKED)).astype(BF16)
            part = nn_dot(weights, values[pl.ds(key_at, width), :])
            if diagonal:
                total[...] = part
            else:
                total[...] += part

        step(at, block, True)

        @pl.when(lax.rem(here, 2) == 1)
        def _():
            step(pl.multiple_of((here - 1) * block, block), block, False)

        def body(j, carry):
            step(pl.multiple_of(j * 2 * block, 2 * block), 2 * block, False)
            return carry

        lax.fori_loop(0, here // 2, body, 0)
        low = low_lanes((block, LANES))
        to = pl.multiple_of(here * 2 * block, 2 * block)
        sums = total[:, LANES:]
        mean = total[:, :LANES] / sums
        made = jnp.where(low, mean[:block], mean[block:]).astype(BF16)
        out_send[g, here] = made
        out_ref[here, :, pl.ds(pl.multiple_of(g * LANES, LANES), LANES)] = made
        logs_ref[g, pl.ds(to, 2 * block), :] = in_three(jnp.log2(sums[:, :1]))

        @pl.when(here != index)
        def _():
            blk_copy(
                out_send.at[g], out_got.at[g], out_sent_sem.at[g], out_got_sem.at[g], here, index
            ).start()

        @pl.when(here == index)
        def _():
            out_got[g, here] = made

    @pl.when(n == pl.num_programs(0) - 1)
    def _():
        for g in range(groups):
            for step in range(1, blocks):
                other = lax.rem(index + step, blocks)
                blk_copy(
                    out_send.at[g], out_got.at[g], out_sent_sem.at[g], out_got_sem.at[g], other, other
                ).wait()
            heads_ref[:, :, g * LANES : (g + 1) * LANES] = out_got[g]


def forward(tokens, gain, wq, wk, wv, q_gain, k_gain, cosine, sine, starts):
    rows, width = tokens.shape
    chips = wk.shape[1] // LANES
    q_width = wq.shape[1] // chips
    groups, blocks, block = q_width // LANES, 2 * chips, rows // 2
    size = blocks * block

    def keep(shape):
        return pl.BlockSpec(shape, lambda n: (0,) * len(shape), pipeline_mode=pl.Buffered(1))

    def at(n):
        return lax.rem(lax.axis_index("blk") // 2 + 1 + jnp.minimum(n, chips - 1), chips)

    outs = [
        ((rows, width), BF16),
        ((chips, rows, q_width + LANES), F32),
        ((groups, size, 2 * LANES), BF16),
        ((blocks, block, q_width), BF16),
        ((groups, 2 * size, LANES), BF16),
        ((blocks, block, q_width), BF16),
    ]
    out_specs = [keep(shape) for shape, unused in outs]
    out_specs[1] = pl.BlockSpec((1, rows, q_width + LANES), lambda n: (at(n), 0, 0))
    moved, heads = (groups, blocks, block, 2 * LANES), (groups, blocks, block, LANES)
    return pl.pallas_call(
        functools.partial(forward_kernel, chips, groups),
        name="forward",
        grid=(chips + groups * blocks,),
        in_specs=[
            keep((rows, width)),
            keep((1, width)),
            pl.BlockSpec((width, q_width), lambda n: (0, at(n))),
            pl.BlockSpec((width, LANES), lambda n: (0, at(n))),
            pl.BlockSpec((width, LANES), lambda n: (0, at(n))),
            keep((1, LANES)),
            keep((1, LANES)),
            keep((rows, LANES)),
            keep((rows, LANES)),
            keep((size, 1)),
        ],
        out_specs=out_specs,
        out_shape=[jax.ShapeDtypeStruct(shape, kind) for shape, kind in outs],
        scratch_shapes=[
            pltpu.VMEM(moved, BF16),
            pltpu.VMEM(moved, BF16),
            pltpu.VMEM((size, LANES), BF16),
            pltpu.VMEM((size, 2 * LANES), BF16),
            pltpu.VMEM((2 * block, 2 * LANES), F32),
            pltpu.VMEM(heads, BF16),
            pltpu.VMEM(heads, BF16),
        ]
        + [pltpu.SemaphoreType.DMA((groups, blocks))] * 4,
        compiler_params=kernel_params(collective_id=0, has_side_effects=True),
    )(tokens, gain, wq, wk, wv, q_gain, k_gain, cosine, sine, starts)


def pair_of(name):
    z, index = lax.axis_index("dp"), lax.axis_index("blk")
    if isinstance(name, tuple):
        mine = lax.rem(z // name[1], 2)
        return mine, (z + name[1] * (1 - 2 * mine), index)
    mine = lax.rem(index // name, 2)
    return mine, (z, index + name * (1 - 2 * mine))


class Stream:
    def __init__(self, path, names, block, lag, units, swap=None):
        self.path, self.block, self.lag, self.units, self.swap = path, block, lag, units, swap
        self.slots = min(2 * lag, units)
        self.names = [tuple(names)]
        for k, stage in enumerate(path):
            left = tuple(name for name in self.names[-1] if name != stage)
            self.names.append((swap,) + left if swap is not None and k == 0 else left)
        assert not self.names[-1]

    def shape(self, names):
        return (2,) * len(names) + self.block

    def steps(self):
        return self.units + self.lag * len(self.path) + 1

    def slot(self, u):
        return lax.rem(u, self.slots)

    def scratch(self):
        shapes = []
        for k, stage in enumerate(self.path):
            left = tuple(name for name in self.names[k] if name != stage)
            shapes.append(pltpu.VMEM((self.slots,) + self.shape(self.names[k]), BF16))
            shapes.append(pltpu.VMEM((self.slots,) + self.shape(left), BF16))
            shapes += [pltpu.SemaphoreType.DMA((self.slots,))] * 2
        return shapes

    def bind(self, refs, finish, begin=0):
        self.finish, self.begin = finish, begin
        self.work, self.got, self.sent_sem, self.got_sem = refs[::4], refs[1::4], refs[2::4], refs[3::4]
        self.source = self.work[0]

    def copy(self, k, u):
        mine, partner = pair_of(self.path[k])
        whole = (slice(None),) * self.names[k].index(self.path[k])
        slot = self.slot(u)
        copy = pltpu.make_async_remote_copy(
            src_ref=self.work[k].at[(slot,) + whole + (1 - mine,)],
            dst_ref=self.got[k].at[slot],
            send_sem=self.sent_sem[k].at[slot],
            recv_sem=self.got_sem[k].at[slot],
            device_id=partner,
            device_id_type=pl.DeviceIdType.MESH,
        )
        return copy, (slot,) + whole + (mine,), mine

    def send(self, k, step):
        u = step - self.begin - self.lag * k - 1

        @pl.when((u >= 0) & (u < self.units))
        def _():
            self.copy(k, u)[0].start()

    def take(self, k, step):
        u = step - self.begin - self.lag * (k + 1) - 1

        @pl.when((u >= 0) & (u < self.units))
        def _():
            copy, own, mine = self.copy(k, u)
            copy.wait()
            slot = self.slot(u)
            if self.swap is not None and k == 0:
                self.work[1][slot, mine] = self.work[0][own]
                self.work[1][slot, 1 - mine] = self.got[0][slot]
            elif k == len(self.path) - 1:
                self.finish(u, self.work[k][own] + self.got[k][slot])
            else:
                self.work[k + 1][slot] = self.work[k][own] + self.got[k][slot]


def step_streams(streams, step):
    longest = max(len(stream.path) for stream in streams)
    for k in range(longest):
        for stream in streams:
            if k < len(stream.path):
                stream.take(k, step)
    for k in range(longest):
        for stream in streams:
            if k < len(stream.path):
                stream.send(k, step)


def line_bits(line):
    return [("z", 1 << i) for i in range(line.bit_length() - 1)]


def greet_all(blk_count, line):
    barrier = pltpu.get_barrier_semaphore()
    z, index = lax.axis_index("dp"), lax.axis_index("blk")
    peers = [(z, lax.rem(index + step, blk_count)) for step in range(1, blk_count)]
    peers += [pair_of(name)[1] for name in line_bits(line)]
    for peer in peers:
        pl.semaphore_signal(barrier, inc=1, device_id=peer, device_id_type=pl.DeviceIdType.MESH)
    pl.semaphore_wait(barrier, len(peers))


def middle_kernel(
    line,
    bits,
    streams,
    units,
    tokens_ref,
    heads_ref,
    w_out_ref,
    gain_ref,
    dy_own_ref,
    dy_got_ref,
    w_gate_ref,
    w_up_ref,
    w_down_ref,
    output_ref,
    mid_ref,
    gain_grad_ref,
    w_grad_ref,
    grad_heads_ref,
    acts_ref,
    gate_out_ref,
    up_out_ref,
    hidden,
    flipped,
    out_sum,
    back_sum,
    gate_grads,
    up_grads,
    part_send,
    part_got,
    low_grad,
    do_send,
    do_got,
    hidden_sem,
    part_sent_sem,
    part_got_sem,
    do_sent_sem,
    do_got_sem,
    *refs,
):
    n = pl.program_id(0)
    steps = pl.num_programs(0)
    z, index = lax.axis_index("dp"), lax.axis_index("blk")
    sibling = pair_of(1)[1]
    own_rows, width = tokens_ref.shape
    rows = 2 * own_rows
    blk_count, tok_count, head_lanes = heads_ref.shape
    chips = blk_count // 2
    chunk = 256
    gate_stream, up_stream, both_stream = streams
    gate_rows = gate_stream.block[0]
    own, other = pl.ds(0, own_rows), pl.ds(own_rows, own_rows)

    def finish_gate(u, value):
        gate_out_ref[:gate_rows, pl.ds(pl.multiple_of(u * FF_TILE, FF_TILE), FF_TILE)] = value

    def finish_up(u, value):
        up_out_ref[:gate_rows, pl.ds(pl.multiple_of(u * FF_TILE, FF_TILE), FF_TILE)] = value

    def finish_both(u, value):
        here = pl.ds(pl.multiple_of(u * FF_TILE, FF_TILE), FF_TILE)
        gate_out_ref[gate_rows:, here] = value[:, :FF_TILE]
        up_out_ref[gate_rows:, here] = value[:, FF_TILE:]

    at = 0
    for stream, finish in zip(streams, (finish_gate, finish_up, finish_both)):
        count = len(stream.scratch())
        stream.bind(refs[at : at + count], finish)
        at += count

    def hidden_copy():
        return pltpu.make_async_remote_copy(
            src_ref=hidden.at[own],
            dst_ref=hidden.at[other],
            send_sem=hidden_sem.at[0],
            recv_sem=hidden_sem.at[1],
            device_id=sibling,
            device_id_type=pl.DeviceIdType.MESH,
        )

    def part_copy(i):
        return pltpu.make_async_remote_copy(
            src_ref=part_send.at[i],
            dst_ref=part_got.at[i],
            send_sem=part_sent_sem.at[i],
            recv_sem=part_got_sem.at[i],
            device_id=sibling,
            device_id_type=pl.DeviceIdType.MESH,
        )

    def do_copy(target, source):
        return pltpu.make_async_remote_copy(
            src_ref=do_send.at[target],
            dst_ref=do_got.at[source],
            send_sem=do_sent_sem.at[target],
            recv_sem=do_got_sem.at[source],
            device_id=(z, target),
            device_id_type=pl.DeviceIdType.MESH,
        )

    def flip(start):
        for r in range(start, start + own_rows, chunk):
            for c in range(0, width, chunk):
                flipped[c : c + chunk, r : r + chunk] = hidden[r : r + chunk, c : c + chunk].T

    @pl.when(n == 0)
    def _():
        greet_all(blk_count, line)
        total = tokens_ref[...].astype(F32)
        for p in range(chips):
            block = jnp.concatenate([heads_ref[2 * p], heads_ref[2 * p + 1]], axis=0)
            total = total + nn_dot(block, w_out_ref[p * head_lanes : (p + 1) * head_lanes, :])
        mid_ref[...] = total
        scale = lax.rsqrt(jnp.mean(total * total, axis=-1, keepdims=True) + EPSILON)
        hidden[own] = (total * scale * gain_ref[...]).astype(BF16)
        hidden_copy().start()
        out_sum[...] = jnp.zeros_like(out_sum)
        back_sum[...] = jnp.zeros_like(back_sum)
        flip(0)

    @pl.when(n == 1)
    def _():
        hidden_copy().wait()
        flip(own_rows)

    step_streams(streams, n - 1)

    @pl.when((n >= 1) & (n <= units))
    def _():
        for m in range(rows // chunk):
            part = slice(m * chunk, (m + 1) * chunk)
            gate = nn_dot(hidden[part, :], w_gate_ref[...])
            up = nn_dot(hidden[part, :], w_up_ref[...])
            at = m * chunk % own_rows
            dy_ref = dy_own_ref if m * chunk < own_rows else dy_got_ref
            pushed = nt_dot(dy_ref[at : at + chunk, :], w_down_ref[...])
            opened = jax.nn.sigmoid(gate)
            silu = gate * opened
            act = (silu * up).astype(BF16)
            gate_grad = (pushed * up * opened * (1.0 + gate * (1.0 - opened))).astype(BF16)
            up_grad = (pushed * silu).astype(BF16)
            acts_ref[:, part] = act.T
            gate_grads[part, :] = gate_grad
            up_grads[part, :] = up_grad
            out_sum[part, :] += nn_dot(act, w_down_ref[...])
            back_sum[part, :] += nt_dot(gate_grad, w_gate_ref[...]) + nt_dot(up_grad, w_up_ref[...])
        u = n - 1
        slot = gate_stream.slot(u)
        each = width // line
        zs = line.bit_length() - 1
        shape = gate_stream.shape(gate_stream.names[0])[zs:-2] + (-1, FF_TILE)
        for m in range(line):
            at = (slot,) + tuple(m >> i & 1 for i in reversed(range(zs)))
            part = slice(m * each, (m + 1) * each)
            gate_part = nn_dot(flipped[part, :], gate_grads[...]).astype(BF16)
            up_part = nn_dot(flipped[part, :], up_grads[...]).astype(BF16)
            gate_part, up_part = gate_part.reshape(shape), up_part.reshape(shape)
            gate_stream.source[at] = gate_part[..., :gate_rows, :]
            up_stream.source[at] = up_part[..., :gate_rows, :]
            both_stream.source[at + (..., slice(0, FF_TILE))] = gate_part[..., gate_rows:, :]
            both_stream.source[at + (..., slice(FF_TILE, None))] = up_part[..., gate_rows:, :]

    @pl.when(n == units)
    def _():
        part_send[0] = back_sum[other].astype(BF16)
        part_copy(0).start()
        part_send[1] = out_sum[other].astype(BF16)
        part_copy(1).start()

    @pl.when(n == units + 1)
    def _():
        part_copy(0).wait()
        values = mid_ref[...]
        scale = lax.rsqrt(jnp.mean(values * values, axis=-1, keepdims=True) + EPSILON)
        normal = values * scale
        back = back_sum[own] + part_got[0].astype(F32)
        gain_grad_ref[...] = jnp.sum(back * normal, axis=0, keepdims=True)
        pushed = back * gain_ref[...]
        inner = jnp.mean(pushed * normal, axis=-1, keepdims=True)
        mid = dy_own_ref[...].astype(F32) + scale * (pushed - normal * inner)
        part_copy(1).wait()
        mid_ref[...] = mid
        low_grad[...] = mid.astype(BF16)
        output_ref[...] = (values + (out_sum[own] + part_got[1].astype(F32))).astype(BF16)

    @pl.when((n > units + 1) & (n <= units + 1 + chips))
    def _():
        p = n - units - 2
        grad = low_grad[...]
        lanes = pl.ds(pl.multiple_of(p * head_lanes, head_lanes), head_lanes)
        send = nt_dot(grad, w_out_ref[lanes, :]).astype(BF16)
        for half in range(2):
            target = 2 * p + half
            do_send[target] = send[half * tok_count : (half + 1) * tok_count]

            @pl.when(target != index)
            def _():
                do_copy(target, index).start()

            @pl.when(target == index)
            def _():
                do_got[target] = send[half * tok_count : (half + 1) * tok_count]

        heads = jnp.concatenate([heads_ref[2 * p], heads_ref[2 * p + 1]], axis=0)
        w_grad_ref[lanes, :] = tn_dot(heads, grad).astype(BF16)

    @pl.when(n == steps - 1)
    def _():
        for other_index in range(blk_count):

            @pl.when(other_index != index)
            def _():
                do_copy(other_index, other_index).wait()

        grad_heads_ref[...] = do_got[...]


def column_streams(line, bits, each, units):
    late = each // 4
    zs = line_bits(line)
    names = zs[::-1] + bits
    return [
        Stream(bits[::-1] + zs, names, (each - late, FF_TILE), LAG, units),
        Stream(bits + zs, names, (each - late, FF_TILE), LAG, units),
        Stream(zs + bits, names, (late, 2 * FF_TILE), LAG, units),
    ]


def middle_layer(line, bits, tokens, heads, w_out, gain, dy_own, dy_got, w_gate, w_up, w_down):
    own_rows, width = tokens.shape
    rows = 2 * own_rows
    blk_count, tok_count, head_lanes = heads.shape
    units = w_gate.shape[1] // 2 // FF_TILE
    chips = line * 2 ** len(bits)
    each = width // chips
    streams = column_streams(line, bits, each, units)
    steps = max([1 + stream.steps() for stream in streams] + [units + 3 + blk_count // 2])

    def keep(shape):
        return pl.BlockSpec(shape, lambda n: (0,) * len(shape), pipeline_mode=pl.Buffered(1))

    def tile(n):
        return jnp.clip(n - 1, 0, units - 1)

    def mine(n):
        return lax.rem(lax.axis_index("blk"), 2) * units + tile(n)

    scratch = [
        pltpu.VMEM((rows, width), BF16),
        pltpu.VMEM((width, rows), BF16),
        pltpu.VMEM((rows, width), F32),
        pltpu.VMEM((rows, width), F32),
        pltpu.VMEM((rows, FF_TILE), BF16),
        pltpu.VMEM((rows, FF_TILE), BF16),
        pltpu.VMEM((2, own_rows, width), BF16),
        pltpu.VMEM((2, own_rows, width), BF16),
        pltpu.VMEM((own_rows, width), BF16),
        pltpu.VMEM(heads.shape, BF16),
        pltpu.VMEM(heads.shape, BF16),
        pltpu.SemaphoreType.DMA((2,)),
        pltpu.SemaphoreType.DMA((2,)),
        pltpu.SemaphoreType.DMA((2,)),
        pltpu.SemaphoreType.DMA((blk_count,)),
        pltpu.SemaphoreType.DMA((blk_count,)),
    ]
    for stream in streams:
        scratch += stream.scratch()
    outs = [
        ((own_rows, width), BF16),
        ((own_rows, width), F32),
        ((1, width), F32),
        (w_out.shape, BF16),
        (heads.shape, BF16),
        ((units * FF_TILE, rows), BF16),
        ((each, units * FF_TILE), BF16),
        ((each, units * FF_TILE), BF16),
    ]
    out_specs = [keep(shape) for shape, unused in outs]
    out_specs[5] = pl.BlockSpec((FF_TILE, rows), lambda n: (tile(n), 0))
    return pl.pallas_call(
        functools.partial(middle_kernel, line, bits, streams, units),
        name="middle",
        grid=(steps,),
        in_specs=[
            keep(tokens.shape),
            keep(heads.shape),
            keep(w_out.shape),
            keep(gain.shape),
            keep(dy_own.shape),
            keep(dy_got.shape),
            pl.BlockSpec((width, FF_TILE), lambda n: (0, mine(n))),
            pl.BlockSpec((width, FF_TILE), lambda n: (0, mine(n))),
            pl.BlockSpec((FF_TILE, width), lambda n: (mine(n), 0)),
        ],
        out_specs=out_specs,
        out_shape=[jax.ShapeDtypeStruct(shape, kind) for shape, kind in outs],
        scratch_shapes=scratch,
        compiler_params=kernel_params(collective_id=6, has_side_effects=True),
    )(tokens, heads, w_out, gain, dy_own, dy_got, w_gate, w_up, w_down)


def back_kernel(
    groups,
    block,
    line,
    bits,
    streams,
    units,
    qkv_ref,
    logs_ref,
    out_ref,
    grad_ref,
    starts_ref,
    dy_own_ref,
    dy_got_ref,
    acts_ref,
    w_out_parts_ref,
    moved_ref,
    down_out_ref,
    w_out_ref,
    queries,
    keys,
    values,
    grads,
    query_grad,
    pair_grad,
    result,
    moved,
    sent_sem,
    got_sem,
    *refs,
):
    size = qkv_ref.shape[1]
    blocks = size // block
    n = pl.program_id(0)
    index = lax.axis_index("blk")
    core = lax.rem(index, 2)

    def move(g, target, source):
        return blk_copy(result.at[g], moved.at[g], sent_sem.at[g], got_sem.at[g], target, source)

    half = streams[0].block[1]

    def finish_low(u, value):
        rows = value.shape[0]
        down_out_ref[pl.ds(pl.multiple_of(u * rows, rows), rows), :half] = value

    def finish_high(u, value):
        rows = value.shape[0]
        down_out_ref[pl.ds(pl.multiple_of(u * rows, rows), rows), half:] = value

    def finish_w_out(u, value):
        w_out_ref[:, pl.ds(pl.multiple_of(u * LANES, LANES), LANES)] = value

    columns = w_out_ref.shape[1] // LANES
    at = 0
    for stream, finish in zip(streams, (finish_low, finish_high, finish_w_out)):
        size_of = len(stream.scratch())
        stream.bind(refs[at : at + size_of], finish)
        at += size_of

    @pl.when(n == 0)
    def _():
        greet_all(blocks, line)

    step_streams(streams, n)

    @pl.when(n == 1)
    def _():
        query_grad[...] = jnp.zeros_like(query_grad)
        pair_grad[...] = jnp.zeros_like(pair_grad)
        for g in range(groups):
            lanes = slice(g * LANES, (g + 1) * LANES)
            key, value = parted(qkv_ref[g, :, LANES:])
            keys[g, :, :LANES] = key
            keys[g, :, LANES:] = minus_three(size)
            values[g, :, :LANES] = value
            values[g, :, LANES:] = minus_three(size)

            def fill(i, carry):
                at = pl.multiple_of(i * block, block)
                to = pl.multiple_of(i * 2 * block, 2 * block)
                queries[g, pl.ds(to, 2 * block), :LANES] = stacked_heads(qkv_ref[g, pl.ds(at, block), :LANES])
                queries[g, pl.ds(to, 2 * block), LANES:] = logs_ref[g, pl.ds(to, 2 * block), :]
                grad = stacked_heads(grad_ref[pl.ds(at, block), lanes])
                mean = stacked_heads(out_ref[pl.ds(at, block), lanes])
                delta = jnp.sum(grad.astype(F32) * mean.astype(F32), axis=1, keepdims=True)
                grads[g, pl.ds(to, 2 * block), :LANES] = grad
                grads[g, pl.ds(to, 2 * block), LANES:] = in_three(delta)
                return carry

            lax.fori_loop(0, blocks, fill, 0)

    @pl.when(n < units)
    def _():
        acts = acts_ref[...].reshape(-1, acts_ref.shape[-1])
        rows = dy_own_ref.shape[0]
        made = nn_dot(acts[:, :rows], dy_own_ref[...]) + nn_dot(acts[:, rows:], dy_got_ref[...])
        made = made.astype(BF16)
        for i, stream in enumerate(streams[:2]):
            shape = stream.shape(stream.names[0])[1:]
            for side in range(2):
                at = (2 * side + i) * half
                stream.source[stream.slot(n), side] = made[:, at : at + half].reshape(shape)

    @pl.when(n < columns)
    def _():
        stream = streams[2]
        stream.source[stream.slot(n)] = w_out_parts_ref[...].reshape(stream.shape(stream.names[0]))

    row = lax.broadcasted_iota(jnp.int32, (block, 2 * block), 0)
    column = lax.broadcasted_iota(jnp.int32, (block, 2 * block), 1) % block

    pairs = (blocks + 1) * (blocks // 2)
    each = ATTEND_PAIRS
    rounds = groups * pairs // each

    @pl.when((n >= 1) & (n <= rounds))
    def _():
        def pair(at, carry):
            number = (n - 1) * each + at
            g = number // pairs
            place = lax.rem(number, pairs)
            turn = place // (blocks // 2)
            m = lax.rem(place, blocks // 2)
            late = (turn + m) // blocks
            j = m + late * (blocks - 1 - 2 * m)
            i = (1 - late) * (m + turn) + late * (turn - 1)
            key_at = pl.multiple_of(j * block, block)
            at = pl.multiple_of(i * 2 * block, 2 * block)
            key_rows = pl.ds(key_at, block)
            stack = pl.ds(at, 2 * block)
            allowed = (row >= starts_ref[:, stack] - key_at) & (row - column <= (i - j) * block)
            query = queries[g, stack, :]
            grad = grads[g, stack, :]
            key = keys[g, key_rows, :]
            scores = nt_dot(key, query)
            probs = jnp.exp2(jnp.where(allowed, scores, MASKED))
            pushed = (probs * nt_dot(values[g, key_rows, :], grad)).astype(BF16)
            pair_grad[g, key_rows, LANES:] += nn_dot(probs.astype(BF16), grad[:, :LANES])
            pair_grad[g, key_rows, :LANES] += nn_dot(pushed, query[:, :LANES])
            query_grad[g, stack, :] += tn_dot(pushed, key[:, :LANES])
            return carry

        lax.fori_loop(0, each, pair, 0, unroll=True)

    for g in range(groups):

        @pl.when(n == (g + 1) * rounds // groups + 1)
        def _():
            low = low_lanes((block, LANES))

            def finish(i, carry):
                at = pl.multiple_of(i * block, block)
                to = pl.multiple_of(i * 2 * block, 2 * block)
                here = pl.ds(at, block)
                first = query_grad[g, pl.ds(to, block), :]
                second = query_grad[g, pl.ds(to + block, block), :]
                joined = jnp.where(low, first, second) * HEAD_DIM ** (-0.5)
                result[g, i, :, :LANES] = joined.astype(BF16)
                key = pair_grad[g, here, :LANES] * (1.0 / LOG2_E)
                value = pair_grad[g, here, LANES:]
                key = key + pltpu.roll(key, HEAD_DIM, 1)
                value = value + pltpu.roll(value, HEAD_DIM, 1)
                result[g, i, :, LANES:] = jnp.where(low, key, value).astype(BF16)
                return carry

            lax.fori_loop(0, blocks, finish, 0)
            for step in range(blocks - 1, 0, -1):
                move(g, lax.rem(index + step, blocks), index).start()
            moved[g, index] = result[g, index]

    @pl.when(n == pl.num_programs(0) - 1)
    def _():
        for g in range(groups):
            for step in range(1, blocks):
                other = lax.rem(index + step, blocks)
                move(g, other, other).wait()
            moved_ref[:, :, 2 * g * LANES : 2 * (g + 1) * LANES] = moved[g]


def back(line, bits, qkv, logs, out, grad, starts, block, dy_own, dy_got, acts, w_out_parts):
    groups, size, width = qkv.shape
    model = dy_own.shape[1]
    rows = acts.shape[1]
    units = acts.shape[0] // FF_TILE
    chips = line * 2 ** len(bits)
    down_rows = acts.shape[0] // (chips // 2)
    down_each = down_rows // units
    w_rows = w_out_parts.shape[0] // chips // 2
    columns = w_out_parts.shape[1] // LANES
    zs = line_bits(line)
    names = [1] + zs[-2::-1] + bits
    streams = [
        Stream([1] + zs + bits, names, (down_each, model // 4), LAG, units, swap=zs[-1]),
        Stream([1] + bits[::-1] + zs, names, (down_each, model // 4), LAG, units, swap=zs[-1]),
        Stream([1] + bits + zs, zs[::-1] + bits + [1], (w_rows, LANES), LAG, columns),
    ]
    steps = max(
        [stream.steps() for stream in streams]
        + [groups * (size // block + 1) * (size // block // 2) // ATTEND_PAIRS + 3]
    )

    def keep(shape):
        return pl.BlockSpec(shape, lambda n: (0,) * len(shape), pipeline_mode=pl.Buffered(1))

    acts = acts.reshape(chips // 2, down_rows, rows)
    scratch = [
        pltpu.VMEM((groups, 2 * size, 2 * LANES), BF16),
        pltpu.VMEM((groups, size, 2 * LANES), BF16),
        pltpu.VMEM((groups, size, 2 * LANES), BF16),
        pltpu.VMEM((groups, 2 * size, 2 * LANES), BF16),
        pltpu.VMEM((groups, 2 * size, LANES), F32),
        pltpu.VMEM((groups, size, 2 * LANES), F32),
        pltpu.VMEM((groups, size // block, block, 2 * LANES), BF16),
        pltpu.VMEM((groups, size // block, block, 2 * LANES), BF16),
        pltpu.SemaphoreType.DMA((groups, size // block)),
        pltpu.SemaphoreType.DMA((groups, size // block)),
    ]
    for stream in streams:
        scratch += stream.scratch()

    outs = [
        (size // block, block, groups * width),
        (down_rows, model // 2),
        (w_rows, w_out_parts.shape[1]),
    ]
    return pl.pallas_call(
        functools.partial(back_kernel, groups, block, line, bits, streams, units),
        name="back",
        grid=(steps,),
        in_specs=[
            keep(qkv.shape),
            keep(logs.shape),
            keep(out.shape),
            keep(grad.shape),
            keep(starts.shape),
            keep(dy_own.shape),
            keep(dy_got.shape),
            pl.BlockSpec(
                (chips // 2, down_each, rows), lambda n: (0, jnp.minimum(n, units - 1), 0)
            ),
            pl.BlockSpec((w_out_parts.shape[0], LANES), lambda n: (0, jnp.minimum(n, columns - 1))),
        ],
        out_specs=[keep(shape) for shape in outs],
        out_shape=[jax.ShapeDtypeStruct(shape, BF16) for shape in outs],
        scratch_shapes=scratch,
        compiler_params=kernel_params(collective_id=4, has_side_effects=True),
    )(qkv, logs, out, grad, starts, dy_own, dy_got, acts, w_out_parts)


def sum_gains(rounds, n, first, gains, gains_got, sent_sem, got_sem):
    for r, partner in enumerate(rounds):

        def copy():
            return pltpu.make_async_remote_copy(
                src_ref=gains.at[r],
                dst_ref=gains_got.at[r],
                send_sem=sent_sem.at[r],
                recv_sem=got_sem.at[r],
                device_id=partner,
                device_id_type=pl.DeviceIdType.MESH,
            )

        @pl.when(n == first + r + 1)
        def _():
            copy().wait()
            gains[r + 1] = gains[r] + gains_got[r]

    for r, partner in enumerate(rounds):

        @pl.when(n == first + r)
        def _():
            pltpu.make_async_remote_copy(
                src_ref=gains.at[r],
                dst_ref=gains_got.at[r],
                send_sem=sent_sem.at[r],
                recv_sem=got_sem.at[r],
                device_id=partner,
                device_id_type=pl.DeviceIdType.MESH,
            ).start()


def finish_kernel(
    line,
    bits,
    streams,
    units,
    got_ref,
    proj_ref,
    hidden_ref,
    tokens_ref,
    mid_ref,
    gain_ref,
    wq_ref,
    wk_ref,
    wv_ref,
    q_gain_ref,
    k_gain_ref,
    cos_ref,
    sin_ref,
    ffn_gain_ref,
    gate_ref,
    up_ref,
    down_ref,
    input_ref,
    gains_ref,
    gq_ref,
    gk_ref,
    gv_ref,
    gate_out_ref,
    up_out_ref,
    down_out_ref,
    total,
    gains,
    gains_got,
    gains_sent_sem,
    gains_got_sem,
    half_got,
    down_got,
    half_sent_sem,
    half_got_sem,
    *refs,
):
    n = pl.program_id(0)
    z, index = lax.axis_index("dp"), lax.axis_index("blk")
    core, sibling = pair_of(1)
    steps = pl.num_programs(0)
    query_stream, pair_stream = streams
    q_width = wq_ref.shape[1]

    def finish_query(u, value):
        gq_ref[:, pl.ds(pl.multiple_of(u * q_width, q_width), q_width)] = value

    def finish_pair(u, value):
        here = pl.ds(pl.multiple_of(u * LANES, LANES), LANES)
        gk_ref[:, here] = value[:, :LANES]
        gv_ref[:, here] = value[:, LANES:]

    at = 0
    for stream, finish in ((query_stream, finish_query), (pair_stream, finish_pair)):
        count = len(stream.scratch())
        stream.bind(refs[at : at + count], finish)
        at += count

    rounds = [pair_of(name)[1] for name in [1] + list(bits) + line_bits(line)]

    rows = gate_ref.shape[0] // 2
    columns = gate_ref.shape[1]
    down_rows = down_ref.shape[0] // 2
    give = pl.ds(pl.multiple_of((1 - core) * rows, rows), rows)
    keep = pl.ds(pl.multiple_of(core * rows, rows), rows)
    down_give = pl.ds(pl.multiple_of((1 - core) * down_rows, down_rows), down_rows)
    down_keep = pl.ds(pl.multiple_of(core * down_rows, down_rows), down_rows)

    def half_copies():
        sources = (gate_ref.at[give, :], up_ref.at[give, :], down_ref.at[down_give, :])
        targets = (half_got.at[0], half_got.at[1], down_got)
        return [
            pltpu.make_async_remote_copy(
                src_ref=source,
                dst_ref=target,
                send_sem=half_sent_sem.at[i],
                recv_sem=half_got_sem.at[i],
                device_id=sibling,
                device_id_type=pl.DeviceIdType.MESH,
            )
            for i, (source, target) in enumerate(zip(sources, targets))
        ]

    @pl.when(n == 0)
    def _():
        barrier = pltpu.get_barrier_semaphore()
        for peer in rounds:
            pl.semaphore_signal(barrier, inc=1, device_id=peer, device_id_type=pl.DeviceIdType.MESH)
        pl.semaphore_wait(barrier, len(rounds))
        for copy in half_copies():
            copy.start()
        total[...] = jnp.zeros_like(total)
        gains[0] = jnp.zeros_like(gains[0])

    @pl.when(n == units)
    def _():
        for copy in half_copies():
            copy.wait()
        own = pl.ds(pl.multiple_of(core * columns, LANES), columns)
        other = pl.ds(pl.multiple_of((1 - core) * columns, LANES), columns)
        gate_out_ref[:, own] = gate_ref[keep, :]
        gate_out_ref[:, other] = half_got[0]
        up_out_ref[:, own] = up_ref[keep, :]
        up_out_ref[:, other] = half_got[1]
        half = down_ref.shape[1]
        down_out_ref[:, pl.ds(pl.multiple_of(core * half, LANES), half)] = down_ref[down_keep, :]
        down_out_ref[:, pl.ds(pl.multiple_of((1 - core) * half, LANES), half)] = down_got[...]

    step_streams(streams, n)
    sum_gains(rounds, n, units, gains, gains_got, gains_sent_sem, gains_got_sem)

    @pl.when(n == steps - 1)
    def _():
        gains_ref[...] = gains[len(rounds)]

    @pl.when(n < units)
    def _():
        hidden = hidden_ref[...]

        def got_lanes(lane):
            return jnp.concatenate(
                [got_ref[0, :, lane : lane + LANES], got_ref[1, :, lane : lane + LANES]], axis=0
            ).astype(F32)

        def back(got, lane, head_gain, place):
            turned = got * cos_ref[...] - half_partner(got) * sin_ref[...]
            block = proj_ref[0, :, lane : lane + LANES]
            scale = lax.rsqrt(head_means(block * block) + EPSILON)
            normal = block * scale
            gains[0, place : place + 1, :] += jnp.sum(turned * normal, axis=0, keepdims=True)
            pushed = turned * head_gain[...]
            inner = head_means(pushed * normal)
            return (scale * (pushed - normal * inner)).astype(BF16)

        width = tokens_ref.shape[1]
        lines = width // LANES
        query = jnp.concatenate(
            [back(got_lanes(2 * at), at, q_gain_ref, 2 * lines) for at in range(0, q_width, LANES)],
            axis=1,
        )
        first, second = got_lanes(LANES), got_lanes(3 * LANES)
        low = low_lanes(first.shape)
        key = jnp.where(low, first, pltpu.roll(second, HEAD_DIM, 1))
        key = back(key, q_width, k_gain_ref, 2 * lines + 1)
        value = jnp.where(low, pltpu.roll(first, HEAD_DIM, 1), second).astype(BF16)
        for stream, part in ((query_stream, query), (pair_stream, jnp.concatenate([key, value], axis=1))):
            shape = stream.shape(stream.names[0])
            stream.source[stream.slot(n)] = tn_dot(hidden, part).astype(BF16).reshape(shape)

        total[...] += (
            nt_dot(query, wq_ref[...]) + nt_dot(key, wk_ref[...]) + nt_dot(value, wv_ref[...])
        )

        @pl.when(n == units - 1)
        def _():
            inputs = tokens_ref[...].astype(F32)
            scale = lax.rsqrt(jnp.mean(inputs * inputs, axis=-1, keepdims=True) + EPSILON)
            normal = inputs * scale
            grad = total[...]
            gain_grad = jnp.sum(grad * normal, axis=0, keepdims=True)
            for i in range(lines):
                here = slice(i * LANES, (i + 1) * LANES)
                gains[0, i : i + 1, :] = gain_grad[:, here]
                gains[0, lines + i : lines + i + 1, :] = ffn_gain_ref[:, here]
            pushed = grad * gain_ref[...]
            inner = jnp.mean(pushed * normal, axis=-1, keepdims=True)
            input_ref[...] = (mid_ref[...] + scale * (pushed - normal * inner)).astype(BF16)


def finish(
    line,
    bits,
    got,
    proj,
    hidden,
    tokens,
    mid,
    gain,
    wq,
    wk,
    wv,
    q_gain,
    k_gain,
    cosine,
    sine,
    ffn_gain,
    gate_sum,
    up_sum,
    down_sum,
):
    rows, width = tokens.shape
    count, half, lanes = got.shape
    units = count // 2
    q_width = wq.shape[1] // units
    chips = line * 2 ** len(bits)
    mine = width // chips // 2
    zs = line_bits(line)
    names = zs[::-1] + bits + [1]
    streams = [
        Stream([1] + bits[::-1] + zs, names, (mine, q_width), LAST_LAG, units),
        Stream([1] + bits + zs, names, (mine, 2 * LANES), LAST_LAG, units),
    ]
    rounds = 1 + len(bits) + (line - 1).bit_length()
    steps = max([stream.steps() for stream in streams] + [units + rounds + 2])
    gain_rows = -(-(2 * width // LANES + 2) // 8) * 8
    half_rows = gate_sum.shape[0] // 2
    down_rows = down_sum.shape[0] // 2
    columns = gate_sum.shape[1]

    def keep(shape):
        return pl.BlockSpec(shape, lambda n: (0,) * len(shape), pipeline_mode=pl.Buffered(1))

    def at(n):
        return jnp.minimum(n, units - 1)

    scratch = [
        pltpu.VMEM((rows, width), F32),
        pltpu.VMEM((rounds + 1, gain_rows, LANES), F32),
        pltpu.VMEM((rounds, gain_rows, LANES), F32),
        pltpu.SemaphoreType.DMA((rounds,)),
        pltpu.SemaphoreType.DMA((rounds,)),
        pltpu.VMEM((2, half_rows, columns), BF16),
        pltpu.VMEM((down_rows, down_sum.shape[1]), BF16),
        pltpu.SemaphoreType.DMA((3,)),
        pltpu.SemaphoreType.DMA((3,)),
    ]
    for stream in streams:
        scratch += stream.scratch()
    outs = [
        ((rows, width), BF16),
        ((gain_rows, LANES), F32),
        ((mine, wq.shape[1]), BF16),
        ((mine, wk.shape[1]), BF16),
        ((mine, wv.shape[1]), BF16),
        ((half_rows, 2 * columns), BF16),
        ((half_rows, 2 * columns), BF16),
        ((down_rows, 2 * down_sum.shape[1]), BF16),
    ]
    return pl.pallas_call(
        functools.partial(finish_kernel, line, bits, streams, units),
        name="finish",
        grid=(steps,),
        in_specs=[
            pl.BlockSpec((2, half, lanes), lambda n: (at(n), 0, 0)),
            pl.BlockSpec((1, rows, q_width + LANES), lambda n: (at(n), 0, 0)),
            keep((rows, width)),
            keep((rows, width)),
            keep((rows, width)),
            keep((1, width)),
            pl.BlockSpec((width, q_width), lambda n: (0, at(n))),
            pl.BlockSpec((width, LANES), lambda n: (0, at(n))),
            pl.BlockSpec((width, LANES), lambda n: (0, at(n))),
            keep((1, LANES)),
            keep((1, LANES)),
            keep((rows, LANES)),
            keep((rows, LANES)),
            keep((1, width)),
            keep(gate_sum.shape),
            keep(up_sum.shape),
            keep(down_sum.shape),
        ],
        out_specs=[keep(shape) for shape, unused in outs],
        out_shape=[jax.ShapeDtypeStruct(shape, kind) for shape, kind in outs],
        scratch_shapes=scratch,
        compiler_params=kernel_params(collective_id=5, has_side_effects=True),
    )(
        got,
        proj,
        hidden,
        tokens,
        mid,
        gain,
        wq,
        wk,
        wv,
        q_gain,
        k_gain,
        cosine,
        sine,
        ffn_gain,
        gate_sum,
        up_sum,
        down_sum,
    )


def widen_kernel(count, gains_ref, *refs):
    for source, target in zip(refs[:count], refs[count : 2 * count]):
        target[...] = source[...].astype(F32)
    attn_ref, ffn_ref, heads_ref = refs[2 * count :]
    lines = attn_ref.shape[0]
    attn_ref[...] = gains_ref[:lines, :]
    ffn_ref[...] = gains_ref[lines : 2 * lines, :]
    both = gains_ref[2 * lines : 2 * lines + 2, :]
    heads_ref[...] = both + pltpu.roll(both, HEAD_DIM, 1)


def widen(gains, lines, parts):
    shapes = [part.shape for part in parts] + [(lines, LANES), (lines, LANES), (2, LANES)]
    return pl.pallas_call(
        functools.partial(widen_kernel, len(parts)),
        name="widen",
        out_shape=[jax.ShapeDtypeStruct(shape, F32) for shape in shapes],
        compiler_params=kernel_params(),
    )(gains, *parts)


def flip_pairs(count, bit):
    return [(i, i ^ bit) for i in range(count)]


def swap_core(block, blk_count):
    return lax.ppermute(block, "blk", flip_pairs(blk_count, 1))


def fast_local(
    dp_count,
    blk_count,
    tokens,
    doc_lengths,
    g_attn,
    w_query,
    w_key,
    w_value,
    q_gain,
    k_gain,
    w_out,
    g_ffn,
    w_gate,
    w_up,
    w_down,
    cotangent,
):
    row_count, tok_count, width = tokens.shape
    rows = row_count * tok_count
    chips = blk_count // 2
    size = tok_count * blk_count
    index = lax.axis_index("blk")
    core = index % 2
    bits = []
    bit = blk_count // 2
    while bit > 1:
        bits.append(bit)
        bit //= 2
    chip_dims = (dp_count,) + (2,) * len(bits)
    all_chips = dp_count * chips
    which = jnp.arange(doc_lengths.shape[1])
    ends = jnp.sum(jnp.where(which[:, None] <= which[None, :], doc_lengths[:, :, None], 0), axis=1)
    places = index * tok_count + jnp.arange(tok_count, dtype=jnp.int32)[None]
    begins = jnp.max(jnp.where(places[:, :, None] >= ends[:, None, :], ends[:, None, :], 0), axis=2)
    positions = (places - begins).reshape(rows, 1).astype(F32)
    half_head = HEAD_DIM // 2
    lane = jnp.arange(LANES)
    freqs = ROPE_BASE ** (-(lane % half_head).astype(F32) / half_head)
    angles = positions * freqs
    cosine = jnp.cos(angles)
    sine = jnp.sin(angles) * jnp.where(lane % HEAD_DIM < half_head, -1.0, 1.0)
    q_gain2 = jnp.tile(q_gain, 2)[None]
    k_gain2 = jnp.tile(k_gain, 2)[None]
    all_places = jnp.arange(size, dtype=jnp.int32)
    own_ends = lax.dynamic_slice_in_dim(ends, core, 1, axis=0)
    starts = jnp.max(jnp.where(all_places[:, None] >= own_ends, own_ends, 0), axis=1)
    starts_two = jnp.broadcast_to(
        starts.reshape(blk_count, 1, tok_count), (blk_count, 2, tok_count)
    ).reshape(1, 2 * size)
    flat = tokens.reshape(rows, width)
    grad_own = cotangent.reshape(rows, width)
    grad_got = swap_core(grad_own, blk_count)

    hidden_in, proj, qkv, attended, logs, heads = forward(
        flat,
        g_attn[None],
        w_query,
        w_key,
        w_value,
        q_gain2,
        k_gain2,
        cosine,
        sine,
        starts[:, None],
    )
    output, mid, ffn_gain_grad, w_out_parts, grad_heads, acts, gate_sum, up_sum = middle_layer(
        dp_count,
        bits,
        flat,
        heads,
        w_out,
        g_ffn[None],
        grad_own,
        grad_got,
        w_gate,
        w_up,
        w_down,
    )
    got, down_sum, w_out_sum = back(
        dp_count,
        bits,
        qkv,
        logs,
        attended.reshape(size, -1),
        grad_heads.reshape(size, -1),
        starts_two,
        tok_count,
        grad_own,
        grad_got,
        acts,
        w_out_parts,
    )
    input_grad, gains, *sums = finish(
        dp_count,
        bits,
        got,
        proj,
        hidden_in,
        flat,
        mid,
        g_attn[None],
        w_query,
        w_key,
        w_value,
        q_gain2,
        k_gain2,
        cosine,
        sine,
        ffn_gain_grad,
        gate_sum,
        up_sum,
        down_sum,
    )
    *sums, gain_attn, gain_ffn, gain_heads = widen(gains, width // LANES, sums + [w_out_sum])
    grad_w_query, grad_w_key, grad_w_value, grad_w_gate, grad_w_up, grad_w_down, grad_w_out = sums
    gain_attn, gain_ffn = gain_attn.reshape(width), gain_ffn.reshape(width)
    gain_query, gain_key = gain_heads[0, :HEAD_DIM], gain_heads[1, :HEAD_DIM]
    return (
        output.reshape(tokens.shape),
        input_grad.reshape(tokens.shape),
        gain_attn,
        grad_w_query,
        grad_w_key,
        grad_w_value,
        gain_query,
        gain_key,
        grad_w_out,
        gain_ffn,
        grad_w_gate,
        grad_w_up,
        grad_w_down,
    )


def fits(mesh):
    blk_count = mesh.shape["blk"]
    chips = blk_count // 2
    line = mesh.shape["dp"]
    power = blk_count & (blk_count - 1) == 0 and line & (line - 1) == 0
    return power and blk_count > 2 and line > 1 and (KV_HEADS * HEAD_DIM) == chips * LANES


def solution(mesh):
    if fits(mesh):
        body = functools.partial(fast_local, mesh.shape["dp"], mesh.shape["blk"])
    else:
        body = local
    return jax.shard_map(
        body,
        mesh=mesh,
        in_specs=(
            P("dp", "blk", None),
            P("dp", None),
            P(),
            P(),
            P(),
            P(),
            P(),
            P(),
            P(),
            P(),
            P(),
            P(),
            P(),
            P("dp", "blk", None),
        ),
        out_specs=(
            P("dp", "blk", None),
            P("dp", "blk", None),
            P(),
            P(("dp", "blk"), None),
            P(("dp", "blk"), None),
            P(("dp", "blk"), None),
            P(),
            P(),
            P(("dp", "blk"), None),
            P(),
            P(("dp", "blk"), None),
            P(("dp", "blk"), None),
            P(("dp", "blk"), None),
        ),
        check_vma=False,
    )
```

```python
import functools
import math

import jax
import jax.numpy as jnp
from jax import lax
from jax.experimental import pallas as pl
from jax.experimental.pallas import tpu as pltpu
from jax.sharding import PartitionSpec as P

HEADS = 16
KV_HEADS = 8
HEAD_DIM = 64


EPSILON = 1e-05
ROPE_BASE = 1000000.0
NEGATIVE = -1e30


def norm_rows(values, norm_gain):
    row_scale = lax.rsqrt(jnp.mean(values * values, axis=-1, keepdims=True) + EPSILON)
    normal = values * row_scale
    return (normal * norm_gain, normal, row_scale)


def norm_back(normal, row_scale, norm_gain, grad_out):
    pushed = grad_out * norm_gain
    inner = jnp.mean(pushed * normal, axis=-1, keepdims=True)
    grad_in = row_scale * (pushed - normal * inner)
    leading = tuple(range(grad_out.ndim - 1))
    return (grad_in, jnp.sum(grad_out * normal, axis=leading))


def doc_layout(lengths, places):
    ends = jnp.cumsum(lengths, axis=1)
    past = places[None, :, None] >= ends[:, None, :]
    docs = jnp.sum(past.astype(jnp.int32), axis=2)
    before = jnp.sum(jnp.where(past, lengths[:, None, :], 0), axis=2)
    return (docs, places[None, :] - before)


def rope_angles(positions):
    half = HEAD_DIM // 2
    freqs = ROPE_BASE ** (-jnp.arange(half, dtype=jnp.float32) / half)
    angles = positions.astype(jnp.float32)[..., None] * freqs
    return (jnp.cos(angles), jnp.sin(angles))


def rotate(values, cosine, sine):
    half = values.shape[-1] // 2
    first_half = values[..., :half]
    second_half = values[..., half:]
    cos_col = cosine[:, :, None, :]
    sin_col = sine[:, :, None, :]
    return jnp.concatenate(
        [
            first_half * cos_col - second_half * sin_col,
            second_half * cos_col + first_half * sin_col,
        ],
        axis=-1,
    )


def local(
    tokens,
    doc_lengths,
    g_attn,
    w_query,
    w_key,
    w_value,
    q_gain,
    k_gain,
    w_out,
    g_ffn,
    w_gate,
    w_up,
    w_down,
    cotangent,
):
    row_count, tok_count, width = tokens.shape
    grouping = HEADS // KV_HEADS
    flat_rows = row_count * tok_count
    kv_width = KV_HEADS * HEAD_DIM
    softmax_scale = HEAD_DIM ** (-0.5)
    places = lax.axis_index("blk") * tok_count + jnp.arange(tok_count, dtype=jnp.int32)
    query_docs, query_pos = doc_layout(doc_lengths, places)
    cosine, sine = rope_angles(query_pos)
    inputs = tokens.reshape(flat_rows, width).astype(jnp.float32)
    normed, normal_in, scale_in = norm_rows(inputs, g_attn)
    hidden_in = normed.astype(jnp.bfloat16)
    query_proj = jnp.dot(hidden_in, w_query, preferred_element_type=jnp.float32).reshape(
        row_count, tok_count, HEADS, HEAD_DIM
    )
    key_proj = jnp.dot(hidden_in, w_key, preferred_element_type=jnp.float32).reshape(
        row_count, tok_count, KV_HEADS, HEAD_DIM
    )
    value_b = (
        jnp.dot(hidden_in, w_value, preferred_element_type=jnp.float32)
        .astype(jnp.bfloat16)
        .reshape(row_count, tok_count, kv_width)
    )
    query_norm, query_normal, query_scale = norm_rows(query_proj, q_gain)
    key_norm, key_normal, key_scale = norm_rows(key_proj, k_gain)
    query_b = (
        rotate(query_norm, cosine, sine)
        .astype(jnp.bfloat16)
        .reshape(row_count, tok_count, KV_HEADS, grouping, HEAD_DIM)
    )
    key_b = (
        rotate(key_norm, cosine, sine).astype(jnp.bfloat16).reshape(row_count, tok_count, kv_width)
    )

    def piece_mask(size):
        key_places = jnp.arange(size, dtype=jnp.int32)
        key_docs, unused = doc_layout(doc_lengths, key_places)
        return (key_places[None, None, :] <= places[None, :, None]) & (
            key_docs[:, None, :] == query_docs[:, :, None]
        )

    def piece_scores(key_piece, allowed):
        key_heads = key_piece.reshape(row_count, key_piece.shape[1], KV_HEADS, HEAD_DIM)
        raw_scores = (
            jnp.einsum("rqkgd,rpkd->rkgqp", query_b, key_heads, preferred_element_type=jnp.float32)
            * softmax_scale
        )
        return (jnp.where(allowed[:, None, None], raw_scores, -jnp.inf), key_heads)

    stat_shape = (row_count, KV_HEADS, grouping, tok_count)
    key_piece = lax.all_gather(key_b, "blk", axis=1, tiled=True)
    value_piece = lax.all_gather(value_b, "blk", axis=1, tiled=True)
    allowed = piece_mask(key_piece.shape[1])
    running_max = jnp.full(stat_shape, NEGATIVE, jnp.float32)
    scores, key_heads = piece_scores(key_piece, allowed)
    new_max = jnp.maximum(running_max, jnp.max(scores, axis=-1))
    weights = jnp.exp(scores - new_max[..., None])
    value_heads = value_piece.reshape(row_count, value_piece.shape[1], KV_HEADS, HEAD_DIM)
    added = jnp.einsum(
        "rkgqp,rpkd->rkgqd",
        weights.astype(jnp.bfloat16),
        value_heads,
        preferred_element_type=jnp.float32,
    )
    running_sum = jnp.sum(weights, axis=-1)
    attended = added / running_sum[..., None]
    log_total = new_max + jnp.log(running_sum)
    attended_b = (
        jnp.transpose(attended, (0, 3, 1, 2, 4))
        .reshape(flat_rows, HEADS * HEAD_DIM)
        .astype(jnp.bfloat16)
    )
    middle = inputs + jnp.dot(attended_b, w_out, preferred_element_type=jnp.float32)
    normed_ffn, normal_ffn, scale_ffn = norm_rows(middle, g_ffn)
    hidden_ffn = normed_ffn.astype(jnp.bfloat16)
    gate = jnp.dot(hidden_ffn, w_gate, preferred_element_type=jnp.float32)
    up_proj = jnp.dot(hidden_ffn, w_up, preferred_element_type=jnp.float32)
    sigmoid_gate = jax.nn.sigmoid(gate)
    silu_gate = gate * sigmoid_gate
    hidden = (silu_gate * up_proj).astype(jnp.bfloat16)
    result = middle + jnp.dot(hidden, w_down, preferred_element_type=jnp.float32)
    output = result.astype(jnp.bfloat16).reshape(row_count, tok_count, width)
    grad_out = cotangent.reshape(flat_rows, width)
    grad_w_down = jnp.einsum("tf,td->fd", hidden, grad_out, preferred_element_type=jnp.float32)
    grad_hidden = jnp.einsum("td,fd->tf", grad_out, w_down, preferred_element_type=jnp.float32)
    grad_gate = (grad_hidden * up_proj * sigmoid_gate * (1.0 + gate * (1.0 - sigmoid_gate))).astype(
        jnp.bfloat16
    )
    grad_up = (grad_hidden * silu_gate).astype(jnp.bfloat16)
    grad_w_gate = jnp.einsum("td,tf->df", hidden_ffn, grad_gate, preferred_element_type=jnp.float32)
    grad_w_up = jnp.einsum("td,tf->df", hidden_ffn, grad_up, preferred_element_type=jnp.float32)
    grad_h2 = jnp.einsum(
        "tf,df->td", grad_gate, w_gate, preferred_element_type=jnp.float32
    ) + jnp.einsum("tf,df->td", grad_up, w_up, preferred_element_type=jnp.float32)
    grad_mid, grad_ffn_gain = norm_back(normal_ffn, scale_ffn, g_ffn, grad_h2)
    grad_mid = grad_out.astype(jnp.float32) + grad_mid
    grad_attn = grad_mid.astype(jnp.bfloat16)
    grad_w_out = jnp.einsum("tc,td->cd", attended_b, grad_attn, preferred_element_type=jnp.float32)
    grad_attended = jnp.einsum(
        "td,cd->tc", grad_attn, w_out, preferred_element_type=jnp.float32
    ).astype(jnp.bfloat16)
    grad_heads = grad_attended.reshape(row_count, tok_count, KV_HEADS, grouping, HEAD_DIM)
    deltas = jnp.einsum("rqkgd,rkgqd->rkgq", grad_heads.astype(jnp.float32), attended)
    key_piece = lax.all_gather(key_b, "blk", axis=1, tiled=True)
    value_piece = lax.all_gather(value_b, "blk", axis=1, tiled=True)
    size = key_piece.shape[1]
    allowed = piece_mask(size)
    scores, key_heads = piece_scores(key_piece, allowed)
    probs = jnp.exp(scores - log_total[..., None])
    value_heads = value_piece.reshape(row_count, size, KV_HEADS, HEAD_DIM)
    value_piece_grad = jnp.einsum(
        "rkgqp,rqkgd->rpkd",
        probs.astype(jnp.bfloat16),
        grad_heads,
        preferred_element_type=jnp.float32,
    )
    grad_probs = jnp.einsum(
        "rqkgd,rpkd->rkgqp", grad_heads, value_heads, preferred_element_type=jnp.float32
    )
    grad_scores = (probs * (grad_probs - deltas[..., None])).astype(jnp.bfloat16)
    grad_query = jnp.einsum(
        "rkgqp,rpkd->rkgqd", grad_scores, key_heads, preferred_element_type=jnp.float32
    )
    key_piece_grad = jnp.einsum(
        "rkgqp,rqkgd->rpkd", grad_scores, query_b, preferred_element_type=jnp.float32
    )
    grad_keys = key_piece_grad.reshape(row_count, size, kv_width)
    grad_values = value_piece_grad.reshape(row_count, size, kv_width)
    grad_query, grad_keys, grad_values = (grad_query, grad_keys, grad_values)
    key_grad_mine, value_grad_mine = (
        lax.psum_scatter(
            grad_keys.astype(jnp.bfloat16), "blk", scatter_dimension=1, tiled=True
        ).astype(jnp.float32),
        lax.psum_scatter(
            grad_values.astype(jnp.bfloat16), "blk", scatter_dimension=1, tiled=True
        ).astype(jnp.float32),
    )
    grad_q_rot = (jnp.transpose(grad_query, (0, 3, 1, 2, 4)) * softmax_scale).reshape(
        row_count, tok_count, HEADS, HEAD_DIM
    )
    grad_k_rot = (key_grad_mine * softmax_scale).reshape(row_count, tok_count, KV_HEADS, HEAD_DIM)
    grad_q_proj, grad_query_gain = norm_back(
        query_normal, query_scale, q_gain, rotate(grad_q_rot, cosine, -sine)
    )
    grad_k_proj, grad_key_gain = norm_back(
        key_normal, key_scale, k_gain, rotate(grad_k_rot, cosine, -sine)
    )
    grad_q_b = grad_q_proj.astype(jnp.bfloat16).reshape(flat_rows, HEADS * HEAD_DIM)
    grad_k_b = grad_k_proj.astype(jnp.bfloat16).reshape(flat_rows, kv_width)
    grad_v_b = value_grad_mine.astype(jnp.bfloat16).reshape(flat_rows, kv_width)
    grad_w_query = jnp.einsum("td,tc->dc", hidden_in, grad_q_b, preferred_element_type=jnp.float32)
    grad_w_key = jnp.einsum("td,tc->dc", hidden_in, grad_k_b, preferred_element_type=jnp.float32)
    grad_w_value = jnp.einsum("td,tc->dc", hidden_in, grad_v_b, preferred_element_type=jnp.float32)
    grad_h1 = jnp.einsum("tc,dc->td", grad_q_b, w_query, preferred_element_type=jnp.float32)
    grad_h1 = grad_h1 + jnp.einsum("tc,dc->td", grad_k_b, w_key, preferred_element_type=jnp.float32)
    grad_h1 = grad_h1 + jnp.einsum(
        "tc,dc->td", grad_v_b, w_value, preferred_element_type=jnp.float32
    )
    grad_base, grad_attn_gain = norm_back(normal_in, scale_in, g_attn, grad_h1)
    input_grad = (grad_mid + grad_base).astype(jnp.bfloat16).reshape(row_count, tok_count, width)
    gain_attn, gain_query, gain_key, gain_ffn = lax.psum(
        (grad_attn_gain, grad_query_gain, grad_key_gain, grad_ffn_gain), ("dp", "blk")
    )
    locals_all = (
        grad_w_query,
        grad_w_key,
        grad_w_value,
        grad_w_out,
        grad_w_gate,
        grad_w_up,
        grad_w_down,
    )
    shared = (
        lax.psum_scatter(locals_all[0], ("dp", "blk"), scatter_dimension=0, tiled=True),
        lax.psum_scatter(locals_all[1], ("dp", "blk"), scatter_dimension=0, tiled=True),
        lax.psum_scatter(locals_all[2], ("dp", "blk"), scatter_dimension=0, tiled=True),
        lax.psum_scatter(locals_all[3], ("dp", "blk"), scatter_dimension=0, tiled=True),
        lax.psum_scatter(locals_all[4], ("dp", "blk"), scatter_dimension=0, tiled=True),
        lax.psum_scatter(locals_all[5], ("dp", "blk"), scatter_dimension=0, tiled=True),
        lax.psum_scatter(locals_all[6], ("dp", "blk"), scatter_dimension=0, tiled=True),
    )
    return (
        output,
        input_grad,
        gain_attn,
        shared[0],
        shared[1],
        shared[2],
        gain_query,
        gain_key,
        shared[3],
        gain_ffn,
        shared[4],
        shared[5],
        shared[6],
    )


BF16 = jnp.bfloat16
F32 = jnp.float32
LANES = 128
FF_TILE = 256
LAG = 2
LAST_LAG = 1
ATTEND_PAIRS = 6
VMEM_BYTES = 60 * 1024 * 1024
LOG2_E = math.log2(math.e)
QUERY_SCALE = HEAD_DIM ** (-0.5) * LOG2_E
MASKED = -1e30


def nn_dot(left, right):
    return lax.dot_general(left, right, (((1,), (0,)), ((), ())), preferred_element_type=F32)


def nt_dot(left, right):
    return lax.dot_general(left, right, (((1,), (1,)), ((), ())), preferred_element_type=F32)


def tn_dot(left, right):
    return lax.dot_general(left, right, (((0,), (0,)), ((), ())), preferred_element_type=F32)


def kernel_params(**more):
    return pltpu.CompilerParams(vmem_limit_bytes=VMEM_BYTES, **more)


def whole_block(shape):
    return pl.BlockSpec(shape, lambda *ids: (0,) * len(shape))


def greet_blk(count):
    barrier = pltpu.get_barrier_semaphore()
    z, index = lax.axis_index("dp"), lax.axis_index("blk")
    for step in range(1, count):
        pl.semaphore_signal(
            barrier,
            inc=1,
            device_id=(z, lax.rem(index + step, count)),
            device_id_type=pl.DeviceIdType.MESH,
        )
    pl.semaphore_wait(barrier, count - 1)


def blk_copy(send, got, sent_sem, got_sem, target, source):
    return pltpu.make_async_remote_copy(
        src_ref=send.at[target],
        dst_ref=got.at[source],
        send_sem=sent_sem.at[target],
        recv_sem=got_sem.at[source],
        device_id=(lax.axis_index("dp"), target),
        device_id_type=pl.DeviceIdType.MESH,
    )


def head_means(values):
    rows = lax.broadcasted_iota(jnp.int32, (LANES, LANES), 0) // HEAD_DIM
    cols = lax.broadcasted_iota(jnp.int32, (LANES, LANES), 1) // HEAD_DIM
    spread = jnp.where(rows == cols, 1.0 / HEAD_DIM, 0.0).astype(BF16)
    high = values.astype(BF16)
    low = (values - high.astype(F32)).astype(BF16)
    return nn_dot(high, spread) + nn_dot(low, spread)


def half_partner(values):
    lane = lax.broadcasted_iota(jnp.int32, values.shape, 1)
    half = HEAD_DIM // 2
    ahead = pltpu.roll(values, LANES - half, 1)
    behind = pltpu.roll(values, half, 1)
    return jnp.where(lane % HEAD_DIM < half, ahead, behind)


def low_lanes(shape):
    return lax.broadcasted_iota(jnp.int32, shape, 1) < HEAD_DIM


def parted(packed):
    turned = pltpu.roll(packed.astype(F32), HEAD_DIM, 1).astype(BF16)
    low = low_lanes(packed.shape)
    return jnp.where(low, packed, turned), jnp.where(low, turned, packed)


def stacked_heads(pair):
    low = low_lanes(pair.shape)
    none = jnp.zeros_like(pair)
    return jnp.concatenate([jnp.where(low, pair, none), jnp.where(low, none, pair)], axis=0)


def in_three(column):
    lane = lax.broadcasted_iota(jnp.int32, (column.shape[0], LANES), 1)
    wide = jnp.broadcast_to(column, (column.shape[0], LANES))
    first = wide.astype(BF16).astype(F32)
    second = (wide - first).astype(BF16).astype(F32)
    third = wide - first - second
    return jnp.where(
        lane == 0, first, jnp.where(lane == 1, second, jnp.where(lane == 2, third, 0.0))
    ).astype(BF16)


def minus_three(rows):
    lane = lax.broadcasted_iota(jnp.int32, (rows, LANES), 1)
    return jnp.where(lane < 3, -1.0, 0.0).astype(BF16)


def forward_kernel(
    chips,
    groups,
    tokens_ref,
    gain_ref,
    wq_ref,
    wk_ref,
    wv_ref,
    head_gains_ref,
    cos_ref,
    sin_ref,
    starts_ref,
    hidden_ref,
    proj_ref,
    qkv_ref,
    out_ref,
    logs_ref,
    heads_ref,
    send,
    got,
    keys,
    values,
    total,
    out_send,
    out_got,
    sent_sem,
    got_sem,
    out_sent_sem,
    out_got_sem,
):
    n = pl.program_id(0)
    blocks, block = send.shape[1:3]
    size = blocks * block
    index = lax.axis_index("blk")
    p = lax.rem(index // 2 + 1 + n, chips)

    def give(g, p):
        for part in range(2):
            target = 2 * p + part

            @pl.when(target != index)
            def _():
                blk_copy(send.at[g], got.at[g], sent_sem.at[g], got_sem.at[g], target, index).start()

            @pl.when(target == index)
            def _():
                got[g, target] = send[g, target]

    @pl.when(n == 0)
    def _():
        greet_blk(blocks)
        inputs = tokens_ref[...].astype(F32)
        scale = lax.rsqrt(jnp.mean(inputs * inputs, axis=-1, keepdims=True) + EPSILON)
        hidden_ref[...] = (inputs * scale * gain_ref[...]).astype(BF16)

    @pl.when(n < chips)
    def _():
        hidden = hidden_ref[...]
        queries = nn_dot(hidden, wq_ref[...])
        keys_of = nn_dot(hidden, wk_ref[...])
        values_of = nn_dot(hidden, wv_ref[...])

        def turn(part, lane, head_gain):
            proj_ref[0, :, lane : lane + LANES] = part
            scale = lax.rsqrt(head_means(part * part) + EPSILON)
            normed = part * scale * head_gain
            return normed * cos_ref[...] + half_partner(normed) * sin_ref[...]

        def put(g, lane, part):
            for half in range(2):
                send[g, 2 * p + half, :, lane : lane + LANES] = part[half * block : (half + 1) * block].astype(BF16)

        q_gain, k_gain = head_gains_ref[0:1, :], head_gains_ref[1:2, :]
        key = turn(keys_of, groups * LANES, k_gain)
        low = low_lanes(key.shape)
        for g in range(groups):
            lanes = slice(g * LANES, (g + 1) * LANES)
            put(g, 0, turn(queries[:, lanes], g * LANES, q_gain) * QUERY_SCALE)
            if g == 0:
                put(g, LANES, jnp.where(low, key, pltpu.roll(values_of, HEAD_DIM, 1)))
            else:
                put(g, LANES, jnp.where(low, pltpu.roll(key, HEAD_DIM, 1), values_of))
        give(0, p)

    @pl.when(n == chips - 1)
    def _():
        for step in range(chips):
            give(1, lax.rem(index // 2 + 1 + step, chips))

    for g in range(groups):

        @pl.when(n == chips + g * blocks)
        def _():
            for step in range(1, blocks):
                other = lax.rem(index + step, blocks)
                blk_copy(send.at[g], got.at[g], sent_sem.at[g], got_sem.at[g], other, other).wait()
            for i in range(blocks):
                here = slice(i * block, (i + 1) * block)
                qkv_ref[g, here, :] = got[g, i]
                keys[here, :], values[here, :LANES] = parted(got[g, i, :, LANES:])
                values[here, LANES:] = jnp.ones((block, LANES), BF16)

    @pl.when(n >= chips)
    def _():
        g = (n - chips) // blocks
        here = lax.rem(index + 1 + lax.rem(n - chips, blocks), blocks)
        at = pl.multiple_of(here * block, block)
        row_at = pl.multiple_of(here * 2 * block, 2 * block)
        lines = jnp.broadcast_to(starts_ref[:, pl.ds(row_at, 2 * block)], (LANES, 2 * block))
        starts = lines.T[:, :1]
        query = stacked_heads(got[g, here, :, :LANES])

        def step(key_at, width, diagonal):
            column = lax.broadcasted_iota(jnp.int32, (2 * block, width), 1)
            allowed = column >= starts - key_at
            if diagonal:
                row = lax.broadcasted_iota(jnp.int32, (2 * block, width), 0) % block
                allowed = allowed & (column <= row)
            scores = nt_dot(query, keys[pl.ds(key_at, width), :])
            weights = jnp.exp2(jnp.where(allowed, scores, MASKED)).astype(BF16)
            part = nn_dot(weights, values[pl.ds(key_at, width), :])
            if diagonal:
                total[...] = part
            else:
                total[...] += part

        step(at, block, True)

        @pl.when(lax.rem(here, 2) == 1)
        def _():
            step(pl.multiple_of((here - 1) * block, block), block, False)

        def body(j, carry):
            step(pl.multiple_of(j * 2 * block, 2 * block), 2 * block, False)
            return carry

        lax.fori_loop(0, here // 2, body, 0)
        low = low_lanes((block, LANES))
        to = pl.multiple_of(here * 2 * block, 2 * block)
        sums = total[:, LANES:]
        mean = total[:, :LANES] / sums
        made = jnp.where(low, mean[:block], mean[block:]).astype(BF16)
        out_send[g, here] = made
        out_ref[here, :, pl.ds(pl.multiple_of(g * LANES, LANES), LANES)] = made
        logs_ref[g, pl.ds(to, 2 * block), :] = in_three(jnp.log2(sums[:, :1]))

        @pl.when(here != index)
        def _():
            blk_copy(
                out_send.at[g], out_got.at[g], out_sent_sem.at[g], out_got_sem.at[g], here, index
            ).start()

        @pl.when(here == index)
        def _():
            out_got[g, here] = made

    @pl.when(n == pl.num_programs(0) - 1)
    def _():
        for g in range(groups):
            for step in range(1, blocks):
                other = lax.rem(index + step, blocks)
                blk_copy(
                    out_send.at[g], out_got.at[g], out_sent_sem.at[g], out_got_sem.at[g], other, other
                ).wait()
            heads_ref[:, :, g * LANES : (g + 1) * LANES] = out_got[g]


def forward(tokens, gain, wq, wk, wv, head_gains, cosine, sine, starts):
    rows, width = tokens.shape
    chips = wk.shape[1] // LANES
    q_width = wq.shape[1] // chips
    groups, blocks, block = q_width // LANES, 2 * chips, rows // 2
    size = blocks * block

    def keep(shape):
        return pl.BlockSpec(shape, lambda n: (0,) * len(shape), pipeline_mode=pl.Buffered(1))

    def at(n):
        return lax.rem(lax.axis_index("blk") // 2 + 1 + jnp.minimum(n, chips - 1), chips)

    outs = [
        ((rows, width), BF16),
        ((chips, rows, q_width + LANES), F32),
        ((groups, size, 2 * LANES), BF16),
        ((blocks, block, q_width), BF16),
        ((groups, 2 * size, LANES), BF16),
        ((blocks, block, q_width), BF16),
    ]
    out_specs = [keep(shape) for shape, unused in outs]
    out_specs[1] = pl.BlockSpec((1, rows, q_width + LANES), lambda n: (at(n), 0, 0))
    moved, heads = (groups, blocks, block, 2 * LANES), (groups, blocks, block, LANES)
    return pl.pallas_call(
        functools.partial(forward_kernel, chips, groups),
        name="forward",
        grid=(chips + groups * blocks,),
        in_specs=[
            keep((rows, width)),
            keep((1, width)),
            pl.BlockSpec((width, q_width), lambda n: (0, at(n))),
            pl.BlockSpec((width, LANES), lambda n: (0, at(n))),
            pl.BlockSpec((width, LANES), lambda n: (0, at(n))),
            keep((2, LANES)),
            keep((rows, LANES)),
            keep((rows, LANES)),
            keep((1, 2 * size)),
        ],
        out_specs=out_specs,
        out_shape=[jax.ShapeDtypeStruct(shape, kind) for shape, kind in outs],
        scratch_shapes=[
            pltpu.VMEM(moved, BF16),
            pltpu.VMEM(moved, BF16),
            pltpu.VMEM((size, LANES), BF16),
            pltpu.VMEM((size, 2 * LANES), BF16),
            pltpu.VMEM((2 * block, 2 * LANES), F32),
            pltpu.VMEM(heads, BF16),
            pltpu.VMEM(heads, BF16),
        ]
        + [pltpu.SemaphoreType.DMA((groups, blocks))] * 4,
        compiler_params=kernel_params(collective_id=0, has_side_effects=True),
    )(tokens, gain, wq, wk, wv, head_gains, cosine, sine, starts)


def pair_of(name):
    z, index = lax.axis_index("dp"), lax.axis_index("blk")
    if isinstance(name, tuple):
        mine = lax.rem(z // name[1], 2)
        return mine, (z + name[1] * (1 - 2 * mine), index)
    mine = lax.rem(index // name, 2)
    return mine, (z, index + name * (1 - 2 * mine))


class Stream:
    def __init__(self, path, names, block, lag, units, swap=None):
        self.path, self.block, self.lag, self.units, self.swap = path, block, lag, units, swap
        self.slots = min(2 * lag, units)
        self.names = [tuple(names)]
        for k, stage in enumerate(path):
            left = tuple(name for name in self.names[-1] if name != stage)
            self.names.append((swap,) + left if swap is not None and k == 0 else left)
        assert not self.names[-1]

    def shape(self, names):
        return (2,) * len(names) + self.block

    def steps(self):
        return self.units + self.lag * len(self.path) + 1

    def slot(self, u):
        return lax.rem(u, self.slots)

    def scratch(self):
        shapes = []
        for k, stage in enumerate(self.path):
            left = tuple(name for name in self.names[k] if name != stage)
            shapes.append(pltpu.VMEM((self.slots,) + self.shape(self.names[k]), BF16))
            shapes.append(pltpu.VMEM((self.slots,) + self.shape(left), BF16))
            shapes += [pltpu.SemaphoreType.DMA((self.slots,))] * 2
        return shapes

    def bind(self, refs, finish, begin=0):
        self.finish, self.begin = finish, begin
        self.work, self.got, self.sent_sem, self.got_sem = refs[::4], refs[1::4], refs[2::4], refs[3::4]
        self.source = self.work[0]

    def copy(self, k, u):
        mine, partner = pair_of(self.path[k])
        whole = (slice(None),) * self.names[k].index(self.path[k])
        slot = self.slot(u)
        copy = pltpu.make_async_remote_copy(
            src_ref=self.work[k].at[(slot,) + whole + (1 - mine,)],
            dst_ref=self.got[k].at[slot],
            send_sem=self.sent_sem[k].at[slot],
            recv_sem=self.got_sem[k].at[slot],
            device_id=partner,
            device_id_type=pl.DeviceIdType.MESH,
        )
        return copy, (slot,) + whole + (mine,), mine

    def send(self, k, step):
        u = step - self.begin - self.lag * k - 1

        @pl.when((u >= 0) & (u < self.units))
        def _():
            self.copy(k, u)[0].start()

    def take(self, k, step):
        u = step - self.begin - self.lag * (k + 1) - 1

        @pl.when((u >= 0) & (u < self.units))
        def _():
            copy, own, mine = self.copy(k, u)
            copy.wait()
            slot = self.slot(u)
            if self.swap is not None and k == 0:
                self.work[1][slot, mine] = self.work[0][own]
                self.work[1][slot, 1 - mine] = self.got[0][slot]
            elif k == len(self.path) - 1:
                self.finish(u, self.work[k][own] + self.got[k][slot])
            else:
                self.work[k + 1][slot] = self.work[k][own] + self.got[k][slot]


def step_streams(streams, step):
    for stream in streams:
        for k in range(len(stream.path)):
            stream.take(k, step)
            stream.send(k, step)


def line_bits(line):
    return [("z", 1 << i) for i in range(line.bit_length() - 1)]


def greet_all(blk_count, line):
    barrier = pltpu.get_barrier_semaphore()
    z, index = lax.axis_index("dp"), lax.axis_index("blk")
    peers = [(z, lax.rem(index + step, blk_count)) for step in range(1, blk_count)]
    peers += [pair_of(name)[1] for name in line_bits(line)]
    for peer in peers:
        pl.semaphore_signal(barrier, inc=1, device_id=peer, device_id_type=pl.DeviceIdType.MESH)
    pl.semaphore_wait(barrier, len(peers))


def middle_kernel(
    line,
    bits,
    streams,
    units,
    tokens_ref,
    heads_ref,
    w_out_ref,
    gain_ref,
    dy_own_ref,
    dy_got_ref,
    w_gate_ref,
    w_up_ref,
    w_down_ref,
    output_ref,
    mid_ref,
    gain_grad_ref,
    w_grad_ref,
    grad_heads_ref,
    acts_ref,
    gate_out_ref,
    up_out_ref,
    hidden,
    flipped,
    out_sum,
    back_sum,
    gate_grads,
    up_grads,
    part_send,
    part_got,
    low_grad,
    do_send,
    do_got,
    hidden_sem,
    part_sent_sem,
    part_got_sem,
    do_sent_sem,
    do_got_sem,
    *refs,
):
    n = pl.program_id(0)
    steps = pl.num_programs(0)
    z, index = lax.axis_index("dp"), lax.axis_index("blk")
    sibling = pair_of(1)[1]
    own_rows, width = tokens_ref.shape
    rows = 2 * own_rows
    blk_count, tok_count, head_lanes = heads_ref.shape
    chips = blk_count // 2
    chunk = 256
    gate_stream, up_stream, both_stream = streams
    gate_rows = gate_stream.block[0]
    own, other = pl.ds(0, own_rows), pl.ds(own_rows, own_rows)

    def finish_gate(u, value):
        gate_out_ref[:gate_rows, pl.ds(pl.multiple_of(u * FF_TILE, FF_TILE), FF_TILE)] = value

    def finish_up(u, value):
        up_out_ref[:gate_rows, pl.ds(pl.multiple_of(u * FF_TILE, FF_TILE), FF_TILE)] = value

    def finish_both(u, value):
        here = pl.ds(pl.multiple_of(u * FF_TILE, FF_TILE), FF_TILE)
        gate_out_ref[gate_rows:, here] = value[:, :FF_TILE]
        up_out_ref[gate_rows:, here] = value[:, FF_TILE:]

    at = 0
    for stream, finish in zip(streams, (finish_gate, finish_up, finish_both)):
        count = len(stream.scratch())
        stream.bind(refs[at : at + count], finish)
        at += count

    def hidden_copy():
        return pltpu.make_async_remote_copy(
            src_ref=hidden.at[own],
            dst_ref=hidden.at[other],
            send_sem=hidden_sem.at[0],
            recv_sem=hidden_sem.at[1],
            device_id=sibling,
            device_id_type=pl.DeviceIdType.MESH,
        )

    def part_copy(i):
        return pltpu.make_async_remote_copy(
            src_ref=part_send.at[i],
            dst_ref=part_got.at[i],
            send_sem=part_sent_sem.at[i],
            recv_sem=part_got_sem.at[i],
            device_id=sibling,
            device_id_type=pl.DeviceIdType.MESH,
        )

    def do_copy(target, source):
        return pltpu.make_async_remote_copy(
            src_ref=do_send.at[target],
            dst_ref=do_got.at[source],
            send_sem=do_sent_sem.at[target],
            recv_sem=do_got_sem.at[source],
            device_id=(z, target),
            device_id_type=pl.DeviceIdType.MESH,
        )

    def flip(start):
        for r in range(start, start + own_rows, chunk):
            for c in range(0, width, chunk):
                flipped[c : c + chunk, r : r + chunk] = hidden[r : r + chunk, c : c + chunk].T

    @pl.when(n == 0)
    def _():
        greet_all(blk_count, line)
        total = tokens_ref[...].astype(F32)
        for p in range(chips):
            block = jnp.concatenate([heads_ref[2 * p], heads_ref[2 * p + 1]], axis=0)
            total = total + nn_dot(block, w_out_ref[p * head_lanes : (p + 1) * head_lanes, :])
        mid_ref[...] = total
        scale = lax.rsqrt(jnp.mean(total * total, axis=-1, keepdims=True) + EPSILON)
        hidden[own] = (total * scale * gain_ref[...]).astype(BF16)
        hidden_copy().start()
        out_sum[...] = jnp.zeros_like(out_sum)
        back_sum[...] = jnp.zeros_like(back_sum)
        flip(0)

    @pl.when(n == 1)
    def _():
        hidden_copy().wait()
        flip(own_rows)

    step_streams(streams, n - 1)

    @pl.when((n >= 1) & (n <= units))
    def _():
        for m in range(rows // chunk):
            part = slice(m * chunk, (m + 1) * chunk)
            gate = nn_dot(hidden[part, :], w_gate_ref[...])
            up = nn_dot(hidden[part, :], w_up_ref[...])
            at = m * chunk % own_rows
            dy_ref = dy_own_ref if m * chunk < own_rows else dy_got_ref
            pushed = nt_dot(dy_ref[at : at + chunk, :], w_down_ref[...])
            opened = jax.nn.sigmoid(gate)
            silu = gate * opened
            act = (silu * up).astype(BF16)
            gate_grad = (pushed * up * opened * (1.0 + gate * (1.0 - opened))).astype(BF16)
            up_grad = (pushed * silu).astype(BF16)
            acts_ref[:, part] = act.T
            gate_grads[part, :] = gate_grad
            up_grads[part, :] = up_grad
            out_sum[part, :] += nn_dot(act, w_down_ref[...])
            back_sum[part, :] += nt_dot(gate_grad, w_gate_ref[...]) + nt_dot(up_grad, w_up_ref[...])
        u = n - 1
        slot = gate_stream.slot(u)
        each = width // line
        zs = line.bit_length() - 1
        shape = gate_stream.shape(gate_stream.names[0])[zs:-2] + (-1, FF_TILE)
        for m in range(line):
            at = (slot,) + tuple(m >> i & 1 for i in reversed(range(zs)))
            part = slice(m * each, (m + 1) * each)
            gate_part = nn_dot(flipped[part, :], gate_grads[...]).astype(BF16)
            up_part = nn_dot(flipped[part, :], up_grads[...]).astype(BF16)
            gate_part, up_part = gate_part.reshape(shape), up_part.reshape(shape)
            gate_stream.source[at] = gate_part[..., :gate_rows, :]
            up_stream.source[at] = up_part[..., :gate_rows, :]
            both_stream.source[at + (..., slice(0, FF_TILE))] = gate_part[..., gate_rows:, :]
            both_stream.source[at + (..., slice(FF_TILE, None))] = up_part[..., gate_rows:, :]

    @pl.when(n == units)
    def _():
        part_send[0] = back_sum[other].astype(BF16)
        part_copy(0).start()
        part_send[1] = out_sum[other].astype(BF16)
        part_copy(1).start()

    @pl.when(n == units + 1)
    def _():
        part_copy(0).wait()
        values = mid_ref[...]
        scale = lax.rsqrt(jnp.mean(values * values, axis=-1, keepdims=True) + EPSILON)
        normal = values * scale
        back = back_sum[own] + part_got[0].astype(F32)
        gain_grad_ref[...] = jnp.sum(back * normal, axis=0, keepdims=True)
        pushed = back * gain_ref[...]
        inner = jnp.mean(pushed * normal, axis=-1, keepdims=True)
        mid = dy_own_ref[...].astype(F32) + scale * (pushed - normal * inner)
        part_copy(1).wait()
        mid_ref[...] = mid
        low_grad[...] = mid.astype(BF16)
        output_ref[...] = (values + (out_sum[own] + part_got[1].astype(F32))).astype(BF16)

    @pl.when((n > units + 1) & (n <= units + 1 + chips))
    def _():
        p = n - units - 2
        grad = low_grad[...]
        lanes = pl.ds(pl.multiple_of(p * head_lanes, head_lanes), head_lanes)
        send = nt_dot(grad, w_out_ref[lanes, :]).astype(BF16)
        for half in range(2):
            target = 2 * p + half
            do_send[target] = send[half * tok_count : (half + 1) * tok_count]

            @pl.when(target != index)
            def _():
                do_copy(target, index).start()

            @pl.when(target == index)
            def _():
                do_got[target] = send[half * tok_count : (half + 1) * tok_count]

        heads = jnp.concatenate([heads_ref[2 * p], heads_ref[2 * p + 1]], axis=0)
        w_grad_ref[lanes, :] = tn_dot(heads, grad).astype(BF16)

    @pl.when(n == steps - 1)
    def _():
        for other_index in range(blk_count):

            @pl.when(other_index != index)
            def _():
                do_copy(other_index, other_index).wait()

        grad_heads_ref[...] = do_got[...]


def column_streams(line, bits, each, units):
    late = each // 4
    zs = line_bits(line)
    names = zs[::-1] + bits
    return [
        Stream(bits[::-1] + zs, names, (each - late, FF_TILE), LAG, units),
        Stream(bits + zs, names, (each - late, FF_TILE), LAG, units),
        Stream(zs + bits, names, (late, 2 * FF_TILE), LAG, units),
    ]


def middle_layer(line, bits, tokens, heads, w_out, gain, dy_own, dy_got, w_gate, w_up, w_down):
    own_rows, width = tokens.shape
    rows = 2 * own_rows
    blk_count, tok_count, head_lanes = heads.shape
    units = w_gate.shape[1] // 2 // FF_TILE
    chips = line * 2 ** len(bits)
    each = width // chips
    streams = column_streams(line, bits, each, units)
    steps = max([1 + stream.steps() for stream in streams] + [units + 3 + blk_count // 2])

    def keep(shape):
        return pl.BlockSpec(shape, lambda n: (0,) * len(shape), pipeline_mode=pl.Buffered(1))

    def tile(n):
        return jnp.clip(n - 1, 0, units - 1)

    def mine(n):
        return lax.rem(lax.axis_index("blk"), 2) * units + tile(n)

    scratch = [
        pltpu.VMEM((rows, width), BF16),
        pltpu.VMEM((width, rows), BF16),
        pltpu.VMEM((rows, width), F32),
        pltpu.VMEM((rows, width), F32),
        pltpu.VMEM((rows, FF_TILE), BF16),
        pltpu.VMEM((rows, FF_TILE), BF16),
        pltpu.VMEM((2, own_rows, width), BF16),
        pltpu.VMEM((2, own_rows, width), BF16),
        pltpu.VMEM((own_rows, width), BF16),
        pltpu.VMEM(heads.shape, BF16),
        pltpu.VMEM(heads.shape, BF16),
        pltpu.SemaphoreType.DMA((2,)),
        pltpu.SemaphoreType.DMA((2,)),
        pltpu.SemaphoreType.DMA((2,)),
        pltpu.SemaphoreType.DMA((blk_count,)),
        pltpu.SemaphoreType.DMA((blk_count,)),
    ]
    for stream in streams:
        scratch += stream.scratch()
    outs = [
        ((own_rows, width), BF16),
        ((own_rows, width), F32),
        ((1, width), F32),
        (w_out.shape, BF16),
        (heads.shape, BF16),
        ((units * FF_TILE, rows), BF16),
        ((each, units * FF_TILE), BF16),
        ((each, units * FF_TILE), BF16),
    ]
    out_specs = [keep(shape) for shape, unused in outs]
    out_specs[5] = pl.BlockSpec((FF_TILE, rows), lambda n: (tile(n), 0))
    return pl.pallas_call(
        functools.partial(middle_kernel, line, bits, streams, units),
        name="middle",
        grid=(steps,),
        in_specs=[
            keep(tokens.shape),
            keep(heads.shape),
            keep(w_out.shape),
            keep(gain.shape),
            keep(dy_own.shape),
            keep(dy_got.shape),
            pl.BlockSpec((width, FF_TILE), lambda n: (0, mine(n))),
            pl.BlockSpec((width, FF_TILE), lambda n: (0, mine(n))),
            pl.BlockSpec((FF_TILE, width), lambda n: (mine(n), 0)),
        ],
        out_specs=out_specs,
        out_shape=[jax.ShapeDtypeStruct(shape, kind) for shape, kind in outs],
        scratch_shapes=scratch,
        compiler_params=kernel_params(collective_id=6, has_side_effects=True),
    )(tokens, heads, w_out, gain, dy_own, dy_got, w_gate, w_up, w_down)


def back_kernel(
    groups,
    block,
    line,
    bits,
    streams,
    units,
    qkv_ref,
    logs_ref,
    out_ref,
    grad_ref,
    starts_ref,
    dy_own_ref,
    dy_got_ref,
    acts_ref,
    w_out_parts_ref,
    moved_ref,
    down_out_ref,
    w_out_ref,
    queries,
    keys,
    values,
    grads,
    query_grad,
    pair_grad,
    result,
    moved,
    sent_sem,
    got_sem,
    *refs,
):
    size = qkv_ref.shape[1]
    blocks = size // block
    n = pl.program_id(0)
    index = lax.axis_index("blk")
    core = lax.rem(index, 2)

    def move(g, target, source):
        return blk_copy(result.at[g], moved.at[g], sent_sem.at[g], got_sem.at[g], target, source)

    half = streams[0].block[1]

    def finish_low(u, value):
        rows = value.shape[0]
        down_out_ref[pl.ds(pl.multiple_of(u * rows, rows), rows), :half] = value

    def finish_high(u, value):
        rows = value.shape[0]
        down_out_ref[pl.ds(pl.multiple_of(u * rows, rows), rows), half:] = value

    def finish_w_out(u, value):
        w_out_ref[:, pl.ds(pl.multiple_of(u * LANES, LANES), LANES)] = value

    columns = w_out_ref.shape[1] // LANES
    at = 0
    for stream, finish in zip(streams, (finish_low, finish_high, finish_w_out)):
        size_of = len(stream.scratch())
        stream.bind(refs[at : at + size_of], finish)
        at += size_of

    @pl.when(n == 0)
    def _():
        greet_all(blocks, line)

    step_streams(streams, n)

    @pl.when(n == 1)
    def _():
        query_grad[...] = jnp.zeros_like(query_grad)
        pair_grad[...] = jnp.zeros_like(pair_grad)
        for g in range(groups):
            lanes = slice(g * LANES, (g + 1) * LANES)
            key, value = parted(qkv_ref[g, :, LANES:])
            keys[g, :, :LANES] = key
            keys[g, :, LANES:] = minus_three(size)
            values[g, :, :LANES] = value
            values[g, :, LANES:] = minus_three(size)

            def fill(i, carry):
                at = pl.multiple_of(i * block, block)
                to = pl.multiple_of(i * 2 * block, 2 * block)
                queries[g, pl.ds(to, 2 * block), :LANES] = stacked_heads(qkv_ref[g, pl.ds(at, block), :LANES])
                queries[g, pl.ds(to, 2 * block), LANES:] = logs_ref[g, pl.ds(to, 2 * block), :]
                grad = stacked_heads(grad_ref[pl.ds(at, block), lanes])
                mean = stacked_heads(out_ref[pl.ds(at, block), lanes])
                delta = jnp.sum(grad.astype(F32) * mean.astype(F32), axis=1, keepdims=True)
                grads[g, pl.ds(to, 2 * block), :LANES] = grad
                grads[g, pl.ds(to, 2 * block), LANES:] = in_three(delta)
                return carry

            lax.fori_loop(0, blocks, fill, 0)

    @pl.when(n < units)
    def _():
        acts = acts_ref[...].reshape(-1, acts_ref.shape[-1])
        rows = dy_own_ref.shape[0]
        made = nn_dot(acts[:, :rows], dy_own_ref[...]) + nn_dot(acts[:, rows:], dy_got_ref[...])
        made = made.astype(BF16)
        for i, stream in enumerate(streams[:2]):
            shape = stream.shape(stream.names[0])[1:]
            for side in range(2):
                at = (2 * side + i) * half
                stream.source[stream.slot(n), side] = made[:, at : at + half].reshape(shape)

    @pl.when(n < columns)
    def _():
        stream = streams[2]
        stream.source[stream.slot(n)] = w_out_parts_ref[...].reshape(stream.shape(stream.names[0]))

    row = lax.broadcasted_iota(jnp.int32, (block, 2 * block), 0)
    column = lax.broadcasted_iota(jnp.int32, (block, 2 * block), 1) % block

    pairs = (blocks + 1) * (blocks // 2)
    each = ATTEND_PAIRS
    rounds = groups * pairs // each

    @pl.when((n >= 1) & (n <= rounds))
    def _():
        def pair(at, carry):
            number = (n - 1) * each + at
            g = number // pairs
            place = lax.rem(number, pairs)
            turn = place // (blocks // 2)
            m = lax.rem(place, blocks // 2)
            late = (turn + m) // blocks
            j = m + late * (blocks - 1 - 2 * m)
            i = (1 - late) * (m + turn) + late * (turn - 1)
            key_at = pl.multiple_of(j * block, block)
            at = pl.multiple_of(i * 2 * block, 2 * block)
            key_rows = pl.ds(key_at, block)
            stack = pl.ds(at, 2 * block)
            allowed = (row >= starts_ref[:, stack] - key_at) & (row - column <= (i - j) * block)
            query = queries[g, stack, :]
            grad = grads[g, stack, :]
            key = keys[g, key_rows, :]
            scores = nt_dot(key, query)
            probs = jnp.exp2(jnp.where(allowed, scores, MASKED))
            pushed = (probs * nt_dot(values[g, key_rows, :], grad)).astype(BF16)
            pair_grad[g, key_rows, LANES:] += nn_dot(probs.astype(BF16), grad[:, :LANES])
            pair_grad[g, key_rows, :LANES] += nn_dot(pushed, query[:, :LANES])
            query_grad[g, stack, :] += tn_dot(pushed, key[:, :LANES])
            return carry

        lax.fori_loop(0, each, pair, 0, unroll=True)

    for g in range(groups):

        @pl.when(n == (g + 1) * rounds // groups + 1)
        def _():
            low = low_lanes((block, LANES))

            def finish(i, carry):
                at = pl.multiple_of(i * block, block)
                to = pl.multiple_of(i * 2 * block, 2 * block)
                here = pl.ds(at, block)
                first = query_grad[g, pl.ds(to, block), :]
                second = query_grad[g, pl.ds(to + block, block), :]
                joined = jnp.where(low, first, second) * HEAD_DIM ** (-0.5)
                result[g, i, :, :LANES] = joined.astype(BF16)
                key = pair_grad[g, here, :LANES] * (1.0 / LOG2_E)
                value = pair_grad[g, here, LANES:]
                key = key + pltpu.roll(key, HEAD_DIM, 1)
                value = value + pltpu.roll(value, HEAD_DIM, 1)
                result[g, i, :, LANES:] = jnp.where(low, key, value).astype(BF16)
                return carry

            lax.fori_loop(0, blocks, finish, 0)
            for step in range(blocks - 1, 0, -1):
                move(g, lax.rem(index + step, blocks), index).start()
            moved[g, index] = result[g, index]

    @pl.when(n == pl.num_programs(0) - 1)
    def _():
        for g in range(groups):
            for step in range(1, blocks):
                other = lax.rem(index + step, blocks)
                move(g, other, other).wait()
            moved_ref[:, :, 2 * g * LANES : 2 * (g + 1) * LANES] = moved[g]


def back(line, bits, qkv, logs, out, grad, starts, block, dy_own, dy_got, acts, w_out_parts):
    groups, size, width = qkv.shape
    model = dy_own.shape[1]
    rows = acts.shape[1]
    units = acts.shape[0] // FF_TILE
    chips = line * 2 ** len(bits)
    down_rows = acts.shape[0] // (chips // 2)
    down_each = down_rows // units
    w_rows = w_out_parts.shape[0] // chips // 2
    columns = w_out_parts.shape[1] // LANES
    zs = line_bits(line)
    names = [1] + zs[-2::-1] + bits
    streams = [
        Stream([1] + zs + bits, names, (down_each, model // 4), LAG, units, swap=zs[-1]),
        Stream([1] + bits[::-1] + zs, names, (down_each, model // 4), LAG, units, swap=zs[-1]),
        Stream([1] + bits + zs, zs[::-1] + bits + [1], (w_rows, LANES), LAG, columns),
    ]
    steps = max(
        [stream.steps() for stream in streams]
        + [groups * (size // block + 1) * (size // block // 2) // ATTEND_PAIRS + 3]
    )

    def keep(shape):
        return pl.BlockSpec(shape, lambda n: (0,) * len(shape), pipeline_mode=pl.Buffered(1))

    acts = acts.reshape(chips // 2, down_rows, rows)
    scratch = [
        pltpu.VMEM((groups, 2 * size, 2 * LANES), BF16),
        pltpu.VMEM((groups, size, 2 * LANES), BF16),
        pltpu.VMEM((groups, size, 2 * LANES), BF16),
        pltpu.VMEM((groups, 2 * size, 2 * LANES), BF16),
        pltpu.VMEM((groups, 2 * size, LANES), F32),
        pltpu.VMEM((groups, size, 2 * LANES), F32),
        pltpu.VMEM((groups, size // block, block, 2 * LANES), BF16),
        pltpu.VMEM((groups, size // block, block, 2 * LANES), BF16),
        pltpu.SemaphoreType.DMA((groups, size // block)),
        pltpu.SemaphoreType.DMA((groups, size // block)),
    ]
    for stream in streams:
        scratch += stream.scratch()

    outs = [
        (size // block, block, groups * width),
        (down_rows, model // 2),
        (w_rows, w_out_parts.shape[1]),
    ]
    return pl.pallas_call(
        functools.partial(back_kernel, groups, block, line, bits, streams, units),
        name="back",
        grid=(steps,),
        in_specs=[
            keep(qkv.shape),
            keep(logs.shape),
            keep(out.shape),
            keep(grad.shape),
            keep(starts.shape),
            keep(dy_own.shape),
            keep(dy_got.shape),
            pl.BlockSpec(
                (chips // 2, down_each, rows), lambda n: (0, jnp.minimum(n, units - 1), 0)
            ),
            pl.BlockSpec((w_out_parts.shape[0], LANES), lambda n: (0, jnp.minimum(n, columns - 1))),
        ],
        out_specs=[keep(shape) for shape in outs],
        out_shape=[jax.ShapeDtypeStruct(shape, BF16) for shape in outs],
        scratch_shapes=scratch,
        compiler_params=kernel_params(collective_id=4, has_side_effects=True),
    )(qkv, logs, out, grad, starts, dy_own, dy_got, acts, w_out_parts)


def sum_gains(rounds, n, first, gains, gains_got, sent_sem, got_sem):
    for r, partner in enumerate(rounds):

        def copy():
            return pltpu.make_async_remote_copy(
                src_ref=gains.at[r],
                dst_ref=gains_got.at[r],
                send_sem=sent_sem.at[r],
                recv_sem=got_sem.at[r],
                device_id=partner,
                device_id_type=pl.DeviceIdType.MESH,
            )

        @pl.when(n == first + r + 1)
        def _():
            copy().wait()
            gains[r + 1] = gains[r] + gains_got[r]

    for r, partner in enumerate(rounds):

        @pl.when(n == first + r)
        def _():
            pltpu.make_async_remote_copy(
                src_ref=gains.at[r],
                dst_ref=gains_got.at[r],
                send_sem=sent_sem.at[r],
                recv_sem=got_sem.at[r],
                device_id=partner,
                device_id_type=pl.DeviceIdType.MESH,
            ).start()


def finish_kernel(
    line,
    bits,
    streams,
    units,
    got_ref,
    proj_ref,
    hidden_ref,
    tokens_ref,
    mid_ref,
    gain_ref,
    wq_ref,
    wk_ref,
    wv_ref,
    head_gains_ref,
    cos_ref,
    sin_ref,
    ffn_gain_ref,
    gate_ref,
    up_ref,
    down_ref,
    input_ref,
    gains_ref,
    gq_ref,
    gk_ref,
    gv_ref,
    gate_out_ref,
    up_out_ref,
    down_out_ref,
    total,
    gains,
    gains_got,
    gains_sent_sem,
    gains_got_sem,
    half_got,
    down_got,
    half_sent_sem,
    half_got_sem,
    *refs,
):
    n = pl.program_id(0)
    z, index = lax.axis_index("dp"), lax.axis_index("blk")
    core, sibling = pair_of(1)
    steps = pl.num_programs(0)
    query_stream, pair_stream = streams
    q_width = wq_ref.shape[1]

    def finish_query(u, value):
        gq_ref[:, pl.ds(pl.multiple_of(u * q_width, q_width), q_width)] = value

    def finish_pair(u, value):
        here = pl.ds(pl.multiple_of(u * LANES, LANES), LANES)
        gk_ref[:, here] = value[:, :LANES]
        gv_ref[:, here] = value[:, LANES:]

    at = 0
    for stream, finish in ((query_stream, finish_query), (pair_stream, finish_pair)):
        count = len(stream.scratch())
        stream.bind(refs[at : at + count], finish)
        at += count

    rounds = [pair_of(name)[1] for name in [1] + list(bits) + line_bits(line)]

    rows = gate_ref.shape[0] // 2
    columns = gate_ref.shape[1]
    down_rows = down_ref.shape[0] // 2
    give = pl.ds(pl.multiple_of((1 - core) * rows, rows), rows)
    keep = pl.ds(pl.multiple_of(core * rows, rows), rows)
    down_give = pl.ds(pl.multiple_of((1 - core) * down_rows, down_rows), down_rows)
    down_keep = pl.ds(pl.multiple_of(core * down_rows, down_rows), down_rows)

    def half_copies():
        sources = (gate_ref.at[give, :], up_ref.at[give, :], down_ref.at[down_give, :])
        targets = (half_got.at[0], half_got.at[1], down_got)
        return [
            pltpu.make_async_remote_copy(
                src_ref=source,
                dst_ref=target,
                send_sem=half_sent_sem.at[i],
                recv_sem=half_got_sem.at[i],
                device_id=sibling,
                device_id_type=pl.DeviceIdType.MESH,
            )
            for i, (source, target) in enumerate(zip(sources, targets))
        ]

    @pl.when(n == 0)
    def _():
        barrier = pltpu.get_barrier_semaphore()
        for peer in rounds:
            pl.semaphore_signal(barrier, inc=1, device_id=peer, device_id_type=pl.DeviceIdType.MESH)
        pl.semaphore_wait(barrier, len(rounds))
        for copy in half_copies():
            copy.start()
        total[...] = jnp.zeros_like(total)
        gains[0] = jnp.zeros_like(gains[0])

    @pl.when(n == units)
    def _():
        for copy in half_copies():
            copy.wait()
        own = pl.ds(pl.multiple_of(core * columns, LANES), columns)
        other = pl.ds(pl.multiple_of((1 - core) * columns, LANES), columns)
        gate_out_ref[:, own] = gate_ref[keep, :]
        gate_out_ref[:, other] = half_got[0]
        up_out_ref[:, own] = up_ref[keep, :]
        up_out_ref[:, other] = half_got[1]
        half = down_ref.shape[1]
        down_out_ref[:, pl.ds(pl.multiple_of(core * half, LANES), half)] = down_ref[down_keep, :]
        down_out_ref[:, pl.ds(pl.multiple_of((1 - core) * half, LANES), half)] = down_got[...]

    step_streams(streams, n)
    sum_gains(rounds, n, units, gains, gains_got, gains_sent_sem, gains_got_sem)

    @pl.when(n == steps - 1)
    def _():
        gains_ref[...] = gains[len(rounds)]

    @pl.when(n < units)
    def _():
        hidden = hidden_ref[...]

        q_gain, k_gain = head_gains_ref[0:1, :], head_gains_ref[1:2, :]

        def got_lanes(lane):
            return jnp.concatenate(
                [got_ref[0, :, lane : lane + LANES], got_ref[1, :, lane : lane + LANES]], axis=0
            ).astype(F32)

        def back(got, lane, head_gain, place):
            turned = got * cos_ref[...] - half_partner(got) * sin_ref[...]
            block = proj_ref[0, :, lane : lane + LANES]
            scale = lax.rsqrt(head_means(block * block) + EPSILON)
            normal = block * scale
            gains[0, place : place + 1, :] += jnp.sum(turned * normal, axis=0, keepdims=True)
            pushed = turned * head_gain
            inner = head_means(pushed * normal)
            return (scale * (pushed - normal * inner)).astype(BF16)

        width = tokens_ref.shape[1]
        lines = width // LANES
        query = jnp.concatenate(
            [back(got_lanes(2 * at), at, q_gain, 2 * lines) for at in range(0, q_width, LANES)],
            axis=1,
        )
        first, second = got_lanes(LANES), got_lanes(3 * LANES)
        low = low_lanes(first.shape)
        key = jnp.where(low, first, pltpu.roll(second, HEAD_DIM, 1))
        key = back(key, q_width, k_gain, 2 * lines + 1)
        value = jnp.where(low, pltpu.roll(first, HEAD_DIM, 1), second).astype(BF16)
        for stream, part in ((query_stream, query), (pair_stream, jnp.concatenate([key, value], axis=1))):
            shape = stream.shape(stream.names[0])
            stream.source[stream.slot(n)] = tn_dot(hidden, part).astype(BF16).reshape(shape)

        total[...] += (
            nt_dot(query, wq_ref[...]) + nt_dot(key, wk_ref[...]) + nt_dot(value, wv_ref[...])
        )

        @pl.when(n == units - 1)
        def _():
            inputs = tokens_ref[...].astype(F32)
            scale = lax.rsqrt(jnp.mean(inputs * inputs, axis=-1, keepdims=True) + EPSILON)
            normal = inputs * scale
            grad = total[...]
            gain_grad = jnp.sum(grad * normal, axis=0, keepdims=True)
            for i in range(lines):
                here = slice(i * LANES, (i + 1) * LANES)
                gains[0, i : i + 1, :] = gain_grad[:, here]
                gains[0, lines + i : lines + i + 1, :] = ffn_gain_ref[:, here]
            pushed = grad * gain_ref[...]
            inner = jnp.mean(pushed * normal, axis=-1, keepdims=True)
            input_ref[...] = (mid_ref[...] + scale * (pushed - normal * inner)).astype(BF16)


def finish(
    line,
    bits,
    got,
    proj,
    hidden,
    tokens,
    mid,
    gain,
    wq,
    wk,
    wv,
    head_gains,
    cosine,
    sine,
    ffn_gain,
    gate_sum,
    up_sum,
    down_sum,
):
    rows, width = tokens.shape
    count, half, lanes = got.shape
    units = count // 2
    q_width = wq.shape[1] // units
    chips = line * 2 ** len(bits)
    mine = width // chips // 2
    zs = line_bits(line)
    names = zs[::-1] + bits + [1]
    streams = [
        Stream([1] + bits[::-1] + zs, names, (mine, q_width), LAST_LAG, units),
        Stream([1] + bits + zs, names, (mine, 2 * LANES), LAST_LAG, units),
    ]
    rounds = 1 + len(bits) + (line - 1).bit_length()
    steps = max([stream.steps() for stream in streams] + [units + rounds + 2])
    gain_rows = -(-(2 * width // LANES + 2) // 8) * 8
    half_rows = gate_sum.shape[0] // 2
    down_rows = down_sum.shape[0] // 2
    columns = gate_sum.shape[1]

    def keep(shape):
        return pl.BlockSpec(shape, lambda n: (0,) * len(shape), pipeline_mode=pl.Buffered(1))

    def at(n):
        return jnp.minimum(n, units - 1)

    scratch = [
        pltpu.VMEM((rows, width), F32),
        pltpu.VMEM((rounds + 1, gain_rows, LANES), F32),
        pltpu.VMEM((rounds, gain_rows, LANES), F32),
        pltpu.SemaphoreType.DMA((rounds,)),
        pltpu.SemaphoreType.DMA((rounds,)),
        pltpu.VMEM((2, half_rows, columns), BF16),
        pltpu.VMEM((down_rows, down_sum.shape[1]), BF16),
        pltpu.SemaphoreType.DMA((3,)),
        pltpu.SemaphoreType.DMA((3,)),
    ]
    for stream in streams:
        scratch += stream.scratch()
    outs = [
        ((rows, width), BF16),
        ((gain_rows, LANES), F32),
        ((mine, wq.shape[1]), BF16),
        ((mine, wk.shape[1]), BF16),
        ((mine, wv.shape[1]), BF16),
        ((half_rows, 2 * columns), BF16),
        ((half_rows, 2 * columns), BF16),
        ((down_rows, 2 * down_sum.shape[1]), BF16),
    ]
    return pl.pallas_call(
        functools.partial(finish_kernel, line, bits, streams, units),
        name="finish",
        grid=(steps,),
        in_specs=[
            pl.BlockSpec((2, half, lanes), lambda n: (at(n), 0, 0)),
            pl.BlockSpec((1, rows, q_width + LANES), lambda n: (at(n), 0, 0)),
            keep((rows, width)),
            keep((rows, width)),
            keep((rows, width)),
            keep((1, width)),
            pl.BlockSpec((width, q_width), lambda n: (0, at(n))),
            pl.BlockSpec((width, LANES), lambda n: (0, at(n))),
            pl.BlockSpec((width, LANES), lambda n: (0, at(n))),
            keep((2, LANES)),
            keep((rows, LANES)),
            keep((rows, LANES)),
            keep((1, width)),
            keep(gate_sum.shape),
            keep(up_sum.shape),
            keep(down_sum.shape),
        ],
        out_specs=[keep(shape) for shape, unused in outs],
        out_shape=[jax.ShapeDtypeStruct(shape, kind) for shape, kind in outs],
        scratch_shapes=scratch,
        compiler_params=kernel_params(collective_id=5, has_side_effects=True),
    )(
        got,
        proj,
        hidden,
        tokens,
        mid,
        gain,
        wq,
        wk,
        wv,
        head_gains,
        cosine,
        sine,
        ffn_gain,
        gate_sum,
        up_sum,
        down_sum,
    )


def widen_kernel(count, gains_ref, *refs):
    for source, target in zip(refs[:count], refs[count : 2 * count]):
        target[...] = source[...].astype(F32)
    attn_ref, ffn_ref, query_ref, key_ref = refs[2 * count :]
    lines = attn_ref.shape[0]
    attn_ref[...] = gains_ref[:lines, :]
    ffn_ref[...] = gains_ref[lines : 2 * lines, :]
    both = gains_ref[2 * lines : 2 * lines + 2, :]
    both = (both + pltpu.roll(both, HEAD_DIM, 1))[:, :HEAD_DIM]
    query_ref[...] = both[0:1]
    key_ref[...] = both[1:2]


def widen(gains, lines, parts):
    shapes = [part.shape for part in parts] + [(lines, LANES)] * 2 + [(1, HEAD_DIM)] * 2
    return pl.pallas_call(
        functools.partial(widen_kernel, len(parts)),
        name="widen",
        out_shape=[jax.ShapeDtypeStruct(shape, F32) for shape in shapes],
        compiler_params=kernel_params(),
    )(gains, *parts)


def flip_pairs(count, bit):
    return [(i, i ^ bit) for i in range(count)]


def swap_core(block, blk_count):
    return lax.ppermute(block, "blk", flip_pairs(blk_count, 1))


def fast_local(
    dp_count,
    blk_count,
    tokens,
    doc_lengths,
    g_attn,
    w_query,
    w_key,
    w_value,
    q_gain,
    k_gain,
    w_out,
    g_ffn,
    w_gate,
    w_up,
    w_down,
    cotangent,
):
    row_count, tok_count, width = tokens.shape
    rows = row_count * tok_count
    chips = blk_count // 2
    size = tok_count * blk_count
    index = lax.axis_index("blk")
    core = index % 2
    bits = []
    bit = blk_count // 2
    while bit > 1:
        bits.append(bit)
        bit //= 2
    chip_dims = (dp_count,) + (2,) * len(bits)
    all_chips = dp_count * chips
    which = jnp.arange(doc_lengths.shape[1])
    ends = jnp.sum(jnp.where(which[:, None] <= which[None, :], doc_lengths[:, :, None], 0), axis=1)
    places = index * tok_count + jnp.arange(tok_count, dtype=jnp.int32)[None]
    begins = jnp.max(jnp.where(places[:, :, None] >= ends[:, None, :], ends[:, None, :], 0), axis=2)
    positions = (places - begins).reshape(rows, 1).astype(F32)
    half_head = HEAD_DIM // 2
    lane = jnp.arange(LANES)
    freqs = ROPE_BASE ** (-(lane % half_head).astype(F32) / half_head)
    angles = positions * freqs
    cosine = jnp.cos(angles)
    sine = jnp.sin(angles) * jnp.where(lane % HEAD_DIM < half_head, -1.0, 1.0)
    head_gains = jnp.concatenate([q_gain, q_gain, k_gain, k_gain]).reshape(2, LANES)
    all_places = jnp.arange(size, dtype=jnp.int32)
    own_ends = lax.dynamic_slice_in_dim(ends, core, 1, axis=0)
    starts = jnp.max(jnp.where(all_places[:, None] >= own_ends, own_ends, 0), axis=1)
    starts_two = jnp.broadcast_to(
        starts.reshape(blk_count, 1, tok_count), (blk_count, 2, tok_count)
    ).reshape(1, 2 * size)
    flat = tokens.reshape(rows, width)
    grad_own = cotangent.reshape(rows, width)
    grad_got = swap_core(grad_own, blk_count)

    hidden_in, proj, qkv, attended, logs, heads = forward(
        flat,
        g_attn[None],
        w_query,
        w_key,
        w_value,
        head_gains,
        cosine,
        sine,
        starts_two,
    )
    output, mid, ffn_gain_grad, w_out_parts, grad_heads, acts, gate_sum, up_sum = middle_layer(
        dp_count,
        bits,
        flat,
        heads,
        w_out,
        g_ffn[None],
        grad_own,
        grad_got,
        w_gate,
        w_up,
        w_down,
    )
    got, down_sum, w_out_sum = back(
        dp_count,
        bits,
        qkv,
        logs,
        attended.reshape(size, -1),
        grad_heads.reshape(size, -1),
        starts_two,
        tok_count,
        grad_own,
        grad_got,
        acts,
        w_out_parts,
    )
    input_grad, gains, *sums = finish(
        dp_count,
        bits,
        got,
        proj,
        hidden_in,
        flat,
        mid,
        g_attn[None],
        w_query,
        w_key,
        w_value,
        head_gains,
        cosine,
        sine,
        ffn_gain_grad,
        gate_sum,
        up_sum,
        down_sum,
    )
    *sums, gain_attn, gain_ffn, gain_query, gain_key = widen(gains, width // LANES, sums + [w_out_sum])
    grad_w_query, grad_w_key, grad_w_value, grad_w_gate, grad_w_up, grad_w_down, grad_w_out = sums
    gain_attn, gain_ffn = gain_attn.reshape(width), gain_ffn.reshape(width)
    gain_query, gain_key = gain_query[0], gain_key[0]
    return (
        output.reshape(tokens.shape),
        input_grad.reshape(tokens.shape),
        gain_attn,
        grad_w_query,
        grad_w_key,
        grad_w_value,
        gain_query,
        gain_key,
        grad_w_out,
        gain_ffn,
        grad_w_gate,
        grad_w_up,
        grad_w_down,
    )


def fits(mesh):
    blk_count = mesh.shape["blk"]
    chips = blk_count // 2
    line = mesh.shape["dp"]
    power = blk_count & (blk_count - 1) == 0 and line & (line - 1) == 0
    return power and blk_count > 2 and line > 1 and (KV_HEADS * HEAD_DIM) == chips * LANES


def solution(mesh):
    if fits(mesh):
        body = functools.partial(fast_local, mesh.shape["dp"], mesh.shape["blk"])
    else:
        body = local
    return jax.shard_map(
        body,
        mesh=mesh,
        in_specs=(
            P("dp", "blk", None),
            P("dp", None),
            P(),
            P(),
            P(),
            P(),
            P(),
            P(),
            P(),
            P(),
            P(),
            P(),
            P(),
            P("dp", "blk", None),
        ),
        out_specs=(
            P("dp", "blk", None),
            P("dp", "blk", None),
            P(),
            P(("dp", "blk"), None),
            P(("dp", "blk"), None),
            P(("dp", "blk"), None),
            P(),
            P(),
            P(("dp", "blk"), None),
            P(),
            P(("dp", "blk"), None),
            P(("dp", "blk"), None),
            P(("dp", "blk"), None),
        ),
        check_vma=False,
    )
```

```python
import functools
import math

import jax
import jax.numpy as jnp
from jax import lax
from jax.experimental import pallas as pl
from jax.experimental.pallas import tpu as pltpu
from jax.sharding import PartitionSpec as P

HEADS = 16
KV_HEADS = 8
HEAD_DIM = 64


EPSILON = 1e-05
ROPE_BASE = 1000000.0
NEGATIVE = -1e30


def norm_rows(values, norm_gain):
    row_scale = lax.rsqrt(jnp.mean(values * values, axis=-1, keepdims=True) + EPSILON)
    normal = values * row_scale
    return (normal * norm_gain, normal, row_scale)


def norm_back(normal, row_scale, norm_gain, grad_out):
    pushed = grad_out * norm_gain
    inner = jnp.mean(pushed * normal, axis=-1, keepdims=True)
    grad_in = row_scale * (pushed - normal * inner)
    leading = tuple(range(grad_out.ndim - 1))
    return (grad_in, jnp.sum(grad_out * normal, axis=leading))


def doc_layout(lengths, places):
    ends = jnp.cumsum(lengths, axis=1)
    past = places[None, :, None] >= ends[:, None, :]
    docs = jnp.sum(past.astype(jnp.int32), axis=2)
    before = jnp.sum(jnp.where(past, lengths[:, None, :], 0), axis=2)
    return (docs, places[None, :] - before)


def rope_angles(positions):
    half = HEAD_DIM // 2
    freqs = ROPE_BASE ** (-jnp.arange(half, dtype=jnp.float32) / half)
    angles = positions.astype(jnp.float32)[..., None] * freqs
    return (jnp.cos(angles), jnp.sin(angles))


def rotate(values, cosine, sine):
    half = values.shape[-1] // 2
    first_half = values[..., :half]
    second_half = values[..., half:]
    cos_col = cosine[:, :, None, :]
    sin_col = sine[:, :, None, :]
    return jnp.concatenate(
        [
            first_half * cos_col - second_half * sin_col,
            second_half * cos_col + first_half * sin_col,
        ],
        axis=-1,
    )


def local(
    tokens,
    doc_lengths,
    g_attn,
    w_query,
    w_key,
    w_value,
    q_gain,
    k_gain,
    w_out,
    g_ffn,
    w_gate,
    w_up,
    w_down,
    cotangent,
):
    row_count, tok_count, width = tokens.shape
    grouping = HEADS // KV_HEADS
    flat_rows = row_count * tok_count
    kv_width = KV_HEADS * HEAD_DIM
    softmax_scale = HEAD_DIM ** (-0.5)
    places = lax.axis_index("blk") * tok_count + jnp.arange(tok_count, dtype=jnp.int32)
    query_docs, query_pos = doc_layout(doc_lengths, places)
    cosine, sine = rope_angles(query_pos)
    inputs = tokens.reshape(flat_rows, width).astype(jnp.float32)
    normed, normal_in, scale_in = norm_rows(inputs, g_attn)
    hidden_in = normed.astype(jnp.bfloat16)
    query_proj = jnp.dot(hidden_in, w_query, preferred_element_type=jnp.float32).reshape(
        row_count, tok_count, HEADS, HEAD_DIM
    )
    key_proj = jnp.dot(hidden_in, w_key, preferred_element_type=jnp.float32).reshape(
        row_count, tok_count, KV_HEADS, HEAD_DIM
    )
    value_b = (
        jnp.dot(hidden_in, w_value, preferred_element_type=jnp.float32)
        .astype(jnp.bfloat16)
        .reshape(row_count, tok_count, kv_width)
    )
    query_norm, query_normal, query_scale = norm_rows(query_proj, q_gain)
    key_norm, key_normal, key_scale = norm_rows(key_proj, k_gain)
    query_b = (
        rotate(query_norm, cosine, sine)
        .astype(jnp.bfloat16)
        .reshape(row_count, tok_count, KV_HEADS, grouping, HEAD_DIM)
    )
    key_b = (
        rotate(key_norm, cosine, sine).astype(jnp.bfloat16).reshape(row_count, tok_count, kv_width)
    )

    def piece_mask(size):
        key_places = jnp.arange(size, dtype=jnp.int32)
        key_docs, unused = doc_layout(doc_lengths, key_places)
        return (key_places[None, None, :] <= places[None, :, None]) & (
            key_docs[:, None, :] == query_docs[:, :, None]
        )

    def piece_scores(key_piece, allowed):
        key_heads = key_piece.reshape(row_count, key_piece.shape[1], KV_HEADS, HEAD_DIM)
        raw_scores = (
            jnp.einsum("rqkgd,rpkd->rkgqp", query_b, key_heads, preferred_element_type=jnp.float32)
            * softmax_scale
        )
        return (jnp.where(allowed[:, None, None], raw_scores, -jnp.inf), key_heads)

    stat_shape = (row_count, KV_HEADS, grouping, tok_count)
    key_piece = lax.all_gather(key_b, "blk", axis=1, tiled=True)
    value_piece = lax.all_gather(value_b, "blk", axis=1, tiled=True)
    allowed = piece_mask(key_piece.shape[1])
    running_max = jnp.full(stat_shape, NEGATIVE, jnp.float32)
    scores, key_heads = piece_scores(key_piece, allowed)
    new_max = jnp.maximum(running_max, jnp.max(scores, axis=-1))
    weights = jnp.exp(scores - new_max[..., None])
    value_heads = value_piece.reshape(row_count, value_piece.shape[1], KV_HEADS, HEAD_DIM)
    added = jnp.einsum(
        "rkgqp,rpkd->rkgqd",
        weights.astype(jnp.bfloat16),
        value_heads,
        preferred_element_type=jnp.float32,
    )
    running_sum = jnp.sum(weights, axis=-1)
    attended = added / running_sum[..., None]
    log_total = new_max + jnp.log(running_sum)
    attended_b = (
        jnp.transpose(attended, (0, 3, 1, 2, 4))
        .reshape(flat_rows, HEADS * HEAD_DIM)
        .astype(jnp.bfloat16)
    )
    middle = inputs + jnp.dot(attended_b, w_out, preferred_element_type=jnp.float32)
    normed_ffn, normal_ffn, scale_ffn = norm_rows(middle, g_ffn)
    hidden_ffn = normed_ffn.astype(jnp.bfloat16)
    gate = jnp.dot(hidden_ffn, w_gate, preferred_element_type=jnp.float32)
    up_proj = jnp.dot(hidden_ffn, w_up, preferred_element_type=jnp.float32)
    sigmoid_gate = jax.nn.sigmoid(gate)
    silu_gate = gate * sigmoid_gate
    hidden = (silu_gate * up_proj).astype(jnp.bfloat16)
    result = middle + jnp.dot(hidden, w_down, preferred_element_type=jnp.float32)
    output = result.astype(jnp.bfloat16).reshape(row_count, tok_count, width)
    grad_out = cotangent.reshape(flat_rows, width)
    grad_w_down = jnp.einsum("tf,td->fd", hidden, grad_out, preferred_element_type=jnp.float32)
    grad_hidden = jnp.einsum("td,fd->tf", grad_out, w_down, preferred_element_type=jnp.float32)
    grad_gate = (grad_hidden * up_proj * sigmoid_gate * (1.0 + gate * (1.0 - sigmoid_gate))).astype(
        jnp.bfloat16
    )
    grad_up = (grad_hidden * silu_gate).astype(jnp.bfloat16)
    grad_w_gate = jnp.einsum("td,tf->df", hidden_ffn, grad_gate, preferred_element_type=jnp.float32)
    grad_w_up = jnp.einsum("td,tf->df", hidden_ffn, grad_up, preferred_element_type=jnp.float32)
    grad_h2 = jnp.einsum(
        "tf,df->td", grad_gate, w_gate, preferred_element_type=jnp.float32
    ) + jnp.einsum("tf,df->td", grad_up, w_up, preferred_element_type=jnp.float32)
    grad_mid, grad_ffn_gain = norm_back(normal_ffn, scale_ffn, g_ffn, grad_h2)
    grad_mid = grad_out.astype(jnp.float32) + grad_mid
    grad_attn = grad_mid.astype(jnp.bfloat16)
    grad_w_out = jnp.einsum("tc,td->cd", attended_b, grad_attn, preferred_element_type=jnp.float32)
    grad_attended = jnp.einsum(
        "td,cd->tc", grad_attn, w_out, preferred_element_type=jnp.float32
    ).astype(jnp.bfloat16)
    grad_heads = grad_attended.reshape(row_count, tok_count, KV_HEADS, grouping, HEAD_DIM)
    deltas = jnp.einsum("rqkgd,rkgqd->rkgq", grad_heads.astype(jnp.float32), attended)
    key_piece = lax.all_gather(key_b, "blk", axis=1, tiled=True)
    value_piece = lax.all_gather(value_b, "blk", axis=1, tiled=True)
    size = key_piece.shape[1]
    allowed = piece_mask(size)
    scores, key_heads = piece_scores(key_piece, allowed)
    probs = jnp.exp(scores - log_total[..., None])
    value_heads = value_piece.reshape(row_count, size, KV_HEADS, HEAD_DIM)
    value_piece_grad = jnp.einsum(
        "rkgqp,rqkgd->rpkd",
        probs.astype(jnp.bfloat16),
        grad_heads,
        preferred_element_type=jnp.float32,
    )
    grad_probs = jnp.einsum(
        "rqkgd,rpkd->rkgqp", grad_heads, value_heads, preferred_element_type=jnp.float32
    )
    grad_scores = (probs * (grad_probs - deltas[..., None])).astype(jnp.bfloat16)
    grad_query = jnp.einsum(
        "rkgqp,rpkd->rkgqd", grad_scores, key_heads, preferred_element_type=jnp.float32
    )
    key_piece_grad = jnp.einsum(
        "rkgqp,rqkgd->rpkd", grad_scores, query_b, preferred_element_type=jnp.float32
    )
    grad_keys = key_piece_grad.reshape(row_count, size, kv_width)
    grad_values = value_piece_grad.reshape(row_count, size, kv_width)
    grad_query, grad_keys, grad_values = (grad_query, grad_keys, grad_values)
    key_grad_mine, value_grad_mine = (
        lax.psum_scatter(
            grad_keys.astype(jnp.bfloat16), "blk", scatter_dimension=1, tiled=True
        ).astype(jnp.float32),
        lax.psum_scatter(
            grad_values.astype(jnp.bfloat16), "blk", scatter_dimension=1, tiled=True
        ).astype(jnp.float32),
    )
    grad_q_rot = (jnp.transpose(grad_query, (0, 3, 1, 2, 4)) * softmax_scale).reshape(
        row_count, tok_count, HEADS, HEAD_DIM
    )
    grad_k_rot = (key_grad_mine * softmax_scale).reshape(row_count, tok_count, KV_HEADS, HEAD_DIM)
    grad_q_proj, grad_query_gain = norm_back(
        query_normal, query_scale, q_gain, rotate(grad_q_rot, cosine, -sine)
    )
    grad_k_proj, grad_key_gain = norm_back(
        key_normal, key_scale, k_gain, rotate(grad_k_rot, cosine, -sine)
    )
    grad_q_b = grad_q_proj.astype(jnp.bfloat16).reshape(flat_rows, HEADS * HEAD_DIM)
    grad_k_b = grad_k_proj.astype(jnp.bfloat16).reshape(flat_rows, kv_width)
    grad_v_b = value_grad_mine.astype(jnp.bfloat16).reshape(flat_rows, kv_width)
    grad_w_query = jnp.einsum("td,tc->dc", hidden_in, grad_q_b, preferred_element_type=jnp.float32)
    grad_w_key = jnp.einsum("td,tc->dc", hidden_in, grad_k_b, preferred_element_type=jnp.float32)
    grad_w_value = jnp.einsum("td,tc->dc", hidden_in, grad_v_b, preferred_element_type=jnp.float32)
    grad_h1 = jnp.einsum("tc,dc->td", grad_q_b, w_query, preferred_element_type=jnp.float32)
    grad_h1 = grad_h1 + jnp.einsum("tc,dc->td", grad_k_b, w_key, preferred_element_type=jnp.float32)
    grad_h1 = grad_h1 + jnp.einsum(
        "tc,dc->td", grad_v_b, w_value, preferred_element_type=jnp.float32
    )
    grad_base, grad_attn_gain = norm_back(normal_in, scale_in, g_attn, grad_h1)
    input_grad = (grad_mid + grad_base).astype(jnp.bfloat16).reshape(row_count, tok_count, width)
    gain_attn, gain_query, gain_key, gain_ffn = lax.psum(
        (grad_attn_gain, grad_query_gain, grad_key_gain, grad_ffn_gain), ("dp", "blk")
    )
    locals_all = (
        grad_w_query,
        grad_w_key,
        grad_w_value,
        grad_w_out,
        grad_w_gate,
        grad_w_up,
        grad_w_down,
    )
    shared = (
        lax.psum_scatter(locals_all[0], ("dp", "blk"), scatter_dimension=0, tiled=True),
        lax.psum_scatter(locals_all[1], ("dp", "blk"), scatter_dimension=0, tiled=True),
        lax.psum_scatter(locals_all[2], ("dp", "blk"), scatter_dimension=0, tiled=True),
        lax.psum_scatter(locals_all[3], ("dp", "blk"), scatter_dimension=0, tiled=True),
        lax.psum_scatter(locals_all[4], ("dp", "blk"), scatter_dimension=0, tiled=True),
        lax.psum_scatter(locals_all[5], ("dp", "blk"), scatter_dimension=0, tiled=True),
        lax.psum_scatter(locals_all[6], ("dp", "blk"), scatter_dimension=0, tiled=True),
    )
    return (
        output,
        input_grad,
        gain_attn,
        shared[0],
        shared[1],
        shared[2],
        gain_query,
        gain_key,
        shared[3],
        gain_ffn,
        shared[4],
        shared[5],
        shared[6],
    )


BF16 = jnp.bfloat16
F32 = jnp.float32
LANES = 128
FF_TILE = 256
LAG = 2
LAST_LAG = 1
ATTEND_PAIRS = 6
VMEM_BYTES = 60 * 1024 * 1024
LOG2_E = math.log2(math.e)
QUERY_SCALE = HEAD_DIM ** (-0.5) * LOG2_E
MASKED = -1e30


def nn_dot(left, right):
    return lax.dot_general(left, right, (((1,), (0,)), ((), ())), preferred_element_type=F32)


def nt_dot(left, right):
    return lax.dot_general(left, right, (((1,), (1,)), ((), ())), preferred_element_type=F32)


def tn_dot(left, right):
    return lax.dot_general(left, right, (((0,), (0,)), ((), ())), preferred_element_type=F32)


def kernel_params(**more):
    return pltpu.CompilerParams(vmem_limit_bytes=VMEM_BYTES, **more)


def whole_block(shape):
    return pl.BlockSpec(shape, lambda *ids: (0,) * len(shape))


def greet_blk(count):
    barrier = pltpu.get_barrier_semaphore()
    z, index = lax.axis_index("dp"), lax.axis_index("blk")
    for step in range(1, count):
        pl.semaphore_signal(
            barrier,
            inc=1,
            device_id=(z, lax.rem(index + step, count)),
            device_id_type=pl.DeviceIdType.MESH,
        )
    pl.semaphore_wait(barrier, count - 1)


def blk_copy(send, got, sent_sem, got_sem, target, source):
    return pltpu.make_async_remote_copy(
        src_ref=send.at[target],
        dst_ref=got.at[source],
        send_sem=sent_sem.at[target],
        recv_sem=got_sem.at[source],
        device_id=(lax.axis_index("dp"), target),
        device_id_type=pl.DeviceIdType.MESH,
    )


def head_means(values):
    rows = lax.broadcasted_iota(jnp.int32, (LANES, LANES), 0) // HEAD_DIM
    cols = lax.broadcasted_iota(jnp.int32, (LANES, LANES), 1) // HEAD_DIM
    spread = jnp.where(rows == cols, 1.0 / HEAD_DIM, 0.0).astype(BF16)
    high = values.astype(BF16)
    low = (values - high.astype(F32)).astype(BF16)
    return nn_dot(high, spread) + nn_dot(low, spread)


def half_partner(values):
    lane = lax.broadcasted_iota(jnp.int32, values.shape, 1)
    half = HEAD_DIM // 2
    ahead = pltpu.roll(values, LANES - half, 1)
    behind = pltpu.roll(values, half, 1)
    return jnp.where(lane % HEAD_DIM < half, ahead, behind)


def low_lanes(shape):
    return lax.broadcasted_iota(jnp.int32, shape, 1) < HEAD_DIM


def parted(packed):
    turned = pltpu.roll(packed.astype(F32), HEAD_DIM, 1).astype(BF16)
    low = low_lanes(packed.shape)
    return jnp.where(low, packed, turned), jnp.where(low, turned, packed)


def stacked_heads(pair):
    low = low_lanes(pair.shape)
    none = jnp.zeros_like(pair)
    return jnp.concatenate([jnp.where(low, pair, none), jnp.where(low, none, pair)], axis=0)


def in_three(column):
    lane = lax.broadcasted_iota(jnp.int32, (column.shape[0], LANES), 1)
    wide = jnp.broadcast_to(column, (column.shape[0], LANES))
    first = wide.astype(BF16).astype(F32)
    second = (wide - first).astype(BF16).astype(F32)
    third = wide - first - second
    return jnp.where(
        lane == 0, first, jnp.where(lane == 1, second, jnp.where(lane == 2, third, 0.0))
    ).astype(BF16)


def minus_three(rows):
    lane = lax.broadcasted_iota(jnp.int32, (rows, LANES), 1)
    return jnp.where(lane < 3, -1.0, 0.0).astype(BF16)


def forward_kernel(
    chips,
    groups,
    tokens_ref,
    gain_ref,
    wq_ref,
    wk_ref,
    wv_ref,
    head_gains_ref,
    cos_ref,
    sin_ref,
    starts_ref,
    hidden_ref,
    proj_ref,
    qkv_ref,
    out_ref,
    logs_ref,
    heads_ref,
    send,
    got,
    keys,
    values,
    total,
    out_send,
    out_got,
    sent_sem,
    got_sem,
    out_sent_sem,
    out_got_sem,
):
    n = pl.program_id(0)
    blocks, block = send.shape[1:3]
    size = blocks * block
    index = lax.axis_index("blk")
    p = lax.rem(index // 2 + 1 + n, chips)

    def give(g, p):
        for part in range(2):
            target = 2 * p + part

            @pl.when(target != index)
            def _():
                blk_copy(send.at[g], got.at[g], sent_sem.at[g], got_sem.at[g], target, index).start()

            @pl.when(target == index)
            def _():
                got[g, target] = send[g, target]

    @pl.when(n == 0)
    def _():
        greet_blk(blocks)
        inputs = tokens_ref[...].astype(F32)
        scale = lax.rsqrt(jnp.mean(inputs * inputs, axis=-1, keepdims=True) + EPSILON)
        hidden_ref[...] = (inputs * scale * gain_ref[...]).astype(BF16)

    @pl.when(n < chips)
    def _():
        hidden = hidden_ref[...]
        queries = nn_dot(hidden, wq_ref[...])
        keys_of = nn_dot(hidden, wk_ref[...])
        values_of = nn_dot(hidden, wv_ref[...])

        def turn(part, lane, head_gain):
            proj_ref[0, :, lane : lane + LANES] = part
            scale = lax.rsqrt(head_means(part * part) + EPSILON)
            normed = part * scale * head_gain
            return normed * cos_ref[...] + half_partner(normed) * sin_ref[...]

        def put(g, lane, part):
            for half in range(2):
                send[g, 2 * p + half, :, lane : lane + LANES] = part[half * block : (half + 1) * block].astype(BF16)

        q_gain, k_gain = head_gains_ref[0:1, :], head_gains_ref[1:2, :]
        key = turn(keys_of, groups * LANES, k_gain)
        low = low_lanes(key.shape)
        for g in range(groups):
            lanes = slice(g * LANES, (g + 1) * LANES)
            put(g, 0, turn(queries[:, lanes], g * LANES, q_gain) * QUERY_SCALE)
            if g == 0:
                put(g, LANES, jnp.where(low, key, pltpu.roll(values_of, HEAD_DIM, 1)))
            else:
                put(g, LANES, jnp.where(low, pltpu.roll(key, HEAD_DIM, 1), values_of))
        give(0, p)

    for g in range(groups):

        @pl.when(n == chips + g * blocks)
        def _():
            for step in range(1, blocks):
                other = lax.rem(index + step, blocks)
                blk_copy(send.at[g], got.at[g], sent_sem.at[g], got_sem.at[g], other, other).wait()
            if g + 1 < groups:
                for step in range(chips):
                    give(g + 1, lax.rem(index // 2 + 1 + step, chips))
            for i in range(blocks):
                here = slice(i * block, (i + 1) * block)
                qkv_ref[g, here, :] = got[g, i]
                keys[here, :], values[here, :LANES] = parted(got[g, i, :, LANES:])
                values[here, LANES:] = jnp.ones((block, LANES), BF16)

    @pl.when(n >= chips)
    def _():
        g = (n - chips) // blocks
        here = lax.rem(index + 1 + lax.rem(n - chips, blocks), blocks)
        at = pl.multiple_of(here * block, block)
        row_at = pl.multiple_of(here * 2 * block, 2 * block)
        lines = jnp.broadcast_to(starts_ref[:, pl.ds(row_at, 2 * block)], (LANES, 2 * block))
        starts = lines.T[:, :1]
        query = stacked_heads(got[g, here, :, :LANES])

        def step(key_at, width, diagonal):
            column = lax.broadcasted_iota(jnp.int32, (2 * block, width), 1)
            allowed = column >= starts - key_at
            if diagonal:
                row = lax.broadcasted_iota(jnp.int32, (2 * block, width), 0) % block
                allowed = allowed & (column <= row)
            scores = nt_dot(query, keys[pl.ds(key_at, width), :])
            weights = jnp.exp2(jnp.where(allowed, scores, MASKED)).astype(BF16)
            part = nn_dot(weights, values[pl.ds(key_at, width), :])
            if diagonal:
                total[...] = part
            else:
                total[...] += part

        step(at, block, True)

        @pl.when(lax.rem(here, 2) == 1)
        def _():
            step(pl.multiple_of((here - 1) * block, block), block, False)

        def body(j, carry):
            step(pl.multiple_of(j * 2 * block, 2 * block), 2 * block, False)
            return carry

        lax.fori_loop(0, here // 2, body, 0)
        low = low_lanes((block, LANES))
        to = pl.multiple_of(here * 2 * block, 2 * block)
        sums = total[:, LANES:]
        mean = total[:, :LANES] / sums
        made = jnp.where(low, mean[:block], mean[block:]).astype(BF16)
        out_send[g, here] = made
        out_ref[here, :, pl.ds(pl.multiple_of(g * LANES, LANES), LANES)] = made
        logs_ref[g, pl.ds(to, 2 * block), :] = in_three(jnp.log2(sums[:, :1]))

        @pl.when(here != index)
        def _():
            blk_copy(
                out_send.at[g], out_got.at[g], out_sent_sem.at[g], out_got_sem.at[g], here, index
            ).start()

        @pl.when(here == index)
        def _():
            out_got[g, here] = made

    @pl.when(n == pl.num_programs(0) - 1)
    def _():
        for g in range(groups):
            for step in range(1, blocks):
                other = lax.rem(index + step, blocks)
                blk_copy(
                    out_send.at[g], out_got.at[g], out_sent_sem.at[g], out_got_sem.at[g], other, other
                ).wait()
            heads_ref[:, :, g * LANES : (g + 1) * LANES] = out_got[g]


def forward(tokens, gain, wq, wk, wv, head_gains, cosine, sine, starts):
    rows, width = tokens.shape
    chips = wk.shape[1] // LANES
    q_width = wq.shape[1] // chips
    groups, blocks, block = q_width // LANES, 2 * chips, rows // 2
    size = blocks * block

    def keep(shape):
        return pl.BlockSpec(shape, lambda n: (0,) * len(shape), pipeline_mode=pl.Buffered(1))

    def at(n):
        return lax.rem(lax.axis_index("blk") // 2 + 1 + jnp.minimum(n, chips - 1), chips)

    outs = [
        ((rows, width), BF16),
        ((chips, rows, q_width + LANES), F32),
        ((groups, size, 2 * LANES), BF16),
        ((blocks, block, q_width), BF16),
        ((groups, 2 * size, LANES), BF16),
        ((blocks, block, q_width), BF16),
    ]
    out_specs = [keep(shape) for shape, unused in outs]
    out_specs[1] = pl.BlockSpec((1, rows, q_width + LANES), lambda n: (at(n), 0, 0))
    moved, heads = (groups, blocks, block, 2 * LANES), (groups, blocks, block, LANES)
    return pl.pallas_call(
        functools.partial(forward_kernel, chips, groups),
        name="forward",
        grid=(chips + groups * blocks,),
        in_specs=[
            keep((rows, width)),
            keep((1, width)),
            pl.BlockSpec((width, q_width), lambda n: (0, at(n))),
            pl.BlockSpec((width, LANES), lambda n: (0, at(n))),
            pl.BlockSpec((width, LANES), lambda n: (0, at(n))),
            keep((2, LANES)),
            keep((rows, LANES)),
            keep((rows, LANES)),
            keep((1, 2 * size)),
        ],
        out_specs=out_specs,
        out_shape=[jax.ShapeDtypeStruct(shape, kind) for shape, kind in outs],
        scratch_shapes=[
            pltpu.VMEM(moved, BF16),
            pltpu.VMEM(moved, BF16),
            pltpu.VMEM((size, LANES), BF16),
            pltpu.VMEM((size, 2 * LANES), BF16),
            pltpu.VMEM((2 * block, 2 * LANES), F32),
            pltpu.VMEM(heads, BF16),
            pltpu.VMEM(heads, BF16),
        ]
        + [pltpu.SemaphoreType.DMA((groups, blocks))] * 4,
        compiler_params=kernel_params(collective_id=0, has_side_effects=True),
    )(tokens, gain, wq, wk, wv, head_gains, cosine, sine, starts)


def pair_of(name):
    z, index = lax.axis_index("dp"), lax.axis_index("blk")
    if isinstance(name, tuple):
        mine = lax.rem(z // name[1], 2)
        return mine, (z + name[1] * (1 - 2 * mine), index)
    mine = lax.rem(index // name, 2)
    return mine, (z, index + name * (1 - 2 * mine))


class Stream:
    def __init__(self, path, names, block, lag, units, swap=None):
        self.path, self.block, self.lag, self.units, self.swap = path, block, lag, units, swap
        self.slots = min(2 * lag, units)
        self.names = [tuple(names)]
        for k, stage in enumerate(path):
            left = tuple(name for name in self.names[-1] if name != stage)
            self.names.append((swap,) + left if swap is not None and k == 0 else left)
        assert not self.names[-1]

    def shape(self, names):
        return (2,) * len(names) + self.block

    def steps(self):
        return self.units + self.lag * len(self.path) + 1

    def slot(self, u):
        return lax.rem(u, self.slots)

    def scratch(self):
        shapes = []
        for k, stage in enumerate(self.path):
            left = tuple(name for name in self.names[k] if name != stage)
            shapes.append(pltpu.VMEM((self.slots,) + self.shape(self.names[k]), BF16))
            shapes.append(pltpu.VMEM((self.slots,) + self.shape(left), BF16))
            shapes += [pltpu.SemaphoreType.DMA((self.slots,))] * 2
        return shapes

    def bind(self, refs, finish, begin=0):
        self.finish, self.begin = finish, begin
        self.work, self.got, self.sent_sem, self.got_sem = refs[::4], refs[1::4], refs[2::4], refs[3::4]
        self.source = self.work[0]

    def copy(self, k, u):
        mine, partner = pair_of(self.path[k])
        whole = (slice(None),) * self.names[k].index(self.path[k])
        slot = self.slot(u)
        copy = pltpu.make_async_remote_copy(
            src_ref=self.work[k].at[(slot,) + whole + (1 - mine,)],
            dst_ref=self.got[k].at[slot],
            send_sem=self.sent_sem[k].at[slot],
            recv_sem=self.got_sem[k].at[slot],
            device_id=partner,
            device_id_type=pl.DeviceIdType.MESH,
        )
        return copy, (slot,) + whole + (mine,), mine

    def send(self, k, step):
        u = step - self.begin - self.lag * k - 1

        @pl.when((u >= 0) & (u < self.units))
        def _():
            self.copy(k, u)[0].start()

    def take(self, k, step):
        u = step - self.begin - self.lag * (k + 1) - 1

        @pl.when((u >= 0) & (u < self.units))
        def _():
            copy, own, mine = self.copy(k, u)
            copy.wait()
            slot = self.slot(u)
            if self.swap is not None and k == 0:
                self.work[1][slot, mine] = self.work[0][own]
                self.work[1][slot, 1 - mine] = self.got[0][slot]
            elif k == len(self.path) - 1:
                self.finish(u, self.work[k][own] + self.got[k][slot])
            else:
                self.work[k + 1][slot] = self.work[k][own] + self.got[k][slot]


def step_streams(streams, step):
    for stream in streams:
        for k in range(len(stream.path)):
            stream.take(k, step)
            stream.send(k, step)


def line_bits(line):
    return [("z", 1 << i) for i in range(line.bit_length() - 1)]


def greet_all(blk_count, line):
    barrier = pltpu.get_barrier_semaphore()
    z, index = lax.axis_index("dp"), lax.axis_index("blk")
    peers = [(z, lax.rem(index + step, blk_count)) for step in range(1, blk_count)]
    peers += [pair_of(name)[1] for name in line_bits(line)]
    for peer in peers:
        pl.semaphore_signal(barrier, inc=1, device_id=peer, device_id_type=pl.DeviceIdType.MESH)
    pl.semaphore_wait(barrier, len(peers))


def middle_kernel(
    line,
    bits,
    streams,
    units,
    tokens_ref,
    heads_ref,
    w_out_ref,
    gain_ref,
    dy_own_ref,
    dy_got_ref,
    w_gate_ref,
    w_up_ref,
    w_down_ref,
    output_ref,
    mid_ref,
    gain_grad_ref,
    w_grad_ref,
    grad_heads_ref,
    acts_ref,
    gate_out_ref,
    up_out_ref,
    hidden,
    flipped,
    out_sum,
    back_sum,
    gate_grads,
    up_grads,
    part_send,
    part_got,
    low_grad,
    do_send,
    do_got,
    hidden_sem,
    part_sent_sem,
    part_got_sem,
    do_sent_sem,
    do_got_sem,
    *refs,
):
    n = pl.program_id(0)
    steps = pl.num_programs(0)
    z, index = lax.axis_index("dp"), lax.axis_index("blk")
    sibling = pair_of(1)[1]
    own_rows, width = tokens_ref.shape
    rows = 2 * own_rows
    blk_count, tok_count, head_lanes = heads_ref.shape
    chips = blk_count // 2
    chunk = 256
    gate_stream, up_stream, both_stream = streams
    gate_rows = gate_stream.block[0]
    own, other = pl.ds(0, own_rows), pl.ds(own_rows, own_rows)

    def finish_gate(u, value):
        gate_out_ref[:gate_rows, pl.ds(pl.multiple_of(u * FF_TILE, FF_TILE), FF_TILE)] = value

    def finish_up(u, value):
        up_out_ref[:gate_rows, pl.ds(pl.multiple_of(u * FF_TILE, FF_TILE), FF_TILE)] = value

    def finish_both(u, value):
        here = pl.ds(pl.multiple_of(u * FF_TILE, FF_TILE), FF_TILE)
        gate_out_ref[gate_rows:, here] = value[:, :FF_TILE]
        up_out_ref[gate_rows:, here] = value[:, FF_TILE:]

    at = 0
    for stream, finish in zip(streams, (finish_gate, finish_up, finish_both)):
        count = len(stream.scratch())
        stream.bind(refs[at : at + count], finish)
        at += count

    def hidden_copy():
        return pltpu.make_async_remote_copy(
            src_ref=hidden.at[own],
            dst_ref=hidden.at[other],
            send_sem=hidden_sem.at[0],
            recv_sem=hidden_sem.at[1],
            device_id=sibling,
            device_id_type=pl.DeviceIdType.MESH,
        )

    def part_copy(i):
        return pltpu.make_async_remote_copy(
            src_ref=part_send.at[i],
            dst_ref=part_got.at[i],
            send_sem=part_sent_sem.at[i],
            recv_sem=part_got_sem.at[i],
            device_id=sibling,
            device_id_type=pl.DeviceIdType.MESH,
        )

    def do_copy(target, source):
        return pltpu.make_async_remote_copy(
            src_ref=do_send.at[target],
            dst_ref=do_got.at[source],
            send_sem=do_sent_sem.at[target],
            recv_sem=do_got_sem.at[source],
            device_id=(z, target),
            device_id_type=pl.DeviceIdType.MESH,
        )

    def flip(start):
        for r in range(start, start + own_rows, chunk):
            for c in range(0, width, chunk):
                flipped[c : c + chunk, r : r + chunk] = hidden[r : r + chunk, c : c + chunk].T

    @pl.when(n == 0)
    def _():
        greet_all(blk_count, line)
        total = tokens_ref[...].astype(F32)
        for p in range(chips):
            block = jnp.concatenate([heads_ref[2 * p], heads_ref[2 * p + 1]], axis=0)
            total = total + nn_dot(block, w_out_ref[p * head_lanes : (p + 1) * head_lanes, :])
        mid_ref[...] = total
        scale = lax.rsqrt(jnp.mean(total * total, axis=-1, keepdims=True) + EPSILON)
        hidden[own] = (total * scale * gain_ref[...]).astype(BF16)
        hidden_copy().start()
        out_sum[...] = jnp.zeros_like(out_sum)
        back_sum[...] = jnp.zeros_like(back_sum)
        flip(0)

    @pl.when(n == 1)
    def _():
        hidden_copy().wait()
        flip(own_rows)

    step_streams(streams, n - 1)

    @pl.when((n >= 1) & (n <= units))
    def _():
        for m in range(rows // chunk):
            part = slice(m * chunk, (m + 1) * chunk)
            gate = nn_dot(hidden[part, :], w_gate_ref[...])
            up = nn_dot(hidden[part, :], w_up_ref[...])
            at = m * chunk % own_rows
            dy_ref = dy_own_ref if m * chunk < own_rows else dy_got_ref
            pushed = nt_dot(dy_ref[at : at + chunk, :], w_down_ref[...])
            opened = jax.nn.sigmoid(gate)
            silu = gate * opened
            act = (silu * up).astype(BF16)
            gate_grad = (pushed * up * opened * (1.0 + gate * (1.0 - opened))).astype(BF16)
            up_grad = (pushed * silu).astype(BF16)
            acts_ref[:, part] = act.T
            gate_grads[part, :] = gate_grad
            up_grads[part, :] = up_grad
            out_sum[part, :] += nn_dot(act, w_down_ref[...])
            back_sum[part, :] += nt_dot(gate_grad, w_gate_ref[...]) + nt_dot(up_grad, w_up_ref[...])
        u = n - 1
        slot = gate_stream.slot(u)
        each = width // line
        zs = line.bit_length() - 1
        shape = gate_stream.shape(gate_stream.names[0])[zs:-2] + (-1, FF_TILE)
        for m in range(line):
            at = (slot,) + tuple(m >> i & 1 for i in reversed(range(zs)))
            part = slice(m * each, (m + 1) * each)
            gate_part = nn_dot(flipped[part, :], gate_grads[...]).astype(BF16)
            up_part = nn_dot(flipped[part, :], up_grads[...]).astype(BF16)
            gate_part, up_part = gate_part.reshape(shape), up_part.reshape(shape)
            gate_stream.source[at] = gate_part[..., :gate_rows, :]
            up_stream.source[at] = up_part[..., :gate_rows, :]
            both_stream.source[at + (..., slice(0, FF_TILE))] = gate_part[..., gate_rows:, :]
            both_stream.source[at + (..., slice(FF_TILE, None))] = up_part[..., gate_rows:, :]

    @pl.when(n == units)
    def _():
        part_send[0] = back_sum[other].astype(BF16)
        part_copy(0).start()
        part_send[1] = out_sum[other].astype(BF16)
        part_copy(1).start()

    @pl.when(n == units + 1)
    def _():
        part_copy(0).wait()
        values = mid_ref[...]
        scale = lax.rsqrt(jnp.mean(values * values, axis=-1, keepdims=True) + EPSILON)
        normal = values * scale
        back = back_sum[own] + part_got[0].astype(F32)
        gain_grad_ref[...] = jnp.sum(back * normal, axis=0, keepdims=True)
        pushed = back * gain_ref[...]
        inner = jnp.mean(pushed * normal, axis=-1, keepdims=True)
        mid = dy_own_ref[...].astype(F32) + scale * (pushed - normal * inner)
        part_copy(1).wait()
        mid_ref[...] = mid
        low_grad[...] = mid.astype(BF16)
        output_ref[...] = (values + (out_sum[own] + part_got[1].astype(F32))).astype(BF16)

    @pl.when((n > units + 1) & (n <= units + 1 + chips))
    def _():
        p = n - units - 2
        grad = low_grad[...]
        lanes = pl.ds(pl.multiple_of(p * head_lanes, head_lanes), head_lanes)
        send = nt_dot(grad, w_out_ref[lanes, :]).astype(BF16)
        for half in range(2):
            target = 2 * p + half
            do_send[target] = send[half * tok_count : (half + 1) * tok_count]

            @pl.when(target != index)
            def _():
                do_copy(target, index).start()

            @pl.when(target == index)
            def _():
                do_got[target] = send[half * tok_count : (half + 1) * tok_count]

        heads = jnp.concatenate([heads_ref[2 * p], heads_ref[2 * p + 1]], axis=0)
        w_grad_ref[lanes, :] = tn_dot(heads, grad).astype(BF16)

    @pl.when(n == steps - 1)
    def _():
        for other_index in range(blk_count):

            @pl.when(other_index != index)
            def _():
                do_copy(other_index, other_index).wait()

        grad_heads_ref[...] = do_got[...]


def column_streams(line, bits, each, units):
    late = each // 4
    zs = line_bits(line)
    names = zs[::-1] + bits
    return [
        Stream(bits[::-1] + zs, names, (each - late, FF_TILE), LAG, units),
        Stream(bits + zs, names, (each - late, FF_TILE), LAG, units),
        Stream(zs + bits, names, (late, 2 * FF_TILE), LAG, units),
    ]


def middle_layer(line, bits, tokens, heads, w_out, gain, dy_own, dy_got, w_gate, w_up, w_down):
    own_rows, width = tokens.shape
    rows = 2 * own_rows
    blk_count, tok_count, head_lanes = heads.shape
    units = w_gate.shape[1] // 2 // FF_TILE
    chips = line * 2 ** len(bits)
    each = width // chips
    streams = column_streams(line, bits, each, units)
    steps = max([1 + stream.steps() for stream in streams] + [units + 3 + blk_count // 2])

    def keep(shape):
        return pl.BlockSpec(shape, lambda n: (0,) * len(shape), pipeline_mode=pl.Buffered(1))

    def tile(n):
        return jnp.clip(n - 1, 0, units - 1)

    def mine(n):
        return lax.rem(lax.axis_index("blk"), 2) * units + tile(n)

    scratch = [
        pltpu.VMEM((rows, width), BF16),
        pltpu.VMEM((width, rows), BF16),
        pltpu.VMEM((rows, width), F32),
        pltpu.VMEM((rows, width), F32),
        pltpu.VMEM((rows, FF_TILE), BF16),
        pltpu.VMEM((rows, FF_TILE), BF16),
        pltpu.VMEM((2, own_rows, width), BF16),
        pltpu.VMEM((2, own_rows, width), BF16),
        pltpu.VMEM((own_rows, width), BF16),
        pltpu.VMEM(heads.shape, BF16),
        pltpu.VMEM(heads.shape, BF16),
        pltpu.SemaphoreType.DMA((2,)),
        pltpu.SemaphoreType.DMA((2,)),
        pltpu.SemaphoreType.DMA((2,)),
        pltpu.SemaphoreType.DMA((blk_count,)),
        pltpu.SemaphoreType.DMA((blk_count,)),
    ]
    for stream in streams:
        scratch += stream.scratch()
    outs = [
        ((own_rows, width), BF16),
        ((own_rows, width), F32),
        ((1, width), F32),
        (w_out.shape, BF16),
        (heads.shape, BF16),
        ((units * FF_TILE, rows), BF16),
        ((each, units * FF_TILE), BF16),
        ((each, units * FF_TILE), BF16),
    ]
    out_specs = [keep(shape) for shape, unused in outs]
    out_specs[5] = pl.BlockSpec((FF_TILE, rows), lambda n: (tile(n), 0))
    return pl.pallas_call(
        functools.partial(middle_kernel, line, bits, streams, units),
        name="middle",
        grid=(steps,),
        in_specs=[
            keep(tokens.shape),
            keep(heads.shape),
            keep(w_out.shape),
            keep(gain.shape),
            keep(dy_own.shape),
            keep(dy_got.shape),
            pl.BlockSpec((width, FF_TILE), lambda n: (0, mine(n))),
            pl.BlockSpec((width, FF_TILE), lambda n: (0, mine(n))),
            pl.BlockSpec((FF_TILE, width), lambda n: (mine(n), 0)),
        ],
        out_specs=out_specs,
        out_shape=[jax.ShapeDtypeStruct(shape, kind) for shape, kind in outs],
        scratch_shapes=scratch,
        compiler_params=kernel_params(collective_id=6, has_side_effects=True),
    )(tokens, heads, w_out, gain, dy_own, dy_got, w_gate, w_up, w_down)


def back_kernel(
    groups,
    block,
    line,
    bits,
    streams,
    units,
    qkv_ref,
    logs_ref,
    out_ref,
    grad_ref,
    starts_ref,
    dy_own_ref,
    dy_got_ref,
    acts_ref,
    w_out_parts_ref,
    moved_ref,
    down_out_ref,
    w_out_ref,
    queries,
    keys,
    values,
    grads,
    query_grad,
    pair_grad,
    result,
    moved,
    sent_sem,
    got_sem,
    *refs,
):
    size = qkv_ref.shape[1]
    blocks = size // block
    n = pl.program_id(0)
    index = lax.axis_index("blk")
    core = lax.rem(index, 2)

    def move(g, target, source):
        return blk_copy(result.at[g], moved.at[g], sent_sem.at[g], got_sem.at[g], target, source)

    half = streams[0].block[1]

    def finish_low(u, value):
        rows = value.shape[0]
        down_out_ref[pl.ds(pl.multiple_of(u * rows, rows), rows), :half] = value

    def finish_high(u, value):
        rows = value.shape[0]
        down_out_ref[pl.ds(pl.multiple_of(u * rows, rows), rows), half:] = value

    def finish_w_out(u, value):
        w_out_ref[:, pl.ds(pl.multiple_of(u * LANES, LANES), LANES)] = value

    columns = w_out_ref.shape[1] // LANES
    at = 0
    for stream, finish in zip(streams, (finish_low, finish_high, finish_w_out)):
        size_of = len(stream.scratch())
        stream.bind(refs[at : at + size_of], finish)
        at += size_of

    @pl.when(n == 0)
    def _():
        greet_all(blocks, line)

    step_streams(streams, n)

    @pl.when(n == 1)
    def _():
        query_grad[...] = jnp.zeros_like(query_grad)
        pair_grad[...] = jnp.zeros_like(pair_grad)
        for g in range(groups):
            lanes = slice(g * LANES, (g + 1) * LANES)
            key, value = parted(qkv_ref[g, :, LANES:])
            keys[g, :, :LANES] = key
            keys[g, :, LANES:] = minus_three(size)
            values[g, :, :LANES] = value
            values[g, :, LANES:] = minus_three(size)

            def fill(i, carry):
                at = pl.multiple_of(i * block, block)
                to = pl.multiple_of(i * 2 * block, 2 * block)
                queries[g, pl.ds(to, 2 * block), :LANES] = stacked_heads(qkv_ref[g, pl.ds(at, block), :LANES])
                queries[g, pl.ds(to, 2 * block), LANES:] = logs_ref[g, pl.ds(to, 2 * block), :]
                grad = stacked_heads(grad_ref[pl.ds(at, block), lanes])
                mean = stacked_heads(out_ref[pl.ds(at, block), lanes])
                delta = jnp.sum(grad.astype(F32) * mean.astype(F32), axis=1, keepdims=True)
                grads[g, pl.ds(to, 2 * block), :LANES] = grad
                grads[g, pl.ds(to, 2 * block), LANES:] = in_three(delta)
                return carry

            lax.fori_loop(0, blocks, fill, 0)

    @pl.when(n < units)
    def _():
        acts = acts_ref[...].reshape(-1, acts_ref.shape[-1])
        rows = dy_own_ref.shape[0]
        made = nn_dot(acts[:, :rows], dy_own_ref[...]) + nn_dot(acts[:, rows:], dy_got_ref[...])
        made = made.astype(BF16)
        for i, stream in enumerate(streams[:2]):
            shape = stream.shape(stream.names[0])[1:]
            for side in range(2):
                at = (2 * side + i) * half
                stream.source[stream.slot(n), side] = made[:, at : at + half].reshape(shape)

    @pl.when(n < columns)
    def _():
        stream = streams[2]
        stream.source[stream.slot(n)] = w_out_parts_ref[...].reshape(stream.shape(stream.names[0]))

    row = lax.broadcasted_iota(jnp.int32, (block, 2 * block), 0)
    column = lax.broadcasted_iota(jnp.int32, (block, 2 * block), 1) % block

    pairs = (blocks + 1) * (blocks // 2)
    each = ATTEND_PAIRS
    rounds = groups * pairs // each

    @pl.when((n >= 1) & (n <= rounds))
    def _():
        def pair(at, carry):
            number = (n - 1) * each + at
            g = number // pairs
            place = lax.rem(number, pairs)
            turn = place // (blocks // 2)
            m = lax.rem(place, blocks // 2)
            late = (turn + m) // blocks
            j = m + late * (blocks - 1 - 2 * m)
            i = (1 - late) * (m + turn) + late * (turn - 1)
            key_at = pl.multiple_of(j * block, block)
            at = pl.multiple_of(i * 2 * block, 2 * block)
            key_rows = pl.ds(key_at, block)
            stack = pl.ds(at, 2 * block)
            allowed = (row >= starts_ref[:, stack] - key_at) & (row - column <= (i - j) * block)
            query = queries[g, stack, :]
            grad = grads[g, stack, :]
            key = keys[g, key_rows, :]
            scores = nt_dot(key, query)
            probs = jnp.exp2(jnp.where(allowed, scores, MASKED))
            pushed = (probs * nt_dot(values[g, key_rows, :], grad)).astype(BF16)
            pair_grad[g, key_rows, LANES:] += nn_dot(probs.astype(BF16), grad[:, :LANES])
            pair_grad[g, key_rows, :LANES] += nn_dot(pushed, query[:, :LANES])
            query_grad[g, stack, :] += tn_dot(pushed, key[:, :LANES])
            return carry

        lax.fori_loop(0, each, pair, 0, unroll=True)

    for g in range(groups):

        @pl.when(n == (g + 1) * rounds // groups + 1)
        def _():
            low = low_lanes((block, LANES))

            def finish(i, carry):
                at = pl.multiple_of(i * block, block)
                to = pl.multiple_of(i * 2 * block, 2 * block)
                here = pl.ds(at, block)
                first = query_grad[g, pl.ds(to, block), :]
                second = query_grad[g, pl.ds(to + block, block), :]
                joined = jnp.where(low, first, second) * HEAD_DIM ** (-0.5)
                result[g, i, :, :LANES] = joined.astype(BF16)
                key = pair_grad[g, here, :LANES] * (1.0 / LOG2_E)
                value = pair_grad[g, here, LANES:]
                key = key + pltpu.roll(key, HEAD_DIM, 1)
                value = value + pltpu.roll(value, HEAD_DIM, 1)
                result[g, i, :, LANES:] = jnp.where(low, key, value).astype(BF16)
                return carry

            lax.fori_loop(0, blocks, finish, 0)
            for step in range(blocks - 1, 0, -1):
                move(g, lax.rem(index + step, blocks), index).start()
            moved[g, index] = result[g, index]

    @pl.when(n == pl.num_programs(0) - 1)
    def _():
        for g in range(groups):
            for step in range(1, blocks):
                other = lax.rem(index + step, blocks)
                move(g, other, other).wait()
            moved_ref[:, :, 2 * g * LANES : 2 * (g + 1) * LANES] = moved[g]


def back(line, bits, qkv, logs, out, grad, starts, block, dy_own, dy_got, acts, w_out_parts):
    groups, size, width = qkv.shape
    model = dy_own.shape[1]
    rows = acts.shape[1]
    units = acts.shape[0] // FF_TILE
    chips = line * 2 ** len(bits)
    down_rows = acts.shape[0] // (chips // 2)
    down_each = down_rows // units
    w_rows = w_out_parts.shape[0] // chips // 2
    columns = w_out_parts.shape[1] // LANES
    zs = line_bits(line)
    names = [1] + zs[-2::-1] + bits
    streams = [
        Stream([1] + zs + bits, names, (down_each, model // 4), LAG, units, swap=zs[-1]),
        Stream([1] + bits[::-1] + zs, names, (down_each, model // 4), LAG, units, swap=zs[-1]),
        Stream([1] + bits + zs, zs[::-1] + bits + [1], (w_rows, LANES), LAG, columns),
    ]
    steps = max(
        [stream.steps() for stream in streams]
        + [groups * (size // block + 1) * (size // block // 2) // ATTEND_PAIRS + 3]
    )

    def keep(shape):
        return pl.BlockSpec(shape, lambda n: (0,) * len(shape), pipeline_mode=pl.Buffered(1))

    acts = acts.reshape(chips // 2, down_rows, rows)
    scratch = [
        pltpu.VMEM((groups, 2 * size, 2 * LANES), BF16),
        pltpu.VMEM((groups, size, 2 * LANES), BF16),
        pltpu.VMEM((groups, size, 2 * LANES), BF16),
        pltpu.VMEM((groups, 2 * size, 2 * LANES), BF16),
        pltpu.VMEM((groups, 2 * size, LANES), F32),
        pltpu.VMEM((groups, size, 2 * LANES), F32),
        pltpu.VMEM((groups, size // block, block, 2 * LANES), BF16),
        pltpu.VMEM((groups, size // block, block, 2 * LANES), BF16),
        pltpu.SemaphoreType.DMA((groups, size // block)),
        pltpu.SemaphoreType.DMA((groups, size // block)),
    ]
    for stream in streams:
        scratch += stream.scratch()

    outs = [
        (size // block, block, groups * width),
        (down_rows, model // 2),
        (w_rows, w_out_parts.shape[1]),
    ]
    return pl.pallas_call(
        functools.partial(back_kernel, groups, block, line, bits, streams, units),
        name="back",
        grid=(steps,),
        in_specs=[
            keep(qkv.shape),
            keep(logs.shape),
            keep(out.shape),
            keep(grad.shape),
            keep(starts.shape),
            keep(dy_own.shape),
            keep(dy_got.shape),
            pl.BlockSpec(
                (chips // 2, down_each, rows), lambda n: (0, jnp.minimum(n, units - 1), 0)
            ),
            pl.BlockSpec((w_out_parts.shape[0], LANES), lambda n: (0, jnp.minimum(n, columns - 1))),
        ],
        out_specs=[keep(shape) for shape in outs],
        out_shape=[jax.ShapeDtypeStruct(shape, BF16) for shape in outs],
        scratch_shapes=scratch,
        compiler_params=kernel_params(collective_id=4, has_side_effects=True),
    )(qkv, logs, out, grad, starts, dy_own, dy_got, acts, w_out_parts)


def sum_gains(rounds, n, first, gains, gains_got, sent_sem, got_sem):
    for r, partner in enumerate(rounds):

        def copy():
            return pltpu.make_async_remote_copy(
                src_ref=gains.at[r],
                dst_ref=gains_got.at[r],
                send_sem=sent_sem.at[r],
                recv_sem=got_sem.at[r],
                device_id=partner,
                device_id_type=pl.DeviceIdType.MESH,
            )

        @pl.when(n == first + r + 1)
        def _():
            copy().wait()
            gains[r + 1] = gains[r] + gains_got[r]

    for r, partner in enumerate(rounds):

        @pl.when(n == first + r)
        def _():
            pltpu.make_async_remote_copy(
                src_ref=gains.at[r],
                dst_ref=gains_got.at[r],
                send_sem=sent_sem.at[r],
                recv_sem=got_sem.at[r],
                device_id=partner,
                device_id_type=pl.DeviceIdType.MESH,
            ).start()


def finish_kernel(
    line,
    bits,
    streams,
    units,
    got_ref,
    proj_ref,
    hidden_ref,
    tokens_ref,
    mid_ref,
    gain_ref,
    wq_ref,
    wk_ref,
    wv_ref,
    head_gains_ref,
    cos_ref,
    sin_ref,
    ffn_gain_ref,
    gate_ref,
    up_ref,
    down_ref,
    input_ref,
    gains_ref,
    gq_ref,
    gk_ref,
    gv_ref,
    gate_out_ref,
    up_out_ref,
    down_out_ref,
    total,
    gains,
    gains_got,
    gains_sent_sem,
    gains_got_sem,
    half_got,
    down_got,
    half_sent_sem,
    half_got_sem,
    *refs,
):
    n = pl.program_id(0)
    z, index = lax.axis_index("dp"), lax.axis_index("blk")
    core, sibling = pair_of(1)
    steps = pl.num_programs(0)
    query_stream, pair_stream = streams
    q_width = wq_ref.shape[1]

    def finish_query(u, value):
        gq_ref[:, pl.ds(pl.multiple_of(u * q_width, q_width), q_width)] = value

    def finish_pair(u, value):
        here = pl.ds(pl.multiple_of(u * LANES, LANES), LANES)
        gk_ref[:, here] = value[:, :LANES]
        gv_ref[:, here] = value[:, LANES:]

    at = 0
    for stream, finish in ((query_stream, finish_query), (pair_stream, finish_pair)):
        count = len(stream.scratch())
        stream.bind(refs[at : at + count], finish)
        at += count

    rounds = [pair_of(name)[1] for name in [1] + list(bits) + line_bits(line)]

    rows = gate_ref.shape[0] // 2
    columns = gate_ref.shape[1]
    down_rows = down_ref.shape[0] // 2
    give = pl.ds(pl.multiple_of((1 - core) * rows, rows), rows)
    keep = pl.ds(pl.multiple_of(core * rows, rows), rows)
    down_give = pl.ds(pl.multiple_of((1 - core) * down_rows, down_rows), down_rows)
    down_keep = pl.ds(pl.multiple_of(core * down_rows, down_rows), down_rows)

    def half_copies():
        sources = (gate_ref.at[give, :], up_ref.at[give, :], down_ref.at[down_give, :])
        targets = (half_got.at[0], half_got.at[1], down_got)
        return [
            pltpu.make_async_remote_copy(
                src_ref=source,
                dst_ref=target,
                send_sem=half_sent_sem.at[i],
                recv_sem=half_got_sem.at[i],
                device_id=sibling,
                device_id_type=pl.DeviceIdType.MESH,
            )
            for i, (source, target) in enumerate(zip(sources, targets))
        ]

    @pl.when(n == 0)
    def _():
        barrier = pltpu.get_barrier_semaphore()
        for peer in rounds:
            pl.semaphore_signal(barrier, inc=1, device_id=peer, device_id_type=pl.DeviceIdType.MESH)
        pl.semaphore_wait(barrier, len(rounds))
        for copy in half_copies():
            copy.start()
        total[...] = jnp.zeros_like(total)
        gains[0] = jnp.zeros_like(gains[0])

    @pl.when(n == units)
    def _():
        for copy in half_copies():
            copy.wait()
        own = pl.ds(pl.multiple_of(core * columns, LANES), columns)
        other = pl.ds(pl.multiple_of((1 - core) * columns, LANES), columns)
        gate_out_ref[:, own] = gate_ref[keep, :]
        gate_out_ref[:, other] = half_got[0]
        up_out_ref[:, own] = up_ref[keep, :]
        up_out_ref[:, other] = half_got[1]
        half = down_ref.shape[1]
        down_out_ref[:, pl.ds(pl.multiple_of(core * half, LANES), half)] = down_ref[down_keep, :]
        down_out_ref[:, pl.ds(pl.multiple_of((1 - core) * half, LANES), half)] = down_got[...]

    step_streams(streams, n)
    sum_gains(rounds, n, units, gains, gains_got, gains_sent_sem, gains_got_sem)

    @pl.when(n == steps - 1)
    def _():
        gains_ref[...] = gains[len(rounds)]

    @pl.when(n < units)
    def _():
        hidden = hidden_ref[...]

        q_gain, k_gain = head_gains_ref[0:1, :], head_gains_ref[1:2, :]

        def got_lanes(lane):
            return jnp.concatenate(
                [got_ref[0, :, lane : lane + LANES], got_ref[1, :, lane : lane + LANES]], axis=0
            ).astype(F32)

        def back(got, lane, head_gain, place):
            turned = got * cos_ref[...] - half_partner(got) * sin_ref[...]
            block = proj_ref[0, :, lane : lane + LANES]
            scale = lax.rsqrt(head_means(block * block) + EPSILON)
            normal = block * scale
            gains[0, place : place + 1, :] += jnp.sum(turned * normal, axis=0, keepdims=True)
            pushed = turned * head_gain
            inner = head_means(pushed * normal)
            return (scale * (pushed - normal * inner)).astype(BF16)

        width = tokens_ref.shape[1]
        lines = width // LANES
        query = jnp.concatenate(
            [back(got_lanes(2 * at), at, q_gain, 2 * lines) for at in range(0, q_width, LANES)],
            axis=1,
        )
        first, second = got_lanes(LANES), got_lanes(3 * LANES)
        low = low_lanes(first.shape)
        key = jnp.where(low, first, pltpu.roll(second, HEAD_DIM, 1))
        key = back(key, q_width, k_gain, 2 * lines + 1)
        value = jnp.where(low, pltpu.roll(first, HEAD_DIM, 1), second).astype(BF16)
        for stream, part in ((query_stream, query), (pair_stream, jnp.concatenate([key, value], axis=1))):
            shape = stream.shape(stream.names[0])
            stream.source[stream.slot(n)] = tn_dot(hidden, part).astype(BF16).reshape(shape)

        total[...] += (
            nt_dot(query, wq_ref[...]) + nt_dot(key, wk_ref[...]) + nt_dot(value, wv_ref[...])
        )

        @pl.when(n == units - 1)
        def _():
            inputs = tokens_ref[...].astype(F32)
            scale = lax.rsqrt(jnp.mean(inputs * inputs, axis=-1, keepdims=True) + EPSILON)
            normal = inputs * scale
            grad = total[...]
            gain_grad = jnp.sum(grad * normal, axis=0, keepdims=True)
            for i in range(lines):
                here = slice(i * LANES, (i + 1) * LANES)
                gains[0, i : i + 1, :] = gain_grad[:, here]
                gains[0, lines + i : lines + i + 1, :] = ffn_gain_ref[:, here]
            pushed = grad * gain_ref[...]
            inner = jnp.mean(pushed * normal, axis=-1, keepdims=True)
            input_ref[...] = (mid_ref[...] + scale * (pushed - normal * inner)).astype(BF16)


def finish(
    line,
    bits,
    got,
    proj,
    hidden,
    tokens,
    mid,
    gain,
    wq,
    wk,
    wv,
    head_gains,
    cosine,
    sine,
    ffn_gain,
    gate_sum,
    up_sum,
    down_sum,
):
    rows, width = tokens.shape
    count, half, lanes = got.shape
    units = count // 2
    q_width = wq.shape[1] // units
    chips = line * 2 ** len(bits)
    mine = width // chips // 2
    zs = line_bits(line)
    names = zs[::-1] + bits + [1]
    streams = [
        Stream([1] + bits[::-1] + zs, names, (mine, q_width), LAST_LAG, units),
        Stream([1] + bits + zs, names, (mine, 2 * LANES), LAST_LAG, units),
    ]
    rounds = 1 + len(bits) + (line - 1).bit_length()
    steps = max([stream.steps() for stream in streams] + [units + rounds + 2])
    gain_rows = -(-(2 * width // LANES + 2) // 8) * 8
    half_rows = gate_sum.shape[0] // 2
    down_rows = down_sum.shape[0] // 2
    columns = gate_sum.shape[1]

    def keep(shape):
        return pl.BlockSpec(shape, lambda n: (0,) * len(shape), pipeline_mode=pl.Buffered(1))

    def at(n):
        return jnp.minimum(n, units - 1)

    scratch = [
        pltpu.VMEM((rows, width), F32),
        pltpu.VMEM((rounds + 1, gain_rows, LANES), F32),
        pltpu.VMEM((rounds, gain_rows, LANES), F32),
        pltpu.SemaphoreType.DMA((rounds,)),
        pltpu.SemaphoreType.DMA((rounds,)),
        pltpu.VMEM((2, half_rows, columns), BF16),
        pltpu.VMEM((down_rows, down_sum.shape[1]), BF16),
        pltpu.SemaphoreType.DMA((3,)),
        pltpu.SemaphoreType.DMA((3,)),
    ]
    for stream in streams:
        scratch += stream.scratch()
    outs = [
        ((rows, width), BF16),
        ((gain_rows, LANES), F32),
        ((mine, wq.shape[1]), BF16),
        ((mine, wk.shape[1]), BF16),
        ((mine, wv.shape[1]), BF16),
        ((half_rows, 2 * columns), BF16),
        ((half_rows, 2 * columns), BF16),
        ((down_rows, 2 * down_sum.shape[1]), BF16),
    ]
    return pl.pallas_call(
        functools.partial(finish_kernel, line, bits, streams, units),
        name="finish",
        grid=(steps,),
        in_specs=[
            pl.BlockSpec((2, half, lanes), lambda n: (at(n), 0, 0)),
            pl.BlockSpec((1, rows, q_width + LANES), lambda n: (at(n), 0, 0)),
            keep((rows, width)),
            keep((rows, width)),
            keep((rows, width)),
            keep((1, width)),
            pl.BlockSpec((width, q_width), lambda n: (0, at(n))),
            pl.BlockSpec((width, LANES), lambda n: (0, at(n))),
            pl.BlockSpec((width, LANES), lambda n: (0, at(n))),
            keep((2, LANES)),
            keep((rows, LANES)),
            keep((rows, LANES)),
            keep((1, width)),
            keep(gate_sum.shape),
            keep(up_sum.shape),
            keep(down_sum.shape),
        ],
        out_specs=[keep(shape) for shape, unused in outs],
        out_shape=[jax.ShapeDtypeStruct(shape, kind) for shape, kind in outs],
        scratch_shapes=scratch,
        compiler_params=kernel_params(collective_id=5, has_side_effects=True),
    )(
        got,
        proj,
        hidden,
        tokens,
        mid,
        gain,
        wq,
        wk,
        wv,
        head_gains,
        cosine,
        sine,
        ffn_gain,
        gate_sum,
        up_sum,
        down_sum,
    )


def widen_kernel(count, gains_ref, *refs):
    for source, target in zip(refs[:count], refs[count : 2 * count]):
        target[...] = source[...].astype(F32)
    attn_ref, ffn_ref, query_ref, key_ref = refs[2 * count :]
    lines = attn_ref.shape[0]
    attn_ref[...] = gains_ref[:lines, :]
    ffn_ref[...] = gains_ref[lines : 2 * lines, :]
    both = gains_ref[2 * lines : 2 * lines + 2, :]
    both = (both + pltpu.roll(both, HEAD_DIM, 1))[:, :HEAD_DIM]
    query_ref[...] = both[0:1]
    key_ref[...] = both[1:2]


def widen(gains, lines, parts):
    shapes = [part.shape for part in parts] + [(lines, LANES)] * 2 + [(1, HEAD_DIM)] * 2
    return pl.pallas_call(
        functools.partial(widen_kernel, len(parts)),
        name="widen",
        out_shape=[jax.ShapeDtypeStruct(shape, F32) for shape in shapes],
        compiler_params=kernel_params(),
    )(gains, *parts)


def flip_pairs(count, bit):
    return [(i, i ^ bit) for i in range(count)]


def swap_core(block, blk_count):
    return lax.ppermute(block, "blk", flip_pairs(blk_count, 1))


def fast_local(
    dp_count,
    blk_count,
    tokens,
    doc_lengths,
    g_attn,
    w_query,
    w_key,
    w_value,
    q_gain,
    k_gain,
    w_out,
    g_ffn,
    w_gate,
    w_up,
    w_down,
    cotangent,
):
    row_count, tok_count, width = tokens.shape
    rows = row_count * tok_count
    chips = blk_count // 2
    size = tok_count * blk_count
    index = lax.axis_index("blk")
    core = index % 2
    bits = []
    bit = blk_count // 2
    while bit > 1:
        bits.append(bit)
        bit //= 2
    chip_dims = (dp_count,) + (2,) * len(bits)
    all_chips = dp_count * chips
    which = jnp.arange(doc_lengths.shape[1])
    ends = jnp.sum(jnp.where(which[:, None] <= which[None, :], doc_lengths[:, :, None], 0), axis=1)
    places = index * tok_count + jnp.arange(tok_count, dtype=jnp.int32)[None]
    begins = jnp.max(jnp.where(places[:, :, None] >= ends[:, None, :], ends[:, None, :], 0), axis=2)
    positions = (places - begins).reshape(rows, 1).astype(F32)
    half_head = HEAD_DIM // 2
    lane = jnp.arange(LANES)
    freqs = ROPE_BASE ** (-(lane % half_head).astype(F32) / half_head)
    angles = positions * freqs
    cosine = jnp.cos(angles)
    sine = jnp.sin(angles) * jnp.where(lane % HEAD_DIM < half_head, -1.0, 1.0)
    head_gains = jnp.concatenate([q_gain, q_gain, k_gain, k_gain]).reshape(2, LANES)
    all_places = jnp.arange(size, dtype=jnp.int32)
    own_ends = lax.dynamic_slice_in_dim(ends, core, 1, axis=0)
    starts = jnp.max(jnp.where(all_places[:, None] >= own_ends, own_ends, 0), axis=1)
    starts_two = jnp.broadcast_to(
        starts.reshape(blk_count, 1, tok_count), (blk_count, 2, tok_count)
    ).reshape(1, 2 * size)
    flat = tokens.reshape(rows, width)
    grad_own = cotangent.reshape(rows, width)
    grad_got = swap_core(grad_own, blk_count)

    hidden_in, proj, qkv, attended, logs, heads = forward(
        flat,
        g_attn[None],
        w_query,
        w_key,
        w_value,
        head_gains,
        cosine,
        sine,
        starts_two,
    )
    output, mid, ffn_gain_grad, w_out_parts, grad_heads, acts, gate_sum, up_sum = middle_layer(
        dp_count,
        bits,
        flat,
        heads,
        w_out,
        g_ffn[None],
        grad_own,
        grad_got,
        w_gate,
        w_up,
        w_down,
    )
    got, down_sum, w_out_sum = back(
        dp_count,
        bits,
        qkv,
        logs,
        attended.reshape(size, -1),
        grad_heads.reshape(size, -1),
        starts_two,
        tok_count,
        grad_own,
        grad_got,
        acts,
        w_out_parts,
    )
    input_grad, gains, *sums = finish(
        dp_count,
        bits,
        got,
        proj,
        hidden_in,
        flat,
        mid,
        g_attn[None],
        w_query,
        w_key,
        w_value,
        head_gains,
        cosine,
        sine,
        ffn_gain_grad,
        gate_sum,
        up_sum,
        down_sum,
    )
    *sums, gain_attn, gain_ffn, gain_query, gain_key = widen(gains, width // LANES, sums + [w_out_sum])
    grad_w_query, grad_w_key, grad_w_value, grad_w_gate, grad_w_up, grad_w_down, grad_w_out = sums
    gain_attn, gain_ffn = gain_attn.reshape(width), gain_ffn.reshape(width)
    gain_query, gain_key = gain_query[0], gain_key[0]
    return (
        output.reshape(tokens.shape),
        input_grad.reshape(tokens.shape),
        gain_attn,
        grad_w_query,
        grad_w_key,
        grad_w_value,
        gain_query,
        gain_key,
        grad_w_out,
        gain_ffn,
        grad_w_gate,
        grad_w_up,
        grad_w_down,
    )


def fits(mesh):
    blk_count = mesh.shape["blk"]
    chips = blk_count // 2
    line = mesh.shape["dp"]
    power = blk_count & (blk_count - 1) == 0 and line & (line - 1) == 0
    return power and blk_count > 2 and line > 1 and (KV_HEADS * HEAD_DIM) == chips * LANES


def solution(mesh):
    if fits(mesh):
        body = functools.partial(fast_local, mesh.shape["dp"], mesh.shape["blk"])
    else:
        body = local
    return jax.shard_map(
        body,
        mesh=mesh,
        in_specs=(
            P("dp", "blk", None),
            P("dp", None),
            P(),
            P(),
            P(),
            P(),
            P(),
            P(),
            P(),
            P(),
            P(),
            P(),
            P(),
            P("dp", "blk", None),
        ),
        out_specs=(
            P("dp", "blk", None),
            P("dp", "blk", None),
            P(),
            P(("dp", "blk"), None),
            P(("dp", "blk"), None),
            P(("dp", "blk"), None),
            P(),
            P(),
            P(("dp", "blk"), None),
            P(),
            P(("dp", "blk"), None),
            P(("dp", "blk"), None),
            P(("dp", "blk"), None),
        ),
        check_vma=False,
    )
```
